32 devices in a mesh: dp: 2 (over y), fsdp: 4 (over z), ctx: 4 (over x, core).
Axes of the slice: x: 2, y: 2, z: 4, core: 2. Of those that a mesh axis runs over, the one named last changes fastest.
Arguments:
- inputs: bfloat16 [32, 1024, 1088], P(('dp', 'fsdp'), 'ctx'), may hold values from -6 to 6
- cotangent: bfloat16 [32, 1024, 1088], P(('dp', 'fsdp'), 'ctx'), may hold values from -6 to 6
- first_gain: bfloat16 [1088], P('fsdp'), may hold values from 0.099609375 to 1.8984375
- first_shift: bfloat16 [1088], P('fsdp'), may hold values from -3 to 3
- project_in: bfloat16 [1088, 3264], P('fsdp'), may hold values from -0.1875 to 0.1875
- query_bias: bfloat16 [1088], P('fsdp'), may hold values from -3 to 3
- value_bias: bfloat16 [1088], P('fsdp'), may hold values from -3 to 3
- project_out: bfloat16 [1088, 1088], P('fsdp'), may hold values from -1 to 1
- output_bias: bfloat16 [1088], P('fsdp'), may hold values from -3 to 3
- second_gain: bfloat16 [1088], P('fsdp'), may hold values from 0.099609375 to 1.8984375
- second_shift: bfloat16 [1088], P('fsdp'), may hold values from -3 to 3
- up_weight: bfloat16 [1088, 4352], P('fsdp'), may hold values from -0.1875 to 0.1875
- up_bias: bfloat16 [4352], P('fsdp'), may hold values from -3 to 3
- down_weight: bfloat16 [4352, 1088], P('fsdp'), may hold values from -0.09375 to 0.09375
- down_bias: bfloat16 [1088], P('fsdp'), may hold values from -3 to 3
Outputs:
- outputs: bfloat16 [32, 1024, 1088], P(('dp', 'fsdp'), 'ctx')
- input_gradient: float32 [32, 1024, 1088], P(('dp', 'fsdp'), 'ctx')
- first_gain_gradient: float32 [1088], P('fsdp')
- first_shift_gradient: float32 [1088], P('fsdp')
- project_in_gradient: float32 [1088, 3264], P('fsdp')
- query_bias_gradient: float32 [1088], P('fsdp')
- value_bias_gradient: float32 [1088], P('fsdp')
- project_out_gradient: float32 [1088, 1088], P('fsdp')
- output_bias_gradient: float32 [1088], P('fsdp')
- second_gain_gradient: float32 [1088], P('fsdp')
- second_shift_gradient: float32 [1088], P('fsdp')
- up_weight_gradient: float32 [1088, 4352], P('fsdp')
- up_bias_gradient: float32 [4352], P('fsdp')
- down_weight_gradient: float32 [4352, 1088], P('fsdp')
- down_bias_gradient: float32 [1088], P('fsdp')
The draws below stay inside these ranges and needn't reach their ends.
All inputs are finite; a program needn't handle non-finite values.
Results may differ from the reference program's by a relative error of at most 0.017.
Values may be sent and summed in bfloat16 or wider, within the bound.
No kernel may reach another device: no remote copies, remote signals or barrier semaphores. Data moves between devices by JAX's collectives and lax.ppermute only.
A program may use at most 320 MiB of HBM per device.

```python
import jax
import jax.numpy as jnp
from jax import lax

D = 1088
HEADS = 17
HEAD_DIM = 64
FF = 4352
LENGTH = 1024
SEQUENCES = 32


def steps_of(own_key, dims, cuts, smallest, high):
    def one(position, shards_of):
        heights = jax.random.uniform(jax.random.fold_in(jax.random.fold_in(own_key, 6), position), (shards_of,), jnp.float32, smallest / len(cuts), high / len(cuts))
        return jnp.repeat(jnp.exp(heights), dims[position] // shards_of).reshape((-1,) + (1,) * (len(dims) - position - 1))

    level = one(*cuts[0])
    for cut in cuts[1:]:
        level = level * one(*cut)
    return level


def bell_draw(stream_key, extent, scale, bound, split=(), held_as=jnp.bfloat16):
    level = steps_of(stream_key, extent, split, -0.22, 0.18) if split else 1.0
    values = jax.random.normal(stream_key, extent, jnp.float32) * scale * level
    return jnp.minimum(jnp.maximum(values, -bound), bound).astype(held_as)


def setup_inputs(seed: int = 0) -> dict:
    key_of = jax.random.split(jax.random.key(seed), 16)
    inputs = bell_draw(key_of[0], (SEQUENCES, LENGTH, D), 1.0, 6.0, ((0, 8), (1, 4)))
    cotangent = bell_draw(key_of[1], (SEQUENCES, LENGTH, D), 1.0, 6.0, ((0, 8), (1, 4)))
    first_gain = jnp.clip(1.0 + 0.18 * jax.random.normal(key_of[2], (D,), jnp.float32), 0.099609375, 1.8984375).astype(jnp.bfloat16)
    first_shift = bell_draw(key_of[3], (D,), 0.5, 3.0, ((0, 4),))
    project_in = bell_draw(key_of[4], (D, 3 * D), D ** -0.5, 0.1875, ((0, 4),))
    query_bias = bell_draw(key_of[5], (D,), 0.5, 3.0, ((0, 4),))
    value_bias = bell_draw(key_of[6], (D,), 0.5, 3.0, ((0, 4),))
    project_out = bell_draw(key_of[7], (D, D), (D // 32) ** -0.5, 1.0, ((0, 4),))
    output_bias = bell_draw(key_of[8], (D,), 0.5, 3.0, ((0, 4),))
    second_gain = jnp.clip(1.0 + 0.18 * jax.random.normal(key_of[9], (D,), jnp.float32), 0.099609375, 1.8984375).astype(jnp.bfloat16)
    second_shift = bell_draw(key_of[10], (D,), 0.5, 3.0, ((0, 4),))
    up_weight = bell_draw(key_of[11], (D, FF), D ** -0.5, 0.1875, ((0, 4),))
    up_bias = bell_draw(key_of[12], (FF,), 0.5, 3.0, ((0, 4),))
    down_weight = bell_draw(key_of[13], (FF, D), FF ** -0.5, 0.09375, ((0, 4),))
    down_bias = bell_draw(key_of[14], (D,), 0.5, 3.0, ((0, 4),))
    return dict(inputs=inputs, cotangent=cotangent, first_gain=first_gain, first_shift=first_shift, project_in=project_in, query_bias=query_bias, value_bias=value_bias, project_out=project_out, output_bias=output_bias, second_gain=second_gain, second_shift=second_shift, up_weight=up_weight, up_bias=up_bias, down_weight=down_weight, down_bias=down_bias)


@jax.custom_vjp
def low(v):
    return lax.optimization_barrier(v.astype(jnp.bfloat16)).astype(jnp.float32)

@jax.custom_vjp
def low_back(v):
    return v

def low_keep(v):
    return (low(v), None)

def low_pass(kept, grad):
    return (grad,)

def back_keep(v):
    return (v, None)

def back_low(kept, grad):
    return (low(grad),)
low.defvjp(low_keep, low_pass)
low_back.defvjp(back_keep, back_low)
epsilon = 1e-05
highest = lax.Precision.HIGHEST

def layer_norm(values, gain, shift):
    centred = values - lax.optimization_barrier(jnp.mean(values, axis=-1, keepdims=True))
    spread = lax.optimization_barrier(jnp.mean(centred * centred, axis=-1, keepdims=True))
    return centred * lax.rsqrt(spread + epsilon) * gain + shift

def product(left, right):
    return jnp.dot(left, right, precision=highest)

def attend_one(triple):
    queries, key_rows, value_rows = triple
    scores = jnp.einsum('qhd,khd->hqk', queries, key_rows, precision=highest) * HEAD_DIM ** (-0.5)
    scores = low_back(scores)
    seq_length = queries.shape[0]
    causal = jnp.arange(seq_length)[:, None] >= jnp.arange(seq_length)[None, :]
    scores = jnp.where(causal[None], scores, -1e+30)
    weights = low(jax.nn.softmax(scores, axis=-1))
    return jnp.einsum('hqk,khd->qhd', weights, value_rows, precision=highest)

def block(params, inputs):
    first_gain, first_shift, project_in, query_bias, value_bias, project_out, output_bias, second_gain, second_shift, up_weight, up_bias, down_weight, down_bias = params
    seq_count, seq_length, model_width = inputs.shape
    flat_rows = inputs.reshape(seq_count * seq_length, model_width)
    normed = low(layer_norm(flat_rows, first_gain, first_shift))
    projected = product(normed, project_in)
    queries = low(low_back(projected[:, :model_width] + query_bias))
    key_rows = low(low_back(projected[:, model_width:2 * model_width]))
    value_rows = low(low_back(projected[:, 2 * model_width:] + value_bias))
    head_shape = (seq_count, seq_length, HEADS, HEAD_DIM)
    attended = lax.map(jax.checkpoint(attend_one), (queries.reshape(head_shape), key_rows.reshape(head_shape), value_rows.reshape(head_shape)))
    attended = low(low_back(attended.reshape(seq_count * seq_length, model_width)))
    branch = low_back(product(attended, project_out) + output_bias)
    middle = flat_rows + branch
    normed_two = low(layer_norm(middle, second_gain, second_shift))
    hidden = low_back(product(normed_two, up_weight) + up_bias)
    active = low(jax.nn.gelu(hidden, approximate=True))
    result = middle + low_back(product(active, down_weight) + down_bias)
    return result.reshape(seq_count, seq_length, model_width)

def reference(inputs, cotangent, first_gain, first_shift, project_in, query_bias, value_bias, project_out, output_bias, second_gain, second_shift, up_weight, up_bias, down_weight, down_bias):
    params = tuple((weight.astype(jnp.float32) for weight in (first_gain, first_shift, project_in, query_bias, value_bias, project_out, output_bias, second_gain, second_shift, up_weight, up_bias, down_weight, down_bias)))
    groups = inputs.shape[0] // 4
    input_groups = inputs.astype(jnp.float32).reshape(groups, 4, LENGTH, D)
    cot_groups = cotangent.astype(jnp.float32).reshape(groups, 4, LENGTH, D)

    def one_group(totals, pair):
        group_in, group_cot = pair
        result, pull = jax.vjp(block, params, group_in)
        param_grads, input_grads = pull(group_cot)
        totals = tuple((total + grad for total, grad in zip(totals, param_grads)))
        return (totals, (result.astype(jnp.bfloat16), input_grads))
    zeros_all = tuple((jnp.zeros(weight.shape, jnp.float32) for weight in params))
    totals, (results, input_grads) = lax.scan(one_group, zeros_all, (input_groups, cot_groups))
    gain_one, shift_one, in_grad, qbias_grad, vbias_grad, out_grad, obias_grad, gain_two, shift_two, upw_grad, upb_grad, downw_grad, downb_grad = totals
    return (results.reshape(inputs.shape), input_grads.reshape(inputs.shape), gain_one, shift_one, in_grad, qbias_grad, vbias_grad, out_grad, obias_grad, gain_two, shift_two, upw_grad, upb_grad, downw_grad, downb_grad)
```

```python
import functools

import jax
import jax.numpy as jnp
from jax import lax
from jax.experimental import pallas as pl
from jax.experimental.pallas import tpu as pltpu
from jax.sharding import PartitionSpec as P

HEADS = 17
HEAD_DIM = 64


epsilon = 1e-05


def layer_norm(values, gain, shift):
    centred = values - jnp.mean(values, axis=-1, keepdims=True)
    spread = jnp.mean(centred * centred, axis=-1, keepdims=True)
    return centred * lax.rsqrt(spread + epsilon) * gain + shift


def gelu_tanh(values):
    return jax.nn.gelu(values, approximate=True)


def score_grads(
    query_heads, key_heads, value_heads, grad_heads, log_total, row_delta, query_at, key_at
):
    score_scale = HEAD_DIM ** (-0.5)
    scores = (
        jnp.einsum("sqhd,skhd->shqk", query_heads, key_heads, preferred_element_type=jnp.float32)
        * score_scale
    )
    visible = query_at[:, None] >= key_at[None, :]
    shifted = jnp.where(visible, scores - log_total[..., None], -1e30)
    weights = jnp.where(visible, jnp.exp(shifted), 0.0)
    pressure = jnp.einsum(
        "sqhd,skhd->shqk", grad_heads, value_heads, preferred_element_type=jnp.float32
    )
    score_low = (weights * (pressure - row_delta[..., None])).astype(jnp.bfloat16)
    return (weights.astype(jnp.bfloat16), score_low)


def per_device_gathered(
    inputs,
    cotangent,
    first_gain,
    first_shift,
    project_in,
    query_bias,
    value_bias,
    project_out,
    output_bias,
    second_gain,
    second_shift,
    up_weight,
    up_bias,
    down_weight,
    down_bias,
):
    seq_count, block_len, model_width = inputs.shape
    flat_rows = seq_count * block_len
    cycle_size = lax.axis_size("ctx")
    my_block = lax.axis_index("ctx")
    score_scale = HEAD_DIM ** (-0.5)
    head_shape = (seq_count, block_len, HEADS, HEAD_DIM)
    offsets = jnp.arange(block_len, dtype=jnp.int32)
    query_at = my_block * block_len + offsets
    gain_first, shift_first, full_in, qbias_full, vbias_full, full_out, obias_full = (
        lax.all_gather(first_gain, "fsdp", axis=0, tiled=True),
        lax.all_gather(first_shift, "fsdp", axis=0, tiled=True),
        lax.all_gather(project_in, "fsdp", axis=0, tiled=True),
        lax.all_gather(query_bias, "fsdp", axis=0, tiled=True),
        lax.all_gather(value_bias, "fsdp", axis=0, tiled=True),
        lax.all_gather(project_out, "fsdp", axis=0, tiled=True),
        lax.all_gather(output_bias, "fsdp", axis=0, tiled=True),
    )
    rows_in = inputs.astype(jnp.float32).reshape(flat_rows, model_width)
    normed, norm_first_back = jax.vjp(
        layer_norm, rows_in, gain_first.astype(jnp.float32), shift_first.astype(jnp.float32)
    )
    normed_low = normed.astype(jnp.bfloat16)
    projected = jnp.dot(normed_low, full_in, preferred_element_type=jnp.float32)
    queries = (projected[:, :model_width] + qbias_full).astype(jnp.bfloat16)
    key_rows = projected[:, model_width : 2 * model_width].astype(jnp.bfloat16)
    value_rows = (projected[:, 2 * model_width :] + vbias_full).astype(jnp.bfloat16)
    query_heads = queries.reshape(head_shape)
    running_top = jnp.full((seq_count, HEADS, block_len), -1e30, jnp.float32)
    accumulated = jnp.zeros(head_shape, jnp.float32)
    piece_keys = lax.all_gather(
        key_rows.reshape(seq_count, block_len, model_width), "ctx", axis=1, tiled=True
    )
    piece_values = lax.all_gather(
        value_rows.reshape(seq_count, block_len, model_width), "ctx", axis=1, tiled=True
    )
    piece_len = piece_keys.shape[1]
    key_heads = piece_keys.reshape(seq_count, piece_len, HEADS, HEAD_DIM)
    value_heads = piece_values.reshape(seq_count, piece_len, HEADS, HEAD_DIM)
    scores = (
        jnp.einsum("sqhd,skhd->shqk", query_heads, key_heads, preferred_element_type=jnp.float32)
        * score_scale
    )
    key_at = jnp.arange(piece_len, dtype=jnp.int32)
    visible = query_at[:, None] >= key_at[None, :]
    masked = jnp.where(visible, scores, -1e30)
    new_top = jnp.maximum(running_top, jnp.max(masked, axis=-1))
    factor = jnp.exp(running_top - new_top)
    weights = jnp.where(visible, jnp.exp(masked - new_top[..., None]), 0.0)
    row_total = jnp.sum(weights, axis=-1)
    added = jnp.einsum(
        "shqk,skhd->sqhd",
        weights.astype(jnp.bfloat16),
        value_heads,
        preferred_element_type=jnp.float32,
    )
    accumulated = accumulated * jnp.swapaxes(factor, 1, 2)[..., None] + added
    running_top, row_total, accumulated = (new_top, row_total, accumulated)
    attended = accumulated / jnp.swapaxes(row_total, 1, 2)[..., None]
    log_total = running_top + jnp.log(row_total)
    attended_low = attended.reshape(flat_rows, model_width).astype(jnp.bfloat16)
    middle = (
        rows_in + jnp.dot(attended_low, full_out, preferred_element_type=jnp.float32) + obias_full
    )
    gain_second, shift_second, full_up, ubias_full, full_down, dbias_full = (
        lax.all_gather(second_gain, "fsdp", axis=0, tiled=True),
        lax.all_gather(second_shift, "fsdp", axis=0, tiled=True),
        lax.all_gather(up_weight, "fsdp", axis=0, tiled=True),
        lax.all_gather(up_bias, "fsdp", axis=0, tiled=True),
        lax.all_gather(down_weight, "fsdp", axis=0, tiled=True),
        lax.all_gather(down_bias, "fsdp", axis=0, tiled=True),
    )
    normed_two, norm_second_back = jax.vjp(
        layer_norm, middle, gain_second.astype(jnp.float32), shift_second.astype(jnp.float32)
    )
    normed_two_low = normed_two.astype(jnp.bfloat16)
    hidden = jnp.dot(normed_two_low, full_up, preferred_element_type=jnp.float32) + ubias_full
    active, gelu_back = jax.vjp(gelu_tanh, hidden)
    active_low = active.astype(jnp.bfloat16)
    result = (
        middle + jnp.dot(active_low, full_down, preferred_element_type=jnp.float32) + dbias_full
    )
    outputs = result.astype(jnp.bfloat16).reshape(seq_count, block_len, model_width)
    upstream = cotangent.astype(jnp.float32).reshape(flat_rows, model_width)
    upstream_low = upstream.astype(jnp.bfloat16)
    down_grad = jnp.einsum(
        "rf,rd->fd", active_low, upstream_low, preferred_element_type=jnp.float32
    )
    down_bias_grad = jnp.sum(upstream_low.astype(jnp.float32), axis=0)
    active_grad = jnp.einsum(
        "rd,fd->rf", upstream_low, full_down, preferred_element_type=jnp.float32
    )
    (hidden_grad,) = gelu_back(active_grad)
    hidden_low = hidden_grad.astype(jnp.bfloat16)
    up_grad = jnp.einsum(
        "rd,rf->df", normed_two_low, hidden_low, preferred_element_type=jnp.float32
    )
    up_bias_grad = jnp.sum(hidden_low.astype(jnp.float32), axis=0)
    normed_two_grad = jnp.einsum(
        "rf,df->rd", hidden_low, full_up, preferred_element_type=jnp.float32
    )
    middle_part, gain_two_grad, shift_two_grad = norm_second_back(normed_two_grad)
    middle_grad = upstream + middle_part
    middle_low = middle_grad.astype(jnp.bfloat16)
    out_grad = jnp.einsum("rd,re->de", attended_low, middle_low, preferred_element_type=jnp.float32)
    out_bias_grad = jnp.sum(middle_low.astype(jnp.float32), axis=0)
    attended_grad = jnp.einsum(
        "re,de->rd", middle_low, full_out, preferred_element_type=jnp.float32
    )
    grad_low = attended_grad.astype(jnp.bfloat16).reshape(head_shape)
    row_delta = jnp.swapaxes(jnp.sum(grad_low.astype(jnp.float32) * attended, axis=-1), 1, 2)
    gathered_keys, gathered_values = (
        lax.all_gather(
            key_rows.reshape(1, seq_count, block_len, model_width), "ctx", axis=0, tiled=True
        ),
        lax.all_gather(
            value_rows.reshape(1, seq_count, block_len, model_width), "ctx", axis=0, tiled=True
        ),
    )
    block_ids = jnp.arange(cycle_size, dtype=jnp.int32)

    def key_step(carry, inputs_here):
        key_block, value_block, block_index = inputs_here
        key_heads = key_block.reshape(head_shape)
        value_heads = value_block.reshape(head_shape)
        weights_low, score_low = score_grads(
            query_heads,
            key_heads,
            value_heads,
            grad_low,
            log_total,
            row_delta,
            query_at,
            block_index * block_len + offsets,
        )
        carry = (
            carry
            + jnp.einsum(
                "shqk,skhd->sqhd", score_low, key_heads, preferred_element_type=jnp.float32
            )
            * score_scale
        )
        key_term = (
            jnp.einsum(
                "shqk,sqhd->skhd", score_low, query_heads, preferred_element_type=jnp.float32
            )
            * score_scale
        )
        value_term = jnp.einsum(
            "shqk,sqhd->skhd", weights_low, grad_low, preferred_element_type=jnp.float32
        )
        return (
            carry,
            (
                key_term.reshape(seq_count, block_len, model_width),
                value_term.reshape(seq_count, block_len, model_width),
            ),
        )

    query_grad, (key_terms, value_terms) = lax.scan(
        key_step, jnp.zeros(head_shape, jnp.float32), (gathered_keys, gathered_values, block_ids)
    )
    key_sum, value_sum = (
        lax.psum_scatter(
            key_terms.astype(jnp.bfloat16), "ctx", scatter_dimension=0, tiled=True
        ).astype(jnp.float32),
        lax.psum_scatter(
            value_terms.astype(jnp.bfloat16), "ctx", scatter_dimension=0, tiled=True
        ).astype(jnp.float32),
    )
    key_grad = key_sum.reshape(flat_rows, model_width)
    value_grad = value_sum.reshape(flat_rows, model_width)
    query_low = query_grad.reshape(flat_rows, model_width).astype(jnp.bfloat16)
    key_low = key_grad.astype(jnp.bfloat16)
    value_low = value_grad.astype(jnp.bfloat16)
    stacked = jnp.concatenate([query_low, key_low, value_low], axis=1)
    in_grad = jnp.einsum("rd,re->de", normed_low, stacked, preferred_element_type=jnp.float32)
    query_bias_grad = jnp.sum(query_low.astype(jnp.float32), axis=0)
    value_bias_grad = jnp.sum(value_low.astype(jnp.float32), axis=0)
    normed_grad = jnp.einsum("re,de->rd", stacked, full_in, preferred_element_type=jnp.float32)
    input_part, gain_one_grad, shift_one_grad = norm_first_back(normed_grad)
    input_gradient = (middle_grad + input_part).reshape(seq_count, block_len, model_width)
    (
        gain_one_part,
        shift_one_part,
        in_part,
        qbias_part,
        vbias_part,
        out_part,
        obias_part,
        gain_two_part,
        shift_two_part,
        up_part,
        ubias_part,
        down_part,
        dbias_part,
    ) = (
        lax.psum_scatter(
            gain_one_grad.astype(jnp.bfloat16), "fsdp", scatter_dimension=0, tiled=True
        ).astype(jnp.float32),
        lax.psum_scatter(
            shift_one_grad.astype(jnp.bfloat16), "fsdp", scatter_dimension=0, tiled=True
        ).astype(jnp.float32),
        lax.psum_scatter(
            in_grad.astype(jnp.bfloat16), "fsdp", scatter_dimension=0, tiled=True
        ).astype(jnp.float32),
        lax.psum_scatter(
            query_bias_grad.astype(jnp.bfloat16), "fsdp", scatter_dimension=0, tiled=True
        ).astype(jnp.float32),
        lax.psum_scatter(
            value_bias_grad.astype(jnp.bfloat16), "fsdp", scatter_dimension=0, tiled=True
        ).astype(jnp.float32),
        lax.psum_scatter(
            out_grad.astype(jnp.bfloat16), "fsdp", scatter_dimension=0, tiled=True
        ).astype(jnp.float32),
        lax.psum_scatter(
            out_bias_grad.astype(jnp.bfloat16), "fsdp", scatter_dimension=0, tiled=True
        ).astype(jnp.float32),
        lax.psum_scatter(
            gain_two_grad.astype(jnp.bfloat16), "fsdp", scatter_dimension=0, tiled=True
        ).astype(jnp.float32),
        lax.psum_scatter(
            shift_two_grad.astype(jnp.bfloat16), "fsdp", scatter_dimension=0, tiled=True
        ).astype(jnp.float32),
        lax.psum_scatter(
            up_grad.astype(jnp.bfloat16), "fsdp", scatter_dimension=0, tiled=True
        ).astype(jnp.float32),
        lax.psum_scatter(
            up_bias_grad.astype(jnp.bfloat16), "fsdp", scatter_dimension=0, tiled=True
        ).astype(jnp.float32),
        lax.psum_scatter(
            down_grad.astype(jnp.bfloat16), "fsdp", scatter_dimension=0, tiled=True
        ).astype(jnp.float32),
        lax.psum_scatter(
            down_bias_grad.astype(jnp.bfloat16), "fsdp", scatter_dimension=0, tiled=True
        ).astype(jnp.float32),
    )
    (
        gain_one_sum,
        shift_one_sum,
        in_sum,
        qbias_sum,
        vbias_sum,
        out_sum,
        obias_sum,
        gain_two_sum,
        shift_two_sum,
        up_sum,
        ubias_sum,
        down_sum,
        dbias_sum,
    ) = lax.psum(
        (
            gain_one_part,
            shift_one_part,
            in_part,
            qbias_part,
            vbias_part,
            out_part,
            obias_part,
            gain_two_part,
            shift_two_part,
            up_part,
            ubias_part,
            down_part,
            dbias_part,
        ),
        ("dp", "ctx"),
    )
    return (
        outputs,
        input_gradient,
        gain_one_sum,
        shift_one_sum,
        in_sum,
        qbias_sum,
        vbias_sum,
        out_sum,
        obias_sum,
        gain_two_sum,
        shift_two_sum,
        up_sum,
        ubias_sum,
        down_sum,
        dbias_sum,
    )


NT = (((1,), (1,)), ((), ()))
PAIR = 2 * HEAD_DIM


def attend_kernel(place_ref, q_ref, k_ref, v_ref, o_ref, log_ref, keys, values, *, count, width):
    pair = pl.program_id(0)
    shift = place_ref[0]
    block_len = q_ref.shape[0] // count
    lane = lax.broadcasted_iota(jnp.int32, (1, PAIR), 1)
    valid = lane + pair * PAIR < width
    first = lane < HEAD_DIM

    def rows(block):
        return pl.ds(pl.multiple_of((block ^ shift) * block_len, block_len), block_len)

    for block in range(count):
        here = pl.ds(block * block_len, block_len)
        keys[here, :] = jnp.where(valid, k_ref[rows(block), :], 0)
        values[here, :] = jnp.where(valid, v_ref[rows(block), :], 0)
    diagonal = lax.broadcasted_iota(jnp.int32, (block_len, block_len), 0) >= (
        lax.broadcasted_iota(jnp.int32, (block_len, block_len), 1)
    )
    for block in range(count):
        seen = (block + 1) * block_len
        before = block * block_len
        queries = q_ref[rows(block), :] * jnp.bfloat16(HEAD_DIM**-0.5)
        parts = []
        logs = log_ref[rows(block), :]
        for half in range(2):
            pick = jnp.logical_and(first if half == 0 else jnp.logical_not(first), valid)
            scores = lax.dot_general(
                jnp.where(pick, queries, 0),
                keys[pl.ds(0, seen), :],
                NT,
                preferred_element_type=jnp.float32,
            )
            last = jnp.where(diagonal, scores[:, before:], -1e30)
            scores = last if block == 0 else jnp.concatenate([scores[:, :before], last], axis=1)
            top = jnp.max(scores, axis=1, keepdims=True)
            weights = jnp.exp(scores - top)
            total = jnp.sum(weights, axis=1, keepdims=True)
            added = jnp.dot(
                weights.astype(jnp.bfloat16),
                values[pl.ds(0, seen), :],
                preferred_element_type=jnp.float32,
            )
            parts.append(added / total)
            logs = jnp.where(lane == 2 * pair + half, top + jnp.log(total), logs)
        o_ref[rows(block), :] = jnp.where(first, parts[0], parts[1]).astype(jnp.bfloat16)
        log_ref[rows(block), :] = logs


def attend_back_kernel(
    place_ref,
    q_ref,
    k_ref,
    v_ref,
    g_ref,
    o_ref,
    log_ref,
    dq_ref,
    dk_ref,
    dv_ref,
    queries,
    grads,
    keys,
    values,
    keys_turned,
    logs,
    deltas,
    turned,
    *,
    count,
    width,
):
    pair = pl.program_id(0)
    shift = place_ref[0]
    length = q_ref.shape[0]
    block_len = length // count
    lane = lax.broadcasted_iota(jnp.int32, (1, PAIR), 1)
    valid = lane + pair * PAIR < width
    first = lane < HEAD_DIM
    picks = (jnp.logical_and(first, valid), jnp.logical_and(jnp.logical_not(first), valid))
    half_of = (lax.broadcasted_iota(jnp.int32, (8, PAIR), 1) // HEAD_DIM) == (
        lax.broadcasted_iota(jnp.int32, (8, PAIR), 0)
    )
    ones_of = jnp.where(half_of, 1.0, 0.0)

    def rows(block):
        return pl.ds(pl.multiple_of((block ^ shift) * block_len, block_len), block_len)

    for block in range(count):
        here = pl.ds(block * block_len, block_len)
        key_block = jnp.where(valid, k_ref[rows(block), :], 0)
        keys[here, :] = key_block
        keys_turned[:, here] = key_block.astype(jnp.float32).T.astype(jnp.bfloat16)
        values[here, :] = jnp.where(valid, v_ref[rows(block), :], 0)
        query_block = q_ref[rows(block), :] * jnp.bfloat16(HEAD_DIM**-0.5)
        grad_block = jnp.where(valid, g_ref[rows(block), :], 0)
        for half in range(2):
            queries[half, here, :] = jnp.where(picks[half], query_block, 0)
            grads[half, here, :] = jnp.where(picks[half], grad_block, 0)
        mixed = grad_block.astype(jnp.float32) * jnp.where(
            valid, o_ref[rows(block), :], 0
        ).astype(jnp.float32)
        deltas[:, here] = lax.dot_general(
            ones_of,
            mixed,
            NT,
            preferred_element_type=jnp.float32,
            precision=lax.Precision.HIGHEST,
        )
        logs[:, here] = log_ref[
            0, :, pl.ds(pl.multiple_of((block ^ shift) * block_len, block_len), block_len)
        ]
    diagonal = lax.broadcasted_iota(jnp.int32, (block_len, block_len), 0) <= (
        lax.broadcasted_iota(jnp.int32, (block_len, block_len), 1)
    )
    for block in range(count):
        here = pl.ds(block * block_len, block_len)
        after = pl.ds(block * block_len, length - block * block_len)
        key_total = jnp.zeros((block_len, PAIR), jnp.float32)
        value_total = jnp.zeros((block_len, PAIR), jnp.float32)
        for half in range(2):
            scores = lax.dot_general(
                keys[here, :], queries[half, after, :], NT, preferred_element_type=jnp.float32
            )
            shifted = scores - logs[half : half + 1, after]
            own = jnp.where(diagonal, shifted[:, :block_len], -1e30)
            if block < count - 1:
                own = jnp.concatenate([own, shifted[:, block_len:]], axis=1)
            weights = jnp.exp(own)
            pressure = lax.dot_general(
                values[here, :], grads[half, after, :], NT, preferred_element_type=jnp.float32
            )
            score_low = (weights * (pressure - deltas[half : half + 1, after])).astype(
                jnp.bfloat16
            )
            value_total += jnp.dot(
                weights.astype(jnp.bfloat16),
                grads[half, after, :],
                preferred_element_type=jnp.float32,
            )
            key_total += jnp.dot(
                score_low, queries[half, after, :], preferred_element_type=jnp.float32
            )
            part = pl.ds(half * HEAD_DIM, HEAD_DIM)
            term = jnp.dot(
                keys_turned[part, here], score_low, preferred_element_type=jnp.float32
            )
            if block == 0:
                turned[part, after] = term
            else:
                turned[part, after] += term
        dk_ref[rows(block), :] = key_total.astype(jnp.bfloat16)
        dv_ref[rows(block), :] = value_total.astype(jnp.bfloat16)
    for block in range(count):
        here = pl.ds(block * block_len, block_len)
        dq_ref[rows(block), :] = (turned[:, here].T * HEAD_DIM**-0.5).astype(jnp.bfloat16)


def attend(place, queries, key_rows, value_rows, count):
    length, width = queries.shape
    pairs = pl.cdiv(width, PAIR)
    heads_block = pl.BlockSpec((length, PAIR), lambda pair, place_ref: (0, pair))
    return pl.pallas_call(
        functools.partial(attend_kernel, count=count, width=width),
        grid_spec=pltpu.PrefetchScalarGridSpec(
            num_scalar_prefetch=1,
            grid=(pairs,),
            in_specs=[heads_block] * 3,
            out_specs=[
                heads_block,
                pl.BlockSpec((length, 128), lambda pair, place_ref: (0, 0)),
            ],
            scratch_shapes=[pltpu.VMEM((length, PAIR), jnp.bfloat16)] * 2,
        ),
        out_shape=[
            jax.ShapeDtypeStruct((length, width), jnp.bfloat16),
            jax.ShapeDtypeStruct((length, 128), jnp.float32),
        ],
        compiler_params=pltpu.CompilerParams(vmem_limit_bytes=48 * 2**20),
        cost_estimate=pl.CostEstimate(
            flops=4 * length * length * width,
            bytes_accessed=8 * length * width,
            transcendentals=HEADS * length * length // 2,
        ),
        name="attend",
    )(place, queries, key_rows, value_rows)


def attend_back(place, queries, key_rows, value_rows, grads, attended, logs, count):
    length, width = queries.shape
    pairs = pl.cdiv(width, PAIR)
    heads_block = pl.BlockSpec((length, PAIR), lambda pair, place_ref: (0, pair))
    low_rows = pltpu.VMEM((length, PAIR), jnp.bfloat16)
    low_pair = pltpu.VMEM((2, length, PAIR), jnp.bfloat16)
    return pl.pallas_call(
        functools.partial(attend_back_kernel, count=count, width=width),
        grid_spec=pltpu.PrefetchScalarGridSpec(
            num_scalar_prefetch=1,
            grid=(pairs,),
            in_specs=[heads_block] * 5
            + [pl.BlockSpec((1, 2, length), lambda pair, place_ref: (pair, 0, 0))],
            out_specs=[heads_block] * 3,
            scratch_shapes=[
                low_pair,
                low_pair,
                low_rows,
                low_rows,
                pltpu.VMEM((PAIR, length), jnp.bfloat16),
                pltpu.VMEM((2, length), jnp.float32),
                pltpu.VMEM((8, length), jnp.float32),
                pltpu.VMEM((PAIR, length), jnp.float32),
            ],
        ),
        out_shape=[jax.ShapeDtypeStruct((length, width), jnp.bfloat16)] * 3,
        compiler_params=pltpu.CompilerParams(vmem_limit_bytes=48 * 2**20),
        cost_estimate=pl.CostEstimate(
            flops=10 * length * length * width,
            bytes_accessed=16 * length * width,
            transcendentals=HEADS * length * length // 2,
        ),
        name="attend_back",
    )(place, queries, key_rows, value_rows, grads, attended, logs)


def settle_kernel(place_ref, *refs):
    pieces, out_ref = refs[:-1], refs[-1]
    for at, piece in enumerate(pieces):
        out_ref[place_ref[at]] = piece[...].astype(out_ref.dtype)


def settle(places, pieces, dtype):
    return pl.pallas_call(
        settle_kernel,
        in_specs=[pl.BlockSpec(memory_space=pltpu.SMEM)]
        + [pl.BlockSpec(memory_space=pltpu.VMEM)] * len(pieces),
        out_specs=pl.BlockSpec(memory_space=pltpu.VMEM),
        out_shape=jax.ShapeDtypeStruct((len(pieces),) + pieces[0].shape, dtype),
        compiler_params=pltpu.CompilerParams(vmem_limit_bytes=48 * 2**20),
        name="settle",
    )(places, *pieces)


def plane_partner(device, kind):
    core = device & 1
    if kind == "core":
        return device ^ 1
    if kind == "near":
        return device ^ (2 if core else 4)
    return device ^ (4 if core else 2)


def plane_swap(values, kind):
    return lax.ppermute(
        values, ("dp", "ctx"), [(device, plane_partner(device, kind)) for device in range(8)]
    )


def ctx_swap(values, bits):
    return lax.ppermute(values, "ctx", [(device, device ^ bits) for device in range(4)])


def gather_piece(piece):
    own = lax.all_gather(piece, "fsdp", axis=0, tiled=True)
    near = plane_swap(own, "near")
    return [own, near, plane_swap(own, "core"), plane_swap(near, "core")]


def reduce_pieces(pieces):
    far_two = plane_swap(pieces[3], "core")
    far = plane_swap(pieces[2], "core")
    second = (pieces[1].astype(jnp.float32) + far_two.astype(jnp.float32)).astype(jnp.bfloat16)
    near = plane_swap(second, "near")
    first = (
        pieces[0].astype(jnp.float32) + far.astype(jnp.float32) + near.astype(jnp.float32)
    ).astype(jnp.bfloat16)
    shard = lax.psum_scatter(first, "fsdp", scatter_dimension=0, tiled=True)
    whole = (shard.astype(jnp.float32) + plane_swap(shard, "other").astype(jnp.float32)).astype(
        jnp.bfloat16
    )
    beside = plane_swap(whole, "near")
    return [whole, beside, plane_swap(whole, "core"), plane_swap(beside, "core")]


def chosen(index, options):
    result = options[-1]
    for at in range(len(options) - 2, -1, -1):
        result = jnp.where(index == at, options[at], result)
    return result


def gather_vector(values, z):
    around = [values] + [
        lax.ppermute(values, "fsdp", [(device, (device + step) % 4) for device in range(4)])
        for step in range(1, 4)
    ]
    return jnp.stack([chosen((z - at) % 4, around) for at in range(4)])


def reduce_vector(values, z):
    rows = [values[at] for at in range(4)]
    total = chosen(z, rows)
    for step in range(1, 4):
        total = total + lax.ppermute(
            chosen((z + step) % 4, rows),
            "fsdp",
            [(device, (device + step) % 4) for device in range(4)],
        )
    for bits in (1, 2, 4):
        total = total + lax.ppermute(
            total, ("dp", "ctx"), [(device, device ^ bits) for device in range(8)]
        )
    return total


def normalised(values):
    centred = values - jnp.mean(values, axis=-1, keepdims=True)
    scale = lax.rsqrt(jnp.mean(centred * centred, axis=-1, keepdims=True) + epsilon)
    return centred * scale, scale


def norm_back(values, gain, grad):
    unit, scale = normalised(values)
    turned = grad * gain
    inner = (
        turned
        - jnp.mean(turned, axis=-1, keepdims=True)
        - unit * jnp.mean(turned * unit, axis=-1, keepdims=True)
    )
    return scale * inner, jnp.sum(grad * unit, axis=0), jnp.sum(grad, axis=0)


def product(left, right, dims):
    return lax.dot_general(left, right, ((dims[:1], dims[1:]), ((), ())),
                           preferred_element_type=jnp.float32)


def gelu_pair(values):
    inner = 0.7978845608028654
    squared = values * values
    curve = jnp.tanh(inner * (values + 0.044715 * values * squared))
    active = 0.5 * values * (1.0 + curve)
    slope = 0.5 * (1.0 + curve) + 0.5 * values * (1.0 - curve * curve) * inner * (
        1.0 + 3.0 * 0.044715 * squared
    )
    return active, slope


def per_device_exchanged(
    inputs,
    cotangent,
    first_gain,
    first_shift,
    project_in,
    query_bias,
    value_bias,
    project_out,
    output_bias,
    second_gain,
    second_shift,
    up_weight,
    up_bias,
    down_weight,
    down_bias,
):
    seq_count, block_len, width = inputs.shape
    low = jnp.bfloat16
    wide = jnp.float32
    c = lax.axis_index("ctx")
    y = lax.axis_index("dp")
    z = lax.axis_index("fsdp")
    core = c & 1
    x = c >> 1
    mine = core * 2 + jnp.where(core == 0, y, x)
    across = (1 - core) * 2 + jnp.where(core == 0, x, y)
    classes = [mine, mine ^ 1, across, across ^ 1]
    slot_of = [
        chosen(0, [sum(at * (classes[at] == kind).astype(jnp.int32) for at in range(4))])
        for kind in range(4)
    ]
    quarter = width // 4
    place = jnp.stack([c])
    places = jnp.stack([c ^ at for at in range(4)])
    class_places = jnp.stack(classes)

    def spread(values):
        return jnp.concatenate(
            [lax.dynamic_index_in_dim(values, c, 0, keepdims=False)]
            + [
                ctx_swap(lax.dynamic_index_in_dim(values, c ^ bits, 0, keepdims=False), bits)
                for bits in range(1, 4)
            ],
            axis=0,
        )

    def collect(rows, dtype):
        pieces = [rows[at * block_len : (at + 1) * block_len].astype(low) for at in range(4)]
        moved = [pieces[0]] + [ctx_swap(pieces[bits], bits) for bits in range(1, 4)]
        return settle(places, moved, dtype)

    sections = [
        project_in[:, :width],
        project_in[:, width : 2 * width],
        project_in[:, 2 * width :],
        project_out,
    ]
    attend_slots = gather_piece(chosen(mine, sections))
    up_piece = jnp.concatenate(
        [
            lax.dynamic_slice_in_dim(up_weight, at * width + mine * quarter, quarter, 1)
            for at in range(4)
        ],
        axis=1,
    )
    up_slots = gather_piece(up_piece)
    down_slots = gather_piece(lax.dynamic_slice_in_dim(down_weight, mine * quarter, quarter, 0))
    vectors = gather_vector(
        jnp.concatenate(
            [
                first_gain,
                first_shift,
                query_bias,
                value_bias,
                output_bias,
                second_gain,
                second_shift,
                down_bias,
                up_bias,
            ]
        ),
        z,
    ).astype(wide)
    gain_first, shift_first, qbias, vbias, obias, gain_second, shift_second, dbias = (
        vectors[:, at * quarter : (at + 1) * quarter].reshape(width) for at in range(8)
    )
    ubias = vectors[:, 8 * quarter :].reshape(4, 4, quarter)

    rows_in = spread(inputs)
    wide_in = rows_in.astype(wide)
    unit, _ = normalised(wide_in)
    normed_low = (unit * gain_first + shift_first).astype(low)
    weights = settle(class_places, attend_slots, low)
    queries = (product(normed_low, weights[0], (1, 0)) + qbias).astype(low)
    key_rows = product(normed_low, weights[1], (1, 0)).astype(low)
    value_rows = (product(normed_low, weights[2], (1, 0)) + vbias).astype(low)
    attended, logs = attend(place, queries, key_rows, value_rows, seq_count)
    logs = logs.T.reshape(64, 2, seq_count * block_len)
    middle = wide_in + product(attended, weights[3], (1, 0)) + obias
    unit_two, _ = normalised(middle)
    normed_two_low = (unit_two * gain_second + shift_second).astype(low)
    active, slopes = [], []
    for slot in range(4):
        bias = chosen(classes[slot], [ubias[:, kind] for kind in range(4)]).reshape(width)
        hidden = product(normed_two_low, up_slots[slot], (1, 0)) + bias
        value, slope = gelu_pair(hidden)
        active.append(value.astype(low))
        slopes.append(slope.astype(low))
    result = middle + dbias
    for slot in range(4):
        result = result + product(active[slot], down_slots[slot], (1, 0))
    outputs = collect(result, low)

    upstream_low = spread(cotangent)
    upstream = upstream_low.astype(wide)
    down_parts = reduce_pieces(
        [product(active[slot], upstream_low, (0, 0)).astype(low) for slot in range(4)]
    )
    hidden_low = [
        (product(upstream_low, down_slots[slot], (1, 1)) * slopes[slot].astype(wide)).astype(low)
        for slot in range(4)
    ]
    up_parts = reduce_pieces(
        [product(normed_two_low, hidden_low[slot], (0, 0)).astype(low) for slot in range(4)]
    )
    normed_two_grad = sum(product(hidden_low[slot], up_slots[slot], (1, 1)) for slot in range(4))
    middle_part, gain_two_grad, shift_two_grad = norm_back(middle, gain_second, normed_two_grad)
    middle_grad = upstream + middle_part
    middle_low = middle_grad.astype(low)
    grad_low = product(middle_low, weights[3], (1, 1)).astype(low)
    query_low, key_low, value_low = attend_back(
        place, queries, key_rows, value_rows, grad_low, attended, logs, seq_count
    )
    section_grads = [
        product(normed_low, query_low, (0, 0)).astype(low),
        product(normed_low, key_low, (0, 0)).astype(low),
        product(normed_low, value_low, (0, 0)).astype(low),
        product(attended, middle_low, (0, 0)).astype(low),
    ]
    section_parts = reduce_pieces([chosen(kind, section_grads) for kind in classes])
    normed_grad = (
        product(query_low, weights[0], (1, 1))
        + product(key_low, weights[1], (1, 1))
        + product(value_low, weights[2], (1, 1))
    )
    input_part, gain_one_grad, shift_one_grad = norm_back(wide_in, gain_first, normed_grad)
    input_gradient = collect(middle_grad + input_part, wide)

    def column_sum(values):
        return jnp.sum(values.astype(wide), axis=0)

    hidden_sums = [column_sum(hidden_low[slot]).reshape(4, quarter) for slot in range(4)]
    hidden_sums = jnp.stack(
        [chosen(slot_of[kind], hidden_sums) for kind in range(4)], axis=1
    ).reshape(4, 4 * quarter)
    early = reduce_vector(
        jnp.concatenate(
            [
                values.reshape(4, quarter)
                for values in (
                    column_sum(middle_low),
                    gain_two_grad,
                    shift_two_grad,
                    column_sum(upstream_low),
                )
            ]
            + [hidden_sums],
            axis=1,
        ),
        z,
    )
    late = reduce_vector(
        jnp.concatenate(
            [
                values.reshape(4, quarter)
                for values in (
                    gain_one_grad,
                    shift_one_grad,
                    column_sum(query_low),
                    column_sum(value_low),
                )
            ],
            axis=1,
        ),
        z,
    )
    obias_sum, gain_two_sum, shift_two_sum, dbias_sum = (
        early[at * quarter : (at + 1) * quarter] for at in range(4)
    )
    ubias_sum = early[4 * quarter :]
    gain_one_sum, shift_one_sum, qbias_sum, vbias_sum = (
        late[at * quarter : (at + 1) * quarter] for at in range(4)
    )
    in_parts = [chosen(slot_of[kind], section_parts).astype(wide) for kind in range(4)]
    up_parts = [chosen(slot_of[kind], up_parts) for kind in range(4)]
    up_sum = jnp.concatenate(
        [
            up_parts[kind][:, at * quarter : (at + 1) * quarter]
            for at in range(4)
            for kind in range(4)
        ],
        axis=1,
    ).astype(wide)
    down_sum = settle(class_places, down_parts, wide).reshape(down_weight.shape)
    return (
        outputs,
        input_gradient,
        gain_one_sum,
        shift_one_sum,
        jnp.concatenate(in_parts[:3], axis=1),
        qbias_sum,
        vbias_sum,
        in_parts[3],
        obias_sum,
        gain_two_sum,
        shift_two_sum,
        up_sum,
        ubias_sum,
        down_sum,
        dbias_sum,
    )


def solution(mesh):
    sizes = dict(mesh.shape)
    exchanged = sizes["dp"] == 2 and sizes["fsdp"] == 4 and sizes["ctx"] == 4
    per_device = per_device_exchanged if exchanged else per_device_gathered
    return jax.shard_map(
        per_device,
        mesh=mesh,
        in_specs=(
            P(("dp", "fsdp"), "ctx", None),
            P(("dp", "fsdp"), "ctx", None),
            P("fsdp"),
            P("fsdp"),
            P("fsdp", None),
            P("fsdp"),
            P("fsdp"),
            P("fsdp", None),
            P("fsdp"),
            P("fsdp"),
            P("fsdp"),
            P("fsdp", None),
            P("fsdp"),
            P("fsdp", None),
            P("fsdp"),
        ),
        out_specs=(
            P(("dp", "fsdp"), "ctx", None),
            P(("dp", "fsdp"), "ctx", None),
            P("fsdp"),
            P("fsdp"),
            P("fsdp", None),
            P("fsdp"),
            P("fsdp"),
            P("fsdp", None),
            P("fsdp"),
            P("fsdp"),
            P("fsdp"),
            P("fsdp", None),
            P("fsdp"),
            P("fsdp", None),
            P("fsdp"),
        ),
        check_vma=False,
    )
```

```python
import functools

import jax
import jax.numpy as jnp
from jax import lax
from jax.experimental import pallas as pl
from jax.experimental.pallas import tpu as pltpu
from jax.sharding import PartitionSpec as P

HEADS = 17
HEAD_DIM = 64


epsilon = 1e-05


def layer_norm(values, gain, shift):
    centred = values - jnp.mean(values, axis=-1, keepdims=True)
    spread = jnp.mean(centred * centred, axis=-1, keepdims=True)
    return centred * lax.rsqrt(spread + epsilon) * gain + shift


def gelu_tanh(values):
    return jax.nn.gelu(values, approximate=True)


def score_grads(
    query_heads, key_heads, value_heads, grad_heads, log_total, row_delta, query_at, key_at
):
    score_scale = HEAD_DIM ** (-0.5)
    scores = (
        jnp.einsum("sqhd,skhd->shqk", query_heads, key_heads, preferred_element_type=jnp.float32)
        * score_scale
    )
    visible = query_at[:, None] >= key_at[None, :]
    shifted = jnp.where(visible, scores - log_total[..., None], -1e30)
    weights = jnp.where(visible, jnp.exp(shifted), 0.0)
    pressure = jnp.einsum(
        "sqhd,skhd->shqk", grad_heads, value_heads, preferred_element_type=jnp.float32
    )
    score_low = (weights * (pressure - row_delta[..., None])).astype(jnp.bfloat16)
    return (weights.astype(jnp.bfloat16), score_low)


def per_device_gathered(
    inputs,
    cotangent,
    first_gain,
    first_shift,
    project_in,
    query_bias,
    value_bias,
    project_out,
    output_bias,
    second_gain,
    second_shift,
    up_weight,
    up_bias,
    down_weight,
    down_bias,
):
    seq_count, block_len, model_width = inputs.shape
    flat_rows = seq_count * block_len
    cycle_size = lax.axis_size("ctx")
    my_block = lax.axis_index("ctx")
    score_scale = HEAD_DIM ** (-0.5)
    head_shape = (seq_count, block_len, HEADS, HEAD_DIM)
    offsets = jnp.arange(block_len, dtype=jnp.int32)
    query_at = my_block * block_len + offsets
    gain_first, shift_first, full_in, qbias_full, vbias_full, full_out, obias_full = (
        lax.all_gather(first_gain, "fsdp", axis=0, tiled=True),
        lax.all_gather(first_shift, "fsdp", axis=0, tiled=True),
        lax.all_gather(project_in, "fsdp", axis=0, tiled=True),
        lax.all_gather(query_bias, "fsdp", axis=0, tiled=True),
        lax.all_gather(value_bias, "fsdp", axis=0, tiled=True),
        lax.all_gather(project_out, "fsdp", axis=0, tiled=True),
        lax.all_gather(output_bias, "fsdp", axis=0, tiled=True),
    )
    rows_in = inputs.astype(jnp.float32).reshape(flat_rows, model_width)
    normed, norm_first_back = jax.vjp(
        layer_norm, rows_in, gain_first.astype(jnp.float32), shift_first.astype(jnp.float32)
    )
    normed_low = normed.astype(jnp.bfloat16)
    projected = jnp.dot(normed_low, full_in, preferred_element_type=jnp.float32)
    queries = (projected[:, :model_width] + qbias_full).astype(jnp.bfloat16)
    key_rows = projected[:, model_width : 2 * model_width].astype(jnp.bfloat16)
    value_rows = (projected[:, 2 * model_width :] + vbias_full).astype(jnp.bfloat16)
    query_heads = queries.reshape(head_shape)
    running_top = jnp.full((seq_count, HEADS, block_len), -1e30, jnp.float32)
    accumulated = jnp.zeros(head_shape, jnp.float32)
    piece_keys = lax.all_gather(
        key_rows.reshape(seq_count, block_len, model_width), "ctx", axis=1, tiled=True
    )
    piece_values = lax.all_gather(
        value_rows.reshape(seq_count, block_len, model_width), "ctx", axis=1, tiled=True
    )
    piece_len = piece_keys.shape[1]
    key_heads = piece_keys.reshape(seq_count, piece_len, HEADS, HEAD_DIM)
    value_heads = piece_values.reshape(seq_count, piece_len, HEADS, HEAD_DIM)
    scores = (
        jnp.einsum("sqhd,skhd->shqk", query_heads, key_heads, preferred_element_type=jnp.float32)
        * score_scale
    )
    key_at = jnp.arange(piece_len, dtype=jnp.int32)
    visible = query_at[:, None] >= key_at[None, :]
    masked = jnp.where(visible, scores, -1e30)
    new_top = jnp.maximum(running_top, jnp.max(masked, axis=-1))
    factor = jnp.exp(running_top - new_top)
    weights = jnp.where(visible, jnp.exp(masked - new_top[..., None]), 0.0)
    row_total = jnp.sum(weights, axis=-1)
    added = jnp.einsum(
        "shqk,skhd->sqhd",
        weights.astype(jnp.bfloat16),
        value_heads,
        preferred_element_type=jnp.float32,
    )
    accumulated = accumulated * jnp.swapaxes(factor, 1, 2)[..., None] + added
    running_top, row_total, accumulated = (new_top, row_total, accumulated)
    attended = accumulated / jnp.swapaxes(row_total, 1, 2)[..., None]
    log_total = running_top + jnp.log(row_total)
    attended_low = attended.reshape(flat_rows, model_width).astype(jnp.bfloat16)
    middle = (
        rows_in + jnp.dot(attended_low, full_out, preferred_element_type=jnp.float32) + obias_full
    )
    gain_second, shift_second, full_up, ubias_full, full_down, dbias_full = (
        lax.all_gather(second_gain, "fsdp", axis=0, tiled=True),
        lax.all_gather(second_shift, "fsdp", axis=0, tiled=True),
        lax.all_gather(up_weight, "fsdp", axis=0, tiled=True),
        lax.all_gather(up_bias, "fsdp", axis=0, tiled=True),
        lax.all_gather(down_weight, "fsdp", axis=0, tiled=True),
        lax.all_gather(down_bias, "fsdp", axis=0, tiled=True),
    )
    normed_two, norm_second_back = jax.vjp(
        layer_norm, middle, gain_second.astype(jnp.float32), shift_second.astype(jnp.float32)
    )
    normed_two_low = normed_two.astype(jnp.bfloat16)
    hidden = jnp.dot(normed_two_low, full_up, preferred_element_type=jnp.float32) + ubias_full
    active, gelu_back = jax.vjp(gelu_tanh, hidden)
    active_low = active.astype(jnp.bfloat16)
    result = (
        middle + jnp.dot(active_low, full_down, preferred_element_type=jnp.float32) + dbias_full
    )
    outputs = result.astype(jnp.bfloat16).reshape(seq_count, block_len, model_width)
    upstream = cotangent.astype(jnp.float32).reshape(flat_rows, model_width)
    upstream_low = upstream.astype(jnp.bfloat16)
    down_grad = jnp.einsum(
        "rf,rd->fd", active_low, upstream_low, preferred_element_type=jnp.float32
    )
    down_bias_grad = jnp.sum(upstream_low.astype(jnp.float32), axis=0)
    active_grad = jnp.einsum(
        "rd,fd->rf", upstream_low, full_down, preferred_element_type=jnp.float32
    )
    (hidden_grad,) = gelu_back(active_grad)
    hidden_low = hidden_grad.astype(jnp.bfloat16)
    up_grad = jnp.einsum(
        "rd,rf->df", normed_two_low, hidden_low, preferred_element_type=jnp.float32
    )
    up_bias_grad = jnp.sum(hidden_low.astype(jnp.float32), axis=0)
    normed_two_grad = jnp.einsum(
        "rf,df->rd", hidden_low, full_up, preferred_element_type=jnp.float32
    )
    middle_part, gain_two_grad, shift_two_grad = norm_second_back(normed_two_grad)
    middle_grad = upstream + middle_part
    middle_low = middle_grad.astype(jnp.bfloat16)
    out_grad = jnp.einsum("rd,re->de", attended_low, middle_low, preferred_element_type=jnp.float32)
    out_bias_grad = jnp.sum(middle_low.astype(jnp.float32), axis=0)
    attended_grad = jnp.einsum(
        "re,de->rd", middle_low, full_out, preferred_element_type=jnp.float32
    )
    grad_low = attended_grad.astype(jnp.bfloat16).reshape(head_shape)
    row_delta = jnp.swapaxes(jnp.sum(grad_low.astype(jnp.float32) * attended, axis=-1), 1, 2)
    gathered_keys, gathered_values = (
        lax.all_gather(
            key_rows.reshape(1, seq_count, block_len, model_width), "ctx", axis=0, tiled=True
        ),
        lax.all_gather(
            value_rows.reshape(1, seq_count, block_len, model_width), "ctx", axis=0, tiled=True
        ),
    )
    block_ids = jnp.arange(cycle_size, dtype=jnp.int32)

    def key_step(carry, inputs_here):
        key_block, value_block, block_index = inputs_here
        key_heads = key_block.reshape(head_shape)
        value_heads = value_block.reshape(head_shape)
        weights_low, score_low = score_grads(
            query_heads,
            key_heads,
            value_heads,
            grad_low,
            log_total,
            row_delta,
            query_at,
            block_index * block_len + offsets,
        )
        carry = (
            carry
            + jnp.einsum(
                "shqk,skhd->sqhd", score_low, key_heads, preferred_element_type=jnp.float32
            )
            * score_scale
        )
        key_term = (
            jnp.einsum(
                "shqk,sqhd->skhd", score_low, query_heads, preferred_element_type=jnp.float32
            )
            * score_scale
        )
        value_term = jnp.einsum(
            "shqk,sqhd->skhd", weights_low, grad_low, preferred_element_type=jnp.float32
        )
        return (
            carry,
            (
                key_term.reshape(seq_count, block_len, model_width),
                value_term.reshape(seq_count, block_len, model_width),
            ),
        )

    query_grad, (key_terms, value_terms) = lax.scan(
        key_step, jnp.zeros(head_shape, jnp.float32), (gathered_keys, gathered_values, block_ids)
    )
    key_sum, value_sum = (
        lax.psum_scatter(
            key_terms.astype(jnp.bfloat16), "ctx", scatter_dimension=0, tiled=True
        ).astype(jnp.float32),
        lax.psum_scatter(
            value_terms.astype(jnp.bfloat16), "ctx", scatter_dimension=0, tiled=True
        ).astype(jnp.float32),
    )
    key_grad = key_sum.reshape(flat_rows, model_width)
    value_grad = value_sum.reshape(flat_rows, model_width)
    query_low = query_grad.reshape(flat_rows, model_width).astype(jnp.bfloat16)
    key_low = key_grad.astype(jnp.bfloat16)
    value_low = value_grad.astype(jnp.bfloat16)
    stacked = jnp.concatenate([query_low, key_low, value_low], axis=1)
    in_grad = jnp.einsum("rd,re->de", normed_low, stacked, preferred_element_type=jnp.float32)
    query_bias_grad = jnp.sum(query_low.astype(jnp.float32), axis=0)
    value_bias_grad = jnp.sum(value_low.astype(jnp.float32), axis=0)
    normed_grad = jnp.einsum("re,de->rd", stacked, full_in, preferred_element_type=jnp.float32)
    input_part, gain_one_grad, shift_one_grad = norm_first_back(normed_grad)
    input_gradient = (middle_grad + input_part).reshape(seq_count, block_len, model_width)
    (
        gain_one_part,
        shift_one_part,
        in_part,
        qbias_part,
        vbias_part,
        out_part,
        obias_part,
        gain_two_part,
        shift_two_part,
        up_part,
        ubias_part,
        down_part,
        dbias_part,
    ) = (
        lax.psum_scatter(
            gain_one_grad.astype(jnp.bfloat16), "fsdp", scatter_dimension=0, tiled=True
        ).astype(jnp.float32),
        lax.psum_scatter(
            shift_one_grad.astype(jnp.bfloat16), "fsdp", scatter_dimension=0, tiled=True
        ).astype(jnp.float32),
        lax.psum_scatter(
            in_grad.astype(jnp.bfloat16), "fsdp", scatter_dimension=0, tiled=True
        ).astype(jnp.float32),
        lax.psum_scatter(
            query_bias_grad.astype(jnp.bfloat16), "fsdp", scatter_dimension=0, tiled=True
        ).astype(jnp.float32),
        lax.psum_scatter(
            value_bias_grad.astype(jnp.bfloat16), "fsdp", scatter_dimension=0, tiled=True
        ).astype(jnp.float32),
        lax.psum_scatter(
            out_grad.astype(jnp.bfloat16), "fsdp", scatter_dimension=0, tiled=True
        ).astype(jnp.float32),
        lax.psum_scatter(
            out_bias_grad.astype(jnp.bfloat16), "fsdp", scatter_dimension=0, tiled=True
        ).astype(jnp.float32),
        lax.psum_scatter(
            gain_two_grad.astype(jnp.bfloat16), "fsdp", scatter_dimension=0, tiled=True
        ).astype(jnp.float32),
        lax.psum_scatter(
            shift_two_grad.astype(jnp.bfloat16), "fsdp", scatter_dimension=0, tiled=True
        ).astype(jnp.float32),
        lax.psum_scatter(
            up_grad.astype(jnp.bfloat16), "fsdp", scatter_dimension=0, tiled=True
        ).astype(jnp.float32),
        lax.psum_scatter(
            up_bias_grad.astype(jnp.bfloat16), "fsdp", scatter_dimension=0, tiled=True
        ).astype(jnp.float32),
        lax.psum_scatter(
            down_grad.astype(jnp.bfloat16), "fsdp", scatter_dimension=0, tiled=True
        ).astype(jnp.float32),
        lax.psum_scatter(
            down_bias_grad.astype(jnp.bfloat16), "fsdp", scatter_dimension=0, tiled=True
        ).astype(jnp.float32),
    )
    (
        gain_one_sum,
        shift_one_sum,
        in_sum,
        qbias_sum,
        vbias_sum,
        out_sum,
        obias_sum,
        gain_two_sum,
        shift_two_sum,
        up_sum,
        ubias_sum,
        down_sum,
        dbias_sum,
    ) = lax.psum(
        (
            gain_one_part,
            shift_one_part,
            in_part,
            qbias_part,
            vbias_part,
            out_part,
            obias_part,
            gain_two_part,
            shift_two_part,
            up_part,
            ubias_part,
            down_part,
            dbias_part,
        ),
        ("dp", "ctx"),
    )
    return (
        outputs,
        input_gradient,
        gain_one_sum,
        shift_one_sum,
        in_sum,
        qbias_sum,
        vbias_sum,
        out_sum,
        obias_sum,
        gain_two_sum,
        shift_two_sum,
        up_sum,
        ubias_sum,
        down_sum,
        dbias_sum,
    )


NT = (((1,), (1,)), ((), ()))
PAIR = 2 * HEAD_DIM


def attend_kernel(place_ref, q_ref, k_ref, v_ref, o_ref, log_ref, keys, values, *, count, width):
    pair = pl.program_id(0)
    shift = place_ref[0]
    block_len = q_ref.shape[0] // count
    lane = lax.broadcasted_iota(jnp.int32, (1, PAIR), 1)
    valid = lane + pair * PAIR < width
    first = lane < HEAD_DIM

    def rows(block):
        return pl.ds(pl.multiple_of((block ^ shift) * block_len, block_len), block_len)

    for block in range(count):
        here = pl.ds(block * block_len, block_len)
        keys[here, :] = jnp.where(valid, k_ref[rows(block), :], 0)
        values[here, :] = jnp.where(valid, v_ref[rows(block), :], 0)
    diagonal = lax.broadcasted_iota(jnp.int32, (block_len, block_len), 0) >= (
        lax.broadcasted_iota(jnp.int32, (block_len, block_len), 1)
    )
    for block in range(count):
        seen = (block + 1) * block_len
        before = block * block_len
        queries = q_ref[rows(block), :] * jnp.bfloat16(HEAD_DIM**-0.5)
        parts = []
        logs = log_ref[rows(block), :]
        for half in range(2):
            pick = jnp.logical_and(first if half == 0 else jnp.logical_not(first), valid)
            scores = lax.dot_general(
                jnp.where(pick, queries, 0),
                keys[pl.ds(0, seen), :],
                NT,
                preferred_element_type=jnp.float32,
            )
            last = jnp.where(diagonal, scores[:, before:], -1e30)
            scores = last if block == 0 else jnp.concatenate([scores[:, :before], last], axis=1)
            top = jnp.max(scores, axis=1, keepdims=True)
            weights = jnp.exp(scores - top)
            total = jnp.sum(weights, axis=1, keepdims=True)
            added = jnp.dot(
                weights.astype(jnp.bfloat16),
                values[pl.ds(0, seen), :],
                preferred_element_type=jnp.float32,
            )
            parts.append(added / total)
            logs = jnp.where(lane == 2 * pair + half, top + jnp.log(total), logs)
        o_ref[rows(block), :] = jnp.where(first, parts[0], parts[1]).astype(jnp.bfloat16)
        log_ref[rows(block), :] = logs


def attend_back_kernel(
    place_ref,
    q_ref,
    k_ref,
    v_ref,
    g_ref,
    o_ref,
    log_ref,
    dq_ref,
    dk_ref,
    dv_ref,
    queries,
    grads,
    keys,
    values,
    keys_turned,
    logs,
    deltas,
    turned,
    *,
    count,
    width,
):
    pair = pl.program_id(0)
    shift = place_ref[0]
    length = q_ref.shape[0]
    block_len = length // count
    lane = lax.broadcasted_iota(jnp.int32, (1, PAIR), 1)
    valid = lane + pair * PAIR < width
    first = lane < HEAD_DIM
    picks = (jnp.logical_and(first, valid), jnp.logical_and(jnp.logical_not(first), valid))
    half_of = (lax.broadcasted_iota(jnp.int32, (8, PAIR), 1) // HEAD_DIM) == (
        lax.broadcasted_iota(jnp.int32, (8, PAIR), 0)
    )
    ones_of = jnp.where(half_of, 1.0, 0.0)

    def rows(block):
        return pl.ds(pl.multiple_of((block ^ shift) * block_len, block_len), block_len)

    for block in range(count):
        here = pl.ds(block * block_len, block_len)
        key_block = jnp.where(valid, k_ref[rows(block), :], 0)
        keys[here, :] = key_block
        keys_turned[:, here] = key_block.astype(jnp.float32).T.astype(jnp.bfloat16)
        values[here, :] = jnp.where(valid, v_ref[rows(block), :], 0)
        query_block = q_ref[rows(block), :] * jnp.bfloat16(HEAD_DIM**-0.5)
        grad_block = jnp.where(valid, g_ref[rows(block), :], 0)
        for half in range(2):
            queries[half, here, :] = jnp.where(picks[half], query_block, 0)
            grads[half, here, :] = jnp.where(picks[half], grad_block, 0)
        mixed = grad_block.astype(jnp.float32) * jnp.where(
            valid, o_ref[rows(block), :], 0
        ).astype(jnp.float32)
        deltas[:, here] = lax.dot_general(
            ones_of,
            mixed,
            NT,
            preferred_element_type=jnp.float32,
            precision=lax.Precision.HIGHEST,
        )
        logs[:, here] = log_ref[
            0, :, pl.ds(pl.multiple_of((block ^ shift) * block_len, block_len), block_len)
        ]
    diagonal = lax.broadcasted_iota(jnp.int32, (block_len, block_len), 0) <= (
        lax.broadcasted_iota(jnp.int32, (block_len, block_len), 1)
    )
    for block in range(count):
        here = pl.ds(block * block_len, block_len)
        after = pl.ds(block * block_len, length - block * block_len)
        key_total = jnp.zeros((block_len, PAIR), jnp.float32)
        value_total = jnp.zeros((block_len, PAIR), jnp.float32)
        for half in range(2):
            scores = lax.dot_general(
                keys[here, :], queries[half, after, :], NT, preferred_element_type=jnp.float32
            )
            shifted = scores - logs[half : half + 1, after]
            own = jnp.where(diagonal, shifted[:, :block_len], -1e30)
            if block < count - 1:
                own = jnp.concatenate([own, shifted[:, block_len:]], axis=1)
            weights = jnp.exp(own)
            pressure = lax.dot_general(
                values[here, :], grads[half, after, :], NT, preferred_element_type=jnp.float32
            )
            score_low = (weights * (pressure - deltas[half : half + 1, after])).astype(
                jnp.bfloat16
            )
            value_total += jnp.dot(
                weights.astype(jnp.bfloat16),
                grads[half, after, :],
                preferred_element_type=jnp.float32,
            )
            key_total += jnp.dot(
                score_low, queries[half, after, :], preferred_element_type=jnp.float32
            )
            part = pl.ds(half * HEAD_DIM, HEAD_DIM)
            term = jnp.dot(
                keys_turned[part, here], score_low, preferred_element_type=jnp.float32
            )
            if block == 0:
                turned[part, after] = term
            else:
                turned[part, after] += term
        dk_ref[rows(block), :] = key_total.astype(jnp.bfloat16)
        dv_ref[rows(block), :] = value_total.astype(jnp.bfloat16)
    for block in range(count):
        here = pl.ds(block * block_len, block_len)
        dq_ref[rows(block), :] = (turned[:, here].T * HEAD_DIM**-0.5).astype(jnp.bfloat16)


def attend(place, queries, key_rows, value_rows, count):
    length, width = queries.shape
    pairs = pl.cdiv(width, PAIR)
    heads_block = pl.BlockSpec((length, PAIR), lambda pair, place_ref: (0, pair))
    return pl.pallas_call(
        functools.partial(attend_kernel, count=count, width=width),
        grid_spec=pltpu.PrefetchScalarGridSpec(
            num_scalar_prefetch=1,
            grid=(pairs,),
            in_specs=[heads_block] * 3,
            out_specs=[
                heads_block,
                pl.BlockSpec((length, 128), lambda pair, place_ref: (0, 0)),
            ],
            scratch_shapes=[pltpu.VMEM((length, PAIR), jnp.bfloat16)] * 2,
        ),
        out_shape=[
            jax.ShapeDtypeStruct((length, width), jnp.bfloat16),
            jax.ShapeDtypeStruct((length, 128), jnp.float32),
        ],
        compiler_params=pltpu.CompilerParams(vmem_limit_bytes=48 * 2**20),
        cost_estimate=pl.CostEstimate(
            flops=4 * length * length * width,
            bytes_accessed=8 * length * width,
            transcendentals=HEADS * length * length // 2,
        ),
        name="attend",
    )(place, queries, key_rows, value_rows)


def attend_back(place, queries, key_rows, value_rows, grads, attended, logs, count):
    length, width = queries.shape
    pairs = pl.cdiv(width, PAIR)
    heads_block = pl.BlockSpec((length, PAIR), lambda pair, place_ref: (0, pair))
    low_rows = pltpu.VMEM((length, PAIR), jnp.bfloat16)
    low_pair = pltpu.VMEM((2, length, PAIR), jnp.bfloat16)
    return pl.pallas_call(
        functools.partial(attend_back_kernel, count=count, width=width),
        grid_spec=pltpu.PrefetchScalarGridSpec(
            num_scalar_prefetch=1,
            grid=(pairs,),
            in_specs=[heads_block] * 5
            + [pl.BlockSpec((1, 2, length), lambda pair, place_ref: (pair, 0, 0))],
            out_specs=[heads_block] * 3,
            scratch_shapes=[
                low_pair,
                low_pair,
                low_rows,
                low_rows,
                pltpu.VMEM((PAIR, length), jnp.bfloat16),
                pltpu.VMEM((2, length), jnp.float32),
                pltpu.VMEM((8, length), jnp.float32),
                pltpu.VMEM((PAIR, length), jnp.float32),
            ],
        ),
        out_shape=[jax.ShapeDtypeStruct((length, width), jnp.bfloat16)] * 3,
        compiler_params=pltpu.CompilerParams(vmem_limit_bytes=48 * 2**20),
        cost_estimate=pl.CostEstimate(
            flops=10 * length * length * width,
            bytes_accessed=16 * length * width,
            transcendentals=HEADS * length * length // 2,
        ),
        name="attend_back",
    )(place, queries, key_rows, value_rows, grads, attended, logs)


def settle_kernel(place_ref, *refs):
    pieces, out_ref = refs[:-1], refs[-1]
    for at, piece in enumerate(pieces):
        out_ref[place_ref[at]] = piece[...].astype(out_ref.dtype)


def settle(places, pieces, dtype):
    return pl.pallas_call(
        settle_kernel,
        in_specs=[pl.BlockSpec(memory_space=pltpu.SMEM)]
        + [pl.BlockSpec(memory_space=pltpu.VMEM)] * len(pieces),
        out_specs=pl.BlockSpec(memory_space=pltpu.VMEM),
        out_shape=jax.ShapeDtypeStruct((len(pieces),) + pieces[0].shape, dtype),
        compiler_params=pltpu.CompilerParams(vmem_limit_bytes=48 * 2**20),
        name="settle",
    )(places, *pieces)


def plane_partner(device, kind):
    core = device & 1
    if kind == "core":
        return device ^ 1
    if kind == "near":
        return device ^ (2 if core else 4)
    return device ^ (4 if core else 2)


def plane_swap(values, kind):
    return lax.ppermute(
        values, ("dp", "ctx"), [(device, plane_partner(device, kind)) for device in range(8)]
    )


def ctx_swap(values, bits):
    return lax.ppermute(values, "ctx", [(device, device ^ bits) for device in range(4)])


def reduce_pieces(pieces):
    far_two = plane_swap(pieces[3], "core")
    far = plane_swap(pieces[2], "core")
    second = (pieces[1].astype(jnp.float32) + far_two.astype(jnp.float32)).astype(jnp.bfloat16)
    near = plane_swap(second, "near")
    first = (
        pieces[0].astype(jnp.float32) + far.astype(jnp.float32) + near.astype(jnp.float32)
    ).astype(jnp.bfloat16)
    shard = lax.psum_scatter(first, "fsdp", scatter_dimension=0, tiled=True)
    whole = (shard.astype(jnp.float32) + plane_swap(shard, "other").astype(jnp.float32)).astype(
        jnp.bfloat16
    )
    beside = plane_swap(whole, "near")
    return [whole, beside, plane_swap(whole, "core"), plane_swap(beside, "core")]


def chosen(index, options):
    result = options[-1]
    for at in range(len(options) - 2, -1, -1):
        result = jnp.where(index == at, options[at], result)
    return result


def gather_vector(values, z):
    around = [values] + [
        lax.ppermute(values, "fsdp", [(device, (device + step) % 4) for device in range(4)])
        for step in range(1, 4)
    ]
    return jnp.stack([chosen((z - at) % 4, around) for at in range(4)])


def reduce_vector(values, z):
    rows = [values[at] for at in range(4)]
    total = chosen(z, rows)
    for step in range(1, 4):
        total = total + lax.ppermute(
            chosen((z + step) % 4, rows),
            "fsdp",
            [(device, (device + step) % 4) for device in range(4)],
        )
    for bits in (1, 2, 4):
        total = total + lax.ppermute(
            total, ("dp", "ctx"), [(device, device ^ bits) for device in range(8)]
        )
    return total


def product(left, right, dims):
    return lax.dot_general(left, right, ((dims[:1], dims[1:]), ((), ())),
                           preferred_element_type=jnp.float32)


def gelu_pair(values):
    inner = 0.7978845608028654
    squared = values * values
    curve = jnp.tanh(inner * (values + 0.044715 * values * squared))
    active = 0.5 * values * (1.0 + curve)
    slope = 0.5 * (1.0 + curve) + 0.5 * values * (1.0 - curve * curve) * inner * (
        1.0 + 3.0 * 0.044715 * squared
    )
    return active, slope


def block_flops(rows, width, count):
    return pl.CostEstimate(
        flops=2 * rows * width * width * count,
        bytes_accessed=2 * width * width * count + 4 * rows * width * count,
        transcendentals=0,
    )


def unit_of(values):
    centred = values - jnp.mean(values, axis=-1, keepdims=True)
    scale = lax.rsqrt(jnp.mean(centred * centred, axis=-1, keepdims=True) + epsilon)
    return centred * scale, scale


def fold(values):
    rows, width = values.shape
    return jnp.sum(values.reshape(rows // 8, 8, width), axis=0)


def front_kernel(places_ref, x_ref, vectors_ref, *refs):
    pieces = refs[:16]
    h_ref, q_ref, k_ref, v_ref, all_ref, weights, arrived, left = refs[16:]
    copies = [
        pltpu.make_async_copy(piece, weights.at[places_ref[at]], arrived.at[at])
        for at, piece in enumerate(pieces)
    ]
    for copy in copies:
        copy.start()
    rows, width = x_ref.shape
    step = 256

    def norm(at, carry):
        here = pl.ds(pl.multiple_of(at * step, step), step)
        unit, _ = unit_of(x_ref[here, :].astype(jnp.float32))
        h_ref[here, :] = (unit * vectors_ref[0:1, :] + vectors_ref[1:2, :]).astype(jnp.bfloat16)
        return carry

    lax.fori_loop(0, rows // step, norm, 0)
    for copy in copies:
        copy.wait()
    leave = pltpu.make_async_copy(weights, all_ref, left)
    leave.start()
    for section, out_ref in enumerate((q_ref, k_ref, v_ref)):

        def multiply(at, carry, section=section, out_ref=out_ref):
            here = pl.ds(pl.multiple_of(at * step, step), step)
            matrix = weights[4 * section : 4 * section + 4].reshape(width, width)
            total = jnp.dot(h_ref[here, :], matrix, preferred_element_type=jnp.float32)
            if section != 1:
                row = 2 if section == 0 else 3
                total = total + vectors_ref[row : row + 1, :]
            out_ref[here, :] = total.astype(jnp.bfloat16)
            return carry

        lax.fori_loop(0, rows // step, multiply, 0)
    leave.wait()


def front(places, rows_in, vectors, pieces):
    rows, width = rows_in.shape
    vmem = pl.BlockSpec(memory_space=pltpu.VMEM)
    hbm = pl.BlockSpec(memory_space=pl.ANY)
    shape = jax.ShapeDtypeStruct((rows, width), jnp.bfloat16)
    whole = (16,) + pieces[0].shape
    return pl.pallas_call(
        front_kernel,
        in_specs=[pl.BlockSpec(memory_space=pltpu.SMEM), vmem, vmem] + [hbm] * 16,
        out_specs=[vmem] * 4 + [hbm],
        out_shape=[shape] * 4 + [jax.ShapeDtypeStruct(whole, jnp.bfloat16)],
        scratch_shapes=[
            pltpu.VMEM(whole, jnp.bfloat16),
            pltpu.SemaphoreType.DMA((16,)),
            pltpu.SemaphoreType.DMA,
        ],
        compiler_params=pltpu.CompilerParams(vmem_limit_bytes=56 * 2**20),
        cost_estimate=block_flops(rows, width, 3),
        name="front",
    )(places, rows_in, vectors, *pieces)


def fetch(step, copies):
    @pl.when(step == 0)
    def _():
        for copy in copies:
            copy.start()


def arrive(step, copy):
    @pl.when(step == 0)
    def _():
        copy.wait()


def add_sums(step, sums_ref, terms):
    @pl.when(step == 0)
    def _():
        sums_ref[...] = jnp.zeros_like(sums_ref)

    for at, term in enumerate(terms):
        sums_ref[at] += fold(term)


def middle_kernel(x_ref, o_ref, vectors_ref, all_ref, middle_ref, h_ref, weights, arrived):
    step = pl.program_id(0)
    width = x_ref.shape[1]
    copy = pltpu.make_async_copy(all_ref.at[pl.ds(12, 4)], weights, arrived)
    fetch(step, [copy])
    arrive(step, copy)
    middle = (
        x_ref[...].astype(jnp.float32)
        + jnp.dot(
            o_ref[...], weights[...].reshape(width, width), preferred_element_type=jnp.float32
        )
        + vectors_ref[0:1, :]
    )
    middle_ref[...] = middle
    unit, _ = unit_of(middle)
    h_ref[...] = (unit * vectors_ref[1:2, :] + vectors_ref[2:3, :]).astype(jnp.bfloat16)


def up_kernel(h_ref, biases_ref, *refs):
    sources = refs[:4]
    active_refs, slope_refs = refs[4:8], refs[8:12]
    weights, arrived = refs[12:]
    step = pl.program_id(0)
    copies = [
        pltpu.make_async_copy(source, weights.at[at], arrived.at[at])
        for at, source in enumerate(sources)
    ]
    fetch(step, copies)
    for at in range(4):
        arrive(step, copies[at])
        hidden = (
            jnp.dot(h_ref[...], weights[at], preferred_element_type=jnp.float32)
            + biases_ref[at : at + 1, :]
        )
        active, slope = gelu_pair(hidden)
        active_refs[at][...] = active.astype(jnp.bfloat16)
        slope_refs[at][...] = slope.astype(jnp.bfloat16)


def down_kernel(middle_ref, vectors_ref, *refs):
    actives, sources = refs[:4], refs[4:8]
    out_ref, weights, arrived = refs[8:]
    step = pl.program_id(0)
    copies = [
        pltpu.make_async_copy(source, weights.at[at], arrived.at[at])
        for at, source in enumerate(sources)
    ]
    fetch(step, copies)
    total = middle_ref[...] + vectors_ref[0:1, :]
    for at in range(4):
        arrive(step, copies[at])
        total = total + jnp.dot(
            actives[at][...], weights[at], preferred_element_type=jnp.float32
        )
    out_ref[...] = total.astype(jnp.bfloat16)


def norm_back(values, gain, grad):
    unit, scale = unit_of(values)
    turned = grad * gain
    inner = (
        turned
        - jnp.mean(turned, axis=-1, keepdims=True)
        - unit * jnp.mean(turned * unit, axis=-1, keepdims=True)
    )
    return scale * inner, grad * unit


def back_kernel(g_ref, middle_ref, vectors_ref, *refs):
    slopes, downs, ups, all_ref = refs[:4], refs[4:8], refs[8:12], refs[12]
    hidden_refs = refs[13:17]
    grad_ref, low_ref, out_ref, sums_ref = refs[17:21]
    down_weights, up_weights, out_weights, arrived = refs[21:]
    step = pl.program_id(0)
    width = middle_ref.shape[1]
    copies = []
    for at in range(4):
        copies.append(
            pltpu.make_async_copy(downs[at], down_weights.at[at], arrived.at[2 * at])
        )
        copies.append(
            pltpu.make_async_copy(ups[at], up_weights.at[at], arrived.at[2 * at + 1])
        )
    copies.append(
        pltpu.make_async_copy(all_ref.at[pl.ds(12, 4)], out_weights, arrived.at[8])
    )
    fetch(step, copies)
    upstream = g_ref[...]
    sums = []
    total = jnp.zeros(middle_ref.shape, jnp.float32)
    for at in range(4):
        arrive(step, copies[2 * at])
        hidden = lax.dot_general(
            upstream, down_weights[at], NT, preferred_element_type=jnp.float32
        )
        hidden = (hidden * slopes[at][...].astype(jnp.float32)).astype(jnp.bfloat16)
        hidden_refs[at][...] = hidden
        sums.append(fold(hidden.astype(jnp.float32)))
        arrive(step, copies[2 * at + 1])
        total = total + lax.dot_general(
            hidden, up_weights[at], NT, preferred_element_type=jnp.float32
        )
    part, gain_term = norm_back(middle_ref[...], vectors_ref[0:1, :], total)
    upstream = upstream.astype(jnp.float32)
    grad = upstream + part
    grad_ref[...] = grad
    grad_low = grad.astype(jnp.bfloat16)
    low_ref[...] = grad_low
    sums += [
        fold(gain_term), fold(total), fold(upstream), fold(grad_low.astype(jnp.float32))
    ]
    arrive(step, copies[8])
    out_ref[...] = lax.dot_general(
        grad_low,
        out_weights[...].reshape(width, width),
        NT,
        preferred_element_type=jnp.float32,
    ).astype(jnp.bfloat16)

    @pl.when(step == 0)
    def _():
        sums_ref[...] = jnp.zeros_like(sums_ref)

    for at, term in enumerate(sums):
        sums_ref[at] += term


def last_kernel(q_ref, k_ref, v_ref, x_ref, grad_ref, vectors_ref, all_ref, *refs):
    out_ref, sums_ref, weights, arrived = refs
    step = pl.program_id(0)
    width = x_ref.shape[1]
    copies = [
        pltpu.make_async_copy(
            all_ref.at[pl.ds(4 * at, 4)], weights.at[pl.ds(4 * at, 4)], arrived.at[at]
        )
        for at in range(3)
    ]
    fetch(step, copies)
    total = jnp.zeros(x_ref.shape, jnp.float32)
    for at, ref in enumerate((q_ref, k_ref, v_ref)):
        arrive(step, copies[at])
        total = total + lax.dot_general(
            ref[...],
            weights[4 * at : 4 * at + 4].reshape(width, width),
            NT,
            preferred_element_type=jnp.float32,
        )
    part, gain_term = norm_back(x_ref[...].astype(jnp.float32), vectors_ref[0:1, :], total)
    out_ref[...] = (grad_ref[...] + part).astype(jnp.bfloat16)

    @pl.when(step == 0)
    def _():
        sums_ref[...] = jnp.zeros_like(sums_ref)

    terms = (
        gain_term,
        total,
        q_ref[...].astype(jnp.float32),
        v_ref[...].astype(jnp.float32),
    )
    for at, term in enumerate(terms):
        sums_ref[at] += fold(term)


def by_rows(kernel, name, rows, width, tiled, whole, remote, outs, sums, scratch, sems, blocks):
    step = 256
    tile = pl.BlockSpec((step, width), lambda at: (at, 0))
    out_specs = [tile] * len(outs)
    out_shape = [jax.ShapeDtypeStruct((rows, width), dtype) for dtype in outs]
    if sums:
        out_specs.append(pl.BlockSpec((sums, 8, width), lambda at: (0, 0, 0)))
        out_shape.append(jax.ShapeDtypeStruct((sums, 8, width), jnp.float32))
    return pl.pallas_call(
        kernel,
        grid=(rows // step,),
        in_specs=[tile] * len(tiled[0])
        + [pl.BlockSpec(value.shape, lambda at: (0, 0)) for value in whole]
        + [tile] * len(tiled[1])
        + [pl.BlockSpec(memory_space=pl.ANY)] * len(remote),
        out_specs=out_specs,
        out_shape=out_shape,
        scratch_shapes=[pltpu.VMEM(shape, jnp.bfloat16) for shape in scratch]
        + [pltpu.SemaphoreType.DMA((sems,)) if sems > 1 else pltpu.SemaphoreType.DMA],
        compiler_params=pltpu.CompilerParams(vmem_limit_bytes=60 * 2**20),
        cost_estimate=block_flops(rows, width, blocks),
        name=name,
    )(*tiled[0], *whole, *tiled[1], *remote)


def per_device_exchanged(
    inputs,
    cotangent,
    first_gain,
    first_shift,
    project_in,
    query_bias,
    value_bias,
    project_out,
    output_bias,
    second_gain,
    second_shift,
    up_weight,
    up_bias,
    down_weight,
    down_bias,
):
    seq_count, block_len, width = inputs.shape
    low = jnp.bfloat16
    wide = jnp.float32
    c = lax.axis_index("ctx")
    y = lax.axis_index("dp")
    z = lax.axis_index("fsdp")
    core = c & 1
    x = c >> 1
    mine = core * 2 + jnp.where(core == 0, y, x)
    across = (1 - core) * 2 + jnp.where(core == 0, x, y)
    classes = [mine, mine ^ 1, across, across ^ 1]
    slot_of = [
        chosen(0, [sum(at * (classes[at] == kind).astype(jnp.int32) for at in range(4))])
        for kind in range(4)
    ]
    quarter = width // 4
    rows, area = seq_count * block_len, (width, width)
    pin = lax.optimization_barrier
    place = jnp.stack([c])
    places = jnp.stack([c ^ at for at in range(4)])
    class_places = jnp.stack(classes)

    def spread(values):
        return jnp.concatenate(
            [lax.dynamic_index_in_dim(values, c, 0, keepdims=False)]
            + [
                ctx_swap(lax.dynamic_index_in_dim(values, c ^ bits, 0, keepdims=False), bits)
                for bits in range(1, 4)
            ],
            axis=0,
        )

    def collect(values, dtype):
        pieces = [values[at * block_len : (at + 1) * block_len] for at in range(4)]
        moved = [pieces[0]] + [ctx_swap(pieces[bits], bits) for bits in range(1, 4)]
        return settle(places, moved, dtype)

    sections = [
        project_in[:, :width],
        project_in[:, width : 2 * width],
        project_in[:, 2 * width :],
        project_out,
    ]
    section = chosen(mine, sections)
    shards = [
        lax.ppermute(section, "fsdp", [(device, (device + step) % 4) for device in range(4)])
        for step in range(1, 4)
    ]
    up_piece = jnp.concatenate(
        [
            lax.dynamic_slice_in_dim(up_weight, at * width + mine * quarter, quarter, 1)
            for at in range(4)
        ],
        axis=1,
    )
    up_piece, *shards = pin((up_piece, *shards))
    near_shards = [plane_swap(shard, "near") for shard in shards]
    around = (
        sections
        + shards
        + near_shards
        + [plane_swap(shard, "core") for shard in shards]
        + [plane_swap(shard, "core") for shard in near_shards]
    )
    around_places = jnp.stack(
        [kind * 4 + z for kind in range(4)]
        + [kind * 4 + (z - step) % 4 for kind in classes for step in range(1, 4)]
    )
    up_own = lax.all_gather(up_piece, "fsdp", axis=0, tiled=True)
    down_piece = lax.dynamic_slice_in_dim(down_weight, mine * quarter, quarter, 0)
    down_piece, up_own = pin((down_piece, up_own))
    down_own = lax.all_gather(down_piece, "fsdp", axis=0, tiled=True)

    def exchange(own):
        near = plane_swap(own, "near")
        return [own, near, plane_swap(own, "core"), plane_swap(near, "core")]

    vectors = gather_vector(
        jnp.concatenate(
            [
                first_gain,
                first_shift,
                query_bias,
                value_bias,
                output_bias,
                second_gain,
                second_shift,
                down_bias,
                up_bias,
            ]
        ),
        z,
    ).astype(wide)
    gain_first, shift_first, qbias, vbias, obias, gain_second, shift_second, dbias = (
        vectors[:, at * quarter : (at + 1) * quarter].reshape(1, width) for at in range(8)
    )
    ubias = vectors[:, 8 * quarter :].reshape(4, 4, quarter)
    ubias = jnp.concatenate(
        [
            chosen(kind, [ubias[:, at] for at in range(4)]).reshape(1, width)
            for kind in classes
        ],
        axis=0,
    )

    rows_in = spread(inputs)
    normed_low, queries, key_rows, value_rows, weights = front(
        around_places,
        rows_in,
        jnp.concatenate([gain_first, shift_first, qbias, vbias], axis=0),
        around,
    )
    up_own, late_queries = pin((up_own, queries))
    up_slots = exchange(up_own)
    cotangent, late_queries = pin((cotangent, late_queries))
    upstream_low = spread(cotangent)
    attended, logs = attend(place, queries, key_rows, value_rows, seq_count)
    down_own, late_attended = pin((down_own, attended))
    down_slots = exchange(down_own)
    turned_logs = logs.T.reshape(64, 2, rows)
    middle, normed_two_low = by_rows(
        middle_kernel,
        "middle",
        rows,
        width,
        ([rows_in, attended], []),
        [jnp.concatenate([obias, gain_second, shift_second], axis=0)],
        [weights],
        [wide, low],
        0,
        [(4,) + section.shape],
        1,
        1,
    )
    up_outs = by_rows(
        up_kernel,
        "up",
        rows,
        width,
        ([normed_two_low], []),
        [ubias],
        up_slots,
        [low] * 8,
        0,
        [(4,) + area],
        4,
        4,
    )
    active, slopes = up_outs[:4], up_outs[4:]
    (result,) = by_rows(
        down_kernel,
        "down",
        rows,
        width,
        ([middle], active),
        [dbias],
        down_slots,
        [low],
        0,
        [(4,) + area],
        4,
        4,
    )
    outputs = collect(result, low)

    down_terms = [product(active[slot], upstream_low, (0, 0)).astype(low) for slot in range(4)]
    upstream_low, *down_terms = pin((upstream_low, *down_terms))
    down_parts = reduce_pieces(down_terms)
    back_outs = by_rows(
        back_kernel,
        "back",
        rows,
        width,
        ([upstream_low, middle], slopes),
        [gain_second],
        down_slots + up_slots + [weights],
        [low] * 4 + [wide, low, low],
        8,
        [(4,) + area, (4,) + area, (4,) + section.shape],
        9,
        9,
    )
    hidden_low = back_outs[:4]
    middle_grad, middle_low, grad_low, back_sums = back_outs[4:]
    up_terms = [
        product(normed_two_low, hidden_low[slot], (0, 0)).astype(low) for slot in range(4)
    ]
    out_term = product(attended, middle_low, (0, 0)).astype(low)
    grad_low, out_term, *up_terms = pin((grad_low, out_term, *up_terms))
    up_parts = reduce_pieces(up_terms)
    query_low, key_low, value_low = attend_back(
        place,
        late_queries,
        key_rows,
        value_rows,
        grad_low,
        late_attended,
        turned_logs,
        seq_count,
    )
    in_terms = [
        product(normed_low, grad, (0, 0)).astype(low) for grad in (query_low, key_low, value_low)
    ]
    query_low, key_low, value_low, *in_terms = pin(
        (query_low, key_low, value_low, *in_terms)
    )
    section_grads = in_terms + [out_term]
    section_parts = reduce_pieces([chosen(kind, section_grads) for kind in classes])
    input_low, last_sums = by_rows(
        last_kernel,
        "last",
        rows,
        width,
        ([query_low, key_low, value_low, rows_in, middle_grad], []),
        [gain_first],
        [weights],
        [low],
        4,
        [(12,) + section.shape],
        3,
        3,
    )
    input_gradient = collect(input_low, wide)

    back_sums = jnp.sum(back_sums, axis=1)
    last_sums = jnp.sum(last_sums, axis=1)
    hidden_sums = [back_sums[slot].reshape(4, quarter) for slot in range(4)]
    hidden_sums = jnp.stack(
        [chosen(slot_of[kind], hidden_sums) for kind in range(4)], axis=1
    ).reshape(4, 4 * quarter)
    early = reduce_vector(
        jnp.concatenate(
            [back_sums[at].reshape(4, quarter) for at in range(4, 8)] + [hidden_sums], axis=1
        ),
        z,
    )
    late = reduce_vector(
        jnp.concatenate([last_sums[at].reshape(4, quarter) for at in range(4)], axis=1), z
    )
    gain_two_sum, shift_two_sum, dbias_sum, obias_sum = (
        early[at * quarter : (at + 1) * quarter] for at in range(4)
    )
    ubias_sum = early[4 * quarter :]
    gain_one_sum, shift_one_sum, qbias_sum, vbias_sum = (
        late[at * quarter : (at + 1) * quarter] for at in range(4)
    )
    in_parts = [chosen(slot_of[kind], section_parts).astype(wide) for kind in range(4)]
    up_parts = [chosen(slot_of[kind], up_parts) for kind in range(4)]
    up_sum = jnp.concatenate(
        [
            up_parts[kind][:, at * quarter : (at + 1) * quarter]
            for at in range(4)
            for kind in range(4)
        ],
        axis=1,
    ).astype(wide)
    down_sum = settle(class_places, down_parts, wide).reshape(down_weight.shape)
    return (
        outputs,
        input_gradient,
        gain_one_sum,
        shift_one_sum,
        jnp.concatenate(in_parts[:3], axis=1),
        qbias_sum,
        vbias_sum,
        in_parts[3],
        obias_sum,
        gain_two_sum,
        shift_two_sum,
        up_sum,
        ubias_sum,
        down_sum,
        dbias_sum,
    )


def solution(mesh):
    sizes = dict(mesh.shape)
    exchanged = sizes["dp"] == 2 and sizes["fsdp"] == 4 and sizes["ctx"] == 4
    per_device = per_device_exchanged if exchanged else per_device_gathered
    return jax.shard_map(
        per_device,
        mesh=mesh,
        in_specs=(
            P(("dp", "fsdp"), "ctx", None),
            P(("dp", "fsdp"), "ctx", None),
            P("fsdp"),
            P("fsdp"),
            P("fsdp", None),
            P("fsdp"),
            P("fsdp"),
            P("fsdp", None),
            P("fsdp"),
            P("fsdp"),
            P("fsdp"),
            P("fsdp", None),
            P("fsdp"),
            P("fsdp", None),
            P("fsdp"),
        ),
        out_specs=(
            P(("dp", "fsdp"), "ctx", None),
            P(("dp", "fsdp"), "ctx", None),
            P("fsdp"),
            P("fsdp"),
            P("fsdp", None),
            P("fsdp"),
            P("fsdp"),
            P("fsdp", None),
            P("fsdp"),
            P("fsdp"),
            P("fsdp"),
            P("fsdp", None),
            P("fsdp"),
            P("fsdp", None),
            P("fsdp"),
        ),
        check_vma=False,
    )
```

```python
import functools

import jax
import jax.numpy as jnp
from jax import lax
from jax.experimental import pallas as pl
from jax.experimental.pallas import tpu as pltpu
from jax.sharding import PartitionSpec as P

HEADS = 17
HEAD_DIM = 64


epsilon = 1e-05


def layer_norm(values, gain, shift):
    centred = values - jnp.mean(values, axis=-1, keepdims=True)
    spread = jnp.mean(centred * centred, axis=-1, keepdims=True)
    return centred * lax.rsqrt(spread + epsilon) * gain + shift


def gelu_tanh(values):
    return jax.nn.gelu(values, approximate=True)


def score_grads(
    query_heads, key_heads, value_heads, grad_heads, log_total, row_delta, query_at, key_at
):
    score_scale = HEAD_DIM ** (-0.5)
    scores = (
        jnp.einsum("sqhd,skhd->shqk", query_heads, key_heads, preferred_element_type=jnp.float32)
        * score_scale
    )
    visible = query_at[:, None] >= key_at[None, :]
    shifted = jnp.where(visible, scores - log_total[..., None], -1e30)
    weights = jnp.where(visible, jnp.exp(shifted), 0.0)
    pressure = jnp.einsum(
        "sqhd,skhd->shqk", grad_heads, value_heads, preferred_element_type=jnp.float32
    )
    score_low = (weights * (pressure - row_delta[..., None])).astype(jnp.bfloat16)
    return (weights.astype(jnp.bfloat16), score_low)


def per_device_gathered(
    inputs,
    cotangent,
    first_gain,
    first_shift,
    project_in,
    query_bias,
    value_bias,
    project_out,
    output_bias,
    second_gain,
    second_shift,
    up_weight,
    up_bias,
    down_weight,
    down_bias,
):
    seq_count, block_len, model_width = inputs.shape
    flat_rows = seq_count * block_len
    cycle_size = lax.axis_size("ctx")
    my_block = lax.axis_index("ctx")
    score_scale = HEAD_DIM ** (-0.5)
    head_shape = (seq_count, block_len, HEADS, HEAD_DIM)
    offsets = jnp.arange(block_len, dtype=jnp.int32)
    query_at = my_block * block_len + offsets
    gain_first, shift_first, full_in, qbias_full, vbias_full, full_out, obias_full = (
        lax.all_gather(first_gain, "fsdp", axis=0, tiled=True),
        lax.all_gather(first_shift, "fsdp", axis=0, tiled=True),
        lax.all_gather(project_in, "fsdp", axis=0, tiled=True),
        lax.all_gather(query_bias, "fsdp", axis=0, tiled=True),
        lax.all_gather(value_bias, "fsdp", axis=0, tiled=True),
        lax.all_gather(project_out, "fsdp", axis=0, tiled=True),
        lax.all_gather(output_bias, "fsdp", axis=0, tiled=True),
    )
    rows_in = inputs.astype(jnp.float32).reshape(flat_rows, model_width)
    normed, norm_first_back = jax.vjp(
        layer_norm, rows_in, gain_first.astype(jnp.float32), shift_first.astype(jnp.float32)
    )
    normed_low = normed.astype(jnp.bfloat16)
    projected = jnp.dot(normed_low, full_in, preferred_element_type=jnp.float32)
    queries = (projected[:, :model_width] + qbias_full).astype(jnp.bfloat16)
    key_rows = projected[:, model_width : 2 * model_width].astype(jnp.bfloat16)
    value_rows = (projected[:, 2 * model_width :] + vbias_full).astype(jnp.bfloat16)
    query_heads = queries.reshape(head_shape)
    running_top = jnp.full((seq_count, HEADS, block_len), -1e30, jnp.float32)
    accumulated = jnp.zeros(head_shape, jnp.float32)
    piece_keys = lax.all_gather(
        key_rows.reshape(seq_count, block_len, model_width), "ctx", axis=1, tiled=True
    )
    piece_values = lax.all_gather(
        value_rows.reshape(seq_count, block_len, model_width), "ctx", axis=1, tiled=True
    )
    piece_len = piece_keys.shape[1]
    key_heads = piece_keys.reshape(seq_count, piece_len, HEADS, HEAD_DIM)
    value_heads = piece_values.reshape(seq_count, piece_len, HEADS, HEAD_DIM)
    scores = (
        jnp.einsum("sqhd,skhd->shqk", query_heads, key_heads, preferred_element_type=jnp.float32)
        * score_scale
    )
    key_at = jnp.arange(piece_len, dtype=jnp.int32)
    visible = query_at[:, None] >= key_at[None, :]
    masked = jnp.where(visible, scores, -1e30)
    new_top = jnp.maximum(running_top, jnp.max(masked, axis=-1))
    factor = jnp.exp(running_top - new_top)
    weights = jnp.where(visible, jnp.exp(masked - new_top[..., None]), 0.0)
    row_total = jnp.sum(weights, axis=-1)
    added = jnp.einsum(
        "shqk,skhd->sqhd",
        weights.astype(jnp.bfloat16),
        value_heads,
        preferred_element_type=jnp.float32,
    )
    accumulated = accumulated * jnp.swapaxes(factor, 1, 2)[..., None] + added
    running_top, row_total, accumulated = (new_top, row_total, accumulated)
    attended = accumulated / jnp.swapaxes(row_total, 1, 2)[..., None]
    log_total = running_top + jnp.log(row_total)
    attended_low = attended.reshape(flat_rows, model_width).astype(jnp.bfloat16)
    middle = (
        rows_in + jnp.dot(attended_low, full_out, preferred_element_type=jnp.float32) + obias_full
    )
    gain_second, shift_second, full_up, ubias_full, full_down, dbias_full = (
        lax.all_gather(second_gain, "fsdp", axis=0, tiled=True),
        lax.all_gather(second_shift, "fsdp", axis=0, tiled=True),
        lax.all_gather(up_weight, "fsdp", axis=0, tiled=True),
        lax.all_gather(up_bias, "fsdp", axis=0, tiled=True),
        lax.all_gather(down_weight, "fsdp", axis=0, tiled=True),
        lax.all_gather(down_bias, "fsdp", axis=0, tiled=True),
    )
    normed_two, norm_second_back = jax.vjp(
        layer_norm, middle, gain_second.astype(jnp.float32), shift_second.astype(jnp.float32)
    )
    normed_two_low = normed_two.astype(jnp.bfloat16)
    hidden = jnp.dot(normed_two_low, full_up, preferred_element_type=jnp.float32) + ubias_full
    active, gelu_back = jax.vjp(gelu_tanh, hidden)
    active_low = active.astype(jnp.bfloat16)
    result = (
        middle + jnp.dot(active_low, full_down, preferred_element_type=jnp.float32) + dbias_full
    )
    outputs = result.astype(jnp.bfloat16).reshape(seq_count, block_len, model_width)
    upstream = cotangent.astype(jnp.float32).reshape(flat_rows, model_width)
    upstream_low = upstream.astype(jnp.bfloat16)
    down_grad = jnp.einsum(
        "rf,rd->fd", active_low, upstream_low, preferred_element_type=jnp.float32
    )
    down_bias_grad = jnp.sum(upstream_low.astype(jnp.float32), axis=0)
    active_grad = jnp.einsum(
        "rd,fd->rf", upstream_low, full_down, preferred_element_type=jnp.float32
    )
    (hidden_grad,) = gelu_back(active_grad)
    hidden_low = hidden_grad.astype(jnp.bfloat16)
    up_grad = jnp.einsum(
        "rd,rf->df", normed_two_low, hidden_low, preferred_element_type=jnp.float32
    )
    up_bias_grad = jnp.sum(hidden_low.astype(jnp.float32), axis=0)
    normed_two_grad = jnp.einsum(
        "rf,df->rd", hidden_low, full_up, preferred_element_type=jnp.float32
    )
    middle_part, gain_two_grad, shift_two_grad = norm_second_back(normed_two_grad)
    middle_grad = upstream + middle_part
    middle_low = middle_grad.astype(jnp.bfloat16)
    out_grad = jnp.einsum("rd,re->de", attended_low, middle_low, preferred_element_type=jnp.float32)
    out_bias_grad = jnp.sum(middle_low.astype(jnp.float32), axis=0)
    attended_grad = jnp.einsum(
        "re,de->rd", middle_low, full_out, preferred_element_type=jnp.float32
    )
    grad_low = attended_grad.astype(jnp.bfloat16).reshape(head_shape)
    row_delta = jnp.swapaxes(jnp.sum(grad_low.astype(jnp.float32) * attended, axis=-1), 1, 2)
    gathered_keys, gathered_values = (
        lax.all_gather(
            key_rows.reshape(1, seq_count, block_len, model_width), "ctx", axis=0, tiled=True
        ),
        lax.all_gather(
            value_rows.reshape(1, seq_count, block_len, model_width), "ctx", axis=0, tiled=True
        ),
    )
    block_ids = jnp.arange(cycle_size, dtype=jnp.int32)

    def key_step(carry, inputs_here):
        key_block, value_block, block_index = inputs_here
        key_heads = key_block.reshape(head_shape)
        value_heads = value_block.reshape(head_shape)
        weights_low, score_low = score_grads(
            query_heads,
            key_heads,
            value_heads,
            grad_low,
            log_total,
            row_delta,
            query_at,
            block_index * block_len + offsets,
        )
        carry = (
            carry
            + jnp.einsum(
                "shqk,skhd->sqhd", score_low, key_heads, preferred_element_type=jnp.float32
            )
            * score_scale
        )
        key_term = (
            jnp.einsum(
                "shqk,sqhd->skhd", score_low, query_heads, preferred_element_type=jnp.float32
            )
            * score_scale
        )
        value_term = jnp.einsum(
            "shqk,sqhd->skhd", weights_low, grad_low, preferred_element_type=jnp.float32
        )
        return (
            carry,
            (
                key_term.reshape(seq_count, block_len, model_width),
                value_term.reshape(seq_count, block_len, model_width),
            ),
        )

    query_grad, (key_terms, value_terms) = lax.scan(
        key_step, jnp.zeros(head_shape, jnp.float32), (gathered_keys, gathered_values, block_ids)
    )
    key_sum, value_sum = (
        lax.psum_scatter(
            key_terms.astype(jnp.bfloat16), "ctx", scatter_dimension=0, tiled=True
        ).astype(jnp.float32),
        lax.psum_scatter(
            value_terms.astype(jnp.bfloat16), "ctx", scatter_dimension=0, tiled=True
        ).astype(jnp.float32),
    )
    key_grad = key_sum.reshape(flat_rows, model_width)
    value_grad = value_sum.reshape(flat_rows, model_width)
    query_low = query_grad.reshape(flat_rows, model_width).astype(jnp.bfloat16)
    key_low = key_grad.astype(jnp.bfloat16)
    value_low = value_grad.astype(jnp.bfloat16)
    stacked = jnp.concatenate([query_low, key_low, value_low], axis=1)
    in_grad = jnp.einsum("rd,re->de", normed_low, stacked, preferred_element_type=jnp.float32)
    query_bias_grad = jnp.sum(query_low.astype(jnp.float32), axis=0)
    value_bias_grad = jnp.sum(value_low.astype(jnp.float32), axis=0)
    normed_grad = jnp.einsum("re,de->rd", stacked, full_in, preferred_element_type=jnp.float32)
    input_part, gain_one_grad, shift_one_grad = norm_first_back(normed_grad)
    input_gradient = (middle_grad + input_part).reshape(seq_count, block_len, model_width)
    (
        gain_one_part,
        shift_one_part,
        in_part,
        qbias_part,
        vbias_part,
        out_part,
        obias_part,
        gain_two_part,
        shift_two_part,
        up_part,
        ubias_part,
        down_part,
        dbias_part,
    ) = (
        lax.psum_scatter(
            gain_one_grad.astype(jnp.bfloat16), "fsdp", scatter_dimension=0, tiled=True
        ).astype(jnp.float32),
        lax.psum_scatter(
            shift_one_grad.astype(jnp.bfloat16), "fsdp", scatter_dimension=0, tiled=True
        ).astype(jnp.float32),
        lax.psum_scatter(
            in_grad.astype(jnp.bfloat16), "fsdp", scatter_dimension=0, tiled=True
        ).astype(jnp.float32),
        lax.psum_scatter(
            query_bias_grad.astype(jnp.bfloat16), "fsdp", scatter_dimension=0, tiled=True
        ).astype(jnp.float32),
        lax.psum_scatter(
            value_bias_grad.astype(jnp.bfloat16), "fsdp", scatter_dimension=0, tiled=True
        ).astype(jnp.float32),
        lax.psum_scatter(
            out_grad.astype(jnp.bfloat16), "fsdp", scatter_dimension=0, tiled=True
        ).astype(jnp.float32),
        lax.psum_scatter(
            out_bias_grad.astype(jnp.bfloat16), "fsdp", scatter_dimension=0, tiled=True
        ).astype(jnp.float32),
        lax.psum_scatter(
            gain_two_grad.astype(jnp.bfloat16), "fsdp", scatter_dimension=0, tiled=True
        ).astype(jnp.float32),
        lax.psum_scatter(
            shift_two_grad.astype(jnp.bfloat16), "fsdp", scatter_dimension=0, tiled=True
        ).astype(jnp.float32),
        lax.psum_scatter(
            up_grad.astype(jnp.bfloat16), "fsdp", scatter_dimension=0, tiled=True
        ).astype(jnp.float32),
        lax.psum_scatter(
            up_bias_grad.astype(jnp.bfloat16), "fsdp", scatter_dimension=0, tiled=True
        ).astype(jnp.float32),
        lax.psum_scatter(
            down_grad.astype(jnp.bfloat16), "fsdp", scatter_dimension=0, tiled=True
        ).astype(jnp.float32),
        lax.psum_scatter(
            down_bias_grad.astype(jnp.bfloat16), "fsdp", scatter_dimension=0, tiled=True
        ).astype(jnp.float32),
    )
    (
        gain_one_sum,
        shift_one_sum,
        in_sum,
        qbias_sum,
        vbias_sum,
        out_sum,
        obias_sum,
        gain_two_sum,
        shift_two_sum,
        up_sum,
        ubias_sum,
        down_sum,
        dbias_sum,
    ) = lax.psum(
        (
            gain_one_part,
            shift_one_part,
            in_part,
            qbias_part,
            vbias_part,
            out_part,
            obias_part,
            gain_two_part,
            shift_two_part,
            up_part,
            ubias_part,
            down_part,
            dbias_part,
        ),
        ("dp", "ctx"),
    )
    return (
        outputs,
        input_gradient,
        gain_one_sum,
        shift_one_sum,
        in_sum,
        qbias_sum,
        vbias_sum,
        out_sum,
        obias_sum,
        gain_two_sum,
        shift_two_sum,
        up_sum,
        ubias_sum,
        down_sum,
        dbias_sum,
    )


NT = (((1,), (1,)), ((), ()))
PAIR = 2 * HEAD_DIM


def attend_kernel(place_ref, q_ref, k_ref, v_ref, *refs, count, width, start):
    o_ref, log_ref, keys, values = refs[-4:]
    own_pair = pl.program_id(0)
    pair = own_pair + start
    shift = place_ref[0]
    block_len = q_ref.shape[0] // count
    lane = lax.broadcasted_iota(jnp.int32, (1, PAIR), 1)
    valid = lane + pair * PAIR < width
    first = lane < HEAD_DIM

    def rows(block):
        return pl.ds(pl.multiple_of((block ^ shift) * block_len, block_len), block_len)

    for block in range(count):
        here = pl.ds(block * block_len, block_len)
        keys[here, :] = jnp.where(valid, k_ref[rows(block), :], 0)
        values[here, :] = jnp.where(valid, v_ref[rows(block), :], 0)
    diagonal = lax.broadcasted_iota(jnp.int32, (block_len, block_len), 0) >= (
        lax.broadcasted_iota(jnp.int32, (block_len, block_len), 1)
    )
    for block in range(count):
        seen = (block + 1) * block_len
        before = block * block_len
        queries = q_ref[rows(block), :] * jnp.bfloat16(HEAD_DIM**-0.5)
        parts = []
        logs = log_ref[rows(block), :]
        for half in range(2):
            pick = jnp.logical_and(first if half == 0 else jnp.logical_not(first), valid)
            scores = lax.dot_general(
                jnp.where(pick, queries, 0),
                keys[pl.ds(0, seen), :],
                NT,
                preferred_element_type=jnp.float32,
            )
            last = jnp.where(diagonal, scores[:, before:], -1e30)
            scores = last if block == 0 else jnp.concatenate([scores[:, :before], last], axis=1)
            top = jnp.max(scores, axis=1, keepdims=True)
            weights = jnp.exp(scores - top)
            total = jnp.sum(weights, axis=1, keepdims=True)
            added = jnp.dot(
                weights.astype(jnp.bfloat16),
                values[pl.ds(0, seen), :],
                preferred_element_type=jnp.float32,
            )
            parts.append(added / total)
            logs = jnp.where(lane == 2 * own_pair + half, top + jnp.log(total), logs)
        o_ref[rows(block), :] = jnp.where(first, parts[0], parts[1]).astype(jnp.bfloat16)
        log_ref[rows(block), :] = logs


def attend_back_kernel(
    place_ref,
    q_ref,
    k_ref,
    v_ref,
    g_ref,
    o_ref,
    log_ref,
    *refs,
    count,
    width,
    start,
):
    dq_ref, dk_ref, dv_ref, queries, grads, keys, values = refs[-11:-4]
    keys_turned, logs, deltas, turned = refs[-4:]
    pair = pl.program_id(0) + start
    shift = place_ref[0]
    length = q_ref.shape[0]
    block_len = length // count
    lane = lax.broadcasted_iota(jnp.int32, (1, PAIR), 1)
    valid = lane + pair * PAIR < width
    first = lane < HEAD_DIM
    picks = (jnp.logical_and(first, valid), jnp.logical_and(jnp.logical_not(first), valid))
    half_of = (lax.broadcasted_iota(jnp.int32, (8, PAIR), 1) // HEAD_DIM) == (
        lax.broadcasted_iota(jnp.int32, (8, PAIR), 0)
    )
    ones_of = jnp.where(half_of, 1.0, 0.0)

    def rows(block):
        return pl.ds(pl.multiple_of((block ^ shift) * block_len, block_len), block_len)

    for block in range(count):
        here = pl.ds(block * block_len, block_len)
        key_block = jnp.where(valid, k_ref[rows(block), :], 0)
        keys[here, :] = key_block
        keys_turned[:, here] = key_block.astype(jnp.float32).T.astype(jnp.bfloat16)
        values[here, :] = jnp.where(valid, v_ref[rows(block), :], 0)
        query_block = q_ref[rows(block), :] * jnp.bfloat16(HEAD_DIM**-0.5)
        grad_block = jnp.where(valid, g_ref[rows(block), :], 0)
        for half in range(2):
            queries[half, here, :] = jnp.where(picks[half], query_block, 0)
            grads[half, here, :] = jnp.where(picks[half], grad_block, 0)
        mixed = grad_block.astype(jnp.float32) * jnp.where(
            valid, o_ref[rows(block), :], 0
        ).astype(jnp.float32)
        deltas[:, here] = lax.dot_general(
            ones_of,
            mixed,
            NT,
            preferred_element_type=jnp.float32,
            precision=lax.Precision.HIGHEST,
        )
        logs[:, here] = log_ref[
            0, :, pl.ds(pl.multiple_of((block ^ shift) * block_len, block_len), block_len)
        ]
    diagonal = lax.broadcasted_iota(jnp.int32, (block_len, block_len), 0) <= (
        lax.broadcasted_iota(jnp.int32, (block_len, block_len), 1)
    )
    for block in range(count):
        here = pl.ds(block * block_len, block_len)
        after = pl.ds(block * block_len, length - block * block_len)
        key_total = jnp.zeros((block_len, PAIR), jnp.float32)
        value_total = jnp.zeros((block_len, PAIR), jnp.float32)
        for half in range(2):
            scores = lax.dot_general(
                keys[here, :], queries[half, after, :], NT, preferred_element_type=jnp.float32
            )
            shifted = scores - logs[half : half + 1, after]
            own = jnp.where(diagonal, shifted[:, :block_len], -1e30)
            if block < count - 1:
                own = jnp.concatenate([own, shifted[:, block_len:]], axis=1)
            weights = jnp.exp(own)
            pressure = lax.dot_general(
                values[here, :], grads[half, after, :], NT, preferred_element_type=jnp.float32
            )
            score_low = (weights * (pressure - deltas[half : half + 1, after])).astype(
                jnp.bfloat16
            )
            value_total += jnp.dot(
                weights.astype(jnp.bfloat16),
                grads[half, after, :],
                preferred_element_type=jnp.float32,
            )
            key_total += jnp.dot(
                score_low, queries[half, after, :], preferred_element_type=jnp.float32
            )
            part = pl.ds(half * HEAD_DIM, HEAD_DIM)
            term = jnp.dot(
                keys_turned[part, here], score_low, preferred_element_type=jnp.float32
            )
            if block == 0:
                turned[part, after] = term
            else:
                turned[part, after] += term
        dk_ref[rows(block), :] = key_total.astype(jnp.bfloat16)
        dv_ref[rows(block), :] = value_total.astype(jnp.bfloat16)
    for block in range(count):
        here = pl.ds(block * block_len, block_len)
        dq_ref[rows(block), :] = (turned[:, here].T * HEAD_DIM**-0.5).astype(jnp.bfloat16)


def attend(place, queries, key_rows, value_rows, count, start, pairs, before):
    length, width = queries.shape
    heads_block = pl.BlockSpec((length, PAIR), lambda pair, place_ref: (0, pair + start))
    return pl.pallas_call(
        functools.partial(attend_kernel, count=count, width=width, start=start),
        grid_spec=pltpu.PrefetchScalarGridSpec(
            num_scalar_prefetch=1,
            grid=(pairs,),
            in_specs=[heads_block] * 3 + [pl.BlockSpec(memory_space=pl.ANY)] * len(before),
            out_specs=[
                heads_block,
                pl.BlockSpec((length, 128), lambda pair, place_ref: (0, 0)),
            ],
            scratch_shapes=[pltpu.VMEM((length, PAIR), jnp.bfloat16)] * 2,
        ),
        out_shape=[
            jax.ShapeDtypeStruct((length, width), jnp.bfloat16),
            jax.ShapeDtypeStruct((length, 128), jnp.float32),
        ],
        input_output_aliases={4 + at: at for at in range(len(before))},
        compiler_params=pltpu.CompilerParams(vmem_limit_bytes=48 * 2**20),
        cost_estimate=pl.CostEstimate(
            flops=4 * length * length * PAIR * pairs * 4,
            bytes_accessed=8 * length * PAIR * pairs,
            transcendentals=length * length * pairs,
        ),
        name="attend",
    )(place, queries, key_rows, value_rows, *before)


def attend_back(
    place, queries, key_rows, value_rows, grads, attended, logs, count, start, pairs, before
):
    length, width = queries.shape
    heads_block = pl.BlockSpec((length, PAIR), lambda pair, place_ref: (0, pair + start))
    low_rows = pltpu.VMEM((length, PAIR), jnp.bfloat16)
    low_pair = pltpu.VMEM((2, length, PAIR), jnp.bfloat16)
    return pl.pallas_call(
        functools.partial(attend_back_kernel, count=count, width=width, start=start),
        grid_spec=pltpu.PrefetchScalarGridSpec(
            num_scalar_prefetch=1,
            grid=(pairs,),
            in_specs=[heads_block] * 5
            + [pl.BlockSpec((1, 2, length), lambda pair, place_ref: (pair, 0, 0))]
            + [pl.BlockSpec(memory_space=pl.ANY)] * len(before),
            out_specs=[heads_block] * 3,
            scratch_shapes=[
                low_pair,
                low_pair,
                low_rows,
                low_rows,
                pltpu.VMEM((PAIR, length), jnp.bfloat16),
                pltpu.VMEM((2, length), jnp.float32),
                pltpu.VMEM((8, length), jnp.float32),
                pltpu.VMEM((PAIR, length), jnp.float32),
            ],
        ),
        out_shape=[jax.ShapeDtypeStruct((length, width), jnp.bfloat16)] * 3,
        input_output_aliases={7 + at: at for at in range(len(before))},
        compiler_params=pltpu.CompilerParams(vmem_limit_bytes=48 * 2**20),
        cost_estimate=pl.CostEstimate(
            flops=10 * length * length * PAIR * pairs * 3,
            bytes_accessed=16 * length * PAIR * pairs,
            transcendentals=length * length * pairs,
        ),
        name="attend_back",
    )(place, queries, key_rows, value_rows, grads, attended, logs, *before)


def settle_kernel(place_ref, *refs):
    pieces, out_ref = refs[:-1], refs[-1]
    for at, piece in enumerate(pieces):
        out_ref[place_ref[at]] = piece[...].astype(out_ref.dtype)


def settle(places, pieces, dtype):
    return pl.pallas_call(
        settle_kernel,
        in_specs=[pl.BlockSpec(memory_space=pltpu.SMEM)]
        + [pl.BlockSpec(memory_space=pltpu.VMEM)] * len(pieces),
        out_specs=pl.BlockSpec(memory_space=pltpu.VMEM),
        out_shape=jax.ShapeDtypeStruct((len(pieces),) + pieces[0].shape, dtype),
        compiler_params=pltpu.CompilerParams(vmem_limit_bytes=48 * 2**20),
        name="settle",
    )(places, *pieces)


def plane_partner(device, kind):
    core = device & 1
    if kind == "core":
        return device ^ 1
    if kind == "far":
        return device ^ (3 if core else 5)
    if kind == "near":
        return device ^ (2 if core else 4)
    return device ^ (4 if core else 2)


def plane_swap(values, kind):
    return lax.ppermute(
        values, ("dp", "ctx"), [(device, plane_partner(device, kind)) for device in range(8)]
    )


def ctx_swap(values, bits):
    return lax.ppermute(values, "ctx", [(device, device ^ bits) for device in range(4)])


def low_sum(*terms):
    return sum(term.astype(jnp.float32) for term in terms).astype(jnp.bfloat16)


def reduce_core(pieces):
    return plane_swap(pieces[2], "core"), plane_swap(pieces[3], "core")


def reduce_last(shard):
    whole = low_sum(shard, plane_swap(shard, "other"))
    return [whole] + [plane_swap(whole, kind) for kind in ("near", "core", "far")]


def scatter_rows(values):
    return lax.psum_scatter(values, "fsdp", scatter_dimension=0, tiled=True)


def chosen(index, options):
    result = options[-1]
    for at in range(len(options) - 2, -1, -1):
        result = jnp.where(index == at, options[at], result)
    return result


def gather_vector(values, z):
    around = [values] + [
        lax.ppermute(values, "fsdp", [(device, (device + step) % 4) for device in range(4)])
        for step in range(1, 4)
    ]
    return jnp.stack([chosen((z - at) % 4, around) for at in range(4)])


def reduce_vector(values, z):
    rows = [values[at] for at in range(4)]
    total = chosen(z, rows)
    for step in range(1, 4):
        total = total + lax.ppermute(
            chosen((z + step) % 4, rows),
            "fsdp",
            [(device, (device + step) % 4) for device in range(4)],
        )
    for bits in (1, 2, 4):
        total = total + lax.ppermute(
            total, ("dp", "ctx"), [(device, device ^ bits) for device in range(8)]
        )
    return total


def product(left, right, dims):
    return lax.dot_general(left, right, ((dims[:1], dims[1:]), ((), ())),
                           preferred_element_type=jnp.float32)


def gelu_pair(values):
    inner = 0.7978845608028654
    cubic = inner * 0.044715
    squared = values * values
    curve = jnp.tanh(values * (inner + cubic * squared))
    half = 0.5 * values
    active = half + half * curve
    slope = 0.5 + 0.5 * curve + half * (1.0 - curve * curve) * (inner + 3.0 * cubic * squared)
    return active, slope


def block_flops(rows, width, count):
    return pl.CostEstimate(
        flops=2 * rows * width * width * count,
        bytes_accessed=2 * width * width * count + 4 * rows * width * count,
        transcendentals=0,
    )


def unit_of(values):
    centred = values - jnp.mean(values, axis=-1, keepdims=True)
    scale = lax.rsqrt(jnp.mean(centred * centred, axis=-1, keepdims=True) + epsilon)
    return centred * scale, scale


def fold(values):
    rows, width = values.shape
    return jnp.sum(values.reshape(rows // 8, 8, width), axis=0)


def front_kernel(places_ref, x_ref, vectors_ref, *refs):
    pieces = refs[:16]
    h_ref, q_ref, k_ref, v_ref, all_ref, weights, arrived, left = refs[16:]
    copies = [
        pltpu.make_async_copy(piece, weights.at[places_ref[at]], arrived.at[at])
        for at, piece in enumerate(pieces)
    ]
    for copy in copies:
        copy.start()
    rows, width = x_ref.shape
    step = 256

    def norm(at, carry):
        here = pl.ds(pl.multiple_of(at * step, step), step)
        unit, _ = unit_of(x_ref[here, :].astype(jnp.float32))
        h_ref[here, :] = (unit * vectors_ref[0:1, :] + vectors_ref[1:2, :]).astype(jnp.bfloat16)
        return carry

    lax.fori_loop(0, rows // step, norm, 0)
    for copy in copies:
        copy.wait()
    leave = pltpu.make_async_copy(weights, all_ref, left)
    leave.start()
    for section, out_ref in enumerate((q_ref, k_ref, v_ref)):

        def multiply(at, carry, section=section, out_ref=out_ref):
            here = pl.ds(pl.multiple_of(at * step, step), step)
            matrix = weights[4 * section : 4 * section + 4].reshape(width, width)
            total = jnp.dot(h_ref[here, :], matrix, preferred_element_type=jnp.float32)
            if section != 1:
                row = 2 if section == 0 else 3
                total = total + vectors_ref[row : row + 1, :]
            out_ref[here, :] = total.astype(jnp.bfloat16)
            return carry

        lax.fori_loop(0, rows // step, multiply, 0)
    leave.wait()


def front(places, rows_in, vectors, pieces):
    rows, width = rows_in.shape
    vmem = pl.BlockSpec(memory_space=pltpu.VMEM)
    hbm = pl.BlockSpec(memory_space=pl.ANY)
    shape = jax.ShapeDtypeStruct((rows, width), jnp.bfloat16)
    whole = (16,) + pieces[0].shape
    return pl.pallas_call(
        front_kernel,
        in_specs=[pl.BlockSpec(memory_space=pltpu.SMEM), vmem, vmem] + [hbm] * 16,
        out_specs=[vmem] * 4 + [hbm],
        out_shape=[shape] * 4 + [jax.ShapeDtypeStruct(whole, jnp.bfloat16)],
        scratch_shapes=[
            pltpu.VMEM(whole, jnp.bfloat16),
            pltpu.SemaphoreType.DMA((16,)),
            pltpu.SemaphoreType.DMA,
        ],
        compiler_params=pltpu.CompilerParams(vmem_limit_bytes=56 * 2**20),
        cost_estimate=block_flops(rows, width, 3),
        name="front",
    )(places, rows_in, vectors, *pieces)


def fetch(step, copies):
    @pl.when(step == 0)
    def _():
        for copy in copies:
            copy.start()


def arrive(step, copy):
    @pl.when(step == 0)
    def _():
        copy.wait()


def middle_kernel(x_ref, o_ref, vectors_ref, all_ref, middle_ref, h_ref, weights, arrived):
    step = pl.program_id(0)
    width = x_ref.shape[1]
    copy = pltpu.make_async_copy(all_ref.at[pl.ds(12, 4)], weights, arrived)
    fetch(step, [copy])
    arrive(step, copy)
    middle = (
        x_ref[...].astype(jnp.float32)
        + jnp.dot(
            o_ref[...], weights[...].reshape(width, width), preferred_element_type=jnp.float32
        )
        + vectors_ref[0:1, :]
    )
    middle_ref[...] = middle
    unit, _ = unit_of(middle)
    h_ref[...] = (unit * vectors_ref[1:2, :] + vectors_ref[2:3, :]).astype(jnp.bfloat16)


def up_kernel(h_ref, biases_ref, *refs):
    sources = refs[:2]
    active_refs, slope_refs = refs[2:4], refs[4:6]
    weights, arrived = refs[6:]
    step = pl.program_id(0)
    copies = [
        pltpu.make_async_copy(source, weights.at[at], arrived.at[at])
        for at, source in enumerate(sources)
    ]
    fetch(step, copies)
    for at in range(2):
        arrive(step, copies[at])
        hidden = (
            jnp.dot(h_ref[...], weights[at], preferred_element_type=jnp.float32)
            + biases_ref[at : at + 1, :]
        )
        active, slope = gelu_pair(hidden)
        active_refs[at][...] = active.astype(jnp.bfloat16)
        slope_refs[at][...] = slope.astype(jnp.bfloat16)


def down_kernel(middle_ref, vectors_ref, *refs):
    actives, sources = refs[:4], refs[4:8]
    out_ref, weights, arrived = refs[8:]
    step = pl.program_id(0)
    copies = [
        pltpu.make_async_copy(source, weights.at[at], arrived.at[at])
        for at, source in enumerate(sources)
    ]
    fetch(step, copies)
    total = middle_ref[...] + vectors_ref[0:1, :]
    for at in range(4):
        arrive(step, copies[at])
        total = total + jnp.dot(
            actives[at][...], weights[at], preferred_element_type=jnp.float32
        )
    out_ref[...] = total.astype(jnp.bfloat16)


def norm_back(values, gain, grad):
    unit, scale = unit_of(values)
    turned = grad * gain
    inner = (
        turned
        - jnp.mean(turned, axis=-1, keepdims=True)
        - unit * jnp.mean(turned * unit, axis=-1, keepdims=True)
    )
    return scale * inner, grad * unit


def hidden_kernel(g_ref, *refs):
    slopes, sources = refs[:2], refs[2:4]
    hidden_refs, sums_ref = refs[4:6], refs[6]
    weights, arrived = refs[7:]
    step = pl.program_id(0)
    copies = [
        pltpu.make_async_copy(source, weights.at[at], arrived.at[at])
        for at, source in enumerate(sources)
    ]
    fetch(step, copies)

    @pl.when(step == 0)
    def _():
        sums_ref[...] = jnp.zeros_like(sums_ref)

    upstream = g_ref[...]
    for at in range(2):
        arrive(step, copies[at])
        hidden = lax.dot_general(
            upstream, weights[at], NT, preferred_element_type=jnp.float32
        )
        hidden = (hidden * slopes[at][...].astype(jnp.float32)).astype(jnp.bfloat16)
        hidden_refs[at][...] = hidden
        sums_ref[at] += fold(hidden.astype(jnp.float32))
    sums_ref[2] += fold(upstream.astype(jnp.float32))


def back_kernel(g_ref, middle_ref, vectors_ref, *refs):
    hiddens, sources, all_ref = refs[:4], refs[4:8], refs[8]
    grad_ref, low_ref, out_ref, sums_ref = refs[9:13]
    weights, out_weights, arrived = refs[13:]
    step = pl.program_id(0)
    width = middle_ref.shape[1]
    copies = [
        pltpu.make_async_copy(source, weights.at[at], arrived.at[at])
        for at, source in enumerate(sources)
    ] + [pltpu.make_async_copy(all_ref.at[pl.ds(12, 4)], out_weights, arrived.at[4])]
    fetch(step, copies)

    @pl.when(step == 0)
    def _():
        sums_ref[...] = jnp.zeros_like(sums_ref)

    total = jnp.zeros(middle_ref.shape, jnp.float32)
    for at in range(4):
        arrive(step, copies[at])
        total = total + lax.dot_general(
            hiddens[at][...], weights[at], NT, preferred_element_type=jnp.float32
        )
    part, gain_term = norm_back(middle_ref[...], vectors_ref[0:1, :], total)
    sums_ref[0] += fold(gain_term)
    sums_ref[1] += fold(total)
    grad = g_ref[...].astype(jnp.float32) + part
    grad_ref[...] = grad
    grad_low = grad.astype(jnp.bfloat16)
    low_ref[...] = grad_low
    sums_ref[2] += fold(grad_low.astype(jnp.float32))
    arrive(step, copies[4])
    out_ref[...] = lax.dot_general(
        grad_low,
        out_weights[...].reshape(width, width),
        NT,
        preferred_element_type=jnp.float32,
    ).astype(jnp.bfloat16)


def last_kernel(q_ref, k_ref, v_ref, x_ref, grad_ref, vectors_ref, all_ref, *refs):
    out_ref, sums_ref, weights, arrived = refs
    step = pl.program_id(0)
    width = x_ref.shape[1]
    copies = [
        pltpu.make_async_copy(
            all_ref.at[pl.ds(4 * at, 4)], weights.at[pl.ds(4 * at, 4)], arrived.at[at]
        )
        for at in range(3)
    ]
    fetch(step, copies)
    total = jnp.zeros(x_ref.shape, jnp.float32)
    for at, ref in enumerate((q_ref, k_ref, v_ref)):
        arrive(step, copies[at])
        total = total + lax.dot_general(
            ref[...],
            weights[4 * at : 4 * at + 4].reshape(width, width),
            NT,
            preferred_element_type=jnp.float32,
        )
    part, gain_term = norm_back(x_ref[...].astype(jnp.float32), vectors_ref[0:1, :], total)
    out_ref[...] = (grad_ref[...] + part).astype(jnp.bfloat16)

    @pl.when(step == 0)
    def _():
        sums_ref[...] = jnp.zeros_like(sums_ref)

    terms = (
        gain_term,
        total,
        q_ref[...].astype(jnp.float32),
        v_ref[...].astype(jnp.float32),
    )
    for at, term in enumerate(terms):
        sums_ref[at] += fold(term)


def by_rows(kernel, name, rows, width, tiled, whole, remote, outs, sums, scratch, sems, blocks):
    step = 512
    tile = pl.BlockSpec((step, width), lambda at: (at, 0))
    out_specs = [tile] * len(outs)
    out_shape = [jax.ShapeDtypeStruct((rows, width), dtype) for dtype in outs]
    if sums:
        out_specs.append(pl.BlockSpec((sums, 8, width), lambda at: (0, 0, 0)))
        out_shape.append(jax.ShapeDtypeStruct((sums, 8, width), jnp.float32))
    return pl.pallas_call(
        kernel,
        grid=(rows // step,),
        in_specs=[tile] * len(tiled[0])
        + [pl.BlockSpec(value.shape, lambda at: (0, 0)) for value in whole]
        + [tile] * len(tiled[1])
        + [pl.BlockSpec(memory_space=pl.ANY)] * len(remote),
        out_specs=out_specs,
        out_shape=out_shape,
        scratch_shapes=[pltpu.VMEM(shape, jnp.bfloat16) for shape in scratch]
        + [pltpu.SemaphoreType.DMA((sems,)) if sems > 1 else pltpu.SemaphoreType.DMA],
        compiler_params=pltpu.CompilerParams(vmem_limit_bytes=60 * 2**20),
        cost_estimate=block_flops(rows, width, blocks),
        name=name,
    )(*tiled[0], *whole, *tiled[1], *remote)


def per_device_exchanged(
    inputs,
    cotangent,
    first_gain,
    first_shift,
    project_in,
    query_bias,
    value_bias,
    project_out,
    output_bias,
    second_gain,
    second_shift,
    up_weight,
    up_bias,
    down_weight,
    down_bias,
):
    seq_count, block_len, width = inputs.shape
    low = jnp.bfloat16
    wide = jnp.float32
    c = lax.axis_index("ctx")
    y = lax.axis_index("dp")
    z = lax.axis_index("fsdp")
    core = c & 1
    x = c >> 1
    mine = core * 2 + jnp.where(core == 0, y, x)
    across = (1 - core) * 2 + jnp.where(core == 0, x, y)
    classes = [mine, mine ^ 1, across, across ^ 1]
    slot_of = [
        chosen(0, [sum(at * (classes[at] == kind).astype(jnp.int32) for at in range(4))])
        for kind in range(4)
    ]
    quarter = width // 4
    rows, area = seq_count * block_len, (width, width)
    pin = lax.optimization_barrier
    place = jnp.stack([c])
    places = jnp.stack([c ^ at for at in range(4)])
    class_places = jnp.stack(classes)

    def spread(values):
        return jnp.concatenate(
            [lax.dynamic_index_in_dim(values, c, 0, keepdims=False)]
            + [
                ctx_swap(lax.dynamic_index_in_dim(values, c ^ bits, 0, keepdims=False), bits)
                for bits in range(1, 4)
            ],
            axis=0,
        )

    def collect(values, dtype):
        pieces = [values[at * block_len : (at + 1) * block_len] for at in range(4)]
        moved = [pieces[0]] + [ctx_swap(pieces[bits], bits) for bits in range(1, 4)]
        return settle(places, moved, dtype)

    sections = [
        project_in[:, :width],
        project_in[:, width : 2 * width],
        project_in[:, 2 * width :],
        project_out,
    ]
    section = chosen(mine, sections)
    shards = [
        lax.ppermute(section, "fsdp", [(device, (device + step) % 4) for device in range(4)])
        for step in range(1, 4)
    ]
    up_piece = jnp.concatenate(
        [
            lax.dynamic_slice_in_dim(up_weight, at * width + mine * quarter, quarter, 1)
            for at in range(4)
        ],
        axis=1,
    )
    vectors = gather_vector(
        jnp.concatenate(
            [
                first_gain,
                first_shift,
                query_bias,
                value_bias,
                output_bias,
                second_gain,
                second_shift,
                down_bias,
                up_bias,
            ]
        ),
        z,
    )
    rows_in, upstream_low = spread(inputs), spread(cotangent)
    up_piece, vectors, rows_in, upstream_low, *shards = pin(
        (up_piece, vectors, rows_in, upstream_low, *shards)
    )
    vectors = vectors.astype(wide)
    near_shards = [plane_swap(shard, "near") for shard in shards]
    around = (
        sections
        + shards
        + near_shards
        + [plane_swap(shard, "core") for shard in shards]
        + [plane_swap(shard, "core") for shard in near_shards]
    )
    around_places = jnp.stack(
        [kind * 4 + z for kind in range(4)]
        + [kind * 4 + (z - step) % 4 for kind in classes for step in range(1, 4)]
    )
    up_own = lax.all_gather(up_piece, "fsdp", axis=0, tiled=True)
    down_piece = lax.dynamic_slice_in_dim(down_weight, mine * quarter, quarter, 0)
    gain_first, shift_first, qbias, vbias, obias, gain_second, shift_second, dbias = (
        vectors[:, at * quarter : (at + 1) * quarter].reshape(1, width) for at in range(8)
    )
    ubias = vectors[:, 8 * quarter :].reshape(4, 4, quarter)
    ubias = jnp.concatenate(
        [
            chosen(kind, [ubias[:, at] for at in range(4)]).reshape(1, width)
            for kind in classes
        ],
        axis=0,
    )

    normed_low, queries, key_rows, value_rows, weights = front(
        around_places,
        rows_in,
        jnp.concatenate([gain_first, shift_first, qbias, vbias], axis=0),
        around,
    )
    down_piece, queries = pin((down_piece, queries))
    down_own = lax.all_gather(down_piece, "fsdp", axis=0, tiled=True)
    attended, logs_one = attend(place, queries, key_rows, value_rows, seq_count, 0, 5, [])
    up_own, late_queries, attended = pin((up_own, queries, attended))
    up_near, up_core = plane_swap(up_own, "near"), plane_swap(up_own, "core")
    attended, logs_two = attend(
        place, late_queries, key_rows, value_rows, seq_count, 5, 4, [attended]
    )
    up_core, attended = pin((up_core, attended))
    logs_one, logs_two = (logs.T.reshape(64, 2, rows) for logs in (logs_one, logs_two))
    middle, normed_two_low = by_rows(
        middle_kernel,
        "middle",
        rows,
        width,
        ([rows_in, attended], []),
        [jnp.concatenate([obias, gain_second, shift_second], axis=0)],
        [weights],
        [wide, low],
        0,
        [(4,) + section.shape],
        1,
        1,
    )
    up_near, normed_two_low = pin((up_near, normed_two_low))
    up_slots = [up_own, up_near, up_core, plane_swap(up_near, "core")]
    active, slopes = [None] * 4, [None] * 4

    def up(first):
        outs = by_rows(
            up_kernel,
            "up",
            rows,
            width,
            ([normed_two_low], []),
            [jnp.concatenate([ubias[first : first + 1], ubias[first + 2 : first + 3]], axis=0)],
            [up_slots[first], up_slots[first + 2]],
            [low] * 4,
            0,
            [(2,) + area],
            2,
            2,
        )
        active[first], active[first + 2], slopes[first], slopes[first + 2] = outs

    up(0)
    up_slots[3], active[0], active[2] = pin((up_slots[3], active[0], active[2]))
    up(1)
    down_own, *active = pin((down_own, *active))
    down_near, down_core = plane_swap(down_own, "near"), plane_swap(down_own, "core")

    def turned_product(left, right):
        return product(left, right, (0, 0)).astype(low)

    down_terms = [turned_product(active[slot], upstream_low) for slot in (3, 2)]
    upstream_low, *down_terms = pin((upstream_low, *down_terms))
    down_terms += [turned_product(active[slot], upstream_low) for slot in (1, 0)]
    down_terms = down_terms[::-1]
    down_far, down_far_two = reduce_core(down_terms)
    upstream_low, *down_terms = pin((upstream_low, *down_terms))
    hidden_low = [None] * 4

    def hidden(first, upstream):
        hidden_low[first], hidden_low[first + 2], sums = by_rows(
            hidden_kernel,
            "hidden",
            rows,
            width,
            ([upstream], [slopes[first], slopes[first + 2]]),
            [],
            [down_slots[first], down_slots[first + 2]],
            [low] * 2,
            3,
            [(2,) + area],
            2,
            2,
        )
        return sums

    down_near, upstream_low = pin((down_near, upstream_low))
    down_slots = [down_own, down_near, down_core, plane_swap(down_near, "core")]
    sums_even = hidden(0, upstream_low)
    upstream_late, sums_even = pin((upstream_low, sums_even))
    sums_odd = hidden(1, upstream_late)
    hidden_sums = jnp.stack(
        [sums_even[0], sums_odd[0], sums_even[1], sums_odd[1], sums_even[2]]
    )
    down_second = low_sum(down_terms[1], down_far_two)
    down_second, down_far, *hidden_low = pin((down_second, down_far, *hidden_low))
    down_close = plane_swap(down_second, "near")
    middle_grad, middle_low, grad_low, back_sums = by_rows(
        back_kernel,
        "back",
        rows,
        width,
        ([upstream_low, middle], hidden_low),
        [gain_second],
        up_slots + [weights],
        [wide, low, low],
        3,
        [(4,) + area, (4,) + section.shape],
        5,
        5,
    )
    down_first = low_sum(down_terms[0], down_far, down_close)
    down_first, normed_two_low = pin((down_first, pin((normed_two_low, middle_low))[0]))
    down_shard = scatter_rows(down_first)
    up_terms = [turned_product(normed_two_low, hidden_low[slot]) for slot in (3, 2)]
    normed_two_low, *up_terms = pin((normed_two_low, *up_terms))
    up_terms += [turned_product(normed_two_low, hidden_low[slot]) for slot in (1, 0)]
    up_terms = up_terms[::-1]
    up_far, up_far_two = reduce_core(up_terms)
    out_term = turned_product(attended, middle_low)
    up_second = low_sum(up_terms[1], up_far_two)
    grad_low, up_second, up_far, out_term, *up_terms = pin(
        (grad_low, up_second, up_far, out_term, *up_terms)
    )
    up_close = plane_swap(up_second, "near")
    in_grads = attend_back(
        place, late_queries, key_rows, value_rows, grad_low, attended, logs_one, seq_count, 0, 5, []
    )
    up_first = low_sum(up_terms[0], up_far, up_close)
    up_first, *in_grads = pin((up_first, *in_grads))
    in_grads = attend_back(
        place,
        late_queries,
        key_rows,
        value_rows,
        grad_low,
        attended,
        logs_two,
        seq_count,
        5,
        4,
        in_grads,
    )
    up_first, down_shard, *in_grads = pin((up_first, down_shard, *in_grads))
    up_shard = scatter_rows(up_first)
    down_parts = reduce_last(down_shard)
    in_terms = [turned_product(normed_low, grad) for grad in in_grads]
    section_grads = in_terms + [out_term]
    sections_mine = [chosen(kind, section_grads) for kind in classes]
    far, far_two = reduce_core(sections_mine)
    second = low_sum(sections_mine[1], far_two)
    second, far, *in_grads = pin((second, far, *in_grads))
    close = plane_swap(second, "near")
    query_low, key_low, value_low = in_grads
    input_low, last_sums = by_rows(
        last_kernel,
        "last",
        rows,
        width,
        ([query_low, key_low, value_low, rows_in, middle_grad], []),
        [gain_first],
        [weights],
        [low],
        4,
        [(12,) + section.shape],
        3,
        3,
    )
    first = low_sum(sections_mine[0], far, close)
    first, middle, input_low = pin((first, middle, input_low))
    input_gradient = collect(input_low, wide)
    (result,) = by_rows(
        down_kernel,
        "down",
        rows,
        width,
        ([middle], active),
        [dbias],
        down_slots,
        [low],
        0,
        [(4,) + area],
        4,
        4,
    )
    outputs = collect(result, low)
    up_parts = reduce_last(up_shard)
    section_parts = reduce_last(scatter_rows(first))

    back_sums = jnp.concatenate([hidden_sums, back_sums], axis=0)
    back_sums = jnp.sum(back_sums, axis=1)
    last_sums = jnp.sum(last_sums, axis=1)
    hidden_sums = [back_sums[slot].reshape(4, quarter) for slot in range(4)]
    hidden_sums = jnp.stack(
        [chosen(slot_of[kind], hidden_sums) for kind in range(4)], axis=1
    ).reshape(4, 4 * quarter)
    early = reduce_vector(
        jnp.concatenate(
            [back_sums[at].reshape(4, quarter) for at in range(4, 8)] + [hidden_sums], axis=1
        ),
        z,
    )
    late = reduce_vector(
        jnp.concatenate([last_sums[at].reshape(4, quarter) for at in range(4)], axis=1), z
    )
    dbias_sum, gain_two_sum, shift_two_sum, obias_sum = (
        early[at * quarter : (at + 1) * quarter] for at in range(4)
    )
    ubias_sum = early[4 * quarter :]
    gain_one_sum, shift_one_sum, qbias_sum, vbias_sum = (
        late[at * quarter : (at + 1) * quarter] for at in range(4)
    )
    in_parts = [chosen(slot_of[kind], section_parts).astype(wide) for kind in range(4)]
    up_parts = [chosen(slot_of[kind], up_parts) for kind in range(4)]
    up_sum = jnp.concatenate(
        [
            up_parts[kind][:, at * quarter : (at + 1) * quarter]
            for at in range(4)
            for kind in range(4)
        ],
        axis=1,
    ).astype(wide)
    down_sum = settle(class_places, down_parts, wide).reshape(down_weight.shape)
    return (
        outputs,
        input_gradient,
        gain_one_sum,
        shift_one_sum,
        jnp.concatenate(in_parts[:3], axis=1),
        qbias_sum,
        vbias_sum,
        in_parts[3],
        obias_sum,
        gain_two_sum,
        shift_two_sum,
        up_sum,
        ubias_sum,
        down_sum,
        dbias_sum,
    )


def solution(mesh):
    sizes = dict(mesh.shape)
    exchanged = sizes["dp"] == 2 and sizes["fsdp"] == 4 and sizes["ctx"] == 4
    per_device = per_device_exchanged if exchanged else per_device_gathered
    return jax.shard_map(
        per_device,
        mesh=mesh,
        in_specs=(
            P(("dp", "fsdp"), "ctx", None),
            P(("dp", "fsdp"), "ctx", None),
            P("fsdp"),
            P("fsdp"),
            P("fsdp", None),
            P("fsdp"),
            P("fsdp"),
            P("fsdp", None),
            P("fsdp"),
            P("fsdp"),
            P("fsdp"),
            P("fsdp", None),
            P("fsdp"),
            P("fsdp", None),
            P("fsdp"),
        ),
        out_specs=(
            P(("dp", "fsdp"), "ctx", None),
            P(("dp", "fsdp"), "ctx", None),
            P("fsdp"),
            P("fsdp"),
            P("fsdp", None),
            P("fsdp"),
            P("fsdp"),
            P("fsdp", None),
            P("fsdp"),
            P("fsdp"),
            P("fsdp"),
            P("fsdp", None),
            P("fsdp"),
            P("fsdp", None),
            P("fsdp"),
        ),
        check_vma=False,
    )
```

```python
import functools

import jax
import jax.numpy as jnp
from jax import lax
from jax.experimental import pallas as pl
from jax.experimental.pallas import tpu as pltpu
from jax.sharding import PartitionSpec as P

HEADS = 17
HEAD_DIM = 64


epsilon = 1e-05


def layer_norm(values, gain, shift):
    centred = values - jnp.mean(values, axis=-1, keepdims=True)
    spread = jnp.mean(centred * centred, axis=-1, keepdims=True)
    return centred * lax.rsqrt(spread + epsilon) * gain + shift


def gelu_tanh(values):
    return jax.nn.gelu(values, approximate=True)


def score_grads(
    query_heads, key_heads, value_heads, grad_heads, log_total, row_delta, query_at, key_at
):
    score_scale = HEAD_DIM ** (-0.5)
    scores = (
        jnp.einsum("sqhd,skhd->shqk", query_heads, key_heads, preferred_element_type=jnp.float32)
        * score_scale
    )
    visible = query_at[:, None] >= key_at[None, :]
    shifted = jnp.where(visible, scores - log_total[..., None], -1e30)
    weights = jnp.where(visible, jnp.exp(shifted), 0.0)
    pressure = jnp.einsum(
        "sqhd,skhd->shqk", grad_heads, value_heads, preferred_element_type=jnp.float32
    )
    score_low = (weights * (pressure - row_delta[..., None])).astype(jnp.bfloat16)
    return (weights.astype(jnp.bfloat16), score_low)


def per_device_gathered(
    inputs,
    cotangent,
    first_gain,
    first_shift,
    project_in,
    query_bias,
    value_bias,
    project_out,
    output_bias,
    second_gain,
    second_shift,
    up_weight,
    up_bias,
    down_weight,
    down_bias,
):
    seq_count, block_len, model_width = inputs.shape
    flat_rows = seq_count * block_len
    cycle_size = lax.axis_size("ctx")
    my_block = lax.axis_index("ctx")
    score_scale = HEAD_DIM ** (-0.5)
    head_shape = (seq_count, block_len, HEADS, HEAD_DIM)
    offsets = jnp.arange(block_len, dtype=jnp.int32)
    query_at = my_block * block_len + offsets
    gain_first, shift_first, full_in, qbias_full, vbias_full, full_out, obias_full = (
        lax.all_gather(first_gain, "fsdp", axis=0, tiled=True),
        lax.all_gather(first_shift, "fsdp", axis=0, tiled=True),
        lax.all_gather(project_in, "fsdp", axis=0, tiled=True),
        lax.all_gather(query_bias, "fsdp", axis=0, tiled=True),
        lax.all_gather(value_bias, "fsdp", axis=0, tiled=True),
        lax.all_gather(project_out, "fsdp", axis=0, tiled=True),
        lax.all_gather(output_bias, "fsdp", axis=0, tiled=True),
    )
    rows_in = inputs.astype(jnp.float32).reshape(flat_rows, model_width)
    normed, norm_first_back = jax.vjp(
        layer_norm, rows_in, gain_first.astype(jnp.float32), shift_first.astype(jnp.float32)
    )
    normed_low = normed.astype(jnp.bfloat16)
    projected = jnp.dot(normed_low, full_in, preferred_element_type=jnp.float32)
    queries = (projected[:, :model_width] + qbias_full).astype(jnp.bfloat16)
    key_rows = projected[:, model_width : 2 * model_width].astype(jnp.bfloat16)
    value_rows = (projected[:, 2 * model_width :] + vbias_full).astype(jnp.bfloat16)
    query_heads = queries.reshape(head_shape)
    running_top = jnp.full((seq_count, HEADS, block_len), -1e30, jnp.float32)
    accumulated = jnp.zeros(head_shape, jnp.float32)
    piece_keys = lax.all_gather(
        key_rows.reshape(seq_count, block_len, model_width), "ctx", axis=1, tiled=True
    )
    piece_values = lax.all_gather(
        value_rows.reshape(seq_count, block_len, model_width), "ctx", axis=1, tiled=True
    )
    piece_len = piece_keys.shape[1]
    key_heads = piece_keys.reshape(seq_count, piece_len, HEADS, HEAD_DIM)
    value_heads = piece_values.reshape(seq_count, piece_len, HEADS, HEAD_DIM)
    scores = (
        jnp.einsum("sqhd,skhd->shqk", query_heads, key_heads, preferred_element_type=jnp.float32)
        * score_scale
    )
    key_at = jnp.arange(piece_len, dtype=jnp.int32)
    visible = query_at[:, None] >= key_at[None, :]
    masked = jnp.where(visible, scores, -1e30)
    new_top = jnp.maximum(running_top, jnp.max(masked, axis=-1))
    factor = jnp.exp(running_top - new_top)
    weights = jnp.where(visible, jnp.exp(masked - new_top[..., None]), 0.0)
    row_total = jnp.sum(weights, axis=-1)
    added = jnp.einsum(
        "shqk,skhd->sqhd",
        weights.astype(jnp.bfloat16),
        value_heads,
        preferred_element_type=jnp.float32,
    )
    accumulated = accumulated * jnp.swapaxes(factor, 1, 2)[..., None] + added
    running_top, row_total, accumulated = (new_top, row_total, accumulated)
    attended = accumulated / jnp.swapaxes(row_total, 1, 2)[..., None]
    log_total = running_top + jnp.log(row_total)
    attended_low = attended.reshape(flat_rows, model_width).astype(jnp.bfloat16)
    middle = (
        rows_in + jnp.dot(attended_low, full_out, preferred_element_type=jnp.float32) + obias_full
    )
    gain_second, shift_second, full_up, ubias_full, full_down, dbias_full = (
        lax.all_gather(second_gain, "fsdp", axis=0, tiled=True),
        lax.all_gather(second_shift, "fsdp", axis=0, tiled=True),
        lax.all_gather(up_weight, "fsdp", axis=0, tiled=True),
        lax.all_gather(up_bias, "fsdp", axis=0, tiled=True),
        lax.all_gather(down_weight, "fsdp", axis=0, tiled=True),
        lax.all_gather(down_bias, "fsdp", axis=0, tiled=True),
    )
    normed_two, norm_second_back = jax.vjp(
        layer_norm, middle, gain_second.astype(jnp.float32), shift_second.astype(jnp.float32)
    )
    normed_two_low = normed_two.astype(jnp.bfloat16)
    hidden = jnp.dot(normed_two_low, full_up, preferred_element_type=jnp.float32) + ubias_full
    active, gelu_back = jax.vjp(gelu_tanh, hidden)
    active_low = active.astype(jnp.bfloat16)
    result = (
        middle + jnp.dot(active_low, full_down, preferred_element_type=jnp.float32) + dbias_full
    )
    outputs = result.astype(jnp.bfloat16).reshape(seq_count, block_len, model_width)
    upstream = cotangent.astype(jnp.float32).reshape(flat_rows, model_width)
    upstream_low = upstream.astype(jnp.bfloat16)
    down_grad = jnp.einsum(
        "rf,rd->fd", active_low, upstream_low, preferred_element_type=jnp.float32
    )
    down_bias_grad = jnp.sum(upstream_low.astype(jnp.float32), axis=0)
    active_grad = jnp.einsum(
        "rd,fd->rf", upstream_low, full_down, preferred_element_type=jnp.float32
    )
    (hidden_grad,) = gelu_back(active_grad)
    hidden_low = hidden_grad.astype(jnp.bfloat16)
    up_grad = jnp.einsum(
        "rd,rf->df", normed_two_low, hidden_low, preferred_element_type=jnp.float32
    )
    up_bias_grad = jnp.sum(hidden_low.astype(jnp.float32), axis=0)
    normed_two_grad = jnp.einsum(
        "rf,df->rd", hidden_low, full_up, preferred_element_type=jnp.float32
    )
    middle_part, gain_two_grad, shift_two_grad = norm_second_back(normed_two_grad)
    middle_grad = upstream + middle_part
    middle_low = middle_grad.astype(jnp.bfloat16)
    out_grad = jnp.einsum("rd,re->de", attended_low, middle_low, preferred_element_type=jnp.float32)
    out_bias_grad = jnp.sum(middle_low.astype(jnp.float32), axis=0)
    attended_grad = jnp.einsum(
        "re,de->rd", middle_low, full_out, preferred_element_type=jnp.float32
    )
    grad_low = attended_grad.astype(jnp.bfloat16).reshape(head_shape)
    row_delta = jnp.swapaxes(jnp.sum(grad_low.astype(jnp.float32) * attended, axis=-1), 1, 2)
    gathered_keys, gathered_values = (
        lax.all_gather(
            key_rows.reshape(1, seq_count, block_len, model_width), "ctx", axis=0, tiled=True
        ),
        lax.all_gather(
            value_rows.reshape(1, seq_count, block_len, model_width), "ctx", axis=0, tiled=True
        ),
    )
    block_ids = jnp.arange(cycle_size, dtype=jnp.int32)

    def key_step(carry, inputs_here):
        key_block, value_block, block_index = inputs_here
        key_heads = key_block.reshape(head_shape)
        value_heads = value_block.reshape(head_shape)
        weights_low, score_low = score_grads(
            query_heads,
            key_heads,
            value_heads,
            grad_low,
            log_total,
            row_delta,
            query_at,
            block_index * block_len + offsets,
        )
        carry = (
            carry
            + jnp.einsum(
                "shqk,skhd->sqhd", score_low, key_heads, preferred_element_type=jnp.float32
            )
            * score_scale
        )
        key_term = (
            jnp.einsum(
                "shqk,sqhd->skhd", score_low, query_heads, preferred_element_type=jnp.float32
            )
            * score_scale
        )
        value_term = jnp.einsum(
            "shqk,sqhd->skhd", weights_low, grad_low, preferred_element_type=jnp.float32
        )
        return (
            carry,
            (
                key_term.reshape(seq_count, block_len, model_width),
                value_term.reshape(seq_count, block_len, model_width),
            ),
        )

    query_grad, (key_terms, value_terms) = lax.scan(
        key_step, jnp.zeros(head_shape, jnp.float32), (gathered_keys, gathered_values, block_ids)
    )
    key_sum, value_sum = (
        lax.psum_scatter(
            key_terms.astype(jnp.bfloat16), "ctx", scatter_dimension=0, tiled=True
        ).astype(jnp.float32),
        lax.psum_scatter(
            value_terms.astype(jnp.bfloat16), "ctx", scatter_dimension=0, tiled=True
        ).astype(jnp.float32),
    )
    key_grad = key_sum.reshape(flat_rows, model_width)
    value_grad = value_sum.reshape(flat_rows, model_width)
    query_low = query_grad.reshape(flat_rows, model_width).astype(jnp.bfloat16)
    key_low = key_grad.astype(jnp.bfloat16)
    value_low = value_grad.astype(jnp.bfloat16)
    stacked = jnp.concatenate([query_low, key_low, value_low], axis=1)
    in_grad = jnp.einsum("rd,re->de", normed_low, stacked, preferred_element_type=jnp.float32)
    query_bias_grad = jnp.sum(query_low.astype(jnp.float32), axis=0)
    value_bias_grad = jnp.sum(value_low.astype(jnp.float32), axis=0)
    normed_grad = jnp.einsum("re,de->rd", stacked, full_in, preferred_element_type=jnp.float32)
    input_part, gain_one_grad, shift_one_grad = norm_first_back(normed_grad)
    input_gradient = (middle_grad + input_part).reshape(seq_count, block_len, model_width)
    (
        gain_one_part,
        shift_one_part,
        in_part,
        qbias_part,
        vbias_part,
        out_part,
        obias_part,
        gain_two_part,
        shift_two_part,
        up_part,
        ubias_part,
        down_part,
        dbias_part,
    ) = (
        lax.psum_scatter(
            gain_one_grad.astype(jnp.bfloat16), "fsdp", scatter_dimension=0, tiled=True
        ).astype(jnp.float32),
        lax.psum_scatter(
            shift_one_grad.astype(jnp.bfloat16), "fsdp", scatter_dimension=0, tiled=True
        ).astype(jnp.float32),
        lax.psum_scatter(
            in_grad.astype(jnp.bfloat16), "fsdp", scatter_dimension=0, tiled=True
        ).astype(jnp.float32),
        lax.psum_scatter(
            query_bias_grad.astype(jnp.bfloat16), "fsdp", scatter_dimension=0, tiled=True
        ).astype(jnp.float32),
        lax.psum_scatter(
            value_bias_grad.astype(jnp.bfloat16), "fsdp", scatter_dimension=0, tiled=True
        ).astype(jnp.float32),
        lax.psum_scatter(
            out_grad.astype(jnp.bfloat16), "fsdp", scatter_dimension=0, tiled=True
        ).astype(jnp.float32),
        lax.psum_scatter(
            out_bias_grad.astype(jnp.bfloat16), "fsdp", scatter_dimension=0, tiled=True
        ).astype(jnp.float32),
        lax.psum_scatter(
            gain_two_grad.astype(jnp.bfloat16), "fsdp", scatter_dimension=0, tiled=True
        ).astype(jnp.float32),
        lax.psum_scatter(
            shift_two_grad.astype(jnp.bfloat16), "fsdp", scatter_dimension=0, tiled=True
        ).astype(jnp.float32),
        lax.psum_scatter(
            up_grad.astype(jnp.bfloat16), "fsdp", scatter_dimension=0, tiled=True
        ).astype(jnp.float32),
        lax.psum_scatter(
            up_bias_grad.astype(jnp.bfloat16), "fsdp", scatter_dimension=0, tiled=True
        ).astype(jnp.float32),
        lax.psum_scatter(
            down_grad.astype(jnp.bfloat16), "fsdp", scatter_dimension=0, tiled=True
        ).astype(jnp.float32),
        lax.psum_scatter(
            down_bias_grad.astype(jnp.bfloat16), "fsdp", scatter_dimension=0, tiled=True
        ).astype(jnp.float32),
    )
    (
        gain_one_sum,
        shift_one_sum,
        in_sum,
        qbias_sum,
        vbias_sum,
        out_sum,
        obias_sum,
        gain_two_sum,
        shift_two_sum,
        up_sum,
        ubias_sum,
        down_sum,
        dbias_sum,
    ) = lax.psum(
        (
            gain_one_part,
            shift_one_part,
            in_part,
            qbias_part,
            vbias_part,
            out_part,
            obias_part,
            gain_two_part,
            shift_two_part,
            up_part,
            ubias_part,
            down_part,
            dbias_part,
        ),
        ("dp", "ctx"),
    )
    return (
        outputs,
        input_gradient,
        gain_one_sum,
        shift_one_sum,
        in_sum,
        qbias_sum,
        vbias_sum,
        out_sum,
        obias_sum,
        gain_two_sum,
        shift_two_sum,
        up_sum,
        ubias_sum,
        down_sum,
        dbias_sum,
    )


NT = (((1,), (1,)), ((), ()))
PAIR = 2 * HEAD_DIM


def attend_kernel(place_ref, q_ref, k_ref, v_ref, *refs, count, width, start):
    o_ref, log_ref, keys, values = refs[-4:]
    own_pair = pl.program_id(0)
    pair = own_pair + start
    shift = place_ref[0]
    block_len = q_ref.shape[0] // count
    lane = lax.broadcasted_iota(jnp.int32, (1, PAIR), 1)
    valid = lane + pair * PAIR < width
    first = lane < HEAD_DIM

    def rows(block):
        return pl.ds(pl.multiple_of((block ^ shift) * block_len, block_len), block_len)

    for block in range(count):
        here = pl.ds(block * block_len, block_len)
        keys[here, :] = jnp.where(valid, k_ref[rows(block), :], 0)
        values[here, :] = jnp.where(valid, v_ref[rows(block), :], 0)
    diagonal = lax.broadcasted_iota(jnp.int32, (block_len, block_len), 0) >= (
        lax.broadcasted_iota(jnp.int32, (block_len, block_len), 1)
    )
    for block in range(count):
        seen = (block + 1) * block_len
        before = block * block_len
        queries = q_ref[rows(block), :] * jnp.bfloat16(HEAD_DIM**-0.5)
        parts = []
        logs = log_ref[rows(block), :]
        for half in range(2):
            pick = jnp.logical_and(first if half == 0 else jnp.logical_not(first), valid)
            scores = lax.dot_general(
                jnp.where(pick, queries, 0),
                keys[pl.ds(0, seen), :],
                NT,
                preferred_element_type=jnp.float32,
            )
            last = jnp.where(diagonal, scores[:, before:], -1e30)
            scores = last if block == 0 else jnp.concatenate([scores[:, :before], last], axis=1)
            top = jnp.max(scores, axis=1, keepdims=True)
            weights = jnp.exp(scores - top)
            total = jnp.sum(weights, axis=1, keepdims=True)
            added = jnp.dot(
                weights.astype(jnp.bfloat16),
                values[pl.ds(0, seen), :],
                preferred_element_type=jnp.float32,
            )
            parts.append(added / total)
            logs = jnp.where(lane == 2 * own_pair + half, top + jnp.log(total), logs)
        o_ref[rows(block), :] = jnp.where(first, parts[0], parts[1]).astype(jnp.bfloat16)
        log_ref[rows(block), :] = logs


def attend_back_kernel(
    place_ref,
    q_ref,
    k_ref,
    v_ref,
    g_ref,
    o_ref,
    log_ref,
    *refs,
    count,
    width,
    start,
):
    dq_ref, dk_ref, dv_ref, queries, grads, keys, values = refs[-11:-4]
    keys_turned, logs, deltas, turned = refs[-4:]
    pair = pl.program_id(0) + start
    shift = place_ref[0]
    length = q_ref.shape[0]
    block_len = length // count
    lane = lax.broadcasted_iota(jnp.int32, (1, PAIR), 1)
    valid = lane + pair * PAIR < width
    first = lane < HEAD_DIM
    picks = (jnp.logical_and(first, valid), jnp.logical_and(jnp.logical_not(first), valid))
    half_of = (lax.broadcasted_iota(jnp.int32, (8, PAIR), 1) // HEAD_DIM) == (
        lax.broadcasted_iota(jnp.int32, (8, PAIR), 0)
    )
    ones_of = jnp.where(half_of, 1.0, 0.0)

    def rows(block):
        return pl.ds(pl.multiple_of((block ^ shift) * block_len, block_len), block_len)

    for block in range(count):
        here = pl.ds(block * block_len, block_len)
        key_block = jnp.where(valid, k_ref[rows(block), :], 0)
        keys[here, :] = key_block
        keys_turned[:, here] = key_block.astype(jnp.float32).T.astype(jnp.bfloat16)
        values[here, :] = jnp.where(valid, v_ref[rows(block), :], 0)
        query_block = q_ref[rows(block), :] * jnp.bfloat16(HEAD_DIM**-0.5)
        grad_block = jnp.where(valid, g_ref[rows(block), :], 0)
        for half in range(2):
            queries[half, here, :] = jnp.where(picks[half], query_block, 0)
            grads[half, here, :] = jnp.where(picks[half], grad_block, 0)
        mixed = grad_block.astype(jnp.float32) * jnp.where(
            valid, o_ref[rows(block), :], 0
        ).astype(jnp.float32)
        deltas[:, here] = lax.dot_general(
            ones_of,
            mixed,
            NT,
            preferred_element_type=jnp.float32,
            precision=lax.Precision.HIGHEST,
        )
        logs[:, here] = log_ref[
            0, :, pl.ds(pl.multiple_of((block ^ shift) * block_len, block_len), block_len)
        ]
    diagonal = lax.broadcasted_iota(jnp.int32, (block_len, block_len), 0) <= (
        lax.broadcasted_iota(jnp.int32, (block_len, block_len), 1)
    )
    for block in range(count):
        here = pl.ds(block * block_len, block_len)
        after = pl.ds(block * block_len, length - block * block_len)
        key_total = jnp.zeros((block_len, PAIR), jnp.float32)
        value_total = jnp.zeros((block_len, PAIR), jnp.float32)
        for half in range(2):
            scores = lax.dot_general(
                keys[here, :], queries[half, after, :], NT, preferred_element_type=jnp.float32
            )
            shifted = scores - logs[half : half + 1, after]
            own = jnp.where(diagonal, shifted[:, :block_len], -1e30)
            if block < count - 1:
                own = jnp.concatenate([own, shifted[:, block_len:]], axis=1)
            weights = jnp.exp(own)
            pressure = lax.dot_general(
                values[here, :], grads[half, after, :], NT, preferred_element_type=jnp.float32
            )
            score_low = (weights * (pressure - deltas[half : half + 1, after])).astype(
                jnp.bfloat16
            )
            value_total += jnp.dot(
                weights.astype(jnp.bfloat16),
                grads[half, after, :],
                preferred_element_type=jnp.float32,
            )
            key_total += jnp.dot(
                score_low, queries[half, after, :], preferred_element_type=jnp.float32
            )
            part = pl.ds(half * HEAD_DIM, HEAD_DIM)
            term = jnp.dot(
                keys_turned[part, here], score_low, preferred_element_type=jnp.float32
            )
            if block == 0:
                turned[part, after] = term
            else:
                turned[part, after] += term
        dk_ref[rows(block), :] = key_total.astype(jnp.bfloat16)
        dv_ref[rows(block), :] = value_total.astype(jnp.bfloat16)
    for block in range(count):
        here = pl.ds(block * block_len, block_len)
        dq_ref[rows(block), :] = (turned[:, here].T * HEAD_DIM**-0.5).astype(jnp.bfloat16)


def attend(place, queries, key_rows, value_rows, count, start, pairs, before):
    length, width = queries.shape
    heads_block = pl.BlockSpec((length, PAIR), lambda pair, place_ref: (0, pair + start))
    return pl.pallas_call(
        functools.partial(attend_kernel, count=count, width=width, start=start),
        grid_spec=pltpu.PrefetchScalarGridSpec(
            num_scalar_prefetch=1,
            grid=(pairs,),
            in_specs=[heads_block] * 3 + [pl.BlockSpec(memory_space=pl.ANY)] * len(before),
            out_specs=[
                heads_block,
                pl.BlockSpec((length, 128), lambda pair, place_ref: (0, 0)),
            ],
            scratch_shapes=[pltpu.VMEM((length, PAIR), jnp.bfloat16)] * 2,
        ),
        out_shape=[
            jax.ShapeDtypeStruct((length, width), jnp.bfloat16),
            jax.ShapeDtypeStruct((length, 128), jnp.float32),
        ],
        input_output_aliases={4 + at: at for at in range(len(before))},
        compiler_params=pltpu.CompilerParams(vmem_limit_bytes=48 * 2**20),
        cost_estimate=pl.CostEstimate(
            flops=4 * length * length * PAIR * pairs * 4,
            bytes_accessed=8 * length * PAIR * pairs,
            transcendentals=length * length * pairs,
        ),
        name="attend",
    )(place, queries, key_rows, value_rows, *before)


def attend_back(
    place, queries, key_rows, value_rows, grads, attended, logs, count, start, pairs, before
):
    length, width = queries.shape
    heads_block = pl.BlockSpec((length, PAIR), lambda pair, place_ref: (0, pair + start))
    low_rows = pltpu.VMEM((length, PAIR), jnp.bfloat16)
    low_pair = pltpu.VMEM((2, length, PAIR), jnp.bfloat16)
    return pl.pallas_call(
        functools.partial(attend_back_kernel, count=count, width=width, start=start),
        grid_spec=pltpu.PrefetchScalarGridSpec(
            num_scalar_prefetch=1,
            grid=(pairs,),
            in_specs=[heads_block] * 5
            + [pl.BlockSpec((1, 2, length), lambda pair, place_ref: (pair, 0, 0))]
            + [pl.BlockSpec(memory_space=pl.ANY)] * len(before),
            out_specs=[heads_block] * 3,
            scratch_shapes=[
                low_pair,
                low_pair,
                low_rows,
                low_rows,
                pltpu.VMEM((PAIR, length), jnp.bfloat16),
                pltpu.VMEM((2, length), jnp.float32),
                pltpu.VMEM((8, length), jnp.float32),
                pltpu.VMEM((PAIR, length), jnp.float32),
            ],
        ),
        out_shape=[jax.ShapeDtypeStruct((length, width), jnp.bfloat16)] * 3,
        input_output_aliases={7 + at: at for at in range(len(before))},
        compiler_params=pltpu.CompilerParams(vmem_limit_bytes=48 * 2**20),
        cost_estimate=pl.CostEstimate(
            flops=10 * length * length * PAIR * pairs * 3,
            bytes_accessed=16 * length * PAIR * pairs,
            transcendentals=length * length * pairs,
        ),
        name="attend_back",
    )(place, queries, key_rows, value_rows, grads, attended, logs, *before)


def settle_kernel(place_ref, *refs):
    pieces, out_ref = refs[:-1], refs[-1]
    for at, piece in enumerate(pieces):
        out_ref[place_ref[at]] = piece[...].astype(out_ref.dtype)


def settle(places, pieces, dtype):
    return pl.pallas_call(
        settle_kernel,
        in_specs=[pl.BlockSpec(memory_space=pltpu.SMEM)]
        + [pl.BlockSpec(memory_space=pltpu.VMEM)] * len(pieces),
        out_specs=pl.BlockSpec(memory_space=pltpu.VMEM),
        out_shape=jax.ShapeDtypeStruct((len(pieces),) + pieces[0].shape, dtype),
        compiler_params=pltpu.CompilerParams(vmem_limit_bytes=48 * 2**20),
        name="settle",
    )(places, *pieces)


def plane_partner(device, kind):
    core = device & 1
    if kind == "core":
        return device ^ 1
    if kind == "far":
        return device ^ (3 if core else 5)
    if kind == "near":
        return device ^ (2 if core else 4)
    return device ^ (4 if core else 2)


def plane_swap(values, kind):
    return lax.ppermute(
        values, ("dp", "ctx"), [(device, plane_partner(device, kind)) for device in range(8)]
    )


def ctx_swap(values, bits):
    return lax.ppermute(values, "ctx", [(device, device ^ bits) for device in range(4)])


def low_sum(*terms):
    return sum(term.astype(jnp.float32) for term in terms).astype(jnp.bfloat16)


def reduce_core(pieces):
    return plane_swap(pieces[2], "core"), plane_swap(pieces[3], "core")


def reduce_last(shard):
    whole = low_sum(shard, plane_swap(shard, "other"))
    return [whole] + [plane_swap(whole, kind) for kind in ("near", "core", "far")]


def scatter_rows(values):
    return lax.psum_scatter(values, "fsdp", scatter_dimension=0, tiled=True)


def chosen(index, options):
    result = options[-1]
    for at in range(len(options) - 2, -1, -1):
        result = jnp.where(index == at, options[at], result)
    return result


def gather_vector(values, z):
    around = [values] + [
        lax.ppermute(values, "fsdp", [(device, (device + step) % 4) for device in range(4)])
        for step in range(1, 4)
    ]
    return jnp.stack([chosen((z - at) % 4, around) for at in range(4)])


def reduce_vector(values, z):
    rows = [values[at] for at in range(4)]
    total = chosen(z, rows)
    for step in range(1, 4):
        total = total + lax.ppermute(
            chosen((z + step) % 4, rows),
            "fsdp",
            [(device, (device + step) % 4) for device in range(4)],
        )
    for bits in (1, 2, 4):
        total = total + lax.ppermute(
            total, ("dp", "ctx"), [(device, device ^ bits) for device in range(8)]
        )
    return total


def product(left, right, dims):
    return lax.dot_general(left, right, ((dims[:1], dims[1:]), ((), ())),
                           preferred_element_type=jnp.float32)


def gelu_pair(values):
    inner = 0.7978845608028654
    cubic = inner * 0.044715
    squared = values * values
    curve = jnp.tanh(values * (inner + cubic * squared))
    half = 0.5 * values
    active = half + half * curve
    slope = 0.5 + 0.5 * curve + half * (1.0 - curve * curve) * (inner + 3.0 * cubic * squared)
    return active, slope


def block_flops(rows, width, count):
    return pl.CostEstimate(
        flops=2 * rows * width * width * count,
        bytes_accessed=2 * width * width * count + 4 * rows * width * count,
        transcendentals=0,
    )


def unit_of(values):
    centred = values - jnp.mean(values, axis=-1, keepdims=True)
    scale = lax.rsqrt(jnp.mean(centred * centred, axis=-1, keepdims=True) + epsilon)
    return centred * scale, scale


def fold(values):
    rows, width = values.shape
    return jnp.sum(values.reshape(rows // 8, 8, width), axis=0)


def front_kernel(places_ref, vectors_ref, *refs):
    slots, pieces = refs[:4], refs[4:20]
    x_ref, h_ref, q_ref, k_ref, v_ref, all_ref, weights, arrived, left = refs[20:]
    copies = [
        pltpu.make_async_copy(piece, weights.at[places_ref[at]], arrived.at[at])
        for at, piece in enumerate(pieces)
    ]
    for copy in copies:
        copy.start()
    rows, width = x_ref.shape
    step = rows // 4
    for at, slot in enumerate(slots):
        here = pl.ds(at * step, step)
        values = slot[...].astype(jnp.float32).T
        x_ref[here, :] = values.astype(jnp.bfloat16)
        unit, _ = unit_of(values)
        h_ref[here, :] = (unit * vectors_ref[0:1, :] + vectors_ref[1:2, :]).astype(jnp.bfloat16)
    for copy in copies:
        copy.wait()
    leave = pltpu.make_async_copy(weights, all_ref, left)
    leave.start()
    for section, out_ref in enumerate((q_ref, k_ref, v_ref)):

        def multiply(at, carry, section=section, out_ref=out_ref):
            here = pl.ds(pl.multiple_of(at * step, step), step)
            matrix = weights[4 * section : 4 * section + 4].reshape(width, width)
            total = jnp.dot(h_ref[here, :], matrix, preferred_element_type=jnp.float32)
            if section != 1:
                row = 2 if section == 0 else 3
                total = total + vectors_ref[row : row + 1, :]
            out_ref[here, :] = total.astype(jnp.bfloat16)
            return carry

        lax.fori_loop(0, rows // step, multiply, 0)
    leave.wait()


def front(places, slots, vectors, pieces):
    width, step = slots[0].shape
    rows = 4 * step
    vmem = pl.BlockSpec(memory_space=pltpu.VMEM)
    hbm = pl.BlockSpec(memory_space=pl.ANY)
    shape = jax.ShapeDtypeStruct((rows, width), jnp.bfloat16)
    whole = (16,) + pieces[0].shape
    return pl.pallas_call(
        front_kernel,
        in_specs=[pl.BlockSpec(memory_space=pltpu.SMEM)] + [vmem] * 5 + [hbm] * 16,
        out_specs=[vmem] * 5 + [hbm],
        out_shape=[shape] * 5 + [jax.ShapeDtypeStruct(whole, jnp.bfloat16)],
        scratch_shapes=[
            pltpu.VMEM(whole, jnp.bfloat16),
            pltpu.SemaphoreType.DMA((16,)),
            pltpu.SemaphoreType.DMA,
        ],
        compiler_params=pltpu.CompilerParams(vmem_limit_bytes=56 * 2**20),
        cost_estimate=block_flops(rows, width, 3),
        name="front",
    )(places, vectors, *slots, *pieces)


def turn_kernel(*refs):
    slots, out_ref = refs[:-1], refs[-1]
    step = slots[0].shape[1]
    for at, slot in enumerate(slots):
        out_ref[pl.ds(at * step, step), :] = (
            slot[...].astype(jnp.float32).T.astype(jnp.bfloat16)
        )


def turn(slots):
    width, step = slots[0].shape
    return pl.pallas_call(
        turn_kernel,
        out_shape=jax.ShapeDtypeStruct((len(slots) * step, width), jnp.bfloat16),
        compiler_params=pltpu.CompilerParams(vmem_limit_bytes=48 * 2**20),
        name="turn",
    )(*slots)


def assemble_kernel(place_ref, *refs, plan):
    pieces, outs = refs[:4], refs[4:]
    for at, piece in enumerate(pieces):
        for kind, moves in enumerate(plan):

            @pl.when(place_ref[at] == kind)
            def _(piece=piece, moves=moves):
                for out, source, target, size in moves:
                    outs[out][:, target : target + size] = piece[
                        :, source : source + size
                    ].astype(jnp.float32)


def assemble(places, pieces, plan, shapes):
    vmem = pl.BlockSpec(memory_space=pltpu.VMEM)
    return pl.pallas_call(
        functools.partial(assemble_kernel, plan=plan),
        in_specs=[pl.BlockSpec(memory_space=pltpu.SMEM)] + [vmem] * 4,
        out_specs=[vmem] * len(shapes),
        out_shape=[jax.ShapeDtypeStruct(shape, jnp.float32) for shape in shapes],
        compiler_params=pltpu.CompilerParams(vmem_limit_bytes=48 * 2**20),
        name="assemble",
    )(places, *pieces)


def store_turned(step, refs, values):
    size = refs[0].shape[1]
    share = values.shape[0] // size
    for at, ref in enumerate(refs):

        @pl.when(step == at // share)
        def _(at=at, ref=ref):
            first = (at % share) * size
            ref[...] = values[first : first + size].T.astype(ref.dtype)


def fetch(step, copies):
    @pl.when(step == 0)
    def _():
        for copy in copies:
            copy.start()


def arrive(step, copy):
    @pl.when(step == 0)
    def _():
        copy.wait()


def middle_kernel(x_ref, o_ref, vectors_ref, all_ref, middle_ref, h_ref, weights, arrived):
    step = pl.program_id(0)
    width = x_ref.shape[1]
    copy = pltpu.make_async_copy(all_ref.at[pl.ds(12, 4)], weights, arrived)
    fetch(step, [copy])
    arrive(step, copy)
    middle = (
        x_ref[...].astype(jnp.float32)
        + jnp.dot(
            o_ref[...], weights[...].reshape(width, width), preferred_element_type=jnp.float32
        )
        + vectors_ref[0:1, :]
    )
    middle_ref[...] = middle
    unit, _ = unit_of(middle)
    h_ref[...] = (unit * vectors_ref[1:2, :] + vectors_ref[2:3, :]).astype(jnp.bfloat16)


def up_kernel(h_ref, biases_ref, *refs):
    sources = refs[:2]
    active_refs, slope_refs = refs[2:4], refs[4:6]
    weights, arrived = refs[6:]
    step = pl.program_id(0)
    copies = [
        pltpu.make_async_copy(source, weights.at[at], arrived.at[at])
        for at, source in enumerate(sources)
    ]
    fetch(step, copies)
    for at in range(2):
        arrive(step, copies[at])
        hidden = (
            jnp.dot(h_ref[...], weights[at], preferred_element_type=jnp.float32)
            + biases_ref[at : at + 1, :]
        )
        active, slope = gelu_pair(hidden)
        active_refs[at][...] = active.astype(jnp.bfloat16)
        slope_refs[at][...] = slope.astype(jnp.bfloat16)


def down_kernel(middle_ref, vectors_ref, *refs):
    actives, sources = refs[:4], refs[4:8]
    out_refs = refs[8:12]
    weights, arrived = refs[12:]
    step = pl.program_id(0)
    copies = [
        pltpu.make_async_copy(source, weights.at[at], arrived.at[at])
        for at, source in enumerate(sources)
    ]
    fetch(step, copies)
    total = middle_ref[...] + vectors_ref[0:1, :]
    for at in range(4):
        arrive(step, copies[at])
        total = total + jnp.dot(
            actives[at][...], weights[at], preferred_element_type=jnp.float32
        )
    store_turned(step, out_refs, total)


def norm_back(values, gain, grad):
    unit, scale = unit_of(values)
    turned = grad * gain
    inner = (
        turned
        - jnp.mean(turned, axis=-1, keepdims=True)
        - unit * jnp.mean(turned * unit, axis=-1, keepdims=True)
    )
    return scale * inner, grad * unit


def hidden_kernel(g_ref, *refs):
    slopes, sources = refs[:2], refs[2:4]
    hidden_refs, sums_ref = refs[4:6], refs[6]
    weights, arrived = refs[7:]
    step = pl.program_id(0)
    copies = [
        pltpu.make_async_copy(source, weights.at[at], arrived.at[at])
        for at, source in enumerate(sources)
    ]
    fetch(step, copies)

    @pl.when(step == 0)
    def _():
        sums_ref[...] = jnp.zeros_like(sums_ref)

    upstream = g_ref[...]
    for at in range(2):
        arrive(step, copies[at])
        hidden = lax.dot_general(
            upstream, weights[at], NT, preferred_element_type=jnp.float32
        )
        hidden = (hidden * slopes[at][...].astype(jnp.float32)).astype(jnp.bfloat16)
        hidden_refs[at][...] = hidden
        sums_ref[at] += fold(hidden.astype(jnp.float32))
    sums_ref[2] += fold(upstream.astype(jnp.float32))


def back_kernel(g_ref, middle_ref, vectors_ref, *refs):
    hiddens, sources, all_ref = refs[:4], refs[4:8], refs[8]
    grad_ref, low_ref, out_ref, sums_ref = refs[9:13]
    weights, out_weights, arrived = refs[13:]
    step = pl.program_id(0)
    width = middle_ref.shape[1]
    copies = [
        pltpu.make_async_copy(source, weights.at[at], arrived.at[at])
        for at, source in enumerate(sources)
    ] + [pltpu.make_async_copy(all_ref.at[pl.ds(12, 4)], out_weights, arrived.at[4])]
    fetch(step, copies)

    @pl.when(step == 0)
    def _():
        sums_ref[...] = jnp.zeros_like(sums_ref)

    total = jnp.zeros(middle_ref.shape, jnp.float32)
    for at in range(4):
        arrive(step, copies[at])
        total = total + lax.dot_general(
            hiddens[at][...], weights[at], NT, preferred_element_type=jnp.float32
        )
    part, gain_term = norm_back(middle_ref[...], vectors_ref[0:1, :], total)
    sums_ref[0] += fold(gain_term)
    sums_ref[1] += fold(total)
    grad = g_ref[...].astype(jnp.float32) + part
    grad_ref[...] = grad
    grad_low = grad.astype(jnp.bfloat16)
    low_ref[...] = grad_low
    sums_ref[2] += fold(grad_low.astype(jnp.float32))
    arrive(step, copies[4])
    out_ref[...] = lax.dot_general(
        grad_low,
        out_weights[...].reshape(width, width),
        NT,
        preferred_element_type=jnp.float32,
    ).astype(jnp.bfloat16)


def last_kernel(q_ref, k_ref, v_ref, x_ref, grad_ref, vectors_ref, all_ref, *refs):
    out_refs = refs[:4]
    sums_ref, weights, arrived = refs[4:]
    step = pl.program_id(0)
    width = x_ref.shape[1]
    copies = [
        pltpu.make_async_copy(
            all_ref.at[pl.ds(4 * at, 4)], weights.at[pl.ds(4 * at, 4)], arrived.at[at]
        )
        for at in range(3)
    ]
    fetch(step, copies)
    total = jnp.zeros(x_ref.shape, jnp.float32)
    for at, ref in enumerate((q_ref, k_ref, v_ref)):
        arrive(step, copies[at])
        total = total + lax.dot_general(
            ref[...],
            weights[4 * at : 4 * at + 4].reshape(width, width),
            NT,
            preferred_element_type=jnp.float32,
        )
    part, gain_term = norm_back(x_ref[...].astype(jnp.float32), vectors_ref[0:1, :], total)
    store_turned(step, out_refs, grad_ref[...] + part)

    @pl.when(step == 0)
    def _():
        sums_ref[...] = jnp.zeros_like(sums_ref)

    terms = (
        gain_term,
        total,
        q_ref[...].astype(jnp.float32),
        v_ref[...].astype(jnp.float32),
    )
    for at, term in enumerate(terms):
        sums_ref[at] += fold(term)


def by_rows(kernel, name, rows, width, tiled, whole, remote, outs, sums, scratch, sems, blocks):
    step = 512
    tile = pl.BlockSpec((step, width), lambda at: (at, 0))
    out_specs, out_shape = [], []
    for dtype in outs:
        if dtype is None:
            out_specs += [pl.BlockSpec((width, rows // 4), lambda at: (0, 0))] * 4
            out_shape += [jax.ShapeDtypeStruct((width, rows // 4), jnp.bfloat16)] * 4
        else:
            out_specs.append(tile)
            out_shape.append(jax.ShapeDtypeStruct((rows, width), dtype))
    if sums:
        out_specs.append(pl.BlockSpec((sums, 8, width), lambda at: (0, 0, 0)))
        out_shape.append(jax.ShapeDtypeStruct((sums, 8, width), jnp.float32))
    return pl.pallas_call(
        kernel,
        grid=(rows // step,),
        in_specs=[tile] * len(tiled[0])
        + [pl.BlockSpec(value.shape, lambda at: (0, 0)) for value in whole]
        + [tile] * len(tiled[1])
        + [pl.BlockSpec(memory_space=pl.ANY)] * len(remote),
        out_specs=out_specs,
        out_shape=out_shape,
        scratch_shapes=[pltpu.VMEM(shape, jnp.bfloat16) for shape in scratch]
        + [pltpu.SemaphoreType.DMA((sems,)) if sems > 1 else pltpu.SemaphoreType.DMA],
        compiler_params=pltpu.CompilerParams(vmem_limit_bytes=60 * 2**20),
        cost_estimate=block_flops(rows, width, blocks),
        name=name,
    )(*tiled[0], *whole, *tiled[1], *remote)


def per_device_exchanged(
    inputs,
    cotangent,
    first_gain,
    first_shift,
    project_in,
    query_bias,
    value_bias,
    project_out,
    output_bias,
    second_gain,
    second_shift,
    up_weight,
    up_bias,
    down_weight,
    down_bias,
):
    seq_count, block_len, width = inputs.shape
    low = jnp.bfloat16
    wide = jnp.float32
    c = lax.axis_index("ctx")
    y = lax.axis_index("dp")
    z = lax.axis_index("fsdp")
    core = c & 1
    x = c >> 1
    mine = core * 2 + jnp.where(core == 0, y, x)
    across = (1 - core) * 2 + jnp.where(core == 0, x, y)
    classes = [mine, mine ^ 1, across, across ^ 1]
    slot_of = [
        chosen(0, [sum(at * (classes[at] == kind).astype(jnp.int32) for at in range(4))])
        for kind in range(4)
    ]
    quarter = width // 4
    rows, area = seq_count * block_len, (width, width)
    pin = lax.optimization_barrier
    place = jnp.stack([c])
    places = jnp.stack([c ^ at for at in range(4)])
    class_places = jnp.stack(classes)

    def spread(values):
        values = jnp.swapaxes(values, 1, 2)
        return [lax.dynamic_index_in_dim(values, c, 0, keepdims=False)] + [
            ctx_swap(lax.dynamic_index_in_dim(values, c ^ bits, 0, keepdims=False), bits)
            for bits in range(1, 4)
        ]

    def collect(pieces, dtype):
        moved = [pieces[0]] + [ctx_swap(pieces[bits], bits) for bits in range(1, 4)]
        return jnp.swapaxes(settle(places, moved, dtype), 1, 2)

    sections = [
        project_in[:, :width],
        project_in[:, width : 2 * width],
        project_in[:, 2 * width :],
        project_out,
    ]
    section = chosen(mine, sections)
    section, inputs = pin((section, inputs))
    shards = [
        lax.ppermute(section, "fsdp", [(device, (device + step) % 4) for device in range(4)])
        for step in range(1, 4)
    ]
    slots_in = spread(inputs)
    pieces_in = (
        first_gain,
        first_shift,
        query_bias,
        value_bias,
        output_bias,
        second_gain,
        second_shift,
        down_bias,
        up_bias,
    )
    shards[0], cotangent, up_weight, down_weight, *pieces_in = pin(
        (shards[0], cotangent, up_weight, down_weight, *pieces_in)
    )
    vectors = gather_vector(jnp.concatenate(pieces_in), z).astype(wide)
    slots_back = spread(cotangent)
    up_piece = jnp.concatenate(
        [
            lax.dynamic_slice_in_dim(up_weight, at * width + mine * quarter, quarter, 1)
            for at in range(4)
        ],
        axis=1,
    )
    up_piece, vectors, shards[1], shards[2], *slots_in = pin(
        (up_piece, vectors, shards[1], shards[2], *slots_in)
    )
    near_shards = [plane_swap(shard, "near") for shard in shards]
    around = (
        sections
        + shards
        + near_shards
        + [plane_swap(shard, "core") for shard in shards]
        + [plane_swap(shard, "core") for shard in near_shards]
    )
    around_places = jnp.stack(
        [kind * 4 + z for kind in range(4)]
        + [kind * 4 + (z - step) % 4 for kind in classes for step in range(1, 4)]
    )
    up_own = lax.all_gather(up_piece, "fsdp", axis=0, tiled=True)
    down_piece = lax.dynamic_slice_in_dim(down_weight, mine * quarter, quarter, 0)
    gain_first, shift_first, qbias, vbias, obias, gain_second, shift_second, dbias = (
        vectors[:, at * quarter : (at + 1) * quarter].reshape(1, width) for at in range(8)
    )
    ubias = vectors[:, 8 * quarter :].reshape(4, 4, quarter)
    ubias = jnp.concatenate(
        [
            chosen(kind, [ubias[:, at] for at in range(4)]).reshape(1, width)
            for kind in classes
        ],
        axis=0,
    )

    rows_in, normed_low, queries, key_rows, value_rows, weights = front(
        around_places,
        slots_in,
        jnp.concatenate([gain_first, shift_first, qbias, vbias], axis=0),
        around,
    )
    slots_back[0], down_piece, queries = pin((slots_back[0], down_piece, queries))
    upstream_low = turn(slots_back)
    down_own = lax.all_gather(down_piece, "fsdp", axis=0, tiled=True)
    attended, logs_one = attend(place, queries, key_rows, value_rows, seq_count, 0, 5, [])
    up_own, late_queries, attended = pin((up_own, queries, attended))
    up_near, up_core = plane_swap(up_own, "near"), plane_swap(up_own, "core")
    attended, logs_two = attend(
        place, late_queries, key_rows, value_rows, seq_count, 5, 4, [attended]
    )
    up_core, attended = pin((up_core, attended))
    logs_one, logs_two = (logs.T.reshape(64, 2, rows) for logs in (logs_one, logs_two))
    middle, normed_two_low = by_rows(
        middle_kernel,
        "middle",
        rows,
        width,
        ([rows_in, attended], []),
        [jnp.concatenate([obias, gain_second, shift_second], axis=0)],
        [weights],
        [wide, low],
        0,
        [(4,) + section.shape],
        1,
        1,
    )
    up_near, normed_two_low = pin((up_near, normed_two_low))
    up_slots = [up_own, up_near, up_core, plane_swap(up_near, "core")]
    active, slopes = [None] * 4, [None] * 4

    def up(first):
        outs = by_rows(
            up_kernel,
            "up",
            rows,
            width,
            ([normed_two_low], []),
            [jnp.concatenate([ubias[first : first + 1], ubias[first + 2 : first + 3]], axis=0)],
            [up_slots[first], up_slots[first + 2]],
            [low] * 4,
            0,
            [(2,) + area],
            2,
            2,
        )
        active[first], active[first + 2], slopes[first], slopes[first + 2] = outs

    up(0)
    up_slots[3], active[0], active[2] = pin((up_slots[3], active[0], active[2]))
    up(1)
    down_own, *active = pin((down_own, *active))
    down_near, down_core = plane_swap(down_own, "near"), plane_swap(down_own, "core")

    def turned_product(left, right):
        return product(left, right, (0, 0)).astype(low)

    down_terms = [turned_product(active[slot], upstream_low) for slot in (3, 2)]
    upstream_low, *down_terms = pin((upstream_low, *down_terms))
    down_terms += [turned_product(active[slot], upstream_low) for slot in (1, 0)]
    down_terms = down_terms[::-1]
    down_far, down_far_two = reduce_core(down_terms)
    upstream_low, *down_terms = pin((upstream_low, *down_terms))
    hidden_low = [None] * 4

    def hidden(first, upstream):
        hidden_low[first], hidden_low[first + 2], sums = by_rows(
            hidden_kernel,
            "hidden",
            rows,
            width,
            ([upstream], [slopes[first], slopes[first + 2]]),
            [],
            [down_slots[first], down_slots[first + 2]],
            [low] * 2,
            3,
            [(2,) + area],
            2,
            2,
        )
        return sums

    down_near, upstream_low = pin((down_near, upstream_low))
    down_slots = [down_own, down_near, down_core, plane_swap(down_near, "core")]
    sums_even = hidden(0, upstream_low)
    upstream_late, sums_even = pin((upstream_low, sums_even))
    sums_odd = hidden(1, upstream_late)
    hidden_sums = jnp.stack(
        [sums_even[0], sums_odd[0], sums_even[1], sums_odd[1], sums_even[2]]
    )
    down_second = low_sum(down_terms[1], down_far_two)
    down_second, down_far, *hidden_low = pin((down_second, down_far, *hidden_low))
    down_close = plane_swap(down_second, "near")
    middle_grad, middle_low, grad_low, back_sums = by_rows(
        back_kernel,
        "back",
        rows,
        width,
        ([upstream_low, middle], hidden_low),
        [gain_second],
        up_slots + [weights],
        [wide, low, low],
        3,
        [(4,) + area, (4,) + section.shape],
        5,
        5,
    )
    down_first = low_sum(down_terms[0], down_far, down_close)
    down_first, normed_two_low = pin((down_first, pin((normed_two_low, middle_low))[0]))
    down_shard = scatter_rows(down_first)
    up_terms = [turned_product(normed_two_low, hidden_low[slot]) for slot in (3, 2)]
    normed_two_low, *up_terms = pin((normed_two_low, *up_terms))
    up_terms += [turned_product(normed_two_low, hidden_low[slot]) for slot in (1, 0)]
    up_terms = up_terms[::-1]
    up_far, up_far_two = reduce_core(up_terms)
    out_term = turned_product(attended, middle_low)
    up_second = low_sum(up_terms[1], up_far_two)
    grad_low, up_second, up_far, out_term, *up_terms = pin(
        (grad_low, up_second, up_far, out_term, *up_terms)
    )
    up_close = plane_swap(up_second, "near")
    in_grads = attend_back(
        place, late_queries, key_rows, value_rows, grad_low, attended, logs_one, seq_count, 0, 5, []
    )
    up_first = low_sum(up_terms[0], up_far, up_close)
    up_first, down_shard, *in_grads = pin((up_first, down_shard, *in_grads))
    up_shard = scatter_rows(up_first)
    in_grads = attend_back(
        place,
        late_queries,
        key_rows,
        value_rows,
        grad_low,
        attended,
        logs_two,
        seq_count,
        5,
        4,
        in_grads,
    )
    down_parts = reduce_last(down_shard)
    in_terms = [turned_product(normed_low, grad) for grad in in_grads]
    section_grads = in_terms + [out_term]
    sections_mine = [chosen(kind, section_grads) for kind in classes]
    far, far_two = reduce_core(sections_mine)
    second = low_sum(sections_mine[1], far_two)
    second, far, *in_grads = pin((second, far, *in_grads))
    close = plane_swap(second, "near")
    query_low, key_low, value_low = in_grads
    *input_slots, last_sums = by_rows(
        last_kernel,
        "last",
        rows,
        width,
        ([query_low, key_low, value_low, rows_in, middle_grad], []),
        [gain_first],
        [weights],
        [None],
        4,
        [(12,) + section.shape],
        3,
        3,
    )
    first = low_sum(sections_mine[0], far, close)
    first, middle, up_shard, *input_slots = pin((first, middle, up_shard, *input_slots))
    input_gradient = collect(input_slots, wide)
    result_slots = by_rows(
        down_kernel,
        "down",
        rows,
        width,
        ([middle], active),
        [dbias],
        down_slots,
        [None],
        0,
        [(4,) + area],
        4,
        4,
    )
    outputs = collect(result_slots, low)
    up_parts = reduce_last(up_shard)
    shard = scatter_rows(first)

    back_sums = jnp.concatenate([hidden_sums, back_sums], axis=0)
    back_sums = jnp.sum(back_sums, axis=1)
    last_sums = jnp.sum(last_sums, axis=1)
    hidden_sums = [back_sums[slot].reshape(4, quarter) for slot in range(4)]
    hidden_sums = jnp.stack(
        [chosen(slot_of[kind], hidden_sums) for kind in range(4)], axis=1
    ).reshape(4, 4 * quarter)
    totals = reduce_vector(
        jnp.concatenate(
            [back_sums[at].reshape(4, quarter) for at in range(4, 8)]
            + [last_sums[at].reshape(4, quarter) for at in range(4)]
            + [hidden_sums],
            axis=1,
        ),
        z,
    )
    (up_sum,) = assemble(
        class_places,
        up_parts,
        [
            [(0, at * quarter, at * width + kind * quarter, quarter) for at in range(4)]
            for kind in range(4)
        ],
        [up_weight.shape],
    )
    down_sum = settle(class_places, down_parts, wide).reshape(down_weight.shape)
    shard, outputs, input_gradient, totals, up_sum, down_sum = pin(
        (shard, outputs, input_gradient, totals, up_sum, down_sum)
    )
    in_sum, out_sum = assemble(
        class_places,
        reduce_last(shard),
        [[(0, 0, kind * width, width)] for kind in range(3)] + [[(1, 0, 0, width)]],
        [project_in.shape, project_out.shape],
    )
    (
        dbias_sum,
        gain_two_sum,
        shift_two_sum,
        obias_sum,
        gain_one_sum,
        shift_one_sum,
        qbias_sum,
        vbias_sum,
    ) = (totals[at * quarter : (at + 1) * quarter] for at in range(8))
    ubias_sum = totals[8 * quarter :]
    return (
        outputs,
        input_gradient,
        gain_one_sum,
        shift_one_sum,
        in_sum,
        qbias_sum,
        vbias_sum,
        out_sum,
        obias_sum,
        gain_two_sum,
        shift_two_sum,
        up_sum,
        ubias_sum,
        down_sum,
        dbias_sum,
    )


def solution(mesh):
    sizes = dict(mesh.shape)
    exchanged = sizes["dp"] == 2 and sizes["fsdp"] == 4 and sizes["ctx"] == 4
    per_device = per_device_exchanged if exchanged else per_device_gathered
    return jax.shard_map(
        per_device,
        mesh=mesh,
        in_specs=(
            P(("dp", "fsdp"), "ctx", None),
            P(("dp", "fsdp"), "ctx", None),
            P("fsdp"),
            P("fsdp"),
            P("fsdp", None),
            P("fsdp"),
            P("fsdp"),
            P("fsdp", None),
            P("fsdp"),
            P("fsdp"),
            P("fsdp"),
            P("fsdp", None),
            P("fsdp"),
            P("fsdp", None),
            P("fsdp"),
        ),
        out_specs=(
            P(("dp", "fsdp"), "ctx", None),
            P(("dp", "fsdp"), "ctx", None),
            P("fsdp"),
            P("fsdp"),
            P("fsdp", None),
            P("fsdp"),
            P("fsdp"),
            P("fsdp", None),
            P("fsdp"),
            P("fsdp"),
            P("fsdp"),
            P("fsdp", None),
            P("fsdp"),
            P("fsdp", None),
            P("fsdp"),
        ),
        check_vma=False,
    )
```

```python
import functools

import jax
import jax.numpy as jnp
from jax import lax
from jax.experimental import pallas as pl
from jax.experimental.pallas import tpu as pltpu
from jax.sharding import PartitionSpec as P

HEADS = 17
HEAD_DIM = 64


epsilon = 1e-05


def layer_norm(values, gain, shift):
    centred = values - jnp.mean(values, axis=-1, keepdims=True)
    spread = jnp.mean(centred * centred, axis=-1, keepdims=True)
    return centred * lax.rsqrt(spread + epsilon) * gain + shift


def gelu_tanh(values):
    return jax.nn.gelu(values, approximate=True)


def score_grads(
    query_heads, key_heads, value_heads, grad_heads, log_total, row_delta, query_at, key_at
):
    score_scale = HEAD_DIM ** (-0.5)
    scores = (
        jnp.einsum("sqhd,skhd->shqk", query_heads, key_heads, preferred_element_type=jnp.float32)
        * score_scale
    )
    visible = query_at[:, None] >= key_at[None, :]
    shifted = jnp.where(visible, scores - log_total[..., None], -1e30)
    weights = jnp.where(visible, jnp.exp(shifted), 0.0)
    pressure = jnp.einsum(
        "sqhd,skhd->shqk", grad_heads, value_heads, preferred_element_type=jnp.float32
    )
    score_low = (weights * (pressure - row_delta[..., None])).astype(jnp.bfloat16)
    return (weights.astype(jnp.bfloat16), score_low)


def per_device_gathered(
    inputs,
    cotangent,
    first_gain,
    first_shift,
    project_in,
    query_bias,
    value_bias,
    project_out,
    output_bias,
    second_gain,
    second_shift,
    up_weight,
    up_bias,
    down_weight,
    down_bias,
):
    seq_count, block_len, model_width = inputs.shape
    flat_rows = seq_count * block_len
    cycle_size = lax.axis_size("ctx")
    my_block = lax.axis_index("ctx")
    score_scale = HEAD_DIM ** (-0.5)
    head_shape = (seq_count, block_len, HEADS, HEAD_DIM)
    offsets = jnp.arange(block_len, dtype=jnp.int32)
    query_at = my_block * block_len + offsets
    gain_first, shift_first, full_in, qbias_full, vbias_full, full_out, obias_full = (
        lax.all_gather(first_gain, "fsdp", axis=0, tiled=True),
        lax.all_gather(first_shift, "fsdp", axis=0, tiled=True),
        lax.all_gather(project_in, "fsdp", axis=0, tiled=True),
        lax.all_gather(query_bias, "fsdp", axis=0, tiled=True),
        lax.all_gather(value_bias, "fsdp", axis=0, tiled=True),
        lax.all_gather(project_out, "fsdp", axis=0, tiled=True),
        lax.all_gather(output_bias, "fsdp", axis=0, tiled=True),
    )
    rows_in = inputs.astype(jnp.float32).reshape(flat_rows, model_width)
    normed, norm_first_back = jax.vjp(
        layer_norm, rows_in, gain_first.astype(jnp.float32), shift_first.astype(jnp.float32)
    )
    normed_low = normed.astype(jnp.bfloat16)
    projected = jnp.dot(normed_low, full_in, preferred_element_type=jnp.float32)
    queries = (projected[:, :model_width] + qbias_full).astype(jnp.bfloat16)
    key_rows = projected[:, model_width : 2 * model_width].astype(jnp.bfloat16)
    value_rows = (projected[:, 2 * model_width :] + vbias_full).astype(jnp.bfloat16)
    query_heads = queries.reshape(head_shape)
    running_top = jnp.full((seq_count, HEADS, block_len), -1e30, jnp.float32)
    accumulated = jnp.zeros(head_shape, jnp.float32)
    piece_keys = lax.all_gather(
        key_rows.reshape(seq_count, block_len, model_width), "ctx", axis=1, tiled=True
    )
    piece_values = lax.all_gather(
        value_rows.reshape(seq_count, block_len, model_width), "ctx", axis=1, tiled=True
    )
    piece_len = piece_keys.shape[1]
    key_heads = piece_keys.reshape(seq_count, piece_len, HEADS, HEAD_DIM)
    value_heads = piece_values.reshape(seq_count, piece_len, HEADS, HEAD_DIM)
    scores = (
        jnp.einsum("sqhd,skhd->shqk", query_heads, key_heads, preferred_element_type=jnp.float32)
        * score_scale
    )
    key_at = jnp.arange(piece_len, dtype=jnp.int32)
    visible = query_at[:, None] >= key_at[None, :]
    masked = jnp.where(visible, scores, -1e30)
    new_top = jnp.maximum(running_top, jnp.max(masked, axis=-1))
    factor = jnp.exp(running_top - new_top)
    weights = jnp.where(visible, jnp.exp(masked - new_top[..., None]), 0.0)
    row_total = jnp.sum(weights, axis=-1)
    added = jnp.einsum(
        "shqk,skhd->sqhd",
        weights.astype(jnp.bfloat16),
        value_heads,
        preferred_element_type=jnp.float32,
    )
    accumulated = accumulated * jnp.swapaxes(factor, 1, 2)[..., None] + added
    running_top, row_total, accumulated = (new_top, row_total, accumulated)
    attended = accumulated / jnp.swapaxes(row_total, 1, 2)[..., None]
    log_total = running_top + jnp.log(row_total)
    attended_low = attended.reshape(flat_rows, model_width).astype(jnp.bfloat16)
    middle = (
        rows_in + jnp.dot(attended_low, full_out, preferred_element_type=jnp.float32) + obias_full
    )
    gain_second, shift_second, full_up, ubias_full, full_down, dbias_full = (
        lax.all_gather(second_gain, "fsdp", axis=0, tiled=True),
        lax.all_gather(second_shift, "fsdp", axis=0, tiled=True),
        lax.all_gather(up_weight, "fsdp", axis=0, tiled=True),
        lax.all_gather(up_bias, "fsdp", axis=0, tiled=True),
        lax.all_gather(down_weight, "fsdp", axis=0, tiled=True),
        lax.all_gather(down_bias, "fsdp", axis=0, tiled=True),
    )
    normed_two, norm_second_back = jax.vjp(
        layer_norm, middle, gain_second.astype(jnp.float32), shift_second.astype(jnp.float32)
    )
    normed_two_low = normed_two.astype(jnp.bfloat16)
    hidden = jnp.dot(normed_two_low, full_up, preferred_element_type=jnp.float32) + ubias_full
    active, gelu_back = jax.vjp(gelu_tanh, hidden)
    active_low = active.astype(jnp.bfloat16)
    result = (
        middle + jnp.dot(active_low, full_down, preferred_element_type=jnp.float32) + dbias_full
    )
    outputs = result.astype(jnp.bfloat16).reshape(seq_count, block_len, model_width)
    upstream = cotangent.astype(jnp.float32).reshape(flat_rows, model_width)
    upstream_low = upstream.astype(jnp.bfloat16)
    down_grad = jnp.einsum(
        "rf,rd->fd", active_low, upstream_low, preferred_element_type=jnp.float32
    )
    down_bias_grad = jnp.sum(upstream_low.astype(jnp.float32), axis=0)
    active_grad = jnp.einsum(
        "rd,fd->rf", upstream_low, full_down, preferred_element_type=jnp.float32
    )
    (hidden_grad,) = gelu_back(active_grad)
    hidden_low = hidden_grad.astype(jnp.bfloat16)
    up_grad = jnp.einsum(
        "rd,rf->df", normed_two_low, hidden_low, preferred_element_type=jnp.float32
    )
    up_bias_grad = jnp.sum(hidden_low.astype(jnp.float32), axis=0)
    normed_two_grad = jnp.einsum(
        "rf,df->rd", hidden_low, full_up, preferred_element_type=jnp.float32
    )
    middle_part, gain_two_grad, shift_two_grad = norm_second_back(normed_two_grad)
    middle_grad = upstream + middle_part
    middle_low = middle_grad.astype(jnp.bfloat16)
    out_grad = jnp.einsum("rd,re->de", attended_low, middle_low, preferred_element_type=jnp.float32)
    out_bias_grad = jnp.sum(middle_low.astype(jnp.float32), axis=0)
    attended_grad = jnp.einsum(
        "re,de->rd", middle_low, full_out, preferred_element_type=jnp.float32
    )
    grad_low = attended_grad.astype(jnp.bfloat16).reshape(head_shape)
    row_delta = jnp.swapaxes(jnp.sum(grad_low.astype(jnp.float32) * attended, axis=-1), 1, 2)
    gathered_keys, gathered_values = (
        lax.all_gather(
            key_rows.reshape(1, seq_count, block_len, model_width), "ctx", axis=0, tiled=True
        ),
        lax.all_gather(
            value_rows.reshape(1, seq_count, block_len, model_width), "ctx", axis=0, tiled=True
        ),
    )
    block_ids = jnp.arange(cycle_size, dtype=jnp.int32)

    def key_step(carry, inputs_here):
        key_block, value_block, block_index = inputs_here
        key_heads = key_block.reshape(head_shape)
        value_heads = value_block.reshape(head_shape)
        weights_low, score_low = score_grads(
            query_heads,
            key_heads,
            value_heads,
            grad_low,
            log_total,
            row_delta,
            query_at,
            block_index * block_len + offsets,
        )
        carry = (
            carry
            + jnp.einsum(
                "shqk,skhd->sqhd", score_low, key_heads, preferred_element_type=jnp.float32
            )
            * score_scale
        )
        key_term = (
            jnp.einsum(
                "shqk,sqhd->skhd", score_low, query_heads, preferred_element_type=jnp.float32
            )
            * score_scale
        )
        value_term = jnp.einsum(
            "shqk,sqhd->skhd", weights_low, grad_low, preferred_element_type=jnp.float32
        )
        return (
            carry,
            (
                key_term.reshape(seq_count, block_len, model_width),
                value_term.reshape(seq_count, block_len, model_width),
            ),
        )

    query_grad, (key_terms, value_terms) = lax.scan(
        key_step, jnp.zeros(head_shape, jnp.float32), (gathered_keys, gathered_values, block_ids)
    )
    key_sum, value_sum = (
        lax.psum_scatter(
            key_terms.astype(jnp.bfloat16), "ctx", scatter_dimension=0, tiled=True
        ).astype(jnp.float32),
        lax.psum_scatter(
            value_terms.astype(jnp.bfloat16), "ctx", scatter_dimension=0, tiled=True
        ).astype(jnp.float32),
    )
    key_grad = key_sum.reshape(flat_rows, model_width)
    value_grad = value_sum.reshape(flat_rows, model_width)
    query_low = query_grad.reshape(flat_rows, model_width).astype(jnp.bfloat16)
    key_low = key_grad.astype(jnp.bfloat16)
    value_low = value_grad.astype(jnp.bfloat16)
    stacked = jnp.concatenate([query_low, key_low, value_low], axis=1)
    in_grad = jnp.einsum("rd,re->de", normed_low, stacked, preferred_element_type=jnp.float32)
    query_bias_grad = jnp.sum(query_low.astype(jnp.float32), axis=0)
    value_bias_grad = jnp.sum(value_low.astype(jnp.float32), axis=0)
    normed_grad = jnp.einsum("re,de->rd", stacked, full_in, preferred_element_type=jnp.float32)
    input_part, gain_one_grad, shift_one_grad = norm_first_back(normed_grad)
    input_gradient = (middle_grad + input_part).reshape(seq_count, block_len, model_width)
    (
        gain_one_part,
        shift_one_part,
        in_part,
        qbias_part,
        vbias_part,
        out_part,
        obias_part,
        gain_two_part,
        shift_two_part,
        up_part,
        ubias_part,
        down_part,
        dbias_part,
    ) = (
        lax.psum_scatter(
            gain_one_grad.astype(jnp.bfloat16), "fsdp", scatter_dimension=0, tiled=True
        ).astype(jnp.float32),
        lax.psum_scatter(
            shift_one_grad.astype(jnp.bfloat16), "fsdp", scatter_dimension=0, tiled=True
        ).astype(jnp.float32),
        lax.psum_scatter(
            in_grad.astype(jnp.bfloat16), "fsdp", scatter_dimension=0, tiled=True
        ).astype(jnp.float32),
        lax.psum_scatter(
            query_bias_grad.astype(jnp.bfloat16), "fsdp", scatter_dimension=0, tiled=True
        ).astype(jnp.float32),
        lax.psum_scatter(
            value_bias_grad.astype(jnp.bfloat16), "fsdp", scatter_dimension=0, tiled=True
        ).astype(jnp.float32),
        lax.psum_scatter(
            out_grad.astype(jnp.bfloat16), "fsdp", scatter_dimension=0, tiled=True
        ).astype(jnp.float32),
        lax.psum_scatter(
            out_bias_grad.astype(jnp.bfloat16), "fsdp", scatter_dimension=0, tiled=True
        ).astype(jnp.float32),
        lax.psum_scatter(
            gain_two_grad.astype(jnp.bfloat16), "fsdp", scatter_dimension=0, tiled=True
        ).astype(jnp.float32),
        lax.psum_scatter(
            shift_two_grad.astype(jnp.bfloat16), "fsdp", scatter_dimension=0, tiled=True
        ).astype(jnp.float32),
        lax.psum_scatter(
            up_grad.astype(jnp.bfloat16), "fsdp", scatter_dimension=0, tiled=True
        ).astype(jnp.float32),
        lax.psum_scatter(
            up_bias_grad.astype(jnp.bfloat16), "fsdp", scatter_dimension=0, tiled=True
        ).astype(jnp.float32),
        lax.psum_scatter(
            down_grad.astype(jnp.bfloat16), "fsdp", scatter_dimension=0, tiled=True
        ).astype(jnp.float32),
        lax.psum_scatter(
            down_bias_grad.astype(jnp.bfloat16), "fsdp", scatter_dimension=0, tiled=True
        ).astype(jnp.float32),
    )
    (
        gain_one_sum,
        shift_one_sum,
        in_sum,
        qbias_sum,
        vbias_sum,
        out_sum,
        obias_sum,
        gain_two_sum,
        shift_two_sum,
        up_sum,
        ubias_sum,
        down_sum,
        dbias_sum,
    ) = lax.psum(
        (
            gain_one_part,
            shift_one_part,
            in_part,
            qbias_part,
            vbias_part,
            out_part,
            obias_part,
            gain_two_part,
            shift_two_part,
            up_part,
            ubias_part,
            down_part,
            dbias_part,
        ),
        ("dp", "ctx"),
    )
    return (
        outputs,
        input_gradient,
        gain_one_sum,
        shift_one_sum,
        in_sum,
        qbias_sum,
        vbias_sum,
        out_sum,
        obias_sum,
        gain_two_sum,
        shift_two_sum,
        up_sum,
        ubias_sum,
        down_sum,
        dbias_sum,
    )


NT = (((1,), (1,)), ((), ()))
PAIR = 2 * HEAD_DIM


def attend_kernel(place_ref, q_ref, k_ref, v_ref, *refs, count, width, start):
    o_ref, log_ref, keys, values = refs[-4:]
    own_pair = pl.program_id(0)
    pair = own_pair + start
    shift = place_ref[0]
    block_len = q_ref.shape[0] // count
    lane = lax.broadcasted_iota(jnp.int32, (1, PAIR), 1)
    valid = lane + pair * PAIR < width
    first = lane < HEAD_DIM

    def rows(block):
        return pl.ds(pl.multiple_of((block ^ shift) * block_len, block_len), block_len)

    for block in range(count):
        here = pl.ds(block * block_len, block_len)
        keys[here, :] = jnp.where(valid, k_ref[rows(block), :], 0)
        values[here, :] = jnp.where(valid, v_ref[rows(block), :], 0)
    diagonal = lax.broadcasted_iota(jnp.int32, (block_len, block_len), 0) >= (
        lax.broadcasted_iota(jnp.int32, (block_len, block_len), 1)
    )
    for block in range(count):
        seen = (block + 1) * block_len
        before = block * block_len
        queries = q_ref[rows(block), :] * jnp.bfloat16(HEAD_DIM**-0.5)
        parts = []
        logs = log_ref[rows(block), :]
        for half in range(2):
            pick = jnp.logical_and(first if half == 0 else jnp.logical_not(first), valid)
            scores = lax.dot_general(
                jnp.where(pick, queries, 0),
                keys[pl.ds(0, seen), :],
                NT,
                preferred_element_type=jnp.float32,
            )
            last = jnp.where(diagonal, scores[:, before:], -1e30)
            scores = last if block == 0 else jnp.concatenate([scores[:, :before], last], axis=1)
            top = jnp.max(scores, axis=1, keepdims=True)
            weights = jnp.exp(scores - top)
            total = jnp.sum(weights, axis=1, keepdims=True)
            added = jnp.dot(
                weights.astype(jnp.bfloat16),
                values[pl.ds(0, seen), :],
                preferred_element_type=jnp.float32,
            )
            parts.append(added / total)
            logs = jnp.where(lane == 2 * own_pair + half, top + jnp.log(total), logs)
        o_ref[rows(block), :] = jnp.where(first, parts[0], parts[1]).astype(jnp.bfloat16)
        log_ref[rows(block), :] = logs


def attend_back_kernel(
    place_ref,
    q_ref,
    k_ref,
    v_ref,
    g_ref,
    o_ref,
    log_ref,
    *refs,
    count,
    width,
    start,
):
    dq_ref, dk_ref, dv_ref, queries, grads, keys, values = refs[-11:-4]
    keys_turned, logs, deltas, turned = refs[-4:]
    pair = pl.program_id(0) + start
    shift = place_ref[0]
    length = q_ref.shape[0]
    block_len = length // count
    lane = lax.broadcasted_iota(jnp.int32, (1, PAIR), 1)
    valid = lane + pair * PAIR < width
    first = lane < HEAD_DIM
    picks = (jnp.logical_and(first, valid), jnp.logical_and(jnp.logical_not(first), valid))
    half_of = (lax.broadcasted_iota(jnp.int32, (8, PAIR), 1) // HEAD_DIM) == (
        lax.broadcasted_iota(jnp.int32, (8, PAIR), 0)
    )
    ones_of = jnp.where(half_of, 1.0, 0.0)

    def rows(block):
        return pl.ds(pl.multiple_of((block ^ shift) * block_len, block_len), block_len)

    for block in range(count):
        here = pl.ds(block * block_len, block_len)
        key_block = jnp.where(valid, k_ref[rows(block), :], 0)
        keys[here, :] = key_block
        keys_turned[:, here] = key_block.astype(jnp.float32).T.astype(jnp.bfloat16)
        values[here, :] = jnp.where(valid, v_ref[rows(block), :], 0)
        query_block = q_ref[rows(block), :] * jnp.bfloat16(HEAD_DIM**-0.5)
        grad_block = jnp.where(valid, g_ref[rows(block), :], 0)
        for half in range(2):
            queries[half, here, :] = jnp.where(picks[half], query_block, 0)
            grads[half, here, :] = jnp.where(picks[half], grad_block, 0)
        mixed = grad_block.astype(jnp.float32) * jnp.where(
            valid, o_ref[rows(block), :], 0
        ).astype(jnp.float32)
        deltas[:, here] = lax.dot_general(
            ones_of,
            mixed,
            NT,
            preferred_element_type=jnp.float32,
            precision=lax.Precision.HIGHEST,
        )
        logs[:, here] = log_ref[
            0, :, pl.ds(pl.multiple_of((block ^ shift) * block_len, block_len), block_len)
        ]
    diagonal = lax.broadcasted_iota(jnp.int32, (block_len, block_len), 0) <= (
        lax.broadcasted_iota(jnp.int32, (block_len, block_len), 1)
    )
    for block in range(count):
        here = pl.ds(block * block_len, block_len)
        after = pl.ds(block * block_len, length - block * block_len)
        key_total = jnp.zeros((block_len, PAIR), jnp.float32)
        value_total = jnp.zeros((block_len, PAIR), jnp.float32)
        for half in range(2):
            scores = lax.dot_general(
                keys[here, :], queries[half, after, :], NT, preferred_element_type=jnp.float32
            )
            shifted = scores - logs[half : half + 1, after]
            own = jnp.where(diagonal, shifted[:, :block_len], -1e30)
            if block < count - 1:
                own = jnp.concatenate([own, shifted[:, block_len:]], axis=1)
            weights = jnp.exp(own)
            pressure = lax.dot_general(
                values[here, :], grads[half, after, :], NT, preferred_element_type=jnp.float32
            )
            score_low = (weights * (pressure - deltas[half : half + 1, after])).astype(
                jnp.bfloat16
            )
            value_total += jnp.dot(
                weights.astype(jnp.bfloat16),
                grads[half, after, :],
                preferred_element_type=jnp.float32,
            )
            key_total += jnp.dot(
                score_low, queries[half, after, :], preferred_element_type=jnp.float32
            )
            part = pl.ds(half * HEAD_DIM, HEAD_DIM)
            term = jnp.dot(
                keys_turned[part, here], score_low, preferred_element_type=jnp.float32
            )
            if block == 0:
                turned[part, after] = term
            else:
                turned[part, after] += term
        dk_ref[rows(block), :] = key_total.astype(jnp.bfloat16)
        dv_ref[rows(block), :] = value_total.astype(jnp.bfloat16)
    for block in range(count):
        here = pl.ds(block * block_len, block_len)
        dq_ref[rows(block), :] = (turned[:, here].T * HEAD_DIM**-0.5).astype(jnp.bfloat16)


def attend(place, queries, key_rows, value_rows, count, start, pairs, before):
    length, width = queries.shape
    heads_block = pl.BlockSpec((length, PAIR), lambda pair, place_ref: (0, pair + start))
    return pl.pallas_call(
        functools.partial(attend_kernel, count=count, width=width, start=start),
        grid_spec=pltpu.PrefetchScalarGridSpec(
            num_scalar_prefetch=1,
            grid=(pairs,),
            in_specs=[heads_block] * 3 + [pl.BlockSpec(memory_space=pl.ANY)] * len(before),
            out_specs=[
                heads_block,
                pl.BlockSpec((length, 128), lambda pair, place_ref: (0, 0)),
            ],
            scratch_shapes=[pltpu.VMEM((length, PAIR), jnp.bfloat16)] * 2,
        ),
        out_shape=[
            jax.ShapeDtypeStruct((length, width), jnp.bfloat16),
            jax.ShapeDtypeStruct((length, 128), jnp.float32),
        ],
        input_output_aliases={4 + at: at for at in range(len(before))},
        compiler_params=pltpu.CompilerParams(vmem_limit_bytes=48 * 2**20),
        cost_estimate=pl.CostEstimate(
            flops=4 * length * length * PAIR * pairs * 4,
            bytes_accessed=8 * length * PAIR * pairs,
            transcendentals=length * length * pairs,
        ),
        name="attend",
    )(place, queries, key_rows, value_rows, *before)


def attend_back(
    place, queries, key_rows, value_rows, grads, attended, logs, count, start, pairs, before
):
    length, width = queries.shape
    heads_block = pl.BlockSpec((length, PAIR), lambda pair, place_ref: (0, pair + start))
    low_rows = pltpu.VMEM((length, PAIR), jnp.bfloat16)
    low_pair = pltpu.VMEM((2, length, PAIR), jnp.bfloat16)
    return pl.pallas_call(
        functools.partial(attend_back_kernel, count=count, width=width, start=start),
        grid_spec=pltpu.PrefetchScalarGridSpec(
            num_scalar_prefetch=1,
            grid=(pairs,),
            in_specs=[heads_block] * 5
            + [pl.BlockSpec((1, 2, length), lambda pair, place_ref: (pair, 0, 0))]
            + [pl.BlockSpec(memory_space=pl.ANY)] * len(before),
            out_specs=[heads_block] * 3,
            scratch_shapes=[
                low_pair,
                low_pair,
                low_rows,
                low_rows,
                pltpu.VMEM((PAIR, length), jnp.bfloat16),
                pltpu.VMEM((2, length), jnp.float32),
                pltpu.VMEM((8, length), jnp.float32),
                pltpu.VMEM((PAIR, length), jnp.float32),
            ],
        ),
        out_shape=[jax.ShapeDtypeStruct((length, width), jnp.bfloat16)] * 3,
        input_output_aliases={7 + at: at for at in range(len(before))},
        compiler_params=pltpu.CompilerParams(vmem_limit_bytes=48 * 2**20),
        cost_estimate=pl.CostEstimate(
            flops=10 * length * length * PAIR * pairs * 3,
            bytes_accessed=16 * length * PAIR * pairs,
            transcendentals=length * length * pairs,
        ),
        name="attend_back",
    )(place, queries, key_rows, value_rows, grads, attended, logs, *before)


def settle_kernel(place_ref, *refs):
    pieces, out_ref = refs[:-1], refs[-1]
    for at, piece in enumerate(pieces):
        out_ref[place_ref[at]] = piece[...].astype(out_ref.dtype)


def settle(places, pieces, dtype):
    return pl.pallas_call(
        settle_kernel,
        in_specs=[pl.BlockSpec(memory_space=pltpu.SMEM)]
        + [pl.BlockSpec(memory_space=pltpu.VMEM)] * len(pieces),
        out_specs=pl.BlockSpec(memory_space=pltpu.VMEM),
        out_shape=jax.ShapeDtypeStruct((len(pieces),) + pieces[0].shape, dtype),
        compiler_params=pltpu.CompilerParams(vmem_limit_bytes=48 * 2**20),
        name="settle",
    )(places, *pieces)


def plane_partner(device, kind):
    core = device & 1
    if kind == "core":
        return device ^ 1
    if kind == "far":
        return device ^ (3 if core else 5)
    if kind == "near":
        return device ^ (2 if core else 4)
    return device ^ (4 if core else 2)


def plane_swap(values, kind):
    return lax.ppermute(
        values, ("dp", "ctx"), [(device, plane_partner(device, kind)) for device in range(8)]
    )


def ctx_swap(values, bits):
    return lax.ppermute(values, "ctx", [(device, device ^ bits) for device in range(4)])


def low_sum(*terms):
    return sum(term.astype(jnp.float32) for term in terms).astype(jnp.bfloat16)


def reduce_core(pieces):
    return plane_swap(pieces[2], "core"), plane_swap(pieces[3], "core")


def scatter_rows(values):
    return lax.psum_scatter(values, "fsdp", scatter_dimension=0, tiled=True)


def chosen(index, options):
    result = options[-1]
    for at in range(len(options) - 2, -1, -1):
        result = jnp.where(index == at, options[at], result)
    return result


def gather_vector(values, z):
    around = [values] + [
        lax.ppermute(values, "fsdp", [(device, (device + step) % 4) for device in range(4)])
        for step in range(1, 4)
    ]
    return jnp.stack([chosen((z - at) % 4, around) for at in range(4)])


def reduce_vector(values, z):
    rows = [values[at] for at in range(4)]
    total = chosen(z, rows)
    for step in range(1, 4):
        total = total + lax.ppermute(
            chosen((z + step) % 4, rows),
            "fsdp",
            [(device, (device + step) % 4) for device in range(4)],
        )
    for bits in (1, 2, 4):
        total = total + lax.ppermute(
            total, ("dp", "ctx"), [(device, device ^ bits) for device in range(8)]
        )
    return total


def product(left, right, dims):
    return lax.dot_general(left, right, ((dims[:1], dims[1:]), ((), ())),
                           preferred_element_type=jnp.float32)


def gelu_pair(values):
    inner = 0.7978845608028654
    cubic = inner * 0.044715
    squared = values * values
    curve = jnp.tanh(values * (inner + cubic * squared))
    half = 0.5 * values
    active = half + half * curve
    slope = 0.5 + 0.5 * curve + half * (1.0 - curve * curve) * (inner + 3.0 * cubic * squared)
    return active, slope


def block_flops(rows, width, count):
    return pl.CostEstimate(
        flops=2 * rows * width * width * count,
        bytes_accessed=2 * width * width * count + 4 * rows * width * count,
        transcendentals=0,
    )


def unit_of(values):
    centred = values - jnp.mean(values, axis=-1, keepdims=True)
    scale = lax.rsqrt(jnp.mean(centred * centred, axis=-1, keepdims=True) + epsilon)
    return centred * scale, scale


def fold(values):
    rows, width = values.shape
    return jnp.sum(values.reshape(rows // 8, 8, width), axis=0)


def front_kernel(places_ref, vectors_ref, *refs):
    slots, pieces = refs[:4], refs[4:20]
    x_ref, h_ref, q_ref, k_ref, v_ref, all_ref, weights, arrived, left = refs[20:]
    copies = [
        pltpu.make_async_copy(piece, weights.at[places_ref[at]], arrived.at[at])
        for at, piece in enumerate(pieces)
    ]
    for copy in copies:
        copy.start()
    rows, width = x_ref.shape
    step = rows // 4
    for at, slot in enumerate(slots):
        here = pl.ds(at * step, step)
        values = slot[...].astype(jnp.float32).T
        x_ref[here, :] = values.astype(jnp.bfloat16)
        unit, _ = unit_of(values)
        h_ref[here, :] = (unit * vectors_ref[0:1, :] + vectors_ref[1:2, :]).astype(jnp.bfloat16)
    for copy in copies:
        copy.wait()
    leave = pltpu.make_async_copy(weights, all_ref, left)
    leave.start()
    for section, out_ref in enumerate((q_ref, k_ref, v_ref)):

        def multiply(at, carry, section=section, out_ref=out_ref):
            here = pl.ds(pl.multiple_of(at * step, step), step)
            matrix = weights[4 * section : 4 * section + 4].reshape(width, width)
            total = jnp.dot(h_ref[here, :], matrix, preferred_element_type=jnp.float32)
            if section != 1:
                row = 2 if section == 0 else 3
                total = total + vectors_ref[row : row + 1, :]
            out_ref[here, :] = total.astype(jnp.bfloat16)
            return carry

        lax.fori_loop(0, rows // step, multiply, 0)
    leave.wait()


def front(places, slots, vectors, pieces):
    width, step = slots[0].shape
    rows = 4 * step
    vmem = pl.BlockSpec(memory_space=pltpu.VMEM)
    hbm = pl.BlockSpec(memory_space=pl.ANY)
    shape = jax.ShapeDtypeStruct((rows, width), jnp.bfloat16)
    whole = (16,) + pieces[0].shape
    return pl.pallas_call(
        front_kernel,
        in_specs=[pl.BlockSpec(memory_space=pltpu.SMEM)] + [vmem] * 5 + [hbm] * 16,
        out_specs=[vmem] * 5 + [hbm],
        out_shape=[shape] * 5 + [jax.ShapeDtypeStruct(whole, jnp.bfloat16)],
        scratch_shapes=[
            pltpu.VMEM(whole, jnp.bfloat16),
            pltpu.SemaphoreType.DMA((16,)),
            pltpu.SemaphoreType.DMA,
        ],
        compiler_params=pltpu.CompilerParams(vmem_limit_bytes=56 * 2**20),
        cost_estimate=block_flops(rows, width, 3),
        name="front",
    )(places, vectors, *slots, *pieces)


def turn_kernel(*refs):
    slots, out_ref = refs[:-1], refs[-1]
    step = slots[0].shape[1]
    for at, slot in enumerate(slots):
        out_ref[pl.ds(at * step, step), :] = (
            slot[...].astype(jnp.float32).T.astype(jnp.bfloat16)
        )


def turn(slots):
    width, step = slots[0].shape
    return pl.pallas_call(
        turn_kernel,
        out_shape=jax.ShapeDtypeStruct((len(slots) * step, width), jnp.bfloat16),
        compiler_params=pltpu.CompilerParams(vmem_limit_bytes=48 * 2**20),
        name="turn",
    )(*slots)


def assemble_kernel(place_ref, *refs, plan):
    pieces, outs = refs[:4], refs[4:]
    for at, piece in enumerate(pieces):
        for kind, moves in enumerate(plan):

            @pl.when(place_ref[at] == kind)
            def _(piece=piece, moves=moves):
                for out, source, target, size in moves:
                    outs[out][:, target : target + size] = piece[
                        :, source : source + size
                    ].astype(jnp.float32)


def assemble(places, pieces, plan, shapes):
    vmem = pl.BlockSpec(memory_space=pltpu.VMEM)
    return pl.pallas_call(
        functools.partial(assemble_kernel, plan=plan),
        in_specs=[pl.BlockSpec(memory_space=pltpu.SMEM)] + [vmem] * 4,
        out_specs=[vmem] * len(shapes),
        out_shape=[jax.ShapeDtypeStruct(shape, jnp.float32) for shape in shapes],
        compiler_params=pltpu.CompilerParams(vmem_limit_bytes=48 * 2**20),
        name="assemble",
    )(places, *pieces)


def store_turned(step, refs, values):
    size = refs[0].shape[1]
    share = values.shape[0] // size
    for at, ref in enumerate(refs):

        @pl.when(step == at // share)
        def _(at=at, ref=ref):
            first = (at % share) * size
            ref[...] = values[first : first + size].T.astype(ref.dtype)


def fetch(step, copies):
    @pl.when(step == 0)
    def _():
        for copy in copies:
            copy.start()


def arrive(step, copy):
    @pl.when(step == 0)
    def _():
        copy.wait()


def middle_kernel(x_ref, o_ref, vectors_ref, all_ref, middle_ref, h_ref, weights, arrived):
    step = pl.program_id(0)
    width = x_ref.shape[1]
    copy = pltpu.make_async_copy(all_ref.at[pl.ds(12, 4)], weights, arrived)
    fetch(step, [copy])
    arrive(step, copy)
    middle = (
        x_ref[...].astype(jnp.float32)
        + jnp.dot(
            o_ref[...], weights[...].reshape(width, width), preferred_element_type=jnp.float32
        )
        + vectors_ref[0:1, :]
    )
    middle_ref[...] = middle
    unit, _ = unit_of(middle)
    h_ref[...] = (unit * vectors_ref[1:2, :] + vectors_ref[2:3, :]).astype(jnp.bfloat16)


def up_kernel(h_ref, biases_ref, *refs):
    sources = refs[:2]
    active_refs, slope_refs = refs[2:4], refs[4:6]
    weights, arrived = refs[6:]
    step = pl.program_id(0)
    copies = [
        pltpu.make_async_copy(source, weights.at[at], arrived.at[at])
        for at, source in enumerate(sources)
    ]
    fetch(step, copies)
    for at in range(2):
        arrive(step, copies[at])
        hidden = (
            jnp.dot(h_ref[...], weights[at], preferred_element_type=jnp.float32)
            + biases_ref[at : at + 1, :]
        )
        active, slope = gelu_pair(hidden)
        active_refs[at][...] = active.astype(jnp.bfloat16)
        slope_refs[at][...] = slope.astype(jnp.bfloat16)


def down_kernel(middle_ref, vectors_ref, *refs):
    actives, sources = refs[:4], refs[4:8]
    out_refs = refs[8:12]
    weights, arrived = refs[12:]
    step = pl.program_id(0)
    copies = [
        pltpu.make_async_copy(source, weights.at[at], arrived.at[at])
        for at, source in enumerate(sources)
    ]
    fetch(step, copies)
    total = middle_ref[...] + vectors_ref[0:1, :]
    for at in range(4):
        arrive(step, copies[at])
        total = total + jnp.dot(
            actives[at][...], weights[at], preferred_element_type=jnp.float32
        )
    store_turned(step, out_refs, total)


def norm_back(values, gain, grad):
    unit, scale = unit_of(values)
    turned = grad * gain
    inner = (
        turned
        - jnp.mean(turned, axis=-1, keepdims=True)
        - unit * jnp.mean(turned * unit, axis=-1, keepdims=True)
    )
    return scale * inner, grad * unit


def hidden_kernel(g_ref, *refs):
    slopes, sources = refs[:2], refs[2:4]
    hidden_refs, sums_ref = refs[4:6], refs[6]
    weights, arrived = refs[7:]
    step = pl.program_id(0)
    copies = [
        pltpu.make_async_copy(source, weights.at[at], arrived.at[at])
        for at, source in enumerate(sources)
    ]
    fetch(step, copies)

    @pl.when(step == 0)
    def _():
        sums_ref[...] = jnp.zeros_like(sums_ref)

    upstream = g_ref[...]
    for at in range(2):
        arrive(step, copies[at])
        hidden = lax.dot_general(
            upstream, weights[at], NT, preferred_element_type=jnp.float32
        )
        hidden = (hidden * slopes[at][...].astype(jnp.float32)).astype(jnp.bfloat16)
        hidden_refs[at][...] = hidden
        sums_ref[at] += fold(hidden.astype(jnp.float32))
    sums_ref[2] += fold(upstream.astype(jnp.float32))


def back_kernel(g_ref, middle_ref, vectors_ref, *refs):
    hiddens, sources, all_ref = refs[:4], refs[4:8], refs[8]
    grad_ref, low_ref, out_ref, sums_ref = refs[9:13]
    weights, out_weights, arrived = refs[13:]
    step = pl.program_id(0)
    width = middle_ref.shape[1]
    copies = [
        pltpu.make_async_copy(source, weights.at[at], arrived.at[at])
        for at, source in enumerate(sources)
    ] + [pltpu.make_async_copy(all_ref.at[pl.ds(12, 4)], out_weights, arrived.at[4])]
    fetch(step, copies)

    @pl.when(step == 0)
    def _():
        sums_ref[...] = jnp.zeros_like(sums_ref)

    total = jnp.zeros(middle_ref.shape, jnp.float32)
    for at in range(4):
        arrive(step, copies[at])
        total = total + lax.dot_general(
            hiddens[at][...], weights[at], NT, preferred_element_type=jnp.float32
        )
    part, gain_term = norm_back(middle_ref[...], vectors_ref[0:1, :], total)
    sums_ref[0] += fold(gain_term)
    sums_ref[1] += fold(total)
    grad = g_ref[...].astype(jnp.float32) + part
    grad_ref[...] = grad
    grad_low = grad.astype(jnp.bfloat16)
    low_ref[...] = grad_low
    sums_ref[2] += fold(grad_low.astype(jnp.float32))
    arrive(step, copies[4])
    out_ref[...] = lax.dot_general(
        grad_low,
        out_weights[...].reshape(width, width),
        NT,
        preferred_element_type=jnp.float32,
    ).astype(jnp.bfloat16)


def last_kernel(q_ref, k_ref, v_ref, x_ref, grad_ref, vectors_ref, all_ref, *refs):
    out_refs = refs[:4]
    sums_ref, weights, arrived = refs[4:]
    step = pl.program_id(0)
    width = x_ref.shape[1]
    copies = [
        pltpu.make_async_copy(
            all_ref.at[pl.ds(4 * at, 4)], weights.at[pl.ds(4 * at, 4)], arrived.at[at]
        )
        for at in range(3)
    ]
    fetch(step, copies)
    total = jnp.zeros(x_ref.shape, jnp.float32)
    for at, ref in enumerate((q_ref, k_ref, v_ref)):
        arrive(step, copies[at])
        total = total + lax.dot_general(
            ref[...],
            weights[4 * at : 4 * at + 4].reshape(width, width),
            NT,
            preferred_element_type=jnp.float32,
        )
    part, gain_term = norm_back(x_ref[...].astype(jnp.float32), vectors_ref[0:1, :], total)
    store_turned(step, out_refs, grad_ref[...] + part)

    @pl.when(step == 0)
    def _():
        sums_ref[...] = jnp.zeros_like(sums_ref)

    terms = (
        gain_term,
        total,
        q_ref[...].astype(jnp.float32),
        v_ref[...].astype(jnp.float32),
    )
    for at, term in enumerate(terms):
        sums_ref[at] += fold(term)


def by_rows(kernel, name, rows, width, tiled, whole, remote, outs, sums, scratch, sems, blocks):
    step = 512
    tile = pl.BlockSpec((step, width), lambda at: (at, 0))
    out_specs, out_shape = [], []
    for dtype in outs:
        if dtype is None:
            out_specs += [pl.BlockSpec((width, rows // 4), lambda at: (0, 0))] * 4
            out_shape += [jax.ShapeDtypeStruct((width, rows // 4), jnp.bfloat16)] * 4
        else:
            out_specs.append(tile)
            out_shape.append(jax.ShapeDtypeStruct((rows, width), dtype))
    if sums:
        out_specs.append(pl.BlockSpec((sums, 8, width), lambda at: (0, 0, 0)))
        out_shape.append(jax.ShapeDtypeStruct((sums, 8, width), jnp.float32))
    return pl.pallas_call(
        kernel,
        grid=(rows // step,),
        in_specs=[tile] * len(tiled[0])
        + [pl.BlockSpec(value.shape, lambda at: (0, 0)) for value in whole]
        + [tile] * len(tiled[1])
        + [pl.BlockSpec(memory_space=pl.ANY)] * len(remote),
        out_specs=out_specs,
        out_shape=out_shape,
        scratch_shapes=[pltpu.VMEM(shape, jnp.bfloat16) for shape in scratch]
        + [pltpu.SemaphoreType.DMA((sems,)) if sems > 1 else pltpu.SemaphoreType.DMA],
        compiler_params=pltpu.CompilerParams(vmem_limit_bytes=60 * 2**20),
        cost_estimate=block_flops(rows, width, blocks),
        name=name,
    )(*tiled[0], *whole, *tiled[1], *remote)


def per_device_exchanged(
    inputs,
    cotangent,
    first_gain,
    first_shift,
    project_in,
    query_bias,
    value_bias,
    project_out,
    output_bias,
    second_gain,
    second_shift,
    up_weight,
    up_bias,
    down_weight,
    down_bias,
):
    seq_count, block_len, width = inputs.shape
    low = jnp.bfloat16
    wide = jnp.float32
    c = lax.axis_index("ctx")
    y = lax.axis_index("dp")
    z = lax.axis_index("fsdp")
    core = c & 1
    x = c >> 1
    mine = core * 2 + jnp.where(core == 0, y, x)
    across = (1 - core) * 2 + jnp.where(core == 0, x, y)
    classes = [mine, mine ^ 1, across, across ^ 1]
    slot_of = [
        chosen(0, [sum(at * (classes[at] == kind).astype(jnp.int32) for at in range(4))])
        for kind in range(4)
    ]
    quarter = width // 4
    rows, area = seq_count * block_len, (width, width)
    pin = lax.optimization_barrier
    place = jnp.stack([c])
    places = jnp.stack([c ^ at for at in range(4)])
    class_places = jnp.stack(classes)

    late = jnp.where(core == 0, x, y) == 1
    cut = (width // 2) // 128 * 128
    share = width - cut

    def halve(*terms):
        total = sum(term.astype(wide) for term in terms)
        low_half, high_half = total[:, :share].astype(low), total[:, cut:].astype(low)
        return jnp.where(late, high_half, low_half), jnp.where(late, low_half, high_half)

    def reduce_last(shard):
        other = plane_swap(shard, "other")
        whole = jnp.concatenate(
            [jnp.where(late, other, shard)[:, :cut], jnp.where(late, shard, other)], axis=1
        )
        return [whole] + [plane_swap(whole, kind) for kind in ("near", "core", "far")]

    def spread(values):
        values = jnp.swapaxes(values, 1, 2)
        return [lax.dynamic_index_in_dim(values, c, 0, keepdims=False)] + [
            ctx_swap(lax.dynamic_index_in_dim(values, c ^ bits, 0, keepdims=False), bits)
            for bits in range(1, 4)
        ]

    def collect(pieces, dtype):
        moved = [pieces[0]] + [ctx_swap(pieces[bits], bits) for bits in range(1, 4)]
        return jnp.swapaxes(settle(places, moved, dtype), 1, 2)

    sections = [
        project_in[:, :width],
        project_in[:, width : 2 * width],
        project_in[:, 2 * width :],
        project_out,
    ]
    section = chosen(mine, sections)
    section, inputs = pin((section, inputs))
    shards = [
        lax.ppermute(section, "fsdp", [(device, (device + step) % 4) for device in range(4)])
        for step in range(1, 4)
    ]
    turned_in = jnp.swapaxes(inputs, 1, 2)
    slots_in = [
        lax.dynamic_index_in_dim(turned_in, c ^ bits, 0, keepdims=False) for bits in range(4)
    ]
    pieces_in = (
        first_gain,
        first_shift,
        query_bias,
        value_bias,
        output_bias,
        second_gain,
        second_shift,
        down_bias,
        up_bias,
    )
    slots_in[3], cotangent, up_weight, down_weight, *pieces_in = pin(
        (slots_in[3], cotangent, up_weight, down_weight, *pieces_in)
    )
    slots_in = [slots_in[0]] + [ctx_swap(slots_in[bits], bits) for bits in range(1, 4)]
    vectors = gather_vector(jnp.concatenate(pieces_in), z).astype(wide)
    slots_back = spread(cotangent)
    up_piece = jnp.concatenate(
        [
            lax.dynamic_slice_in_dim(up_weight, at * width + mine * quarter, quarter, 1)
            for at in range(4)
        ],
        axis=1,
    )
    up_piece, shards[1], shards[2] = pin((up_piece, shards[1], shards[2]))
    near_shards = [plane_swap(shard, "near") for shard in shards]
    around = (
        sections
        + shards
        + near_shards
        + [plane_swap(shard, "core") for shard in shards]
        + [plane_swap(shard, "core") for shard in near_shards]
    )
    around_places = jnp.stack(
        [kind * 4 + z for kind in range(4)]
        + [kind * 4 + (z - step) % 4 for kind in classes for step in range(1, 4)]
    )
    up_own = lax.all_gather(up_piece, "fsdp", axis=0, tiled=True)
    down_piece = lax.dynamic_slice_in_dim(down_weight, mine * quarter, quarter, 0)
    gain_first, shift_first, qbias, vbias, obias, gain_second, shift_second, dbias = (
        vectors[:, at * quarter : (at + 1) * quarter].reshape(1, width) for at in range(8)
    )
    ubias = vectors[:, 8 * quarter :].reshape(4, 4, quarter)
    ubias = jnp.concatenate(
        [
            chosen(kind, [ubias[:, at] for at in range(4)]).reshape(1, width)
            for kind in classes
        ],
        axis=0,
    )

    rows_in, normed_low, queries, key_rows, value_rows, weights = front(
        around_places,
        slots_in,
        jnp.concatenate([gain_first, shift_first, qbias, vbias], axis=0),
        around,
    )
    slots_back[0], down_piece, queries = pin((slots_back[0], down_piece, queries))
    upstream_low = turn(slots_back)
    down_own = lax.all_gather(down_piece, "fsdp", axis=0, tiled=True)
    attended, logs_one = attend(place, queries, key_rows, value_rows, seq_count, 0, 5, [])
    up_own, late_queries, attended = pin((up_own, queries, attended))
    up_near, up_core = plane_swap(up_own, "near"), plane_swap(up_own, "core")
    attended, logs_two = attend(
        place, late_queries, key_rows, value_rows, seq_count, 5, 4, [attended]
    )
    up_core, attended = pin((up_core, attended))
    logs_one, logs_two = (logs.T.reshape(64, 2, rows) for logs in (logs_one, logs_two))
    middle, normed_two_low = by_rows(
        middle_kernel,
        "middle",
        rows,
        width,
        ([rows_in, attended], []),
        [jnp.concatenate([obias, gain_second, shift_second], axis=0)],
        [weights],
        [wide, low],
        0,
        [(4,) + section.shape],
        1,
        1,
    )
    up_near, normed_two_low = pin((up_near, normed_two_low))
    up_slots = [up_own, up_near, up_core, plane_swap(up_near, "core")]
    active, slopes = [None] * 4, [None] * 4

    def up(first):
        outs = by_rows(
            up_kernel,
            "up",
            rows,
            width,
            ([normed_two_low], []),
            [jnp.concatenate([ubias[first : first + 1], ubias[first + 2 : first + 3]], axis=0)],
            [up_slots[first], up_slots[first + 2]],
            [low] * 4,
            0,
            [(2,) + area],
            2,
            2,
        )
        active[first], active[first + 2], slopes[first], slopes[first + 2] = outs

    up(0)
    up_slots[3], active[0], active[2] = pin((up_slots[3], active[0], active[2]))
    up(1)
    down_own, *active = pin((down_own, *active))
    down_near, down_core = plane_swap(down_own, "near"), plane_swap(down_own, "core")

    def turned_product(left, right):
        return product(left, right, (0, 0)).astype(low)

    down_terms = [turned_product(active[slot], upstream_low) for slot in (3, 2)]
    upstream_low, *down_terms = pin((upstream_low, *down_terms))
    down_terms += [turned_product(active[slot], upstream_low) for slot in (1, 0)]
    down_terms = down_terms[::-1]
    down_far, down_far_two = reduce_core(down_terms)
    upstream_low, *down_terms = pin((upstream_low, *down_terms))
    hidden_low = [None] * 4

    def hidden(first, upstream):
        hidden_low[first], hidden_low[first + 2], sums = by_rows(
            hidden_kernel,
            "hidden",
            rows,
            width,
            ([upstream], [slopes[first], slopes[first + 2]]),
            [],
            [down_slots[first], down_slots[first + 2]],
            [low] * 2,
            3,
            [(2,) + area],
            2,
            2,
        )
        return sums

    down_near, upstream_low = pin((down_near, upstream_low))
    down_slots = [down_own, down_near, down_core, plane_swap(down_near, "core")]
    sums_even = hidden(0, upstream_low)
    upstream_late, sums_even = pin((upstream_low, sums_even))
    sums_odd = hidden(1, upstream_late)
    hidden_sums = jnp.stack(
        [sums_even[0], sums_odd[0], sums_even[1], sums_odd[1], sums_even[2]]
    )
    down_second = low_sum(down_terms[1], down_far_two)
    down_second, down_far, *hidden_low = pin((down_second, down_far, *hidden_low))
    down_close = plane_swap(down_second, "near")
    middle_grad, middle_low, grad_low, back_sums = by_rows(
        back_kernel,
        "back",
        rows,
        width,
        ([upstream_low, middle], hidden_low),
        [gain_second],
        up_slots + [weights],
        [wide, low, low],
        3,
        [(4,) + area, (4,) + section.shape],
        5,
        5,
    )
    normed_two_low, middle_low = pin((normed_two_low, middle_low))
    down_keep, down_send = halve(down_terms[0], down_far, down_close)
    down_keep, down_send, normed_two_low = pin((down_keep, down_send, normed_two_low))
    down_other = plane_swap(down_send, "other")
    up_terms = [turned_product(normed_two_low, hidden_low[slot]) for slot in (3, 2)]
    normed_two_low, *up_terms = pin((normed_two_low, *up_terms))
    up_terms += [turned_product(normed_two_low, hidden_low[slot]) for slot in (1, 0)]
    up_terms = up_terms[::-1]
    up_far, up_far_two = reduce_core(up_terms)
    out_term = turned_product(attended, middle_low)
    up_second = low_sum(up_terms[1], up_far_two)
    down_half = low_sum(down_keep, down_other)
    grad_low, up_second, up_far, out_term, down_half, *up_terms = pin(
        (grad_low, up_second, up_far, out_term, down_half, *up_terms)
    )
    down_shard = scatter_rows(down_half)
    up_close = plane_swap(up_second, "near")
    in_grads = attend_back(
        place, late_queries, key_rows, value_rows, grad_low, attended, logs_one, seq_count, 0, 5, []
    )
    up_keep, up_send = halve(up_terms[0], up_far, up_close)
    up_keep, up_send, *in_grads = pin((up_keep, up_send, *in_grads))
    up_other = plane_swap(up_send, "other")
    in_grads = attend_back(
        place,
        late_queries,
        key_rows,
        value_rows,
        grad_low,
        attended,
        logs_two,
        seq_count,
        5,
        4,
        in_grads,
    )
    up_half = low_sum(up_keep, up_other)
    up_half, down_shard, *in_grads = pin((up_half, down_shard, *in_grads))
    up_shard = scatter_rows(up_half)
    down_parts = reduce_last(down_shard)
    in_terms = [turned_product(normed_low, grad) for grad in in_grads]
    section_grads = in_terms + [out_term]
    sections_mine = [chosen(kind, section_grads) for kind in classes]
    far, far_two = reduce_core(sections_mine)
    second = low_sum(sections_mine[1], far_two)
    second, far, middle, *in_grads = pin((second, far, middle, *in_grads))
    close = plane_swap(second, "near")
    query_low, key_low, value_low = in_grads
    result_slots = by_rows(
        down_kernel,
        "down",
        rows,
        width,
        ([middle], active),
        [dbias],
        down_slots,
        [None],
        0,
        [(4,) + area],
        4,
        4,
    )
    keep, send = halve(sections_mine[0], far, close)
    keep, send, query_low, *result_slots = pin((keep, send, query_low, *result_slots))
    outputs = collect(result_slots, low)
    other = plane_swap(send, "other")
    *input_slots, last_sums = by_rows(
        last_kernel,
        "last",
        rows,
        width,
        ([query_low, key_low, value_low, rows_in, middle_grad], []),
        [gain_first],
        [weights],
        [None],
        4,
        [(12,) + section.shape],
        3,
        3,
    )
    half = low_sum(keep, other)
    half, up_shard, *input_slots = pin((half, up_shard, *input_slots))
    shard = scatter_rows(half)
    input_gradient = collect(input_slots, wide)
    up_parts = reduce_last(up_shard)

    back_sums = jnp.concatenate([hidden_sums, back_sums], axis=0)
    back_sums = jnp.sum(back_sums, axis=1)
    last_sums = jnp.sum(last_sums, axis=1)
    hidden_sums = [back_sums[slot].reshape(4, quarter) for slot in range(4)]
    hidden_sums = jnp.stack(
        [chosen(slot_of[kind], hidden_sums) for kind in range(4)], axis=1
    ).reshape(4, 4 * quarter)
    totals = reduce_vector(
        jnp.concatenate(
            [back_sums[at].reshape(4, quarter) for at in range(4, 8)]
            + [last_sums[at].reshape(4, quarter) for at in range(4)]
            + [hidden_sums],
            axis=1,
        ),
        z,
    )
    (up_sum,) = assemble(
        class_places,
        up_parts,
        [
            [(0, at * quarter, at * width + kind * quarter, quarter) for at in range(4)]
            for kind in range(4)
        ],
        [up_weight.shape],
    )
    down_sum = settle(class_places, down_parts, wide).reshape(down_weight.shape)
    shard, outputs, input_gradient, totals, up_sum, down_sum = pin(
        (shard, outputs, input_gradient, totals, up_sum, down_sum)
    )
    in_sum, out_sum = assemble(
        class_places,
        reduce_last(shard),
        [[(0, 0, kind * width, width)] for kind in range(3)] + [[(1, 0, 0, width)]],
        [project_in.shape, project_out.shape],
    )
    (
        dbias_sum,
        gain_two_sum,
        shift_two_sum,
        obias_sum,
        gain_one_sum,
        shift_one_sum,
        qbias_sum,
        vbias_sum,
    ) = (totals[at * quarter : (at + 1) * quarter] for at in range(8))
    ubias_sum = totals[8 * quarter :]
    return (
        outputs,
        input_gradient,
        gain_one_sum,
        shift_one_sum,
        in_sum,
        qbias_sum,
        vbias_sum,
        out_sum,
        obias_sum,
        gain_two_sum,
        shift_two_sum,
        up_sum,
        ubias_sum,
        down_sum,
        dbias_sum,
    )


def solution(mesh):
    sizes = dict(mesh.shape)
    exchanged = sizes["dp"] == 2 and sizes["fsdp"] == 4 and sizes["ctx"] == 4
    per_device = per_device_exchanged if exchanged else per_device_gathered
    return jax.shard_map(
        per_device,
        mesh=mesh,
        in_specs=(
            P(("dp", "fsdp"), "ctx", None),
            P(("dp", "fsdp"), "ctx", None),
            P("fsdp"),
            P("fsdp"),
            P("fsdp", None),
            P("fsdp"),
            P("fsdp"),
            P("fsdp", None),
            P("fsdp"),
            P("fsdp"),
            P("fsdp"),
            P("fsdp", None),
            P("fsdp"),
            P("fsdp", None),
            P("fsdp"),
        ),
        out_specs=(
            P(("dp", "fsdp"), "ctx", None),
            P(("dp", "fsdp"), "ctx", None),
            P("fsdp"),
            P("fsdp"),
            P("fsdp", None),
            P("fsdp"),
            P("fsdp"),
            P("fsdp", None),
            P("fsdp"),
            P("fsdp"),
            P("fsdp"),
            P("fsdp", None),
            P("fsdp"),
            P("fsdp", None),
            P("fsdp"),
        ),
        check_vma=False,
    )
```

```python
import functools

import jax
import jax.numpy as jnp
from jax import lax
from jax.experimental import pallas as pl
from jax.experimental.pallas import tpu as pltpu
from jax.sharding import PartitionSpec as P

HEADS = 17
HEAD_DIM = 64


epsilon = 1e-05


def layer_norm(values, gain, shift):
    centred = values - jnp.mean(values, axis=-1, keepdims=True)
    spread = jnp.mean(centred * centred, axis=-1, keepdims=True)
    return centred * lax.rsqrt(spread + epsilon) * gain + shift


def gelu_tanh(values):
    return jax.nn.gelu(values, approximate=True)


def score_grads(
    query_heads, key_heads, value_heads, grad_heads, log_total, row_delta, query_at, key_at
):
    score_scale = HEAD_DIM ** (-0.5)
    scores = (
        jnp.einsum("sqhd,skhd->shqk", query_heads, key_heads, preferred_element_type=jnp.float32)
        * score_scale
    )
    visible = query_at[:, None] >= key_at[None, :]
    shifted = jnp.where(visible, scores - log_total[..., None], -1e30)
    weights = jnp.where(visible, jnp.exp(shifted), 0.0)
    pressure = jnp.einsum(
        "sqhd,skhd->shqk", grad_heads, value_heads, preferred_element_type=jnp.float32
    )
    score_low = (weights * (pressure - row_delta[..., None])).astype(jnp.bfloat16)
    return (weights.astype(jnp.bfloat16), score_low)


def per_device_gathered(
    inputs,
    cotangent,
    first_gain,
    first_shift,
    project_in,
    query_bias,
    value_bias,
    project_out,
    output_bias,
    second_gain,
    second_shift,
    up_weight,
    up_bias,
    down_weight,
    down_bias,
):
    seq_count, block_len, model_width = inputs.shape
    flat_rows = seq_count * block_len
    cycle_size = lax.axis_size("ctx")
    my_block = lax.axis_index("ctx")
    score_scale = HEAD_DIM ** (-0.5)
    head_shape = (seq_count, block_len, HEADS, HEAD_DIM)
    offsets = jnp.arange(block_len, dtype=jnp.int32)
    query_at = my_block * block_len + offsets
    gain_first, shift_first, full_in, qbias_full, vbias_full, full_out, obias_full = (
        lax.all_gather(first_gain, "fsdp", axis=0, tiled=True),
        lax.all_gather(first_shift, "fsdp", axis=0, tiled=True),
        lax.all_gather(project_in, "fsdp", axis=0, tiled=True),
        lax.all_gather(query_bias, "fsdp", axis=0, tiled=True),
        lax.all_gather(value_bias, "fsdp", axis=0, tiled=True),
        lax.all_gather(project_out, "fsdp", axis=0, tiled=True),
        lax.all_gather(output_bias, "fsdp", axis=0, tiled=True),
    )
    rows_in = inputs.astype(jnp.float32).reshape(flat_rows, model_width)
    normed, norm_first_back = jax.vjp(
        layer_norm, rows_in, gain_first.astype(jnp.float32), shift_first.astype(jnp.float32)
    )
    normed_low = normed.astype(jnp.bfloat16)
    projected = jnp.dot(normed_low, full_in, preferred_element_type=jnp.float32)
    queries = (projected[:, :model_width] + qbias_full).astype(jnp.bfloat16)
    key_rows = projected[:, model_width : 2 * model_width].astype(jnp.bfloat16)
    value_rows = (projected[:, 2 * model_width :] + vbias_full).astype(jnp.bfloat16)
    query_heads = queries.reshape(head_shape)
    running_top = jnp.full((seq_count, HEADS, block_len), -1e30, jnp.float32)
    accumulated = jnp.zeros(head_shape, jnp.float32)
    piece_keys = lax.all_gather(
        key_rows.reshape(seq_count, block_len, model_width), "ctx", axis=1, tiled=True
    )
    piece_values = lax.all_gather(
        value_rows.reshape(seq_count, block_len, model_width), "ctx", axis=1, tiled=True
    )
    piece_len = piece_keys.shape[1]
    key_heads = piece_keys.reshape(seq_count, piece_len, HEADS, HEAD_DIM)
    value_heads = piece_values.reshape(seq_count, piece_len, HEADS, HEAD_DIM)
    scores = (
        jnp.einsum("sqhd,skhd->shqk", query_heads, key_heads, preferred_element_type=jnp.float32)
        * score_scale
    )
    key_at = jnp.arange(piece_len, dtype=jnp.int32)
    visible = query_at[:, None] >= key_at[None, :]
    masked = jnp.where(visible, scores, -1e30)
    new_top = jnp.maximum(running_top, jnp.max(masked, axis=-1))
    factor = jnp.exp(running_top - new_top)
    weights = jnp.where(visible, jnp.exp(masked - new_top[..., None]), 0.0)
    row_total = jnp.sum(weights, axis=-1)
    added = jnp.einsum(
        "shqk,skhd->sqhd",
        weights.astype(jnp.bfloat16),
        value_heads,
        preferred_element_type=jnp.float32,
    )
    accumulated = accumulated * jnp.swapaxes(factor, 1, 2)[..., None] + added
    running_top, row_total, accumulated = (new_top, row_total, accumulated)
    attended = accumulated / jnp.swapaxes(row_total, 1, 2)[..., None]
    log_total = running_top + jnp.log(row_total)
    attended_low = attended.reshape(flat_rows, model_width).astype(jnp.bfloat16)
    middle = (
        rows_in + jnp.dot(attended_low, full_out, preferred_element_type=jnp.float32) + obias_full
    )
    gain_second, shift_second, full_up, ubias_full, full_down, dbias_full = (
        lax.all_gather(second_gain, "fsdp", axis=0, tiled=True),
        lax.all_gather(second_shift, "fsdp", axis=0, tiled=True),
        lax.all_gather(up_weight, "fsdp", axis=0, tiled=True),
        lax.all_gather(up_bias, "fsdp", axis=0, tiled=True),
        lax.all_gather(down_weight, "fsdp", axis=0, tiled=True),
        lax.all_gather(down_bias, "fsdp", axis=0, tiled=True),
    )
    normed_two, norm_second_back = jax.vjp(
        layer_norm, middle, gain_second.astype(jnp.float32), shift_second.astype(jnp.float32)
    )
    normed_two_low = normed_two.astype(jnp.bfloat16)
    hidden = jnp.dot(normed_two_low, full_up, preferred_element_type=jnp.float32) + ubias_full
    active, gelu_back = jax.vjp(gelu_tanh, hidden)
    active_low = active.astype(jnp.bfloat16)
    result = (
        middle + jnp.dot(active_low, full_down, preferred_element_type=jnp.float32) + dbias_full
    )
    outputs = result.astype(jnp.bfloat16).reshape(seq_count, block_len, model_width)
    upstream = cotangent.astype(jnp.float32).reshape(flat_rows, model_width)
    upstream_low = upstream.astype(jnp.bfloat16)
    down_grad = jnp.einsum(
        "rf,rd->fd", active_low, upstream_low, preferred_element_type=jnp.float32
    )
    down_bias_grad = jnp.sum(upstream_low.astype(jnp.float32), axis=0)
    active_grad = jnp.einsum(
        "rd,fd->rf", upstream_low, full_down, preferred_element_type=jnp.float32
    )
    (hidden_grad,) = gelu_back(active_grad)
    hidden_low = hidden_grad.astype(jnp.bfloat16)
    up_grad = jnp.einsum(
        "rd,rf->df", normed_two_low, hidden_low, preferred_element_type=jnp.float32
    )
    up_bias_grad = jnp.sum(hidden_low.astype(jnp.float32), axis=0)
    normed_two_grad = jnp.einsum(
        "rf,df->rd", hidden_low, full_up, preferred_element_type=jnp.float32
    )
    middle_part, gain_two_grad, shift_two_grad = norm_second_back(normed_two_grad)
    middle_grad = upstream + middle_part
    middle_low = middle_grad.astype(jnp.bfloat16)
    out_grad = jnp.einsum("rd,re->de", attended_low, middle_low, preferred_element_type=jnp.float32)
    out_bias_grad = jnp.sum(middle_low.astype(jnp.float32), axis=0)
    attended_grad = jnp.einsum(
        "re,de->rd", middle_low, full_out, preferred_element_type=jnp.float32
    )
    grad_low = attended_grad.astype(jnp.bfloat16).reshape(head_shape)
    row_delta = jnp.swapaxes(jnp.sum(grad_low.astype(jnp.float32) * attended, axis=-1), 1, 2)
    gathered_keys, gathered_values = (
        lax.all_gather(
            key_rows.reshape(1, seq_count, block_len, model_width), "ctx", axis=0, tiled=True
        ),
        lax.all_gather(
            value_rows.reshape(1, seq_count, block_len, model_width), "ctx", axis=0, tiled=True
        ),
    )
    block_ids = jnp.arange(cycle_size, dtype=jnp.int32)

    def key_step(carry, inputs_here):
        key_block, value_block, block_index = inputs_here
        key_heads = key_block.reshape(head_shape)
        value_heads = value_block.reshape(head_shape)
        weights_low, score_low = score_grads(
            query_heads,
            key_heads,
            value_heads,
            grad_low,
            log_total,
            row_delta,
            query_at,
            block_index * block_len + offsets,
        )
        carry = (
            carry
            + jnp.einsum(
                "shqk,skhd->sqhd", score_low, key_heads, preferred_element_type=jnp.float32
            )
            * score_scale
        )
        key_term = (
            jnp.einsum(
                "shqk,sqhd->skhd", score_low, query_heads, preferred_element_type=jnp.float32
            )
            * score_scale
        )
        value_term = jnp.einsum(
            "shqk,sqhd->skhd", weights_low, grad_low, preferred_element_type=jnp.float32
        )
        return (
            carry,
            (
                key_term.reshape(seq_count, block_len, model_width),
                value_term.reshape(seq_count, block_len, model_width),
            ),
        )

    query_grad, (key_terms, value_terms) = lax.scan(
        key_step, jnp.zeros(head_shape, jnp.float32), (gathered_keys, gathered_values, block_ids)
    )
    key_sum, value_sum = (
        lax.psum_scatter(
            key_terms.astype(jnp.bfloat16), "ctx", scatter_dimension=0, tiled=True
        ).astype(jnp.float32),
        lax.psum_scatter(
            value_terms.astype(jnp.bfloat16), "ctx", scatter_dimension=0, tiled=True
        ).astype(jnp.float32),
    )
    key_grad = key_sum.reshape(flat_rows, model_width)
    value_grad = value_sum.reshape(flat_rows, model_width)
    query_low = query_grad.reshape(flat_rows, model_width).astype(jnp.bfloat16)
    key_low = key_grad.astype(jnp.bfloat16)
    value_low = value_grad.astype(jnp.bfloat16)
    stacked = jnp.concatenate([query_low, key_low, value_low], axis=1)
    in_grad = jnp.einsum("rd,re->de", normed_low, stacked, preferred_element_type=jnp.float32)
    query_bias_grad = jnp.sum(query_low.astype(jnp.float32), axis=0)
    value_bias_grad = jnp.sum(value_low.astype(jnp.float32), axis=0)
    normed_grad = jnp.einsum("re,de->rd", stacked, full_in, preferred_element_type=jnp.float32)
    input_part, gain_one_grad, shift_one_grad = norm_first_back(normed_grad)
    input_gradient = (middle_grad + input_part).reshape(seq_count, block_len, model_width)
    (
        gain_one_part,
        shift_one_part,
        in_part,
        qbias_part,
        vbias_part,
        out_part,
        obias_part,
        gain_two_part,
        shift_two_part,
        up_part,
        ubias_part,
        down_part,
        dbias_part,
    ) = (
        lax.psum_scatter(
            gain_one_grad.astype(jnp.bfloat16), "fsdp", scatter_dimension=0, tiled=True
        ).astype(jnp.float32),
        lax.psum_scatter(
            shift_one_grad.astype(jnp.bfloat16), "fsdp", scatter_dimension=0, tiled=True
        ).astype(jnp.float32),
        lax.psum_scatter(
            in_grad.astype(jnp.bfloat16), "fsdp", scatter_dimension=0, tiled=True
        ).astype(jnp.float32),
        lax.psum_scatter(
            query_bias_grad.astype(jnp.bfloat16), "fsdp", scatter_dimension=0, tiled=True
        ).astype(jnp.float32),
        lax.psum_scatter(
            value_bias_grad.astype(jnp.bfloat16), "fsdp", scatter_dimension=0, tiled=True
        ).astype(jnp.float32),
        lax.psum_scatter(
            out_grad.astype(jnp.bfloat16), "fsdp", scatter_dimension=0, tiled=True
        ).astype(jnp.float32),
        lax.psum_scatter(
            out_bias_grad.astype(jnp.bfloat16), "fsdp", scatter_dimension=0, tiled=True
        ).astype(jnp.float32),
        lax.psum_scatter(
            gain_two_grad.astype(jnp.bfloat16), "fsdp", scatter_dimension=0, tiled=True
        ).astype(jnp.float32),
        lax.psum_scatter(
            shift_two_grad.astype(jnp.bfloat16), "fsdp", scatter_dimension=0, tiled=True
        ).astype(jnp.float32),
        lax.psum_scatter(
            up_grad.astype(jnp.bfloat16), "fsdp", scatter_dimension=0, tiled=True
        ).astype(jnp.float32),
        lax.psum_scatter(
            up_bias_grad.astype(jnp.bfloat16), "fsdp", scatter_dimension=0, tiled=True
        ).astype(jnp.float32),
        lax.psum_scatter(
            down_grad.astype(jnp.bfloat16), "fsdp", scatter_dimension=0, tiled=True
        ).astype(jnp.float32),
        lax.psum_scatter(
            down_bias_grad.astype(jnp.bfloat16), "fsdp", scatter_dimension=0, tiled=True
        ).astype(jnp.float32),
    )
    (
        gain_one_sum,
        shift_one_sum,
        in_sum,
        qbias_sum,
        vbias_sum,
        out_sum,
        obias_sum,
        gain_two_sum,
        shift_two_sum,
        up_sum,
        ubias_sum,
        down_sum,
        dbias_sum,
    ) = lax.psum(
        (
            gain_one_part,
            shift_one_part,
            in_part,
            qbias_part,
            vbias_part,
            out_part,
            obias_part,
            gain_two_part,
            shift_two_part,
            up_part,
            ubias_part,
            down_part,
            dbias_part,
        ),
        ("dp", "ctx"),
    )
    return (
        outputs,
        input_gradient,
        gain_one_sum,
        shift_one_sum,
        in_sum,
        qbias_sum,
        vbias_sum,
        out_sum,
        obias_sum,
        gain_two_sum,
        shift_two_sum,
        up_sum,
        ubias_sum,
        down_sum,
        dbias_sum,
    )


NT = (((1,), (1,)), ((), ()))
PAIR = 2 * HEAD_DIM


def attend_kernel(place_ref, q_ref, k_ref, v_ref, *refs, count, width, start):
    o_ref, log_ref, keys, values = refs[-4:]
    own_pair = pl.program_id(0)
    pair = own_pair + start
    shift = place_ref[0]
    block_len = q_ref.shape[0] // count
    lane = lax.broadcasted_iota(jnp.int32, (1, PAIR), 1)
    valid = lane + pair * PAIR < width
    first = lane < HEAD_DIM

    def rows(block):
        return pl.ds(pl.multiple_of((block ^ shift) * block_len, block_len), block_len)

    for block in range(count):
        here = pl.ds(block * block_len, block_len)
        keys[here, :] = jnp.where(valid, k_ref[rows(block), :], 0)
        values[here, :] = jnp.where(valid, v_ref[rows(block), :], 0)
    diagonal = lax.broadcasted_iota(jnp.int32, (block_len, block_len), 0) >= (
        lax.broadcasted_iota(jnp.int32, (block_len, block_len), 1)
    )
    for block in range(count):
        seen = (block + 1) * block_len
        before = block * block_len
        queries = q_ref[rows(block), :] * jnp.bfloat16(HEAD_DIM**-0.5)
        parts = []
        logs = log_ref[rows(block), :]
        for half in range(2):
            pick = jnp.logical_and(first if half == 0 else jnp.logical_not(first), valid)
            scores = lax.dot_general(
                jnp.where(pick, queries, 0),
                keys[pl.ds(0, seen), :],
                NT,
                preferred_element_type=jnp.float32,
            )
            last = jnp.where(diagonal, scores[:, before:], -1e30)
            scores = last if block == 0 else jnp.concatenate([scores[:, :before], last], axis=1)
            top = jnp.max(scores, axis=1, keepdims=True)
            weights = jnp.exp(scores - top)
            total = jnp.sum(weights, axis=1, keepdims=True)
            added = jnp.dot(
                weights.astype(jnp.bfloat16),
                values[pl.ds(0, seen), :],
                preferred_element_type=jnp.float32,
            )
            parts.append(added / total)
            logs = jnp.where(lane == 2 * own_pair + half, top + jnp.log(total), logs)
        o_ref[rows(block), :] = jnp.where(first, parts[0], parts[1]).astype(jnp.bfloat16)
        log_ref[rows(block), :] = logs


def attend_back_kernel(
    place_ref,
    q_ref,
    k_ref,
    v_ref,
    g_ref,
    o_ref,
    log_ref,
    *refs,
    count,
    width,
    start,
):
    dq_ref, dk_ref, dv_ref, queries, grads, keys, values = refs[-11:-4]
    keys_turned, logs, deltas, turned = refs[-4:]
    pair = pl.program_id(0) + start
    shift = place_ref[0]
    length = q_ref.shape[0]
    block_len = length // count
    lane = lax.broadcasted_iota(jnp.int32, (1, PAIR), 1)
    valid = lane + pair * PAIR < width
    first = lane < HEAD_DIM
    picks = (jnp.logical_and(first, valid), jnp.logical_and(jnp.logical_not(first), valid))
    half_of = (lax.broadcasted_iota(jnp.int32, (8, PAIR), 1) // HEAD_DIM) == (
        lax.broadcasted_iota(jnp.int32, (8, PAIR), 0)
    )
    ones_of = jnp.where(half_of, 1.0, 0.0)

    def rows(block):
        return pl.ds(pl.multiple_of((block ^ shift) * block_len, block_len), block_len)

    for block in range(count):
        here = pl.ds(block * block_len, block_len)
        key_block = jnp.where(valid, k_ref[rows(block), :], 0)
        keys[here, :] = key_block
        keys_turned[:, here] = key_block.astype(jnp.float32).T.astype(jnp.bfloat16)
        values[here, :] = jnp.where(valid, v_ref[rows(block), :], 0)
        query_block = q_ref[rows(block), :] * jnp.bfloat16(HEAD_DIM**-0.5)
        grad_block = jnp.where(valid, g_ref[rows(block), :], 0)
        for half in range(2):
            queries[half, here, :] = jnp.where(picks[half], query_block, 0)
            grads[half, here, :] = jnp.where(picks[half], grad_block, 0)
        mixed = grad_block.astype(jnp.float32) * jnp.where(
            valid, o_ref[rows(block), :], 0
        ).astype(jnp.float32)
        deltas[:, here] = lax.dot_general(
            ones_of,
            mixed,
            NT,
            preferred_element_type=jnp.float32,
            precision=lax.Precision.HIGHEST,
        )
        logs[:, here] = log_ref[
            0, :, pl.ds(pl.multiple_of((block ^ shift) * block_len, block_len), block_len)
        ]
    diagonal = lax.broadcasted_iota(jnp.int32, (block_len, block_len), 0) <= (
        lax.broadcasted_iota(jnp.int32, (block_len, block_len), 1)
    )
    for block in range(count):
        here = pl.ds(block * block_len, block_len)
        after = pl.ds(block * block_len, length - block * block_len)
        key_total = jnp.zeros((block_len, PAIR), jnp.float32)
        value_total = jnp.zeros((block_len, PAIR), jnp.float32)
        for half in range(2):
            scores = lax.dot_general(
                keys[here, :], queries[half, after, :], NT, preferred_element_type=jnp.float32
            )
            shifted = scores - logs[half : half + 1, after]
            own = jnp.where(diagonal, shifted[:, :block_len], -1e30)
            if block < count - 1:
                own = jnp.concatenate([own, shifted[:, block_len:]], axis=1)
            weights = jnp.exp(own)
            pressure = lax.dot_general(
                values[here, :], grads[half, after, :], NT, preferred_element_type=jnp.float32
            )
            score_low = (weights * (pressure - deltas[half : half + 1, after])).astype(
                jnp.bfloat16
            )
            value_total += jnp.dot(
                weights.astype(jnp.bfloat16),
                grads[half, after, :],
                preferred_element_type=jnp.float32,
            )
            key_total += jnp.dot(
                score_low, queries[half, after, :], preferred_element_type=jnp.float32
            )
            part = pl.ds(half * HEAD_DIM, HEAD_DIM)
            term = jnp.dot(
                keys_turned[part, here], score_low, preferred_element_type=jnp.float32
            )
            if block == 0:
                turned[part, after] = term
            else:
                turned[part, after] += term
        dk_ref[rows(block), :] = key_total.astype(jnp.bfloat16)
        dv_ref[rows(block), :] = value_total.astype(jnp.bfloat16)
    for block in range(count):
        here = pl.ds(block * block_len, block_len)
        dq_ref[rows(block), :] = (turned[:, here].T * HEAD_DIM**-0.5).astype(jnp.bfloat16)


def attend(place, queries, key_rows, value_rows, count, start, pairs, before):
    length, width = queries.shape
    heads_block = pl.BlockSpec((length, PAIR), lambda pair, place_ref: (0, pair + start))
    return pl.pallas_call(
        functools.partial(attend_kernel, count=count, width=width, start=start),
        grid_spec=pltpu.PrefetchScalarGridSpec(
            num_scalar_prefetch=1,
            grid=(pairs,),
            in_specs=[heads_block] * 3 + [pl.BlockSpec(memory_space=pl.ANY)] * len(before),
            out_specs=[
                heads_block,
                pl.BlockSpec((length, 128), lambda pair, place_ref: (0, 0)),
            ],
            scratch_shapes=[pltpu.VMEM((length, PAIR), jnp.bfloat16)] * 2,
        ),
        out_shape=[
            jax.ShapeDtypeStruct((length, width), jnp.bfloat16),
            jax.ShapeDtypeStruct((length, 128), jnp.float32),
        ],
        input_output_aliases={4 + at: at for at in range(len(before))},
        compiler_params=pltpu.CompilerParams(vmem_limit_bytes=48 * 2**20),
        cost_estimate=pl.CostEstimate(
            flops=4 * length * length * PAIR * pairs * 4,
            bytes_accessed=8 * length * PAIR * pairs,
            transcendentals=length * length * pairs,
        ),
        name="attend",
    )(place, queries, key_rows, value_rows, *before)


def attend_back(
    place, queries, key_rows, value_rows, grads, attended, logs, count, start, pairs, before
):
    length, width = queries.shape
    heads_block = pl.BlockSpec((length, PAIR), lambda pair, place_ref: (0, pair + start))
    low_rows = pltpu.VMEM((length, PAIR), jnp.bfloat16)
    low_pair = pltpu.VMEM((2, length, PAIR), jnp.bfloat16)
    return pl.pallas_call(
        functools.partial(attend_back_kernel, count=count, width=width, start=start),
        grid_spec=pltpu.PrefetchScalarGridSpec(
            num_scalar_prefetch=1,
            grid=(pairs,),
            in_specs=[heads_block] * 5
            + [pl.BlockSpec((1, 2, length), lambda pair, place_ref: (pair, 0, 0))]
            + [pl.BlockSpec(memory_space=pl.ANY)] * len(before),
            out_specs=[heads_block] * 3,
            scratch_shapes=[
                low_pair,
                low_pair,
                low_rows,
                low_rows,
                pltpu.VMEM((PAIR, length), jnp.bfloat16),
                pltpu.VMEM((2, length), jnp.float32),
                pltpu.VMEM((8, length), jnp.float32),
                pltpu.VMEM((PAIR, length), jnp.float32),
            ],
        ),
        out_shape=[jax.ShapeDtypeStruct((length, width), jnp.bfloat16)] * 3,
        input_output_aliases={7 + at: at for at in range(len(before))},
        compiler_params=pltpu.CompilerParams(vmem_limit_bytes=48 * 2**20),
        cost_estimate=pl.CostEstimate(
            flops=10 * length * length * PAIR * pairs * 3,
            bytes_accessed=16 * length * PAIR * pairs,
            transcendentals=length * length * pairs,
        ),
        name="attend_back",
    )(place, queries, key_rows, value_rows, grads, attended, logs, *before)


def settle_kernel(place_ref, *refs):
    pieces, out_ref = refs[:-1], refs[-1]
    for at, piece in enumerate(pieces):
        out_ref[place_ref[at]] = piece[...].astype(out_ref.dtype)


def settle(places, pieces, dtype):
    return pl.pallas_call(
        settle_kernel,
        in_specs=[pl.BlockSpec(memory_space=pltpu.SMEM)]
        + [pl.BlockSpec(memory_space=pltpu.VMEM)] * len(pieces),
        out_specs=pl.BlockSpec(memory_space=pltpu.VMEM),
        out_shape=jax.ShapeDtypeStruct((len(pieces),) + pieces[0].shape, dtype),
        compiler_params=pltpu.CompilerParams(vmem_limit_bytes=48 * 2**20),
        name="settle",
    )(places, *pieces)


def plane_partner(device, kind):
    core = device & 1
    if kind == "core":
        return device ^ 1
    if kind == "far":
        return device ^ (3 if core else 5)
    if kind == "near":
        return device ^ (2 if core else 4)
    return device ^ (4 if core else 2)


def plane_swap(values, kind):
    return lax.ppermute(
        values, ("dp", "ctx"), [(device, plane_partner(device, kind)) for device in range(8)]
    )


def ctx_swap(values, bits):
    return lax.ppermute(values, "ctx", [(device, device ^ bits) for device in range(4)])


def low_sum(*terms):
    return sum(term.astype(jnp.float32) for term in terms).astype(jnp.bfloat16)


def reduce_core(pieces):
    return plane_swap(pieces[2], "core"), plane_swap(pieces[3], "core")


def share_out(whole):
    return [whole] + [plane_swap(whole, kind) for kind in ("near", "core", "far")]


def scatter_rows(values):
    return lax.psum_scatter(values, "fsdp", scatter_dimension=0, tiled=True)


def chosen(index, options):
    result = options[-1]
    for at in range(len(options) - 2, -1, -1):
        result = jnp.where(index == at, options[at], result)
    return result


def gather_vector(values, z):
    around = [values] + [
        lax.ppermute(values, "fsdp", [(device, (device + step) % 4) for device in range(4)])
        for step in range(1, 4)
    ]
    return jnp.stack([chosen((z - at) % 4, around) for at in range(4)])


def reduce_vector(values, z):
    rows = [values[at] for at in range(4)]
    total = chosen(z, rows)
    for step in range(1, 4):
        total = total + lax.ppermute(
            chosen((z + step) % 4, rows),
            "fsdp",
            [(device, (device + step) % 4) for device in range(4)],
        )
    for bits in (1, 2, 4):
        total = total + lax.ppermute(
            total, ("dp", "ctx"), [(device, device ^ bits) for device in range(8)]
        )
    return total


def product(left, right, dims):
    return lax.dot_general(left, right, ((dims[:1], dims[1:]), ((), ())),
                           preferred_element_type=jnp.float32)


def gelu_pair(values):
    inner = 0.7978845608028654
    cubic = inner * 0.044715
    squared = values * values
    curve = jnp.tanh(values * (inner + cubic * squared))
    half = 0.5 * values
    active = half + half * curve
    slope = 0.5 + 0.5 * curve + half * (1.0 - curve * curve) * (inner + 3.0 * cubic * squared)
    return active, slope


def block_flops(rows, width, count):
    return pl.CostEstimate(
        flops=2 * rows * width * width * count,
        bytes_accessed=2 * width * width * count + 4 * rows * width * count,
        transcendentals=0,
    )


def unit_of(values):
    centred = values - jnp.mean(values, axis=-1, keepdims=True)
    scale = lax.rsqrt(jnp.mean(centred * centred, axis=-1, keepdims=True) + epsilon)
    return centred * scale, scale


def fold(values):
    rows, width = values.shape
    return jnp.sum(values.reshape(rows // 8, 8, width), axis=0)


def front_kernel(places_ref, vectors_ref, *refs):
    slots, pieces = refs[:4], refs[4:20]
    x_ref, h_ref, q_ref, k_ref, v_ref, all_ref, weights, arrived, left = refs[20:]
    copies = [
        pltpu.make_async_copy(piece, weights.at[places_ref[at]], arrived.at[at])
        for at, piece in enumerate(pieces)
    ]
    for copy in copies:
        copy.start()
    rows, width = x_ref.shape
    step = rows // 4
    for at, slot in enumerate(slots):
        here = pl.ds(at * step, step)
        values = slot[...].astype(jnp.float32).T
        x_ref[here, :] = values.astype(jnp.bfloat16)
        unit, _ = unit_of(values)
        h_ref[here, :] = (unit * vectors_ref[0:1, :] + vectors_ref[1:2, :]).astype(jnp.bfloat16)
    for copy in copies:
        copy.wait()
    leave = pltpu.make_async_copy(weights, all_ref, left)
    leave.start()
    for section, out_ref in enumerate((q_ref, k_ref, v_ref)):

        def multiply(at, carry, section=section, out_ref=out_ref):
            here = pl.ds(pl.multiple_of(at * step, step), step)
            matrix = weights[4 * section : 4 * section + 4].reshape(width, width)
            total = jnp.dot(h_ref[here, :], matrix, preferred_element_type=jnp.float32)
            if section != 1:
                row = 2 if section == 0 else 3
                total = total + vectors_ref[row : row + 1, :]
            out_ref[here, :] = total.astype(jnp.bfloat16)
            return carry

        lax.fori_loop(0, rows // step, multiply, 0)
    leave.wait()


def front(places, slots, vectors, pieces):
    width, step = slots[0].shape
    rows = 4 * step
    vmem = pl.BlockSpec(memory_space=pltpu.VMEM)
    hbm = pl.BlockSpec(memory_space=pl.ANY)
    shape = jax.ShapeDtypeStruct((rows, width), jnp.bfloat16)
    whole = (16,) + pieces[0].shape
    return pl.pallas_call(
        front_kernel,
        in_specs=[pl.BlockSpec(memory_space=pltpu.SMEM)] + [vmem] * 5 + [hbm] * 16,
        out_specs=[vmem] * 5 + [hbm],
        out_shape=[shape] * 5 + [jax.ShapeDtypeStruct(whole, jnp.bfloat16)],
        scratch_shapes=[
            pltpu.VMEM(whole, jnp.bfloat16),
            pltpu.SemaphoreType.DMA((16,)),
            pltpu.SemaphoreType.DMA,
        ],
        compiler_params=pltpu.CompilerParams(vmem_limit_bytes=56 * 2**20),
        cost_estimate=block_flops(rows, width, 3),
        name="front",
    )(places, vectors, *slots, *pieces)


def turn_kernel(*refs):
    slots, out_ref = refs[:-1], refs[-1]
    step = slots[0].shape[1]
    for at, slot in enumerate(slots):
        out_ref[pl.ds(at * step, step), :] = (
            slot[...].astype(jnp.float32).T.astype(jnp.bfloat16)
        )


def turn(slots):
    width, step = slots[0].shape
    return pl.pallas_call(
        turn_kernel,
        out_shape=jax.ShapeDtypeStruct((len(slots) * step, width), jnp.bfloat16),
        compiler_params=pltpu.CompilerParams(vmem_limit_bytes=48 * 2**20),
        name="turn",
    )(*slots)


def assemble_kernel(place_ref, *refs, plan):
    pieces, outs = refs[:4], refs[4:]
    for at, piece in enumerate(pieces):
        for kind, moves in enumerate(plan):

            @pl.when(place_ref[at] == kind)
            def _(piece=piece, moves=moves):
                for out, source, target, size in moves:
                    outs[out][:, target : target + size] = piece[
                        :, source : source + size
                    ].astype(jnp.float32)


def assemble(places, pieces, plan, shapes):
    vmem = pl.BlockSpec(memory_space=pltpu.VMEM)
    return pl.pallas_call(
        functools.partial(assemble_kernel, plan=plan),
        in_specs=[pl.BlockSpec(memory_space=pltpu.SMEM)] + [vmem] * 4,
        out_specs=[vmem] * len(shapes),
        out_shape=[jax.ShapeDtypeStruct(shape, jnp.float32) for shape in shapes],
        compiler_params=pltpu.CompilerParams(vmem_limit_bytes=48 * 2**20),
        name="assemble",
    )(places, *pieces)


def store_turned(step, refs, values):
    size = refs[0].shape[1]
    share = values.shape[0] // size
    for at, ref in enumerate(refs):

        @pl.when(step == at // share)
        def _(at=at, ref=ref):
            first = (at % share) * size
            ref[...] = values[first : first + size].T.astype(ref.dtype)


def fetch(step, copies):
    @pl.when(step == 0)
    def _():
        for copy in copies:
            copy.start()


def arrive(step, copy):
    @pl.when(step == 0)
    def _():
        copy.wait()


def middle_kernel(x_ref, o_ref, vectors_ref, all_ref, middle_ref, h_ref, weights, arrived):
    step = pl.program_id(0)
    width = x_ref.shape[1]
    copy = pltpu.make_async_copy(all_ref.at[pl.ds(12, 4)], weights, arrived)
    fetch(step, [copy])
    arrive(step, copy)
    middle = (
        x_ref[...].astype(jnp.float32)
        + jnp.dot(
            o_ref[...], weights[...].reshape(width, width), preferred_element_type=jnp.float32
        )
        + vectors_ref[0:1, :]
    )
    middle_ref[...] = middle
    unit, _ = unit_of(middle)
    h_ref[...] = (unit * vectors_ref[1:2, :] + vectors_ref[2:3, :]).astype(jnp.bfloat16)


def up_kernel(h_ref, biases_ref, *refs):
    sources = refs[:2]
    active_refs, slope_refs = refs[2:4], refs[4:6]
    weights, arrived = refs[6:]
    step = pl.program_id(0)
    copies = [
        pltpu.make_async_copy(source, weights.at[at], arrived.at[at])
        for at, source in enumerate(sources)
    ]
    fetch(step, copies)
    for at in range(2):
        arrive(step, copies[at])
        hidden = (
            jnp.dot(h_ref[...], weights[at], preferred_element_type=jnp.float32)
            + biases_ref[at : at + 1, :]
        )
        active, slope = gelu_pair(hidden)
        active_refs[at][...] = active.astype(jnp.bfloat16)
        slope_refs[at][...] = slope.astype(jnp.bfloat16)


def down_kernel(middle_ref, vectors_ref, *refs):
    actives, sources = refs[:4], refs[4:8]
    out_refs = refs[8:12]
    weights, arrived = refs[12:]
    step = pl.program_id(0)
    copies = [
        pltpu.make_async_copy(source, weights.at[at], arrived.at[at])
        for at, source in enumerate(sources)
    ]
    fetch(step, copies)
    total = middle_ref[...] + vectors_ref[0:1, :]
    for at in range(4):
        arrive(step, copies[at])
        total = total + jnp.dot(
            actives[at][...], weights[at], preferred_element_type=jnp.float32
        )
    store_turned(step, out_refs, total)


def norm_back(values, gain, grad):
    unit, scale = unit_of(values)
    turned = grad * gain
    inner = (
        turned
        - jnp.mean(turned, axis=-1, keepdims=True)
        - unit * jnp.mean(turned * unit, axis=-1, keepdims=True)
    )
    return scale * inner, grad * unit


def hidden_kernel(g_ref, *refs):
    slopes, sources = refs[:2], refs[2:4]
    hidden_refs, sums_ref = refs[4:6], refs[6]
    weights, arrived = refs[7:]
    step = pl.program_id(0)
    copies = [
        pltpu.make_async_copy(source, weights.at[at], arrived.at[at])
        for at, source in enumerate(sources)
    ]
    fetch(step, copies)

    @pl.when(step == 0)
    def _():
        sums_ref[...] = jnp.zeros_like(sums_ref)

    upstream = g_ref[...]
    for at in range(2):
        arrive(step, copies[at])
        hidden = lax.dot_general(
            upstream, weights[at], NT, preferred_element_type=jnp.float32
        )
        hidden = (hidden * slopes[at][...].astype(jnp.float32)).astype(jnp.bfloat16)
        hidden_refs[at][...] = hidden
        sums_ref[at] += fold(hidden.astype(jnp.float32))
    sums_ref[2] += fold(upstream.astype(jnp.float32))


def back_kernel(g_ref, middle_ref, vectors_ref, *refs):
    hiddens, sources, all_ref = refs[:4], refs[4:8], refs[8]
    grad_ref, low_ref, out_ref, sums_ref = refs[9:13]
    weights, out_weights, arrived = refs[13:]
    step = pl.program_id(0)
    width = middle_ref.shape[1]
    copies = [
        pltpu.make_async_copy(source, weights.at[at], arrived.at[at])
        for at, source in enumerate(sources)
    ] + [pltpu.make_async_copy(all_ref.at[pl.ds(12, 4)], out_weights, arrived.at[4])]
    fetch(step, copies)

    @pl.when(step == 0)
    def _():
        sums_ref[...] = jnp.zeros_like(sums_ref)

    total = jnp.zeros(middle_ref.shape, jnp.float32)
    for at in range(4):
        arrive(step, copies[at])
        total = total + lax.dot_general(
            hiddens[at][...], weights[at], NT, preferred_element_type=jnp.float32
        )
    part, gain_term = norm_back(middle_ref[...], vectors_ref[0:1, :], total)
    sums_ref[0] += fold(gain_term)
    sums_ref[1] += fold(total)
    grad = g_ref[...].astype(jnp.float32) + part
    grad_ref[...] = grad
    grad_low = grad.astype(jnp.bfloat16)
    low_ref[...] = grad_low
    sums_ref[2] += fold(grad_low.astype(jnp.float32))
    arrive(step, copies[4])
    out_ref[...] = lax.dot_general(
        grad_low,
        out_weights[...].reshape(width, width),
        NT,
        preferred_element_type=jnp.float32,
    ).astype(jnp.bfloat16)


def last_kernel(q_ref, k_ref, v_ref, x_ref, grad_ref, vectors_ref, all_ref, *refs):
    out_refs = refs[:4]
    sums_ref, weights, arrived = refs[4:]
    step = pl.program_id(0)
    width = x_ref.shape[1]
    copies = [
        pltpu.make_async_copy(
            all_ref.at[pl.ds(4 * at, 4)], weights.at[pl.ds(4 * at, 4)], arrived.at[at]
        )
        for at in range(3)
    ]
    fetch(step, copies)
    total = jnp.zeros(x_ref.shape, jnp.float32)
    for at, ref in enumerate((q_ref, k_ref, v_ref)):
        arrive(step, copies[at])
        total = total + lax.dot_general(
            ref[...],
            weights[4 * at : 4 * at + 4].reshape(width, width),
            NT,
            preferred_element_type=jnp.float32,
        )
    part, gain_term = norm_back(x_ref[...].astype(jnp.float32), vectors_ref[0:1, :], total)
    store_turned(step, out_refs, grad_ref[...] + part)

    @pl.when(step == 0)
    def _():
        sums_ref[...] = jnp.zeros_like(sums_ref)

    terms = (
        gain_term,
        total,
        q_ref[...].astype(jnp.float32),
        v_ref[...].astype(jnp.float32),
    )
    for at, term in enumerate(terms):
        sums_ref[at] += fold(term)


def by_rows(kernel, name, rows, width, tiled, whole, remote, outs, sums, scratch, sems, blocks):
    step = 512
    tile = pl.BlockSpec((step, width), lambda at: (at, 0))
    out_specs, out_shape = [], []
    for dtype in outs:
        if dtype is None:
            out_specs += [pl.BlockSpec((width, rows // 4), lambda at: (0, 0))] * 4
            out_shape += [jax.ShapeDtypeStruct((width, rows // 4), jnp.bfloat16)] * 4
        else:
            out_specs.append(tile)
            out_shape.append(jax.ShapeDtypeStruct((rows, width), dtype))
    if sums:
        out_specs.append(pl.BlockSpec((sums, 8, width), lambda at: (0, 0, 0)))
        out_shape.append(jax.ShapeDtypeStruct((sums, 8, width), jnp.float32))
    return pl.pallas_call(
        kernel,
        grid=(rows // step,),
        in_specs=[tile] * len(tiled[0])
        + [pl.BlockSpec(value.shape, lambda at: (0, 0)) for value in whole]
        + [tile] * len(tiled[1])
        + [pl.BlockSpec(memory_space=pl.ANY)] * len(remote),
        out_specs=out_specs,
        out_shape=out_shape,
        scratch_shapes=[pltpu.VMEM(shape, jnp.bfloat16) for shape in scratch]
        + [pltpu.SemaphoreType.DMA((sems,)) if sems > 1 else pltpu.SemaphoreType.DMA],
        compiler_params=pltpu.CompilerParams(vmem_limit_bytes=60 * 2**20),
        cost_estimate=block_flops(rows, width, blocks),
        name=name,
    )(*tiled[0], *whole, *tiled[1], *remote)


def per_device_exchanged(
    inputs,
    cotangent,
    first_gain,
    first_shift,
    project_in,
    query_bias,
    value_bias,
    project_out,
    output_bias,
    second_gain,
    second_shift,
    up_weight,
    up_bias,
    down_weight,
    down_bias,
):
    seq_count, block_len, width = inputs.shape
    low = jnp.bfloat16
    wide = jnp.float32
    c = lax.axis_index("ctx")
    y = lax.axis_index("dp")
    z = lax.axis_index("fsdp")
    core = c & 1
    x = c >> 1
    mine = core * 2 + jnp.where(core == 0, y, x)
    across = (1 - core) * 2 + jnp.where(core == 0, x, y)
    classes = [mine, mine ^ 1, across, across ^ 1]
    slot_of = [
        chosen(0, [sum(at * (classes[at] == kind).astype(jnp.int32) for at in range(4))])
        for kind in range(4)
    ]
    quarter = width // 4
    rows, area = seq_count * block_len, (width, width)
    pin = lax.optimization_barrier
    place = jnp.stack([c])
    places = jnp.stack([c ^ at for at in range(4)])
    class_places = jnp.stack(classes)

    def spread(values):
        values = jnp.swapaxes(values, 1, 2)
        return [lax.dynamic_index_in_dim(values, c, 0, keepdims=False)] + [
            ctx_swap(lax.dynamic_index_in_dim(values, c ^ bits, 0, keepdims=False), bits)
            for bits in range(1, 4)
        ]

    def exchange(pieces):
        return [pieces[0]] + [ctx_swap(pieces[bits], bits) for bits in range(1, 4)]

    def collect(moved, dtype):
        return jnp.swapaxes(settle(places, moved, dtype), 1, 2)

    sections = [
        project_in[:, :width],
        project_in[:, width : 2 * width],
        project_in[:, 2 * width :],
        project_out,
    ]
    section = chosen(mine, sections)
    section, inputs = pin((section, inputs))
    shards = [
        lax.ppermute(section, "fsdp", [(device, (device + step) % 4) for device in range(4)])
        for step in range(1, 4)
    ]
    turned_in = jnp.swapaxes(inputs, 1, 2)
    slots_in = [
        lax.dynamic_index_in_dim(turned_in, c ^ bits, 0, keepdims=False) for bits in range(4)
    ]
    pieces_in = (
        first_gain,
        first_shift,
        query_bias,
        value_bias,
        output_bias,
        second_gain,
        second_shift,
        down_bias,
        up_bias,
    )
    slots_in[3], cotangent, up_weight, down_weight, *pieces_in = pin(
        (slots_in[3], cotangent, up_weight, down_weight, *pieces_in)
    )
    slots_in = [slots_in[0]] + [ctx_swap(slots_in[bits], bits) for bits in range(1, 4)]
    vectors = gather_vector(jnp.concatenate(pieces_in), z).astype(wide)
    slots_back = spread(cotangent)
    up_piece = jnp.concatenate(
        [
            lax.dynamic_slice_in_dim(up_weight, at * width + mine * quarter, quarter, 1)
            for at in range(4)
        ],
        axis=1,
    )
    up_piece, vectors, *moved = pin((up_piece, vectors, *shards, *slots_in, *slots_back))
    shards, slots_in, slots_back = moved[:3], moved[3:7], moved[7:]
    near_shards = [plane_swap(shard, "near") for shard in shards]
    around = (
        sections
        + shards
        + near_shards
        + [plane_swap(shard, "core") for shard in shards]
        + [plane_swap(shard, "core") for shard in near_shards]
    )
    around_places = jnp.stack(
        [kind * 4 + z for kind in range(4)]
        + [kind * 4 + (z - step) % 4 for kind in classes for step in range(1, 4)]
    )
    up_own = lax.all_gather(up_piece, "fsdp", axis=0, tiled=True)
    down_piece = lax.dynamic_slice_in_dim(down_weight, mine * quarter, quarter, 0)
    gain_first, shift_first, qbias, vbias, obias, gain_second, shift_second, dbias = (
        vectors[:, at * quarter : (at + 1) * quarter].reshape(1, width) for at in range(8)
    )
    ubias = vectors[:, 8 * quarter :].reshape(4, 4, quarter)
    ubias = jnp.concatenate(
        [
            chosen(kind, [ubias[:, at] for at in range(4)]).reshape(1, width)
            for kind in classes
        ],
        axis=0,
    )

    rows_in, normed_low, queries, key_rows, value_rows, weights = front(
        around_places,
        slots_in,
        jnp.concatenate([gain_first, shift_first, qbias, vbias], axis=0),
        around,
    )
    slots_back[0], up_own, queries = pin((slots_back[0], up_own, queries))
    upstream_low = turn(slots_back)
    up_near, up_core = plane_swap(up_own, "near"), plane_swap(up_own, "core")
    attended, logs = attend(place, queries, key_rows, value_rows, seq_count, 0, 9, [])
    down_piece, up_core, up_near, attended = pin((down_piece, up_core, up_near, attended))
    down_own = lax.all_gather(down_piece, "fsdp", axis=0, tiled=True)
    logs = logs.T.reshape(64, 2, rows)
    logs_one, logs_two = logs[:5], logs[5:9]
    middle, normed_two_low = by_rows(
        middle_kernel,
        "middle",
        rows,
        width,
        ([rows_in, attended], []),
        [jnp.concatenate([obias, gain_second, shift_second], axis=0)],
        [weights],
        [wide, low],
        0,
        [(4,) + section.shape],
        1,
        1,
    )
    up_slots = [up_own, up_near, up_core, plane_swap(up_near, "core")]
    active, slopes = [None] * 4, [None] * 4

    def up(first):
        outs = by_rows(
            up_kernel,
            "up",
            rows,
            width,
            ([normed_two_low], []),
            [jnp.concatenate([ubias[first : first + 1], ubias[first + 2 : first + 3]], axis=0)],
            [up_slots[first], up_slots[first + 2]],
            [low] * 4,
            0,
            [(2,) + area],
            2,
            2,
        )
        active[first], active[first + 2], slopes[first], slopes[first + 2] = outs

    up(0)
    up_slots[3], active[0], active[2] = pin((up_slots[3], active[0], active[2]))
    up(1)
    down_own, *active = pin((down_own, *active))
    down_near, down_core = plane_swap(down_own, "near"), plane_swap(down_own, "core")

    def turned_product(left, right):
        return product(left, right, (0, 0)).astype(low)

    down_terms = [turned_product(active[slot], upstream_low) for slot in (3, 2)]
    upstream_low, *down_terms = pin((upstream_low, *down_terms))
    down_terms += [turned_product(active[slot], upstream_low) for slot in (1, 0)]
    down_terms = down_terms[::-1]
    down_far, down_far_two = reduce_core(down_terms)
    upstream_low, *down_terms = pin((upstream_low, *down_terms))
    hidden_low = [None] * 4

    def hidden(first, upstream):
        hidden_low[first], hidden_low[first + 2], sums = by_rows(
            hidden_kernel,
            "hidden",
            rows,
            width,
            ([upstream], [slopes[first], slopes[first + 2]]),
            [],
            [down_slots[first], down_slots[first + 2]],
            [low] * 2,
            3,
            [(2,) + area],
            2,
            2,
        )
        return sums

    down_near, upstream_low = pin((down_near, upstream_low))
    down_slots = [down_own, down_near, down_core, plane_swap(down_near, "core")]
    sums_even = hidden(0, upstream_low)
    upstream_late, sums_even = pin((upstream_low, sums_even))
    sums_odd = hidden(1, upstream_late)
    hidden_sums = jnp.stack(
        [sums_even[0], sums_odd[0], sums_even[1], sums_odd[1], sums_even[2]]
    )
    down_second = low_sum(down_terms[1], down_far_two)
    down_second, down_far, *hidden_low = pin((down_second, down_far, *hidden_low))
    down_close = plane_swap(down_second, "near")
    middle_grad, middle_low, grad_low, back_sums = by_rows(
        back_kernel,
        "back",
        rows,
        width,
        ([upstream_low, middle], hidden_low),
        [gain_second],
        up_slots + [weights],
        [wide, low, low],
        3,
        [(4,) + area, (4,) + section.shape],
        5,
        5,
    )
    down_first = low_sum(down_terms[0], down_far, down_close)
    down_first, normed_two_low = pin((down_first, pin((normed_two_low, middle_low))[0]))
    down_shard = scatter_rows(down_first)
    up_terms = [turned_product(normed_two_low, hidden_low[slot]) for slot in (3, 2)]
    normed_two_low, *up_terms = pin((normed_two_low, *up_terms))
    up_terms += [turned_product(normed_two_low, hidden_low[slot]) for slot in (1, 0)]
    up_terms = up_terms[::-1]
    up_far, up_far_two = reduce_core(up_terms)
    out_term = turned_product(attended, middle_low)
    up_second = low_sum(up_terms[1], up_far_two)
    grad_low, up_second, up_far, out_term, *up_terms = pin(
        (grad_low, up_second, up_far, out_term, *up_terms)
    )
    up_close = plane_swap(up_second, "near")
    in_grads = attend_back(
        place, queries, key_rows, value_rows, grad_low, attended, logs_one, seq_count, 0, 5, []
    )
    up_first = low_sum(up_terms[0], up_far, up_close)
    up_first, down_shard, *in_grads = pin((up_first, down_shard, *in_grads))
    up_shard = scatter_rows(up_first)
    down_whole = low_sum(down_shard, plane_swap(down_shard, "other"))
    in_grads = attend_back(
        place,
        queries,
        key_rows,
        value_rows,
        grad_low,
        attended,
        logs_two,
        seq_count,
        5,
        4,
        in_grads,
    )
    down_whole, *in_grads = pin((down_whole, *in_grads))
    down_parts = share_out(down_whole)
    in_terms = [turned_product(normed_low, grad) for grad in in_grads]
    section_grads = in_terms + [out_term]
    sections_mine = [chosen(kind, section_grads) for kind in classes]
    far, far_two = reduce_core(sections_mine)
    second = low_sum(sections_mine[1], far_two)
    second, far, middle, *moved = pin((second, far, middle, *in_grads, *down_parts))
    query_low, key_low, value_low = moved[:3]
    down_parts = moved[3:]
    close = plane_swap(second, "near")
    result_slots = by_rows(
        down_kernel,
        "down",
        rows,
        width,
        ([middle], active),
        [dbias],
        down_slots,
        [None],
        0,
        [(4,) + area],
        4,
        4,
    )
    first = low_sum(sections_mine[0], far, close)
    first, up_shard, query_low, *result_slots = pin(
        (first, up_shard, query_low, *result_slots)
    )
    shard = scatter_rows(first)
    outputs = exchange(result_slots)
    up_whole = low_sum(up_shard, plane_swap(up_shard, "other"))
    *input_slots, last_sums = by_rows(
        last_kernel,
        "last",
        rows,
        width,
        ([query_low, key_low, value_low, rows_in, middle_grad], []),
        [gain_first],
        [weights],
        [None],
        4,
        [(12,) + section.shape],
        3,
        3,
    )
    up_whole, last_sums, *moved = pin((up_whole, last_sums, *input_slots, *outputs))
    input_slots, outputs = exchange(moved[:4]), moved[4:]
    up_parts = share_out(up_whole)

    back_sums = jnp.concatenate([hidden_sums, back_sums], axis=0)
    back_sums = jnp.sum(back_sums, axis=1)
    last_sums = jnp.sum(last_sums, axis=1)
    hidden_sums = [back_sums[slot].reshape(4, quarter) for slot in range(4)]
    hidden_sums = jnp.stack(
        [chosen(slot_of[kind], hidden_sums) for kind in range(4)], axis=1
    ).reshape(4, 4 * quarter)
    totals = reduce_vector(
        jnp.concatenate(
            [back_sums[at].reshape(4, quarter) for at in range(4, 8)]
            + [last_sums[at].reshape(4, quarter) for at in range(4)]
            + [hidden_sums],
            axis=1,
        ),
        z,
    )
    moved = pin((*input_slots, *up_parts))
    outputs = collect(outputs, low)
    input_gradient = collect(moved[:4], wide)
    up_parts = moved[4:]
    (up_sum,) = assemble(
        class_places,
        up_parts,
        [
            [(0, at * quarter, at * width + kind * quarter, quarter) for at in range(4)]
            for kind in range(4)
        ],
        [up_weight.shape],
    )
    down_sum = settle(class_places, down_parts, wide).reshape(down_weight.shape)
    shard, outputs, input_gradient, totals, up_sum, down_sum = pin(
        (shard, outputs, input_gradient, totals, up_sum, down_sum)
    )
    in_sum, out_sum = assemble(
        class_places,
        share_out(low_sum(shard, plane_swap(shard, "other"))),
        [[(0, 0, kind * width, width)] for kind in range(3)] + [[(1, 0, 0, width)]],
        [project_in.shape, project_out.shape],
    )
    (
        dbias_sum,
        gain_two_sum,
        shift_two_sum,
        obias_sum,
        gain_one_sum,
        shift_one_sum,
        qbias_sum,
        vbias_sum,
    ) = (totals[at * quarter : (at + 1) * quarter] for at in range(8))
    ubias_sum = totals[8 * quarter :]
    return (
        outputs,
        input_gradient,
        gain_one_sum,
        shift_one_sum,
        in_sum,
        qbias_sum,
        vbias_sum,
        out_sum,
        obias_sum,
        gain_two_sum,
        shift_two_sum,
        up_sum,
        ubias_sum,
        down_sum,
        dbias_sum,
    )


def solution(mesh):
    sizes = dict(mesh.shape)
    exchanged = sizes["dp"] == 2 and sizes["fsdp"] == 4 and sizes["ctx"] == 4
    per_device = per_device_exchanged if exchanged else per_device_gathered
    return jax.shard_map(
        per_device,
        mesh=mesh,
        in_specs=(
            P(("dp", "fsdp"), "ctx", None),
            P(("dp", "fsdp"), "ctx", None),
            P("fsdp"),
            P("fsdp"),
            P("fsdp", None),
            P("fsdp"),
            P("fsdp"),
            P("fsdp", None),
            P("fsdp"),
            P("fsdp"),
            P("fsdp"),
            P("fsdp", None),
            P("fsdp"),
            P("fsdp", None),
            P("fsdp"),
        ),
        out_specs=(
            P(("dp", "fsdp"), "ctx", None),
            P(("dp", "fsdp"), "ctx", None),
            P("fsdp"),
            P("fsdp"),
            P("fsdp", None),
            P("fsdp"),
            P("fsdp"),
            P("fsdp", None),
            P("fsdp"),
            P("fsdp"),
            P("fsdp"),
            P("fsdp", None),
            P("fsdp"),
            P("fsdp", None),
            P("fsdp"),
        ),
        check_vma=False,
    )
```

```python
import functools

import jax
import jax.numpy as jnp
from jax import lax
from jax.experimental import pallas as pl
from jax.experimental.pallas import tpu as pltpu
from jax.sharding import PartitionSpec as P

HEADS = 17
HEAD_DIM = 64


epsilon = 1e-05


def layer_norm(values, gain, shift):
    centred = values - jnp.mean(values, axis=-1, keepdims=True)
    spread = jnp.mean(centred * centred, axis=-1, keepdims=True)
    return centred * lax.rsqrt(spread + epsilon) * gain + shift


def gelu_tanh(values):
    return jax.nn.gelu(values, approximate=True)


def score_grads(
    query_heads, key_heads, value_heads, grad_heads, log_total, row_delta, query_at, key_at
):
    score_scale = HEAD_DIM ** (-0.5)
    scores = (
        jnp.einsum("sqhd,skhd->shqk", query_heads, key_heads, preferred_element_type=jnp.float32)
        * score_scale
    )
    visible = query_at[:, None] >= key_at[None, :]
    shifted = jnp.where(visible, scores - log_total[..., None], -1e30)
    weights = jnp.where(visible, jnp.exp(shifted), 0.0)
    pressure = jnp.einsum(
        "sqhd,skhd->shqk", grad_heads, value_heads, preferred_element_type=jnp.float32
    )
    score_low = (weights * (pressure - row_delta[..., None])).astype(jnp.bfloat16)
    return (weights.astype(jnp.bfloat16), score_low)


def per_device_gathered(
    inputs,
    cotangent,
    first_gain,
    first_shift,
    project_in,
    query_bias,
    value_bias,
    project_out,
    output_bias,
    second_gain,
    second_shift,
    up_weight,
    up_bias,
    down_weight,
    down_bias,
):
    seq_count, block_len, model_width = inputs.shape
    flat_rows = seq_count * block_len
    cycle_size = lax.axis_size("ctx")
    my_block = lax.axis_index("ctx")
    score_scale = HEAD_DIM ** (-0.5)
    head_shape = (seq_count, block_len, HEADS, HEAD_DIM)
    offsets = jnp.arange(block_len, dtype=jnp.int32)
    query_at = my_block * block_len + offsets
    gain_first, shift_first, full_in, qbias_full, vbias_full, full_out, obias_full = (
        lax.all_gather(first_gain, "fsdp", axis=0, tiled=True),
        lax.all_gather(first_shift, "fsdp", axis=0, tiled=True),
        lax.all_gather(project_in, "fsdp", axis=0, tiled=True),
        lax.all_gather(query_bias, "fsdp", axis=0, tiled=True),
        lax.all_gather(value_bias, "fsdp", axis=0, tiled=True),
        lax.all_gather(project_out, "fsdp", axis=0, tiled=True),
        lax.all_gather(output_bias, "fsdp", axis=0, tiled=True),
    )
    rows_in = inputs.astype(jnp.float32).reshape(flat_rows, model_width)
    normed, norm_first_back = jax.vjp(
        layer_norm, rows_in, gain_first.astype(jnp.float32), shift_first.astype(jnp.float32)
    )
    normed_low = normed.astype(jnp.bfloat16)
    projected = jnp.dot(normed_low, full_in, preferred_element_type=jnp.float32)
    queries = (projected[:, :model_width] + qbias_full).astype(jnp.bfloat16)
    key_rows = projected[:, model_width : 2 * model_width].astype(jnp.bfloat16)
    value_rows = (projected[:, 2 * model_width :] + vbias_full).astype(jnp.bfloat16)
    query_heads = queries.reshape(head_shape)
    running_top = jnp.full((seq_count, HEADS, block_len), -1e30, jnp.float32)
    accumulated = jnp.zeros(head_shape, jnp.float32)
    piece_keys = lax.all_gather(
        key_rows.reshape(seq_count, block_len, model_width), "ctx", axis=1, tiled=True
    )
    piece_values = lax.all_gather(
        value_rows.reshape(seq_count, block_len, model_width), "ctx", axis=1, tiled=True
    )
    piece_len = piece_keys.shape[1]
    key_heads = piece_keys.reshape(seq_count, piece_len, HEADS, HEAD_DIM)
    value_heads = piece_values.reshape(seq_count, piece_len, HEADS, HEAD_DIM)
    scores = (
        jnp.einsum("sqhd,skhd->shqk", query_heads, key_heads, preferred_element_type=jnp.float32)
        * score_scale
    )
    key_at = jnp.arange(piece_len, dtype=jnp.int32)
    visible = query_at[:, None] >= key_at[None, :]
    masked = jnp.where(visible, scores, -1e30)
    new_top = jnp.maximum(running_top, jnp.max(masked, axis=-1))
    factor = jnp.exp(running_top - new_top)
    weights = jnp.where(visible, jnp.exp(masked - new_top[..., None]), 0.0)
    row_total = jnp.sum(weights, axis=-1)
    added = jnp.einsum(
        "shqk,skhd->sqhd",
        weights.astype(jnp.bfloat16),
        value_heads,
        preferred_element_type=jnp.float32,
    )
    accumulated = accumulated * jnp.swapaxes(factor, 1, 2)[..., None] + added
    running_top, row_total, accumulated = (new_top, row_total, accumulated)
    attended = accumulated / jnp.swapaxes(row_total, 1, 2)[..., None]
    log_total = running_top + jnp.log(row_total)
    attended_low = attended.reshape(flat_rows, model_width).astype(jnp.bfloat16)
    middle = (
        rows_in + jnp.dot(attended_low, full_out, preferred_element_type=jnp.float32) + obias_full
    )
    gain_second, shift_second, full_up, ubias_full, full_down, dbias_full = (
        lax.all_gather(second_gain, "fsdp", axis=0, tiled=True),
        lax.all_gather(second_shift, "fsdp", axis=0, tiled=True),
        lax.all_gather(up_weight, "fsdp", axis=0, tiled=True),
        lax.all_gather(up_bias, "fsdp", axis=0, tiled=True),
        lax.all_gather(down_weight, "fsdp", axis=0, tiled=True),
        lax.all_gather(down_bias, "fsdp", axis=0, tiled=True),
    )
    normed_two, norm_second_back = jax.vjp(
        layer_norm, middle, gain_second.astype(jnp.float32), shift_second.astype(jnp.float32)
    )
    normed_two_low = normed_two.astype(jnp.bfloat16)
    hidden = jnp.dot(normed_two_low, full_up, preferred_element_type=jnp.float32) + ubias_full
    active, gelu_back = jax.vjp(gelu_tanh, hidden)
    active_low = active.astype(jnp.bfloat16)
    result = (
        middle + jnp.dot(active_low, full_down, preferred_element_type=jnp.float32) + dbias_full
    )
    outputs = result.astype(jnp.bfloat16).reshape(seq_count, block_len, model_width)
    upstream = cotangent.astype(jnp.float32).reshape(flat_rows, model_width)
    upstream_low = upstream.astype(jnp.bfloat16)
    down_grad = jnp.einsum(
        "rf,rd->fd", active_low, upstream_low, preferred_element_type=jnp.float32
    )
    down_bias_grad = jnp.sum(upstream_low.astype(jnp.float32), axis=0)
    active_grad = jnp.einsum(
        "rd,fd->rf", upstream_low, full_down, preferred_element_type=jnp.float32
    )
    (hidden_grad,) = gelu_back(active_grad)
    hidden_low = hidden_grad.astype(jnp.bfloat16)
    up_grad = jnp.einsum(
        "rd,rf->df", normed_two_low, hidden_low, preferred_element_type=jnp.float32
    )
    up_bias_grad = jnp.sum(hidden_low.astype(jnp.float32), axis=0)
    normed_two_grad = jnp.einsum(
        "rf,df->rd", hidden_low, full_up, preferred_element_type=jnp.float32
    )
    middle_part, gain_two_grad, shift_two_grad = norm_second_back(normed_two_grad)
    middle_grad = upstream + middle_part
    middle_low = middle_grad.astype(jnp.bfloat16)
    out_grad = jnp.einsum("rd,re->de", attended_low, middle_low, preferred_element_type=jnp.float32)
    out_bias_grad = jnp.sum(middle_low.astype(jnp.float32), axis=0)
    attended_grad = jnp.einsum(
        "re,de->rd", middle_low, full_out, preferred_element_type=jnp.float32
    )
    grad_low = attended_grad.astype(jnp.bfloat16).reshape(head_shape)
    row_delta = jnp.swapaxes(jnp.sum(grad_low.astype(jnp.float32) * attended, axis=-1), 1, 2)
    gathered_keys, gathered_values = (
        lax.all_gather(
            key_rows.reshape(1, seq_count, block_len, model_width), "ctx", axis=0, tiled=True
        ),
        lax.all_gather(
            value_rows.reshape(1, seq_count, block_len, model_width), "ctx", axis=0, tiled=True
        ),
    )
    block_ids = jnp.arange(cycle_size, dtype=jnp.int32)

    def key_step(carry, inputs_here):
        key_block, value_block, block_index = inputs_here
        key_heads = key_block.reshape(head_shape)
        value_heads = value_block.reshape(head_shape)
        weights_low, score_low = score_grads(
            query_heads,
            key_heads,
            value_heads,
            grad_low,
            log_total,
            row_delta,
            query_at,
            block_index * block_len + offsets,
        )
        carry = (
            carry
            + jnp.einsum(
                "shqk,skhd->sqhd", score_low, key_heads, preferred_element_type=jnp.float32
            )
            * score_scale
        )
        key_term = (
            jnp.einsum(
                "shqk,sqhd->skhd", score_low, query_heads, preferred_element_type=jnp.float32
            )
            * score_scale
        )
        value_term = jnp.einsum(
            "shqk,sqhd->skhd", weights_low, grad_low, preferred_element_type=jnp.float32
        )
        return (
            carry,
            (
                key_term.reshape(seq_count, block_len, model_width),
                value_term.reshape(seq_count, block_len, model_width),
            ),
        )

    query_grad, (key_terms, value_terms) = lax.scan(
        key_step, jnp.zeros(head_shape, jnp.float32), (gathered_keys, gathered_values, block_ids)
    )
    key_sum, value_sum = (
        lax.psum_scatter(
            key_terms.astype(jnp.bfloat16), "ctx", scatter_dimension=0, tiled=True
        ).astype(jnp.float32),
        lax.psum_scatter(
            value_terms.astype(jnp.bfloat16), "ctx", scatter_dimension=0, tiled=True
        ).astype(jnp.float32),
    )
    key_grad = key_sum.reshape(flat_rows, model_width)
    value_grad = value_sum.reshape(flat_rows, model_width)
    query_low = query_grad.reshape(flat_rows, model_width).astype(jnp.bfloat16)
    key_low = key_grad.astype(jnp.bfloat16)
    value_low = value_grad.astype(jnp.bfloat16)
    stacked = jnp.concatenate([query_low, key_low, value_low], axis=1)
    in_grad = jnp.einsum("rd,re->de", normed_low, stacked, preferred_element_type=jnp.float32)
    query_bias_grad = jnp.sum(query_low.astype(jnp.float32), axis=0)
    value_bias_grad = jnp.sum(value_low.astype(jnp.float32), axis=0)
    normed_grad = jnp.einsum("re,de->rd", stacked, full_in, preferred_element_type=jnp.float32)
    input_part, gain_one_grad, shift_one_grad = norm_first_back(normed_grad)
    input_gradient = (middle_grad + input_part).reshape(seq_count, block_len, model_width)
    (
        gain_one_part,
        shift_one_part,
        in_part,
        qbias_part,
        vbias_part,
        out_part,
        obias_part,
        gain_two_part,
        shift_two_part,
        up_part,
        ubias_part,
        down_part,
        dbias_part,
    ) = (
        lax.psum_scatter(
            gain_one_grad.astype(jnp.bfloat16), "fsdp", scatter_dimension=0, tiled=True
        ).astype(jnp.float32),
        lax.psum_scatter(
            shift_one_grad.astype(jnp.bfloat16), "fsdp", scatter_dimension=0, tiled=True
        ).astype(jnp.float32),
        lax.psum_scatter(
            in_grad.astype(jnp.bfloat16), "fsdp", scatter_dimension=0, tiled=True
        ).astype(jnp.float32),
        lax.psum_scatter(
            query_bias_grad.astype(jnp.bfloat16), "fsdp", scatter_dimension=0, tiled=True
        ).astype(jnp.float32),
        lax.psum_scatter(
            value_bias_grad.astype(jnp.bfloat16), "fsdp", scatter_dimension=0, tiled=True
        ).astype(jnp.float32),
        lax.psum_scatter(
            out_grad.astype(jnp.bfloat16), "fsdp", scatter_dimension=0, tiled=True
        ).astype(jnp.float32),
        lax.psum_scatter(
            out_bias_grad.astype(jnp.bfloat16), "fsdp", scatter_dimension=0, tiled=True
        ).astype(jnp.float32),
        lax.psum_scatter(
            gain_two_grad.astype(jnp.bfloat16), "fsdp", scatter_dimension=0, tiled=True
        ).astype(jnp.float32),
        lax.psum_scatter(
            shift_two_grad.astype(jnp.bfloat16), "fsdp", scatter_dimension=0, tiled=True
        ).astype(jnp.float32),
        lax.psum_scatter(
            up_grad.astype(jnp.bfloat16), "fsdp", scatter_dimension=0, tiled=True
        ).astype(jnp.float32),
        lax.psum_scatter(
            up_bias_grad.astype(jnp.bfloat16), "fsdp", scatter_dimension=0, tiled=True
        ).astype(jnp.float32),
        lax.psum_scatter(
            down_grad.astype(jnp.bfloat16), "fsdp", scatter_dimension=0, tiled=True
        ).astype(jnp.float32),
        lax.psum_scatter(
            down_bias_grad.astype(jnp.bfloat16), "fsdp", scatter_dimension=0, tiled=True
        ).astype(jnp.float32),
    )
    (
        gain_one_sum,
        shift_one_sum,
        in_sum,
        qbias_sum,
        vbias_sum,
        out_sum,
        obias_sum,
        gain_two_sum,
        shift_two_sum,
        up_sum,
        ubias_sum,
        down_sum,
        dbias_sum,
    ) = lax.psum(
        (
            gain_one_part,
            shift_one_part,
            in_part,
            qbias_part,
            vbias_part,
            out_part,
            obias_part,
            gain_two_part,
            shift_two_part,
            up_part,
            ubias_part,
            down_part,
            dbias_part,
        ),
        ("dp", "ctx"),
    )
    return (
        outputs,
        input_gradient,
        gain_one_sum,
        shift_one_sum,
        in_sum,
        qbias_sum,
        vbias_sum,
        out_sum,
        obias_sum,
        gain_two_sum,
        shift_two_sum,
        up_sum,
        ubias_sum,
        down_sum,
        dbias_sum,
    )


NT = (((1,), (1,)), ((), ()))
PAIR = 2 * HEAD_DIM


def attend_kernel(place_ref, q_ref, k_ref, v_ref, *refs, count, width, start):
    o_ref, log_ref, keys, values = refs[-4:]
    own_pair = pl.program_id(0)
    pair = own_pair + start
    shift = place_ref[0]
    block_len = q_ref.shape[0] // count
    lane = lax.broadcasted_iota(jnp.int32, (1, PAIR), 1)
    valid = lane + pair * PAIR < width
    first = lane < HEAD_DIM

    def rows(block):
        return pl.ds(pl.multiple_of((block ^ shift) * block_len, block_len), block_len)

    for block in range(count):
        here = pl.ds(block * block_len, block_len)
        keys[here, :] = jnp.where(valid, k_ref[rows(block), :], 0)
        values[here, :] = jnp.where(valid, v_ref[rows(block), :], 0)
    diagonal = lax.broadcasted_iota(jnp.int32, (block_len, block_len), 0) >= (
        lax.broadcasted_iota(jnp.int32, (block_len, block_len), 1)
    )
    for block in range(count):
        seen = (block + 1) * block_len
        before = block * block_len
        queries = q_ref[rows(block), :] * jnp.bfloat16(HEAD_DIM**-0.5)
        parts = []
        logs = log_ref[rows(block), :]
        for half in range(2):
            pick = jnp.logical_and(first if half == 0 else jnp.logical_not(first), valid)
            scores = lax.dot_general(
                jnp.where(pick, queries, 0),
                keys[pl.ds(0, seen), :],
                NT,
                preferred_element_type=jnp.float32,
            )
            last = jnp.where(diagonal, scores[:, before:], -1e30)
            scores = last if block == 0 else jnp.concatenate([scores[:, :before], last], axis=1)
            top = jnp.max(scores, axis=1, keepdims=True)
            weights = jnp.exp(scores - top)
            total = jnp.sum(weights, axis=1, keepdims=True)
            added = jnp.dot(
                weights.astype(jnp.bfloat16),
                values[pl.ds(0, seen), :],
                preferred_element_type=jnp.float32,
            )
            parts.append(added / total)
            logs = jnp.where(lane == 2 * own_pair + half, top + jnp.log(total), logs)
        o_ref[rows(block), :] = jnp.where(first, parts[0], parts[1]).astype(jnp.bfloat16)
        log_ref[rows(block), :] = logs


def attend_back_kernel(
    place_ref,
    q_ref,
    k_ref,
    v_ref,
    g_ref,
    o_ref,
    log_ref,
    *refs,
    count,
    width,
    start,
):
    dq_ref, dk_ref, dv_ref, queries, grads, keys, values = refs[-11:-4]
    keys_turned, logs, deltas, turned = refs[-4:]
    pair = pl.program_id(0) + start
    shift = place_ref[0]
    length = q_ref.shape[0]
    block_len = length // count
    lane = lax.broadcasted_iota(jnp.int32, (1, PAIR), 1)
    valid = lane + pair * PAIR < width
    first = lane < HEAD_DIM
    picks = (jnp.logical_and(first, valid), jnp.logical_and(jnp.logical_not(first), valid))
    half_of = (lax.broadcasted_iota(jnp.int32, (8, PAIR), 1) // HEAD_DIM) == (
        lax.broadcasted_iota(jnp.int32, (8, PAIR), 0)
    )
    ones_of = jnp.where(half_of, 1.0, 0.0)

    def rows(block):
        return pl.ds(pl.multiple_of((block ^ shift) * block_len, block_len), block_len)

    for block in range(count):
        here = pl.ds(block * block_len, block_len)
        key_block = jnp.where(valid, k_ref[rows(block), :], 0)
        keys[here, :] = key_block
        keys_turned[:, here] = key_block.astype(jnp.float32).T.astype(jnp.bfloat16)
        values[here, :] = jnp.where(valid, v_ref[rows(block), :], 0)
        query_block = q_ref[rows(block), :] * jnp.bfloat16(HEAD_DIM**-0.5)
        grad_block = jnp.where(valid, g_ref[rows(block), :], 0)
        for half in range(2):
            queries[half, here, :] = jnp.where(picks[half], query_block, 0)
            grads[half, here, :] = jnp.where(picks[half], grad_block, 0)
        mixed = grad_block.astype(jnp.float32) * jnp.where(
            valid, o_ref[rows(block), :], 0
        ).astype(jnp.float32)
        deltas[:, here] = lax.dot_general(
            ones_of,
            mixed,
            NT,
            preferred_element_type=jnp.float32,
            precision=lax.Precision.HIGHEST,
        )
        logs[:, here] = log_ref[
            0, :, pl.ds(pl.multiple_of((block ^ shift) * block_len, block_len), block_len)
        ]
    diagonal = lax.broadcasted_iota(jnp.int32, (block_len, block_len), 0) <= (
        lax.broadcasted_iota(jnp.int32, (block_len, block_len), 1)
    )
    for block in range(count):
        here = pl.ds(block * block_len, block_len)
        after = pl.ds(block * block_len, length - block * block_len)
        key_total = jnp.zeros((block_len, PAIR), jnp.float32)
        value_total = jnp.zeros((block_len, PAIR), jnp.float32)
        for half in range(2):
            scores = lax.dot_general(
                keys[here, :], queries[half, after, :], NT, preferred_element_type=jnp.float32
            )
            shifted = scores - logs[half : half + 1, after]
            own = jnp.where(diagonal, shifted[:, :block_len], -1e30)
            if block < count - 1:
                own = jnp.concatenate([own, shifted[:, block_len:]], axis=1)
            weights = jnp.exp(own)
            pressure = lax.dot_general(
                values[here, :], grads[half, after, :], NT, preferred_element_type=jnp.float32
            )
            score_low = (weights * (pressure - deltas[half : half + 1, after])).astype(
                jnp.bfloat16
            )
            value_total += jnp.dot(
                weights.astype(jnp.bfloat16),
                grads[half, after, :],
                preferred_element_type=jnp.float32,
            )
            key_total += jnp.dot(
                score_low, queries[half, after, :], preferred_element_type=jnp.float32
            )
            part = pl.ds(half * HEAD_DIM, HEAD_DIM)
            term = jnp.dot(
                keys_turned[part, here], score_low, preferred_element_type=jnp.float32
            )
            if block == 0:
                turned[part, after] = term
            else:
                turned[part, after] += term
        dk_ref[rows(block), :] = key_total.astype(jnp.bfloat16)
        dv_ref[rows(block), :] = value_total.astype(jnp.bfloat16)
    for block in range(count):
        here = pl.ds(block * block_len, block_len)
        dq_ref[rows(block), :] = (turned[:, here].T * HEAD_DIM**-0.5).astype(jnp.bfloat16)


def attend(place, queries, key_rows, value_rows, count, start, pairs, before):
    length, width = queries.shape
    heads_block = pl.BlockSpec((length, PAIR), lambda pair, place_ref: (0, pair + start))
    return pl.pallas_call(
        functools.partial(attend_kernel, count=count, width=width, start=start),
        grid_spec=pltpu.PrefetchScalarGridSpec(
            num_scalar_prefetch=1,
            grid=(pairs,),
            in_specs=[heads_block] * 3 + [pl.BlockSpec(memory_space=pl.ANY)] * len(before),
            out_specs=[
                heads_block,
                pl.BlockSpec((length, 128), lambda pair, place_ref: (0, 0)),
            ],
            scratch_shapes=[pltpu.VMEM((length, PAIR), jnp.bfloat16)] * 2,
        ),
        out_shape=[
            jax.ShapeDtypeStruct((length, width), jnp.bfloat16),
            jax.ShapeDtypeStruct((length, 128), jnp.float32),
        ],
        input_output_aliases={4 + at: at for at in range(len(before))},
        compiler_params=pltpu.CompilerParams(vmem_limit_bytes=48 * 2**20),
        cost_estimate=pl.CostEstimate(
            flops=4 * length * length * PAIR * pairs * 4,
            bytes_accessed=8 * length * PAIR * pairs,
            transcendentals=length * length * pairs,
        ),
        name="attend",
    )(place, queries, key_rows, value_rows, *before)


def attend_back(
    place, queries, key_rows, value_rows, grads, attended, logs, count, start, pairs, before
):
    length, width = queries.shape
    heads_block = pl.BlockSpec((length, PAIR), lambda pair, place_ref: (0, pair + start))
    low_rows = pltpu.VMEM((length, PAIR), jnp.bfloat16)
    low_pair = pltpu.VMEM((2, length, PAIR), jnp.bfloat16)
    return pl.pallas_call(
        functools.partial(attend_back_kernel, count=count, width=width, start=start),
        grid_spec=pltpu.PrefetchScalarGridSpec(
            num_scalar_prefetch=1,
            grid=(pairs,),
            in_specs=[heads_block] * 5
            + [pl.BlockSpec((1, 2, length), lambda pair, place_ref: (pair, 0, 0))]
            + [pl.BlockSpec(memory_space=pl.ANY)] * len(before),
            out_specs=[heads_block] * 3,
            scratch_shapes=[
                low_pair,
                low_pair,
                low_rows,
                low_rows,
                pltpu.VMEM((PAIR, length), jnp.bfloat16),
                pltpu.VMEM((2, length), jnp.float32),
                pltpu.VMEM((8, length), jnp.float32),
                pltpu.VMEM((PAIR, length), jnp.float32),
            ],
        ),
        out_shape=[jax.ShapeDtypeStruct((length, width), jnp.bfloat16)] * 3,
        input_output_aliases={7 + at: at for at in range(len(before))},
        compiler_params=pltpu.CompilerParams(vmem_limit_bytes=48 * 2**20),
        cost_estimate=pl.CostEstimate(
            flops=10 * length * length * PAIR * pairs * 3,
            bytes_accessed=16 * length * PAIR * pairs,
            transcendentals=length * length * pairs,
        ),
        name="attend_back",
    )(place, queries, key_rows, value_rows, grads, attended, logs, *before)


def settle_kernel(place_ref, *refs):
    pieces, out_ref = refs[:-1], refs[-1]
    for at, piece in enumerate(pieces):
        out_ref[place_ref[at]] = piece[...].astype(out_ref.dtype)


def settle(places, pieces, dtype):
    return pl.pallas_call(
        settle_kernel,
        in_specs=[pl.BlockSpec(memory_space=pltpu.SMEM)]
        + [pl.BlockSpec(memory_space=pltpu.VMEM)] * len(pieces),
        out_specs=pl.BlockSpec(memory_space=pltpu.VMEM),
        out_shape=jax.ShapeDtypeStruct((len(pieces),) + pieces[0].shape, dtype),
        compiler_params=pltpu.CompilerParams(vmem_limit_bytes=48 * 2**20),
        name="settle",
    )(places, *pieces)


def plane_partner(device, kind):
    core = device & 1
    if kind == "core":
        return device ^ 1
    if kind == "far":
        return device ^ (3 if core else 5)
    if kind == "near":
        return device ^ (2 if core else 4)
    return device ^ (4 if core else 2)


def plane_swap(values, kind):
    return lax.ppermute(
        values, ("dp", "ctx"), [(device, plane_partner(device, kind)) for device in range(8)]
    )


def ctx_swap(values, bits):
    return lax.ppermute(values, "ctx", [(device, device ^ bits) for device in range(4)])


def low_sum(*terms):
    return sum(term.astype(jnp.float32) for term in terms).astype(jnp.bfloat16)


def reduce_core(pieces):
    return plane_swap(pieces[2], "core"), plane_swap(pieces[3], "core")


def share_out(whole):
    return [whole] + [plane_swap(whole, kind) for kind in ("near", "core", "far")]


def share_by_core(whole):
    near = plane_swap(whole, "near")
    return [whole, near, plane_swap(whole, "core"), plane_swap(near, "core")]


def scatter_rows(values):
    return lax.psum_scatter(values, "fsdp", scatter_dimension=0, tiled=True)


def chosen(index, options):
    result = options[-1]
    for at in range(len(options) - 2, -1, -1):
        result = jnp.where(index == at, options[at], result)
    return result


def gather_vector(values, z):
    around = [values] + [
        lax.ppermute(values, "fsdp", [(device, (device + step) % 4) for device in range(4)])
        for step in range(1, 4)
    ]
    return jnp.stack([chosen((z - at) % 4, around) for at in range(4)])


def scatter_vector(values, z):
    rows = [values[at] for at in range(4)]
    total = chosen(z, rows)
    for step in range(1, 4):
        total = total + lax.ppermute(
            chosen((z + step) % 4, rows),
            "fsdp",
            [(device, (device + step) % 4) for device in range(4)],
        )
    return total


def swap_sum(total, bits):
    return total + lax.ppermute(
        total, ("dp", "ctx"), [(device, device ^ bits) for device in range(8)]
    )


def product(left, right, dims):
    return lax.dot_general(left, right, ((dims[:1], dims[1:]), ((), ())),
                           preferred_element_type=jnp.float32)


def gelu_pair(values):
    inner = 0.7978845608028654
    cubic = inner * 0.044715
    squared = values * values
    curve = jnp.tanh(values * (inner + cubic * squared))
    half = 0.5 * values
    active = half + half * curve
    slope = 0.5 + 0.5 * curve + half * (1.0 - curve * curve) * (inner + 3.0 * cubic * squared)
    return active, slope


def block_flops(rows, width, count):
    return pl.CostEstimate(
        flops=2 * rows * width * width * count,
        bytes_accessed=2 * width * width * count + 4 * rows * width * count,
        transcendentals=0,
    )


def unit_of(values):
    centred = values - jnp.mean(values, axis=-1, keepdims=True)
    scale = lax.rsqrt(jnp.mean(centred * centred, axis=-1, keepdims=True) + epsilon)
    return centred * scale, scale


def fold(values):
    rows, width = values.shape
    return jnp.sum(values.reshape(rows // 8, 8, width), axis=0)


def front_kernel(places_ref, vectors_ref, *refs):
    slots, pieces = refs[:4], refs[4:20]
    x_ref, h_ref, q_ref, k_ref, v_ref, all_ref, weights, arrived, left = refs[20:]
    copies = [
        pltpu.make_async_copy(piece, weights.at[places_ref[at]], arrived.at[at])
        for at, piece in enumerate(pieces)
    ]
    for copy in copies:
        copy.start()
    rows, width = x_ref.shape
    step = rows // 4
    for at, slot in enumerate(slots):
        here = pl.ds(at * step, step)
        values = slot[...].astype(jnp.float32).T
        x_ref[here, :] = values.astype(jnp.bfloat16)
        unit, _ = unit_of(values)
        h_ref[here, :] = (unit * vectors_ref[0:1, :] + vectors_ref[1:2, :]).astype(jnp.bfloat16)
    for copy in copies:
        copy.wait()
    leave = pltpu.make_async_copy(weights, all_ref, left)
    leave.start()
    for section, out_ref in enumerate((q_ref, k_ref, v_ref)):

        def multiply(at, carry, section=section, out_ref=out_ref):
            here = pl.ds(pl.multiple_of(at * step, step), step)
            matrix = weights[4 * section : 4 * section + 4].reshape(width, width)
            total = jnp.dot(h_ref[here, :], matrix, preferred_element_type=jnp.float32)
            if section != 1:
                row = 2 if section == 0 else 3
                total = total + vectors_ref[row : row + 1, :]
            out_ref[here, :] = total.astype(jnp.bfloat16)
            return carry

        lax.fori_loop(0, rows // step, multiply, 0)
    leave.wait()


def front(places, slots, vectors, pieces):
    width, step = slots[0].shape
    rows = 4 * step
    vmem = pl.BlockSpec(memory_space=pltpu.VMEM)
    hbm = pl.BlockSpec(memory_space=pl.ANY)
    shape = jax.ShapeDtypeStruct((rows, width), jnp.bfloat16)
    whole = (16,) + pieces[0].shape
    return pl.pallas_call(
        front_kernel,
        in_specs=[pl.BlockSpec(memory_space=pltpu.SMEM)] + [vmem] * 5 + [hbm] * 16,
        out_specs=[vmem] * 5 + [hbm],
        out_shape=[shape] * 5 + [jax.ShapeDtypeStruct(whole, jnp.bfloat16)],
        scratch_shapes=[
            pltpu.VMEM(whole, jnp.bfloat16),
            pltpu.SemaphoreType.DMA((16,)),
            pltpu.SemaphoreType.DMA,
        ],
        compiler_params=pltpu.CompilerParams(vmem_limit_bytes=56 * 2**20),
        cost_estimate=block_flops(rows, width, 3),
        name="front",
    )(places, vectors, *slots, *pieces)


def turn_kernel(*refs):
    slots, out_ref = refs[:-1], refs[-1]
    step = slots[0].shape[1]
    for at, slot in enumerate(slots):
        out_ref[pl.ds(at * step, step), :] = (
            slot[...].astype(jnp.float32).T.astype(jnp.bfloat16)
        )


def turn(slots):
    width, step = slots[0].shape
    return pl.pallas_call(
        turn_kernel,
        out_shape=jax.ShapeDtypeStruct((len(slots) * step, width), jnp.bfloat16),
        compiler_params=pltpu.CompilerParams(vmem_limit_bytes=48 * 2**20),
        name="turn",
    )(*slots)


def assemble_kernel(place_ref, *refs, plan):
    pieces, outs = refs[:4], refs[4:]
    for at, piece in enumerate(pieces):
        for kind, moves in enumerate(plan):

            @pl.when(place_ref[at] == kind)
            def _(piece=piece, moves=moves):
                for out, source, target, size in moves:
                    outs[out][:, target : target + size] = piece[
                        :, source : source + size
                    ].astype(jnp.float32)


def assemble(places, pieces, plan, shapes):
    vmem = pl.BlockSpec(memory_space=pltpu.VMEM)
    return pl.pallas_call(
        functools.partial(assemble_kernel, plan=plan),
        in_specs=[pl.BlockSpec(memory_space=pltpu.SMEM)] + [vmem] * 4,
        out_specs=[vmem] * len(shapes),
        out_shape=[jax.ShapeDtypeStruct(shape, jnp.float32) for shape in shapes],
        compiler_params=pltpu.CompilerParams(vmem_limit_bytes=48 * 2**20),
        name="assemble",
    )(places, *pieces)


def store_turned(step, refs, values):
    size = refs[0].shape[1]
    share = values.shape[0] // size
    for at, ref in enumerate(refs):

        @pl.when(step == at // share)
        def _(at=at, ref=ref):
            first = (at % share) * size
            ref[...] = values[first : first + size].T.astype(ref.dtype)


def fetch(step, copies):
    @pl.when(step == 0)
    def _():
        for copy in copies:
            copy.start()


def arrive(step, copy):
    @pl.when(step == 0)
    def _():
        copy.wait()


def middle_kernel(x_ref, o_ref, vectors_ref, all_ref, middle_ref, h_ref, weights, arrived):
    step = pl.program_id(0)
    width = x_ref.shape[1]
    copy = pltpu.make_async_copy(all_ref.at[pl.ds(12, 4)], weights, arrived)
    fetch(step, [copy])
    arrive(step, copy)
    middle = (
        x_ref[...].astype(jnp.float32)
        + jnp.dot(
            o_ref[...], weights[...].reshape(width, width), preferred_element_type=jnp.float32
        )
        + vectors_ref[0:1, :]
    )
    middle_ref[...] = middle
    unit, _ = unit_of(middle)
    h_ref[...] = (unit * vectors_ref[1:2, :] + vectors_ref[2:3, :]).astype(jnp.bfloat16)


def up_kernel(h_ref, biases_ref, *refs):
    sources = refs[:2]
    active_refs, slope_refs = refs[2:4], refs[4:6]
    weights, arrived = refs[6:]
    step = pl.program_id(0)
    copies = [
        pltpu.make_async_copy(source, weights.at[at], arrived.at[at])
        for at, source in enumerate(sources)
    ]
    fetch(step, copies)
    for at in range(2):
        arrive(step, copies[at])
        hidden = (
            jnp.dot(h_ref[...], weights[at], preferred_element_type=jnp.float32)
            + biases_ref[at : at + 1, :]
        )
        active, slope = gelu_pair(hidden)
        active_refs[at][...] = active.astype(jnp.bfloat16)
        slope_refs[at][...] = slope.astype(jnp.bfloat16)


def down_kernel(middle_ref, vectors_ref, *refs):
    actives, sources = refs[:4], refs[4:8]
    out_refs = refs[8:12]
    weights, arrived = refs[12:]
    step = pl.program_id(0)
    copies = [
        pltpu.make_async_copy(source, weights.at[at], arrived.at[at])
        for at, source in enumerate(sources)
    ]
    fetch(step, copies)
    total = middle_ref[...] + vectors_ref[0:1, :]
    for at in range(4):
        arrive(step, copies[at])
        total = total + jnp.dot(
            actives[at][...], weights[at], preferred_element_type=jnp.float32
        )
    store_turned(step, out_refs, total)


def norm_back(values, gain, grad):
    unit, scale = unit_of(values)
    turned = grad * gain
    inner = (
        turned
        - jnp.mean(turned, axis=-1, keepdims=True)
        - unit * jnp.mean(turned * unit, axis=-1, keepdims=True)
    )
    return scale * inner, grad * unit


def hidden_kernel(g_ref, *refs):
    slopes, sources = refs[:2], refs[2:4]
    hidden_refs, sums_ref = refs[4:6], refs[6]
    weights, arrived = refs[7:]
    step = pl.program_id(0)
    copies = [
        pltpu.make_async_copy(source, weights.at[at], arrived.at[at])
        for at, source in enumerate(sources)
    ]
    fetch(step, copies)

    @pl.when(step == 0)
    def _():
        sums_ref[...] = jnp.zeros_like(sums_ref)

    upstream = g_ref[...]
    for at in range(2):
        arrive(step, copies[at])
        hidden = lax.dot_general(
            upstream, weights[at], NT, preferred_element_type=jnp.float32
        )
        hidden = (hidden * slopes[at][...].astype(jnp.float32)).astype(jnp.bfloat16)
        hidden_refs[at][...] = hidden
        sums_ref[at] += fold(hidden.astype(jnp.float32))
    sums_ref[2] += fold(upstream.astype(jnp.float32))


def back_kernel(g_ref, middle_ref, vectors_ref, *refs):
    hiddens, sources, all_ref = refs[:4], refs[4:8], refs[8]
    grad_ref, low_ref, out_ref, sums_ref = refs[9:13]
    weights, out_weights, arrived = refs[13:]
    step = pl.program_id(0)
    width = middle_ref.shape[1]
    copies = [
        pltpu.make_async_copy(source, weights.at[at], arrived.at[at])
        for at, source in enumerate(sources)
    ] + [pltpu.make_async_copy(all_ref.at[pl.ds(12, 4)], out_weights, arrived.at[4])]
    fetch(step, copies)

    @pl.when(step == 0)
    def _():
        sums_ref[...] = jnp.zeros_like(sums_ref)

    total = jnp.zeros(middle_ref.shape, jnp.float32)
    for at in range(4):
        arrive(step, copies[at])
        total = total + lax.dot_general(
            hiddens[at][...], weights[at], NT, preferred_element_type=jnp.float32
        )
    part, gain_term = norm_back(middle_ref[...], vectors_ref[0:1, :], total)
    sums_ref[0] += fold(gain_term)
    sums_ref[1] += fold(total)
    grad = g_ref[...].astype(jnp.float32) + part
    grad_ref[...] = grad
    grad_low = grad.astype(jnp.bfloat16)
    low_ref[...] = grad_low
    sums_ref[2] += fold(grad_low.astype(jnp.float32))
    arrive(step, copies[4])
    out_ref[...] = lax.dot_general(
        grad_low,
        out_weights[...].reshape(width, width),
        NT,
        preferred_element_type=jnp.float32,
    ).astype(jnp.bfloat16)


def last_kernel(q_ref, k_ref, v_ref, x_ref, grad_ref, vectors_ref, all_ref, *refs):
    out_refs = refs[:4]
    sums_ref, weights, arrived = refs[4:]
    step = pl.program_id(0)
    width = x_ref.shape[1]
    copies = [
        pltpu.make_async_copy(
            all_ref.at[pl.ds(4 * at, 4)], weights.at[pl.ds(4 * at, 4)], arrived.at[at]
        )
        for at in range(3)
    ]
    fetch(step, copies)
    total = jnp.zeros(x_ref.shape, jnp.float32)
    for at, ref in enumerate((q_ref, k_ref, v_ref)):
        arrive(step, copies[at])
        total = total + lax.dot_general(
            ref[...],
            weights[4 * at : 4 * at + 4].reshape(width, width),
            NT,
            preferred_element_type=jnp.float32,
        )
    part, gain_term = norm_back(x_ref[...].astype(jnp.float32), vectors_ref[0:1, :], total)
    store_turned(step, out_refs, grad_ref[...] + part)

    @pl.when(step == 0)
    def _():
        sums_ref[...] = jnp.zeros_like(sums_ref)

    terms = (
        gain_term,
        total,
        q_ref[...].astype(jnp.float32),
        v_ref[...].astype(jnp.float32),
    )
    for at, term in enumerate(terms):
        sums_ref[at] += fold(term)


def by_rows(kernel, name, rows, width, tiled, whole, remote, outs, sums, scratch, sems, blocks):
    step = 512
    tile = pl.BlockSpec((step, width), lambda at: (at, 0))
    out_specs, out_shape = [], []
    for dtype in outs:
        if dtype is None:
            out_specs += [pl.BlockSpec((width, rows // 4), lambda at: (0, 0))] * 4
            out_shape += [jax.ShapeDtypeStruct((width, rows // 4), jnp.bfloat16)] * 4
        else:
            out_specs.append(tile)
            out_shape.append(jax.ShapeDtypeStruct((rows, width), dtype))
    if sums:
        out_specs.append(pl.BlockSpec((sums, 8, width), lambda at: (0, 0, 0)))
        out_shape.append(jax.ShapeDtypeStruct((sums, 8, width), jnp.float32))
    return pl.pallas_call(
        kernel,
        grid=(rows // step,),
        in_specs=[tile] * len(tiled[0])
        + [pl.BlockSpec(value.shape, lambda at: (0, 0)) for value in whole]
        + [tile] * len(tiled[1])
        + [pl.BlockSpec(memory_space=pl.ANY)] * len(remote),
        out_specs=out_specs,
        out_shape=out_shape,
        scratch_shapes=[pltpu.VMEM(shape, jnp.bfloat16) for shape in scratch]
        + [pltpu.SemaphoreType.DMA((sems,)) if sems > 1 else pltpu.SemaphoreType.DMA],
        compiler_params=pltpu.CompilerParams(vmem_limit_bytes=60 * 2**20),
        cost_estimate=block_flops(rows, width, blocks),
        name=name,
    )(*tiled[0], *whole, *tiled[1], *remote)


def per_device_exchanged(
    inputs,
    cotangent,
    first_gain,
    first_shift,
    project_in,
    query_bias,
    value_bias,
    project_out,
    output_bias,
    second_gain,
    second_shift,
    up_weight,
    up_bias,
    down_weight,
    down_bias,
):
    seq_count, block_len, width = inputs.shape
    low = jnp.bfloat16
    wide = jnp.float32
    c = lax.axis_index("ctx")
    y = lax.axis_index("dp")
    z = lax.axis_index("fsdp")
    core = c & 1
    x = c >> 1
    mine = core * 2 + jnp.where(core == 0, y, x)
    across = (1 - core) * 2 + jnp.where(core == 0, x, y)
    classes = [mine, mine ^ 1, across, across ^ 1]
    slot_of = [
        chosen(0, [sum(at * (classes[at] == kind).astype(jnp.int32) for at in range(4))])
        for kind in range(4)
    ]
    quarter = width // 4
    rows, area = seq_count * block_len, (width, width)
    pin = lax.optimization_barrier
    place = jnp.stack([c])
    places = jnp.stack([c ^ at for at in range(4)])
    class_places = jnp.stack(classes)

    def spread(values):
        values = jnp.swapaxes(values, 1, 2)
        return [lax.dynamic_index_in_dim(values, c, 0, keepdims=False)] + [
            ctx_swap(lax.dynamic_index_in_dim(values, c ^ bits, 0, keepdims=False), bits)
            for bits in range(1, 4)
        ]

    def exchange(pieces):
        return [pieces[0]] + [ctx_swap(pieces[bits], bits) for bits in range(1, 4)]

    def collect(moved, dtype):
        return jnp.swapaxes(settle(places, moved, dtype), 1, 2)

    sections = [
        project_in[:, :width],
        project_in[:, width : 2 * width],
        project_in[:, 2 * width :],
        project_out,
    ]
    section = chosen(mine, sections)
    section, inputs = pin((section, inputs))
    shards = [
        lax.ppermute(section, "fsdp", [(device, (device + step) % 4) for device in range(4)])
        for step in range(1, 4)
    ]
    turned_in = jnp.swapaxes(inputs, 1, 2)
    slots_in = [
        lax.dynamic_index_in_dim(turned_in, c ^ bits, 0, keepdims=False) for bits in range(4)
    ]
    pieces_in = (
        first_gain,
        first_shift,
        query_bias,
        value_bias,
        output_bias,
        second_gain,
        second_shift,
        down_bias,
        up_bias,
    )
    slots_in[3], up_weight, down_weight, *pieces_in = pin(
        (slots_in[3], up_weight, down_weight, *pieces_in)
    )
    slots_in = [slots_in[0]] + [ctx_swap(slots_in[bits], bits) for bits in range(1, 4)]
    vectors = gather_vector(jnp.concatenate(pieces_in), z).astype(wide)
    up_piece = jnp.concatenate(
        [
            lax.dynamic_slice_in_dim(up_weight, at * width + mine * quarter, quarter, 1)
            for at in range(4)
        ],
        axis=1,
    )
    up_piece, vectors, *moved = pin((up_piece, vectors, *shards, *slots_in))
    shards, slots_in = moved[:3], moved[3:]
    near_shards = [plane_swap(shard, "near") for shard in shards]
    cotangent, *near_shards = pin((cotangent, *near_shards))
    slots_back = spread(cotangent)
    around = (
        sections
        + shards
        + near_shards
        + [plane_swap(shard, "core") for shard in shards]
        + [plane_swap(shard, "core") for shard in near_shards]
    )
    around_places = jnp.stack(
        [kind * 4 + z for kind in range(4)]
        + [kind * 4 + (z - step) % 4 for kind in classes for step in range(1, 4)]
    )
    up_own = lax.all_gather(up_piece, "fsdp", axis=0, tiled=True)
    down_piece = lax.dynamic_slice_in_dim(down_weight, mine * quarter, quarter, 0)
    gain_first, shift_first, qbias, vbias, obias, gain_second, shift_second, dbias = (
        vectors[:, at * quarter : (at + 1) * quarter].reshape(1, width) for at in range(8)
    )
    ubias = vectors[:, 8 * quarter :].reshape(4, 4, quarter)
    ubias = jnp.concatenate(
        [
            chosen(kind, [ubias[:, at] for at in range(4)]).reshape(1, width)
            for kind in classes
        ],
        axis=0,
    )

    rows_in, normed_low, queries, key_rows, value_rows, weights = front(
        around_places,
        slots_in,
        jnp.concatenate([gain_first, shift_first, qbias, vbias], axis=0),
        around,
    )
    slots_back[0], up_own, queries = pin((slots_back[0], up_own, queries))
    upstream_low = turn(slots_back)
    up_near, up_core = plane_swap(up_own, "near"), plane_swap(up_own, "core")
    attended, logs = attend(place, queries, key_rows, value_rows, seq_count, 0, 9, [])
    down_piece, up_core, up_near, attended = pin((down_piece, up_core, up_near, attended))
    down_own = lax.all_gather(down_piece, "fsdp", axis=0, tiled=True)
    logs = logs.T.reshape(64, 2, rows)
    logs_one, logs_two = logs[:5], logs[5:9]
    middle, normed_two_low = by_rows(
        middle_kernel,
        "middle",
        rows,
        width,
        ([rows_in, attended], []),
        [jnp.concatenate([obias, gain_second, shift_second], axis=0)],
        [weights],
        [wide, low],
        0,
        [(4,) + section.shape],
        1,
        1,
    )
    up_slots = [up_own, up_near, up_core, plane_swap(up_near, "core")]
    active, slopes = [None] * 4, [None] * 4

    def up(first):
        outs = by_rows(
            up_kernel,
            "up",
            rows,
            width,
            ([normed_two_low], []),
            [jnp.concatenate([ubias[first : first + 1], ubias[first + 2 : first + 3]], axis=0)],
            [up_slots[first], up_slots[first + 2]],
            [low] * 4,
            0,
            [(2,) + area],
            2,
            2,
        )
        active[first], active[first + 2], slopes[first], slopes[first + 2] = outs

    up(0)
    up_slots[3], active[0], active[2] = pin((up_slots[3], active[0], active[2]))
    up(1)
    down_own, *active = pin((down_own, *active))
    down_near, down_core = plane_swap(down_own, "near"), plane_swap(down_own, "core")

    def turned_product(left, right):
        return product(left, right, (0, 0)).astype(low)

    down_terms = [turned_product(active[slot], upstream_low) for slot in (3, 2)]
    upstream_low, *down_terms = pin((upstream_low, *down_terms))
    down_terms += [turned_product(active[slot], upstream_low) for slot in (1, 0)]
    down_terms = down_terms[::-1]
    down_far, down_far_two = reduce_core(down_terms)
    upstream_low, *down_terms = pin((upstream_low, *down_terms))
    hidden_low = [None] * 4

    def hidden(first, upstream):
        hidden_low[first], hidden_low[first + 2], sums = by_rows(
            hidden_kernel,
            "hidden",
            rows,
            width,
            ([upstream], [slopes[first], slopes[first + 2]]),
            [],
            [down_slots[first], down_slots[first + 2]],
            [low] * 2,
            3,
            [(2,) + area],
            2,
            2,
        )
        return sums

    down_near, upstream_low = pin((down_near, upstream_low))
    down_slots = [down_own, down_near, down_core, plane_swap(down_near, "core")]
    sums_even = hidden(0, upstream_low)
    upstream_late, sums_even = pin((upstream_low, sums_even))
    sums_odd = hidden(1, upstream_late)
    hidden_sums = jnp.stack(
        [sums_even[0], sums_odd[0], sums_even[1], sums_odd[1], sums_even[2]]
    )
    down_second = low_sum(down_terms[1], down_far_two)
    down_second, down_far, *hidden_low = pin((down_second, down_far, *hidden_low))
    down_close = plane_swap(down_second, "near")
    up_terms = [turned_product(normed_two_low, hidden_low[slot]) for slot in (3, 2)]
    down_first = low_sum(down_terms[0], down_far, down_close)
    normed_two_low, down_first, *up_terms = pin((normed_two_low, down_first, *up_terms))
    down_shard = scatter_rows(down_first)
    up_terms += [turned_product(normed_two_low, hidden_low[slot]) for slot in (1, 0)]
    up_terms = up_terms[::-1]
    up_far, up_far_two = reduce_core(up_terms)
    up_second = low_sum(up_terms[1], up_far_two)
    up_second, up_far, moved, *hidden_low = pin((up_second, up_far, up_terms[0], *hidden_low))
    up_terms[0] = moved
    up_close = plane_swap(up_second, "near")
    middle_grad, middle_low, grad_low, back_sums = by_rows(
        back_kernel,
        "back",
        rows,
        width,
        ([upstream_low, middle], hidden_low),
        [gain_second],
        up_slots + [weights],
        [wide, low, low],
        3,
        [(4,) + area, (4,) + section.shape],
        5,
        5,
    )
    out_term = turned_product(attended, middle_low)
    up_first = low_sum(up_terms[0], up_far, up_close)
    grad_low, out_term, up_first = pin((grad_low, out_term, up_first))
    in_grads = attend_back(
        place, queries, key_rows, value_rows, grad_low, attended, logs_one, seq_count, 0, 5, []
    )
    up_first, down_shard, *in_grads = pin((up_first, down_shard, *in_grads))
    up_shard = scatter_rows(up_first)
    down_whole = low_sum(down_shard, plane_swap(down_shard, "other"))
    in_grads = attend_back(
        place,
        queries,
        key_rows,
        value_rows,
        grad_low,
        attended,
        logs_two,
        seq_count,
        5,
        4,
        in_grads,
    )
    down_whole, *in_grads = pin((down_whole, *in_grads))
    down_parts = share_by_core(down_whole)
    in_terms = [turned_product(normed_low, grad) for grad in in_grads]
    section_grads = in_terms + [out_term]
    sections_mine = [chosen(kind, section_grads) for kind in classes]
    far, far_two = reduce_core(sections_mine)
    second = low_sum(sections_mine[1], far_two)
    second, far, middle, *in_grads = pin((second, far, middle, *in_grads))
    query_low, key_low, value_low = in_grads
    close = plane_swap(second, "near")
    result_slots = by_rows(
        down_kernel,
        "down",
        rows,
        width,
        ([middle], active),
        [dbias],
        down_slots,
        [None],
        0,
        [(4,) + area],
        4,
        4,
    )
    first = low_sum(sections_mine[0], far, close)
    first, up_shard, query_low, *result_slots = pin(
        (first, up_shard, query_low, *result_slots)
    )
    shard = scatter_rows(first)
    outputs = exchange(result_slots)
    up_whole = low_sum(up_shard, plane_swap(up_shard, "other"))
    *input_slots, last_sums = by_rows(
        last_kernel,
        "last",
        rows,
        width,
        ([query_low, key_low, value_low, rows_in, middle_grad], []),
        [gain_first],
        [weights],
        [None],
        4,
        [(12,) + section.shape],
        3,
        3,
    )
    moved = pin((*input_slots, *outputs, *down_parts))
    input_slots, outputs, down_parts = exchange(moved[:4]), moved[4:8], moved[8:]

    back_sums = jnp.concatenate([hidden_sums, back_sums], axis=0)
    back_sums = jnp.sum(back_sums, axis=1)
    last_sums = jnp.sum(last_sums, axis=1)
    hidden_sums = [back_sums[slot].reshape(4, quarter) for slot in range(4)]
    hidden_sums = jnp.stack(
        [chosen(slot_of[kind], hidden_sums) for kind in range(4)], axis=1
    ).reshape(4, 4 * quarter)
    totals = swap_sum(
        scatter_vector(
            jnp.concatenate(
                [back_sums[at].reshape(4, quarter) for at in range(4, 8)]
                + [last_sums[at].reshape(4, quarter) for at in range(4)]
                + [hidden_sums],
                axis=1,
            ),
            z,
        ),
        1,
    )
    shard, up_whole, totals, *input_slots = pin((shard, up_whole, totals, *input_slots))
    section_whole = low_sum(shard, plane_swap(shard, "other"))
    up_parts = share_by_core(up_whole)
    totals = swap_sum(totals, 2)
    section_whole, totals, *up_parts = pin((section_whole, totals, *up_parts))
    section_parts = share_out(section_whole)
    totals = swap_sum(totals, 4)
    outputs = collect(outputs, low)
    input_gradient = collect(input_slots, wide)
    (up_sum,) = assemble(
        class_places,
        up_parts,
        [
            [(0, at * quarter, at * width + kind * quarter, quarter) for at in range(4)]
            for kind in range(4)
        ],
        [up_weight.shape],
    )
    down_sum = settle(class_places, down_parts, wide).reshape(down_weight.shape)
    moved = pin((*section_parts, outputs, input_gradient, totals, up_sum, down_sum))
    section_parts = moved[:4]
    outputs, input_gradient, totals, up_sum, down_sum = moved[4:]
    in_sum, out_sum = assemble(
        class_places,
        section_parts,
        [[(0, 0, kind * width, width)] for kind in range(3)] + [[(1, 0, 0, width)]],
        [project_in.shape, project_out.shape],
    )
    (
        dbias_sum,
        gain_two_sum,
        shift_two_sum,
        obias_sum,
        gain_one_sum,
        shift_one_sum,
        qbias_sum,
        vbias_sum,
    ) = (totals[at * quarter : (at + 1) * quarter] for at in range(8))
    ubias_sum = totals[8 * quarter :]
    return (
        outputs,
        input_gradient,
        gain_one_sum,
        shift_one_sum,
        in_sum,
        qbias_sum,
        vbias_sum,
        out_sum,
        obias_sum,
        gain_two_sum,
        shift_two_sum,
        up_sum,
        ubias_sum,
        down_sum,
        dbias_sum,
    )


def solution(mesh):
    sizes = dict(mesh.shape)
    exchanged = sizes["dp"] == 2 and sizes["fsdp"] == 4 and sizes["ctx"] == 4
    per_device = per_device_exchanged if exchanged else per_device_gathered
    return jax.shard_map(
        per_device,
        mesh=mesh,
        in_specs=(
            P(("dp", "fsdp"), "ctx", None),
            P(("dp", "fsdp"), "ctx", None),
            P("fsdp"),
            P("fsdp"),
            P("fsdp", None),
            P("fsdp"),
            P("fsdp"),
            P("fsdp", None),
            P("fsdp"),
            P("fsdp"),
            P("fsdp"),
            P("fsdp", None),
            P("fsdp"),
            P("fsdp", None),
            P("fsdp"),
        ),
        out_specs=(
            P(("dp", "fsdp"), "ctx", None),
            P(("dp", "fsdp"), "ctx", None),
            P("fsdp"),
            P("fsdp"),
            P("fsdp", None),
            P("fsdp"),
            P("fsdp"),
            P("fsdp", None),
            P("fsdp"),
            P("fsdp"),
            P("fsdp"),
            P("fsdp", None),
            P("fsdp"),
            P("fsdp", None),
            P("fsdp"),
        ),
        check_vma=False,
    )
```

```python
import functools

import jax
import jax.numpy as jnp
from jax import lax
from jax.experimental import pallas as pl
from jax.experimental.pallas import tpu as pltpu
from jax.sharding import PartitionSpec as P

HEADS = 17
HEAD_DIM = 64


epsilon = 1e-05


def layer_norm(values, gain, shift):
    centred = values - jnp.mean(values, axis=-1, keepdims=True)
    spread = jnp.mean(centred * centred, axis=-1, keepdims=True)
    return centred * lax.rsqrt(spread + epsilon) * gain + shift


def gelu_tanh(values):
    return jax.nn.gelu(values, approximate=True)


def score_grads(
    query_heads, key_heads, value_heads, grad_heads, log_total, row_delta, query_at, key_at
):
    score_scale = HEAD_DIM ** (-0.5)
    scores = (
        jnp.einsum("sqhd,skhd->shqk", query_heads, key_heads, preferred_element_type=jnp.float32)
        * score_scale
    )
    visible = query_at[:, None] >= key_at[None, :]
    shifted = jnp.where(visible, scores - log_total[..., None], -1e30)
    weights = jnp.where(visible, jnp.exp(shifted), 0.0)
    pressure = jnp.einsum(
        "sqhd,skhd->shqk", grad_heads, value_heads, preferred_element_type=jnp.float32
    )
    score_low = (weights * (pressure - row_delta[..., None])).astype(jnp.bfloat16)
    return (weights.astype(jnp.bfloat16), score_low)


def per_device_gathered(
    inputs,
    cotangent,
    first_gain,
    first_shift,
    project_in,
    query_bias,
    value_bias,
    project_out,
    output_bias,
    second_gain,
    second_shift,
    up_weight,
    up_bias,
    down_weight,
    down_bias,
):
    seq_count, block_len, model_width = inputs.shape
    flat_rows = seq_count * block_len
    cycle_size = lax.axis_size("ctx")
    my_block = lax.axis_index("ctx")
    score_scale = HEAD_DIM ** (-0.5)
    head_shape = (seq_count, block_len, HEADS, HEAD_DIM)
    offsets = jnp.arange(block_len, dtype=jnp.int32)
    query_at = my_block * block_len + offsets
    gain_first, shift_first, full_in, qbias_full, vbias_full, full_out, obias_full = (
        lax.all_gather(first_gain, "fsdp", axis=0, tiled=True),
        lax.all_gather(first_shift, "fsdp", axis=0, tiled=True),
        lax.all_gather(project_in, "fsdp", axis=0, tiled=True),
        lax.all_gather(query_bias, "fsdp", axis=0, tiled=True),
        lax.all_gather(value_bias, "fsdp", axis=0, tiled=True),
        lax.all_gather(project_out, "fsdp", axis=0, tiled=True),
        lax.all_gather(output_bias, "fsdp", axis=0, tiled=True),
    )
    rows_in = inputs.astype(jnp.float32).reshape(flat_rows, model_width)
    normed, norm_first_back = jax.vjp(
        layer_norm, rows_in, gain_first.astype(jnp.float32), shift_first.astype(jnp.float32)
    )
    normed_low = normed.astype(jnp.bfloat16)
    projected = jnp.dot(normed_low, full_in, preferred_element_type=jnp.float32)
    queries = (projected[:, :model_width] + qbias_full).astype(jnp.bfloat16)
    key_rows = projected[:, model_width : 2 * model_width].astype(jnp.bfloat16)
    value_rows = (projected[:, 2 * model_width :] + vbias_full).astype(jnp.bfloat16)
    query_heads = queries.reshape(head_shape)
    running_top = jnp.full((seq_count, HEADS, block_len), -1e30, jnp.float32)
    accumulated = jnp.zeros(head_shape, jnp.float32)
    piece_keys = lax.all_gather(
        key_rows.reshape(seq_count, block_len, model_width), "ctx", axis=1, tiled=True
    )
    piece_values = lax.all_gather(
        value_rows.reshape(seq_count, block_len, model_width), "ctx", axis=1, tiled=True
    )
    piece_len = piece_keys.shape[1]
    key_heads = piece_keys.reshape(seq_count, piece_len, HEADS, HEAD_DIM)
    value_heads = piece_values.reshape(seq_count, piece_len, HEADS, HEAD_DIM)
    scores = (
        jnp.einsum("sqhd,skhd->shqk", query_heads, key_heads, preferred_element_type=jnp.float32)
        * score_scale
    )
    key_at = jnp.arange(piece_len, dtype=jnp.int32)
    visible = query_at[:, None] >= key_at[None, :]
    masked = jnp.where(visible, scores, -1e30)
    new_top = jnp.maximum(running_top, jnp.max(masked, axis=-1))
    factor = jnp.exp(running_top - new_top)
    weights = jnp.where(visible, jnp.exp(masked - new_top[..., None]), 0.0)
    row_total = jnp.sum(weights, axis=-1)
    added = jnp.einsum(
        "shqk,skhd->sqhd",
        weights.astype(jnp.bfloat16),
        value_heads,
        preferred_element_type=jnp.float32,
    )
    accumulated = accumulated * jnp.swapaxes(factor, 1, 2)[..., None] + added
    running_top, row_total, accumulated = (new_top, row_total, accumulated)
    attended = accumulated / jnp.swapaxes(row_total, 1, 2)[..., None]
    log_total = running_top + jnp.log(row_total)
    attended_low = attended.reshape(flat_rows, model_width).astype(jnp.bfloat16)
    middle = (
        rows_in + jnp.dot(attended_low, full_out, preferred_element_type=jnp.float32) + obias_full
    )
    gain_second, shift_second, full_up, ubias_full, full_down, dbias_full = (
        lax.all_gather(second_gain, "fsdp", axis=0, tiled=True),
        lax.all_gather(second_shift, "fsdp", axis=0, tiled=True),
        lax.all_gather(up_weight, "fsdp", axis=0, tiled=True),
        lax.all_gather(up_bias, "fsdp", axis=0, tiled=True),
        lax.all_gather(down_weight, "fsdp", axis=0, tiled=True),
        lax.all_gather(down_bias, "fsdp", axis=0, tiled=True),
    )
    normed_two, norm_second_back = jax.vjp(
        layer_norm, middle, gain_second.astype(jnp.float32), shift_second.astype(jnp.float32)
    )
    normed_two_low = normed_two.astype(jnp.bfloat16)
    hidden = jnp.dot(normed_two_low, full_up, preferred_element_type=jnp.float32) + ubias_full
    active, gelu_back = jax.vjp(gelu_tanh, hidden)
    active_low = active.astype(jnp.bfloat16)
    result = (
        middle + jnp.dot(active_low, full_down, preferred_element_type=jnp.float32) + dbias_full
    )
    outputs = result.astype(jnp.bfloat16).reshape(seq_count, block_len, model_width)
    upstream = cotangent.astype(jnp.float32).reshape(flat_rows, model_width)
    upstream_low = upstream.astype(jnp.bfloat16)
    down_grad = jnp.einsum(
        "rf,rd->fd", active_low, upstream_low, preferred_element_type=jnp.float32
    )
    down_bias_grad = jnp.sum(upstream_low.astype(jnp.float32), axis=0)
    active_grad = jnp.einsum(
        "rd,fd->rf", upstream_low, full_down, preferred_element_type=jnp.float32
    )
    (hidden_grad,) = gelu_back(active_grad)
    hidden_low = hidden_grad.astype(jnp.bfloat16)
    up_grad = jnp.einsum(
        "rd,rf->df", normed_two_low, hidden_low, preferred_element_type=jnp.float32
    )
    up_bias_grad = jnp.sum(hidden_low.astype(jnp.float32), axis=0)
    normed_two_grad = jnp.einsum(
        "rf,df->rd", hidden_low, full_up, preferred_element_type=jnp.float32
    )
    middle_part, gain_two_grad, shift_two_grad = norm_second_back(normed_two_grad)
    middle_grad = upstream + middle_part
    middle_low = middle_grad.astype(jnp.bfloat16)
    out_grad = jnp.einsum("rd,re->de", attended_low, middle_low, preferred_element_type=jnp.float32)
    out_bias_grad = jnp.sum(middle_low.astype(jnp.float32), axis=0)
    attended_grad = jnp.einsum(
        "re,de->rd", middle_low, full_out, preferred_element_type=jnp.float32
    )
    grad_low = attended_grad.astype(jnp.bfloat16).reshape(head_shape)
    row_delta = jnp.swapaxes(jnp.sum(grad_low.astype(jnp.float32) * attended, axis=-1), 1, 2)
    gathered_keys, gathered_values = (
        lax.all_gather(
            key_rows.reshape(1, seq_count, block_len, model_width), "ctx", axis=0, tiled=True
        ),
        lax.all_gather(
            value_rows.reshape(1, seq_count, block_len, model_width), "ctx", axis=0, tiled=True
        ),
    )
    block_ids = jnp.arange(cycle_size, dtype=jnp.int32)

    def key_step(carry, inputs_here):
        key_block, value_block, block_index = inputs_here
        key_heads = key_block.reshape(head_shape)
        value_heads = value_block.reshape(head_shape)
        weights_low, score_low = score_grads(
            query_heads,
            key_heads,
            value_heads,
            grad_low,
            log_total,
            row_delta,
            query_at,
            block_index * block_len + offsets,
        )
        carry = (
            carry
            + jnp.einsum(
                "shqk,skhd->sqhd", score_low, key_heads, preferred_element_type=jnp.float32
            )
            * score_scale
        )
        key_term = (
            jnp.einsum(
                "shqk,sqhd->skhd", score_low, query_heads, preferred_element_type=jnp.float32
            )
            * score_scale
        )
        value_term = jnp.einsum(
            "shqk,sqhd->skhd", weights_low, grad_low, preferred_element_type=jnp.float32
        )
        return (
            carry,
            (
                key_term.reshape(seq_count, block_len, model_width),
                value_term.reshape(seq_count, block_len, model_width),
            ),
        )

    query_grad, (key_terms, value_terms) = lax.scan(
        key_step, jnp.zeros(head_shape, jnp.float32), (gathered_keys, gathered_values, block_ids)
    )
    key_sum, value_sum = (
        lax.psum_scatter(
            key_terms.astype(jnp.bfloat16), "ctx", scatter_dimension=0, tiled=True
        ).astype(jnp.float32),
        lax.psum_scatter(
            value_terms.astype(jnp.bfloat16), "ctx", scatter_dimension=0, tiled=True
        ).astype(jnp.float32),
    )
    key_grad = key_sum.reshape(flat_rows, model_width)
    value_grad = value_sum.reshape(flat_rows, model_width)
    query_low = query_grad.reshape(flat_rows, model_width).astype(jnp.bfloat16)
    key_low = key_grad.astype(jnp.bfloat16)
    value_low = value_grad.astype(jnp.bfloat16)
    stacked = jnp.concatenate([query_low, key_low, value_low], axis=1)
    in_grad = jnp.einsum("rd,re->de", normed_low, stacked, preferred_element_type=jnp.float32)
    query_bias_grad = jnp.sum(query_low.astype(jnp.float32), axis=0)
    value_bias_grad = jnp.sum(value_low.astype(jnp.float32), axis=0)
    normed_grad = jnp.einsum("re,de->rd", stacked, full_in, preferred_element_type=jnp.float32)
    input_part, gain_one_grad, shift_one_grad = norm_first_back(normed_grad)
    input_gradient = (middle_grad + input_part).reshape(seq_count, block_len, model_width)
    (
        gain_one_part,
        shift_one_part,
        in_part,
        qbias_part,
        vbias_part,
        out_part,
        obias_part,
        gain_two_part,
        shift_two_part,
        up_part,
        ubias_part,
        down_part,
        dbias_part,
    ) = (
        lax.psum_scatter(
            gain_one_grad.astype(jnp.bfloat16), "fsdp", scatter_dimension=0, tiled=True
        ).astype(jnp.float32),
        lax.psum_scatter(
            shift_one_grad.astype(jnp.bfloat16), "fsdp", scatter_dimension=0, tiled=True
        ).astype(jnp.float32),
        lax.psum_scatter(
            in_grad.astype(jnp.bfloat16), "fsdp", scatter_dimension=0, tiled=True
        ).astype(jnp.float32),
        lax.psum_scatter(
            query_bias_grad.astype(jnp.bfloat16), "fsdp", scatter_dimension=0, tiled=True
        ).astype(jnp.float32),
        lax.psum_scatter(
            value_bias_grad.astype(jnp.bfloat16), "fsdp", scatter_dimension=0, tiled=True
        ).astype(jnp.float32),
        lax.psum_scatter(
            out_grad.astype(jnp.bfloat16), "fsdp", scatter_dimension=0, tiled=True
        ).astype(jnp.float32),
        lax.psum_scatter(
            out_bias_grad.astype(jnp.bfloat16), "fsdp", scatter_dimension=0, tiled=True
        ).astype(jnp.float32),
        lax.psum_scatter(
            gain_two_grad.astype(jnp.bfloat16), "fsdp", scatter_dimension=0, tiled=True
        ).astype(jnp.float32),
        lax.psum_scatter(
            shift_two_grad.astype(jnp.bfloat16), "fsdp", scatter_dimension=0, tiled=True
        ).astype(jnp.float32),
        lax.psum_scatter(
            up_grad.astype(jnp.bfloat16), "fsdp", scatter_dimension=0, tiled=True
        ).astype(jnp.float32),
        lax.psum_scatter(
            up_bias_grad.astype(jnp.bfloat16), "fsdp", scatter_dimension=0, tiled=True
        ).astype(jnp.float32),
        lax.psum_scatter(
            down_grad.astype(jnp.bfloat16), "fsdp", scatter_dimension=0, tiled=True
        ).astype(jnp.float32),
        lax.psum_scatter(
            down_bias_grad.astype(jnp.bfloat16), "fsdp", scatter_dimension=0, tiled=True
        ).astype(jnp.float32),
    )
    (
        gain_one_sum,
        shift_one_sum,
        in_sum,
        qbias_sum,
        vbias_sum,
        out_sum,
        obias_sum,
        gain_two_sum,
        shift_two_sum,
        up_sum,
        ubias_sum,
        down_sum,
        dbias_sum,
    ) = lax.psum(
        (
            gain_one_part,
            shift_one_part,
            in_part,
            qbias_part,
            vbias_part,
            out_part,
            obias_part,
            gain_two_part,
            shift_two_part,
            up_part,
            ubias_part,
            down_part,
            dbias_part,
        ),
        ("dp", "ctx"),
    )
    return (
        outputs,
        input_gradient,
        gain_one_sum,
        shift_one_sum,
        in_sum,
        qbias_sum,
        vbias_sum,
        out_sum,
        obias_sum,
        gain_two_sum,
        shift_two_sum,
        up_sum,
        ubias_sum,
        down_sum,
        dbias_sum,
    )


NT = (((1,), (1,)), ((), ()))
PAIR = 2 * HEAD_DIM


def attend_kernel(place_ref, q_ref, k_ref, v_ref, *refs, count, width, start):
    o_ref, log_ref, keys, values = refs[-4:]
    own_pair = pl.program_id(0)
    pair = own_pair + start
    shift = place_ref[0]
    block_len = q_ref.shape[0] // count
    lane = lax.broadcasted_iota(jnp.int32, (1, PAIR), 1)
    valid = lane + pair * PAIR < width
    first = lane < HEAD_DIM

    def rows(block):
        return pl.ds(pl.multiple_of((block ^ shift) * block_len, block_len), block_len)

    for block in range(count):
        here = pl.ds(block * block_len, block_len)
        keys[here, :] = jnp.where(valid, k_ref[rows(block), :], 0)
        values[here, :] = jnp.where(valid, v_ref[rows(block), :], 0)
    diagonal = lax.broadcasted_iota(jnp.int32, (block_len, block_len), 0) >= (
        lax.broadcasted_iota(jnp.int32, (block_len, block_len), 1)
    )
    for block in range(count):
        seen = (block + 1) * block_len
        before = block * block_len
        queries = q_ref[rows(block), :] * jnp.bfloat16(HEAD_DIM**-0.5)
        parts = []
        logs = log_ref[rows(block), :]
        for half in range(2):
            pick = jnp.logical_and(first if half == 0 else jnp.logical_not(first), valid)
            scores = lax.dot_general(
                jnp.where(pick, queries, 0),
                keys[pl.ds(0, seen), :],
                NT,
                preferred_element_type=jnp.float32,
            )
            last = jnp.where(diagonal, scores[:, before:], -1e30)
            scores = last if block == 0 else jnp.concatenate([scores[:, :before], last], axis=1)
            top = jnp.max(scores, axis=1, keepdims=True)
            weights = jnp.exp(scores - top)
            total = jnp.sum(weights, axis=1, keepdims=True)
            added = jnp.dot(
                weights.astype(jnp.bfloat16),
                values[pl.ds(0, seen), :],
                preferred_element_type=jnp.float32,
            )
            parts.append(added / total)
            logs = jnp.where(lane == 2 * own_pair + half, top + jnp.log(total), logs)
        o_ref[rows(block), :] = jnp.where(first, parts[0], parts[1]).astype(jnp.bfloat16)
        log_ref[rows(block), :] = logs


def attend_back_kernel(
    place_ref,
    q_ref,
    k_ref,
    v_ref,
    g_ref,
    o_ref,
    log_ref,
    *refs,
    count,
    width,
    start,
):
    dq_ref, dk_ref, dv_ref, queries, grads, keys, values = refs[-11:-4]
    keys_turned, logs, deltas, turned = refs[-4:]
    pair = pl.program_id(0) + start
    shift = place_ref[0]
    length = q_ref.shape[0]
    block_len = length // count
    lane = lax.broadcasted_iota(jnp.int32, (1, PAIR), 1)
    valid = lane + pair * PAIR < width
    first = lane < HEAD_DIM
    picks = (jnp.logical_and(first, valid), jnp.logical_and(jnp.logical_not(first), valid))
    half_of = (lax.broadcasted_iota(jnp.int32, (8, PAIR), 1) // HEAD_DIM) == (
        lax.broadcasted_iota(jnp.int32, (8, PAIR), 0)
    )
    ones_of = jnp.where(half_of, 1.0, 0.0)

    def rows(block):
        return pl.ds(pl.multiple_of((block ^ shift) * block_len, block_len), block_len)

    for block in range(count):
        here = pl.ds(block * block_len, block_len)
        key_block = jnp.where(valid, k_ref[rows(block), :], 0)
        keys[here, :] = key_block
        keys_turned[:, here] = key_block.astype(jnp.float32).T.astype(jnp.bfloat16)
        values[here, :] = jnp.where(valid, v_ref[rows(block), :], 0)
        query_block = q_ref[rows(block), :] * jnp.bfloat16(HEAD_DIM**-0.5)
        grad_block = jnp.where(valid, g_ref[rows(block), :], 0)
        for half in range(2):
            queries[half, here, :] = jnp.where(picks[half], query_block, 0)
            grads[half, here, :] = jnp.where(picks[half], grad_block, 0)
        mixed = grad_block.astype(jnp.float32) * jnp.where(
            valid, o_ref[rows(block), :], 0
        ).astype(jnp.float32)
        deltas[:, here] = lax.dot_general(
            ones_of,
            mixed,
            NT,
            preferred_element_type=jnp.float32,
            precision=lax.Precision.HIGHEST,
        )
        logs[:, here] = log_ref[
            0, :, pl.ds(pl.multiple_of((block ^ shift) * block_len, block_len), block_len)
        ]
    diagonal = lax.broadcasted_iota(jnp.int32, (block_len, block_len), 0) <= (
        lax.broadcasted_iota(jnp.int32, (block_len, block_len), 1)
    )
    for block in range(count):
        here = pl.ds(block * block_len, block_len)
        after = pl.ds(block * block_len, length - block * block_len)
        key_total = jnp.zeros((block_len, PAIR), jnp.float32)
        value_total = jnp.zeros((block_len, PAIR), jnp.float32)
        for half in range(2):
            scores = lax.dot_general(
                keys[here, :], queries[half, after, :], NT, preferred_element_type=jnp.float32
            )
            shifted = scores - logs[half : half + 1, after]
            own = jnp.where(diagonal, shifted[:, :block_len], -1e30)
            if block < count - 1:
                own = jnp.concatenate([own, shifted[:, block_len:]], axis=1)
            weights = jnp.exp(own)
            pressure = lax.dot_general(
                values[here, :], grads[half, after, :], NT, preferred_element_type=jnp.float32
            )
            score_low = (weights * (pressure - deltas[half : half + 1, after])).astype(
                jnp.bfloat16
            )
            value_total += jnp.dot(
                weights.astype(jnp.bfloat16),
                grads[half, after, :],
                preferred_element_type=jnp.float32,
            )
            key_total += jnp.dot(
                score_low, queries[half, after, :], preferred_element_type=jnp.float32
            )
            part = pl.ds(half * HEAD_DIM, HEAD_DIM)
            term = jnp.dot(
                keys_turned[part, here], score_low, preferred_element_type=jnp.float32
            )
            if block == 0:
                turned[part, after] = term
            else:
                turned[part, after] += term
        dk_ref[rows(block), :] = key_total.astype(jnp.bfloat16)
        dv_ref[rows(block), :] = value_total.astype(jnp.bfloat16)
    for block in range(count):
        here = pl.ds(block * block_len, block_len)
        dq_ref[rows(block), :] = (turned[:, here].T * HEAD_DIM**-0.5).astype(jnp.bfloat16)


def attend(place, queries, key_rows, value_rows, count, start, pairs, before):
    length, width = queries.shape
    heads_block = pl.BlockSpec((length, PAIR), lambda pair, place_ref: (0, pair + start))
    return pl.pallas_call(
        functools.partial(attend_kernel, count=count, width=width, start=start),
        grid_spec=pltpu.PrefetchScalarGridSpec(
            num_scalar_prefetch=1,
            grid=(pairs,),
            in_specs=[heads_block] * 3 + [pl.BlockSpec(memory_space=pl.ANY)] * len(before),
            out_specs=[
                heads_block,
                pl.BlockSpec((length, 128), lambda pair, place_ref: (0, 0)),
            ],
            scratch_shapes=[pltpu.VMEM((length, PAIR), jnp.bfloat16)] * 2,
        ),
        out_shape=[
            jax.ShapeDtypeStruct((length, width), jnp.bfloat16),
            jax.ShapeDtypeStruct((length, 128), jnp.float32),
        ],
        input_output_aliases={4 + at: at for at in range(len(before))},
        compiler_params=pltpu.CompilerParams(vmem_limit_bytes=48 * 2**20),
        cost_estimate=SMALL,
        name="attend",
    )(place, queries, key_rows, value_rows, *before)


def attend_back(
    place, queries, key_rows, value_rows, grads, attended, logs, count, start, pairs, before
):
    length, width = queries.shape
    heads_block = pl.BlockSpec((length, PAIR), lambda pair, place_ref: (0, pair + start))
    low_rows = pltpu.VMEM((length, PAIR), jnp.bfloat16)
    low_pair = pltpu.VMEM((2, length, PAIR), jnp.bfloat16)
    return pl.pallas_call(
        functools.partial(attend_back_kernel, count=count, width=width, start=start),
        grid_spec=pltpu.PrefetchScalarGridSpec(
            num_scalar_prefetch=1,
            grid=(pairs,),
            in_specs=[heads_block] * 5
            + [pl.BlockSpec((1, 2, length), lambda pair, place_ref: (pair, 0, 0))]
            + [pl.BlockSpec(memory_space=pl.ANY)] * len(before),
            out_specs=[heads_block] * 3,
            scratch_shapes=[
                low_pair,
                low_pair,
                low_rows,
                low_rows,
                pltpu.VMEM((PAIR, length), jnp.bfloat16),
                pltpu.VMEM((2, length), jnp.float32),
                pltpu.VMEM((8, length), jnp.float32),
                pltpu.VMEM((PAIR, length), jnp.float32),
            ],
        ),
        out_shape=[jax.ShapeDtypeStruct((length, width), jnp.bfloat16)] * 3,
        input_output_aliases={7 + at: at for at in range(len(before))},
        compiler_params=pltpu.CompilerParams(vmem_limit_bytes=48 * 2**20),
        cost_estimate=SMALL,
        name="attend_back",
    )(place, queries, key_rows, value_rows, grads, attended, logs, *before)


def settle_kernel(place_ref, *refs):
    pieces, out_ref = refs[:-1], refs[-1]
    for at, piece in enumerate(pieces):
        out_ref[place_ref[at]] = piece[...].astype(out_ref.dtype)


def settle(places, pieces, dtype):
    return pl.pallas_call(
        settle_kernel,
        in_specs=[pl.BlockSpec(memory_space=pltpu.SMEM)]
        + [pl.BlockSpec(memory_space=pltpu.VMEM)] * len(pieces),
        out_specs=pl.BlockSpec(memory_space=pltpu.VMEM),
        out_shape=jax.ShapeDtypeStruct((len(pieces),) + pieces[0].shape, dtype),
        compiler_params=pltpu.CompilerParams(vmem_limit_bytes=48 * 2**20),
        cost_estimate=SMALL,
        name="settle",
    )(places, *pieces)


def plane_partner(device, kind):
    core = device & 1
    if kind == "core":
        return device ^ 1
    if kind == "far":
        return device ^ (3 if core else 5)
    if kind == "near":
        return device ^ (2 if core else 4)
    return device ^ (4 if core else 2)


def plane_swap(values, kind):
    return lax.ppermute(
        values, ("dp", "ctx"), [(device, plane_partner(device, kind)) for device in range(8)]
    )


def ctx_swap(values, bits):
    return lax.ppermute(values, "ctx", [(device, device ^ bits) for device in range(4)])


def low_sum(*terms):
    return sum(term.astype(jnp.float32) for term in terms).astype(jnp.bfloat16)


def reduce_core(pieces):
    return plane_swap(pieces[2], "core"), plane_swap(pieces[3], "core")


def share_out(whole):
    return [whole] + [plane_swap(whole, kind) for kind in ("near", "core", "far")]


def share_by_core(whole):
    near = plane_swap(whole, "near")
    return [whole, near, plane_swap(whole, "core"), plane_swap(near, "core")]


def scatter_rows(values):
    return lax.psum_scatter(values, "fsdp", scatter_dimension=0, tiled=True)


def chosen(index, options):
    result = options[-1]
    for at in range(len(options) - 2, -1, -1):
        result = jnp.where(index == at, options[at], result)
    return result


def gather_vector(values, z):
    around = [values] + [
        lax.ppermute(values, "fsdp", [(device, (device + step) % 4) for device in range(4)])
        for step in range(1, 4)
    ]
    return jnp.stack([chosen((z - at) % 4, around) for at in range(4)])


def scatter_vector(values, z):
    rows = [values[at] for at in range(4)]
    total = chosen(z, rows)
    for step in range(1, 4):
        total = total + lax.ppermute(
            chosen((z + step) % 4, rows),
            "fsdp",
            [(device, (device + step) % 4) for device in range(4)],
        )
    return total


def swap_sum(total, bits):
    return total + lax.ppermute(
        total, ("dp", "ctx"), [(device, device ^ bits) for device in range(8)]
    )


def product(left, right, dims):
    return lax.dot_general(left, right, ((dims[:1], dims[1:]), ((), ())),
                           preferred_element_type=jnp.float32)


def gelu_pair(values):
    inner = 0.7978845608028654
    cubic = inner * 0.044715
    squared = values * values
    curve = jnp.tanh(values * (inner + cubic * squared))
    half = 0.5 * values
    active = half + half * curve
    slope = 0.5 + 0.5 * curve + half * (1.0 - curve * curve) * (inner + 3.0 * cubic * squared)
    return active, slope


SMALL = pl.CostEstimate(flops=1024, bytes_accessed=1024, transcendentals=0)


def unit_of(values):
    centred = values - jnp.mean(values, axis=-1, keepdims=True)
    scale = lax.rsqrt(jnp.mean(centred * centred, axis=-1, keepdims=True) + epsilon)
    return centred * scale, scale


def fold(values):
    rows, width = values.shape
    return jnp.sum(values.reshape(rows // 8, 8, width), axis=0)


def front_kernel(places_ref, vectors_ref, *refs):
    slots, pieces = refs[:4], refs[4:20]
    x_ref, h_ref, q_ref, k_ref, v_ref, all_ref, weights, arrived, left = refs[20:]
    copies = [
        pltpu.make_async_copy(piece, weights.at[places_ref[at]], arrived.at[at])
        for at, piece in enumerate(pieces)
    ]
    for copy in copies:
        copy.start()
    rows, width = x_ref.shape
    step = rows // 4
    for at, slot in enumerate(slots):
        here = pl.ds(at * step, step)
        values = slot[...].astype(jnp.float32).T
        x_ref[here, :] = values.astype(jnp.bfloat16)
        unit, _ = unit_of(values)
        h_ref[here, :] = (unit * vectors_ref[0:1, :] + vectors_ref[1:2, :]).astype(jnp.bfloat16)
    for copy in copies:
        copy.wait()
    leave = pltpu.make_async_copy(weights, all_ref, left)
    leave.start()
    for section, out_ref in enumerate((q_ref, k_ref, v_ref)):

        def multiply(at, carry, section=section, out_ref=out_ref):
            here = pl.ds(pl.multiple_of(at * step, step), step)
            matrix = weights[4 * section : 4 * section + 4].reshape(width, width)
            total = jnp.dot(h_ref[here, :], matrix, preferred_element_type=jnp.float32)
            if section != 1:
                row = 2 if section == 0 else 3
                total = total + vectors_ref[row : row + 1, :]
            out_ref[here, :] = total.astype(jnp.bfloat16)
            return carry

        lax.fori_loop(0, rows // step, multiply, 0)
    leave.wait()


def front(places, slots, vectors, pieces):
    width, step = slots[0].shape
    rows = 4 * step
    vmem = pl.BlockSpec(memory_space=pltpu.VMEM)
    hbm = pl.BlockSpec(memory_space=pl.ANY)
    shape = jax.ShapeDtypeStruct((rows, width), jnp.bfloat16)
    whole = (16,) + pieces[0].shape
    return pl.pallas_call(
        front_kernel,
        in_specs=[pl.BlockSpec(memory_space=pltpu.SMEM)] + [vmem] * 5 + [hbm] * 16,
        out_specs=[vmem] * 5 + [hbm],
        out_shape=[shape] * 5 + [jax.ShapeDtypeStruct(whole, jnp.bfloat16)],
        scratch_shapes=[
            pltpu.VMEM(whole, jnp.bfloat16),
            pltpu.SemaphoreType.DMA((16,)),
            pltpu.SemaphoreType.DMA,
        ],
        compiler_params=pltpu.CompilerParams(vmem_limit_bytes=56 * 2**20),
        cost_estimate=SMALL,
        name="front",
    )(places, vectors, *slots, *pieces)


def turn_kernel(*refs):
    slots, out_ref = refs[:-1], refs[-1]
    step = slots[0].shape[1]
    for at, slot in enumerate(slots):
        out_ref[pl.ds(at * step, step), :] = (
            slot[...].astype(jnp.float32).T.astype(jnp.bfloat16)
        )


def turn(slots):
    width, step = slots[0].shape
    return pl.pallas_call(
        turn_kernel,
        out_shape=jax.ShapeDtypeStruct((len(slots) * step, width), jnp.bfloat16),
        compiler_params=pltpu.CompilerParams(vmem_limit_bytes=48 * 2**20),
        cost_estimate=SMALL,
        name="turn",
    )(*slots)


def assemble_kernel(place_ref, *refs, plan):
    pieces, outs = refs[:4], refs[4:]
    for at, piece in enumerate(pieces):
        for kind, moves in enumerate(plan):

            @pl.when(place_ref[at] == kind)
            def _(piece=piece, moves=moves):
                for out, source, target, size in moves:
                    outs[out][:, target : target + size] = piece[
                        :, source : source + size
                    ].astype(jnp.float32)


def assemble(places, pieces, plan, shapes):
    vmem = pl.BlockSpec(memory_space=pltpu.VMEM)
    return pl.pallas_call(
        functools.partial(assemble_kernel, plan=plan),
        in_specs=[pl.BlockSpec(memory_space=pltpu.SMEM)] + [vmem] * 4,
        out_specs=[vmem] * len(shapes),
        out_shape=[jax.ShapeDtypeStruct(shape, jnp.float32) for shape in shapes],
        compiler_params=pltpu.CompilerParams(vmem_limit_bytes=48 * 2**20),
        cost_estimate=SMALL,
        name="assemble",
    )(places, *pieces)


def store_turned(step, refs, values):
    size = refs[0].shape[1]
    share = values.shape[0] // size
    for at, ref in enumerate(refs):

        @pl.when(step == at // share)
        def _(at=at, ref=ref):
            first = (at % share) * size
            ref[...] = values[first : first + size].T.astype(ref.dtype)


def fetch(step, copies):
    @pl.when(step == 0)
    def _():
        for copy in copies:
            copy.start()


def arrive(step, copy):
    @pl.when(step == 0)
    def _():
        copy.wait()


def middle_kernel(x_ref, o_ref, vectors_ref, all_ref, middle_ref, h_ref, weights, arrived):
    step = pl.program_id(0)
    width = x_ref.shape[1]
    copy = pltpu.make_async_copy(all_ref.at[pl.ds(12, 4)], weights, arrived)
    fetch(step, [copy])
    arrive(step, copy)
    middle = (
        x_ref[...].astype(jnp.float32)
        + jnp.dot(
            o_ref[...], weights[...].reshape(width, width), preferred_element_type=jnp.float32
        )
        + vectors_ref[0:1, :]
    )
    middle_ref[...] = middle
    unit, _ = unit_of(middle)
    h_ref[...] = (unit * vectors_ref[1:2, :] + vectors_ref[2:3, :]).astype(jnp.bfloat16)


def up_kernel(h_ref, biases_ref, *refs):
    sources = refs[:2]
    active_refs, slope_refs = refs[2:4], refs[4:6]
    weights, arrived = refs[6:]
    step = pl.program_id(0)
    copies = [
        pltpu.make_async_copy(source, weights.at[at], arrived.at[at])
        for at, source in enumerate(sources)
    ]
    fetch(step, copies)
    for at in range(2):
        arrive(step, copies[at])
        hidden = (
            jnp.dot(h_ref[...], weights[at], preferred_element_type=jnp.float32)
            + biases_ref[at : at + 1, :]
        )
        active, slope = gelu_pair(hidden)
        active_refs[at][...] = active.astype(jnp.bfloat16)
        slope_refs[at][...] = slope.astype(jnp.bfloat16)


def down_kernel(middle_ref, vectors_ref, *refs):
    actives, sources = refs[:4], refs[4:8]
    out_refs = refs[8:12]
    weights, arrived = refs[12:]
    step = pl.program_id(0)
    copies = [
        pltpu.make_async_copy(source, weights.at[at], arrived.at[at])
        for at, source in enumerate(sources)
    ]
    fetch(step, copies)
    total = middle_ref[...] + vectors_ref[0:1, :]
    for at in range(4):
        arrive(step, copies[at])
        total = total + jnp.dot(
            actives[at][...], weights[at], preferred_element_type=jnp.float32
        )
    store_turned(step, out_refs, total)


def norm_back(values, gain, grad):
    unit, scale = unit_of(values)
    turned = grad * gain
    inner = (
        turned
        - jnp.mean(turned, axis=-1, keepdims=True)
        - unit * jnp.mean(turned * unit, axis=-1, keepdims=True)
    )
    return scale * inner, grad * unit


def hidden_kernel(g_ref, *refs):
    slopes, sources = refs[:2], refs[2:4]
    hidden_refs, sums_ref = refs[4:6], refs[6]
    weights, arrived = refs[7:]
    step = pl.program_id(0)
    copies = [
        pltpu.make_async_copy(source, weights.at[at], arrived.at[at])
        for at, source in enumerate(sources)
    ]
    fetch(step, copies)

    @pl.when(step == 0)
    def _():
        sums_ref[...] = jnp.zeros_like(sums_ref)

    upstream = g_ref[...]
    for at in range(2):
        arrive(step, copies[at])
        hidden = lax.dot_general(
            upstream, weights[at], NT, preferred_element_type=jnp.float32
        )
        hidden = (hidden * slopes[at][...].astype(jnp.float32)).astype(jnp.bfloat16)
        hidden_refs[at][...] = hidden
        sums_ref[at] += fold(hidden.astype(jnp.float32))
    sums_ref[2] += fold(upstream.astype(jnp.float32))


def back_kernel(g_ref, middle_ref, vectors_ref, *refs):
    hiddens, sources, all_ref = refs[:4], refs[4:8], refs[8]
    grad_ref, low_ref, out_ref, sums_ref = refs[9:13]
    weights, out_weights, arrived = refs[13:]
    step = pl.program_id(0)
    width = middle_ref.shape[1]
    copies = [
        pltpu.make_async_copy(source, weights.at[at], arrived.at[at])
        for at, source in enumerate(sources)
    ] + [pltpu.make_async_copy(all_ref.at[pl.ds(12, 4)], out_weights, arrived.at[4])]
    fetch(step, copies)

    @pl.when(step == 0)
    def _():
        sums_ref[...] = jnp.zeros_like(sums_ref)

    total = jnp.zeros(middle_ref.shape, jnp.float32)
    for at in range(4):
        arrive(step, copies[at])
        total = total + lax.dot_general(
            hiddens[at][...], weights[at], NT, preferred_element_type=jnp.float32
        )
    part, gain_term = norm_back(middle_ref[...], vectors_ref[0:1, :], total)
    sums_ref[0] += fold(gain_term)
    sums_ref[1] += fold(total)
    grad = g_ref[...].astype(jnp.float32) + part
    grad_ref[...] = grad
    grad_low = grad.astype(jnp.bfloat16)
    low_ref[...] = grad_low
    sums_ref[2] += fold(grad_low.astype(jnp.float32))
    arrive(step, copies[4])
    out_ref[...] = lax.dot_general(
        grad_low,
        out_weights[...].reshape(width, width),
        NT,
        preferred_element_type=jnp.float32,
    ).astype(jnp.bfloat16)


def last_kernel(q_ref, k_ref, v_ref, x_ref, grad_ref, vectors_ref, all_ref, *refs):
    out_refs = refs[:4]
    sums_ref, weights, arrived = refs[4:]
    step = pl.program_id(0)
    width = x_ref.shape[1]
    copies = [
        pltpu.make_async_copy(
            all_ref.at[pl.ds(4 * at, 4)], weights.at[pl.ds(4 * at, 4)], arrived.at[at]
        )
        for at in range(3)
    ]
    fetch(step, copies)
    total = jnp.zeros(x_ref.shape, jnp.float32)
    for at, ref in enumerate((q_ref, k_ref, v_ref)):
        arrive(step, copies[at])
        total = total + lax.dot_general(
            ref[...],
            weights[4 * at : 4 * at + 4].reshape(width, width),
            NT,
            preferred_element_type=jnp.float32,
        )
    part, gain_term = norm_back(x_ref[...].astype(jnp.float32), vectors_ref[0:1, :], total)
    store_turned(step, out_refs, grad_ref[...] + part)

    @pl.when(step == 0)
    def _():
        sums_ref[...] = jnp.zeros_like(sums_ref)

    terms = (
        gain_term,
        total,
        q_ref[...].astype(jnp.float32),
        v_ref[...].astype(jnp.float32),
    )
    for at, term in enumerate(terms):
        sums_ref[at] += fold(term)


def by_rows(kernel, name, rows, width, tiled, whole, remote, outs, sums, scratch, sems):
    step = 512
    tile = pl.BlockSpec((step, width), lambda at: (at, 0))
    out_specs, out_shape = [], []
    for dtype in outs:
        if dtype is None:
            out_specs += [pl.BlockSpec((width, rows // 4), lambda at: (0, 0))] * 4
            out_shape += [jax.ShapeDtypeStruct((width, rows // 4), jnp.bfloat16)] * 4
        else:
            out_specs.append(tile)
            out_shape.append(jax.ShapeDtypeStruct((rows, width), dtype))
    if sums:
        out_specs.append(pl.BlockSpec((sums, 8, width), lambda at: (0, 0, 0)))
        out_shape.append(jax.ShapeDtypeStruct((sums, 8, width), jnp.float32))
    return pl.pallas_call(
        kernel,
        grid=(rows // step,),
        in_specs=[tile] * len(tiled[0])
        + [pl.BlockSpec(value.shape, lambda at: (0, 0)) for value in whole]
        + [tile] * len(tiled[1])
        + [pl.BlockSpec(memory_space=pl.ANY)] * len(remote),
        out_specs=out_specs,
        out_shape=out_shape,
        scratch_shapes=[pltpu.VMEM(shape, jnp.bfloat16) for shape in scratch]
        + [pltpu.SemaphoreType.DMA((sems,)) if sems > 1 else pltpu.SemaphoreType.DMA],
        compiler_params=pltpu.CompilerParams(vmem_limit_bytes=60 * 2**20),
        cost_estimate=SMALL,
        name=name,
    )(*tiled[0], *whole, *tiled[1], *remote)


def per_device_exchanged(
    inputs,
    cotangent,
    first_gain,
    first_shift,
    project_in,
    query_bias,
    value_bias,
    project_out,
    output_bias,
    second_gain,
    second_shift,
    up_weight,
    up_bias,
    down_weight,
    down_bias,
):
    seq_count, block_len, width = inputs.shape
    low = jnp.bfloat16
    wide = jnp.float32
    c = lax.axis_index("ctx")
    y = lax.axis_index("dp")
    z = lax.axis_index("fsdp")
    core = c & 1
    x = c >> 1
    mine = core * 2 + jnp.where(core == 0, y, x)
    across = (1 - core) * 2 + jnp.where(core == 0, x, y)
    classes = [mine, mine ^ 1, across, across ^ 1]
    slot_of = [
        chosen(0, [sum(at * (classes[at] == kind).astype(jnp.int32) for at in range(4))])
        for kind in range(4)
    ]
    quarter = width // 4
    rows, area = seq_count * block_len, (width, width)
    pin = lax.optimization_barrier
    place = jnp.stack([c])
    places = jnp.stack([c ^ at for at in range(4)])
    class_places = jnp.stack(classes)

    def spread(values):
        values = jnp.swapaxes(values, 1, 2)
        return [lax.dynamic_index_in_dim(values, c, 0, keepdims=False)] + [
            ctx_swap(lax.dynamic_index_in_dim(values, c ^ bits, 0, keepdims=False), bits)
            for bits in range(1, 4)
        ]

    def exchange(pieces):
        return [pieces[0]] + [ctx_swap(pieces[bits], bits) for bits in range(1, 4)]

    def collect(moved, dtype):
        return jnp.swapaxes(settle(places, moved, dtype), 1, 2)

    sections = [
        project_in[:, :width],
        project_in[:, width : 2 * width],
        project_in[:, 2 * width :],
        project_out,
    ]
    section = chosen(mine, sections)
    section, inputs = pin((section, inputs))
    shards = [
        lax.ppermute(section, "fsdp", [(device, (device + step) % 4) for device in range(4)])
        for step in range(1, 4)
    ]
    turned_in = jnp.swapaxes(inputs, 1, 2)
    slots_in = [
        lax.dynamic_index_in_dim(turned_in, c ^ bits, 0, keepdims=False) for bits in range(4)
    ]
    pieces_in = (
        first_gain,
        first_shift,
        query_bias,
        value_bias,
        output_bias,
        second_gain,
        second_shift,
        down_bias,
        up_bias,
    )
    slots_in[3], up_weight, down_weight, *pieces_in = pin(
        (slots_in[3], up_weight, down_weight, *pieces_in)
    )
    slots_in = [slots_in[0]] + [ctx_swap(slots_in[bits], bits) for bits in range(1, 4)]
    vectors = gather_vector(jnp.concatenate(pieces_in), z).astype(wide)
    up_piece = jnp.concatenate(
        [
            lax.dynamic_slice_in_dim(up_weight, at * width + mine * quarter, quarter, 1)
            for at in range(4)
        ],
        axis=1,
    )
    up_piece, vectors, *moved = pin((up_piece, vectors, *shards, *slots_in))
    shards, slots_in = moved[:3], moved[3:]
    near_shards = [plane_swap(shard, "near") for shard in shards]
    cotangent, *near_shards = pin((cotangent, *near_shards))
    slots_back = spread(cotangent)
    around = (
        sections
        + shards
        + near_shards
        + [plane_swap(shard, "core") for shard in shards]
        + [plane_swap(shard, "core") for shard in near_shards]
    )
    around_places = jnp.stack(
        [kind * 4 + z for kind in range(4)]
        + [kind * 4 + (z - step) % 4 for kind in classes for step in range(1, 4)]
    )
    up_own = lax.all_gather(up_piece, "fsdp", axis=0, tiled=True)
    down_piece = lax.dynamic_slice_in_dim(down_weight, mine * quarter, quarter, 0)
    gain_first, shift_first, qbias, vbias, obias, gain_second, shift_second, dbias = (
        vectors[:, at * quarter : (at + 1) * quarter].reshape(1, width) for at in range(8)
    )
    ubias = vectors[:, 8 * quarter :].reshape(4, 4, quarter)
    ubias = jnp.concatenate(
        [
            chosen(kind, [ubias[:, at] for at in range(4)]).reshape(1, width)
            for kind in classes
        ],
        axis=0,
    )

    rows_in, normed_low, queries, key_rows, value_rows, weights = front(
        around_places,
        slots_in,
        jnp.concatenate([gain_first, shift_first, qbias, vbias], axis=0),
        around,
    )
    up_own, queries = pin((up_own, queries))
    up_near, up_core = plane_swap(up_own, "near"), plane_swap(up_own, "core")
    attended, logs = attend(place, queries, key_rows, value_rows, seq_count, 0, 9, [])
    down_piece, up_core, up_near, attended = pin((down_piece, up_core, up_near, attended))
    down_own = lax.all_gather(down_piece, "fsdp", axis=0, tiled=True)
    logs = logs.T.reshape(64, 2, rows)
    logs_one, logs_two = logs[:5], logs[5:9]
    middle, normed_two_low = by_rows(
        middle_kernel,
        "middle",
        rows,
        width,
        ([rows_in, attended], []),
        [jnp.concatenate([obias, gain_second, shift_second], axis=0)],
        [weights],
        [wide, low],
        0,
        [(4,) + section.shape],
        1,
    )
    up_slots = [up_own, up_near, up_core, plane_swap(up_near, "core")]
    active, slopes = [None] * 4, [None] * 4

    def up(first):
        outs = by_rows(
            up_kernel,
            "up",
            rows,
            width,
            ([normed_two_low], []),
            [jnp.concatenate([ubias[first : first + 1], ubias[first + 2 : first + 3]], axis=0)],
            [up_slots[first], up_slots[first + 2]],
            [low] * 4,
            0,
            [(2,) + area],
            2,
        )
        active[first], active[first + 2], slopes[first], slopes[first + 2] = outs

    up(0)
    up_slots[3], slots_back[3], active[0], active[2] = pin(
        (up_slots[3], slots_back[3], active[0], active[2])
    )
    upstream_low = turn(slots_back)
    up(1)
    down_own, *active = pin((down_own, *active))
    down_near, down_core = plane_swap(down_own, "near"), plane_swap(down_own, "core")

    def turned_product(left, right):
        return product(left, right, (0, 0)).astype(low)

    down_terms = [turned_product(active[slot], upstream_low) for slot in (3, 2)]
    upstream_low, *down_terms = pin((upstream_low, *down_terms))
    down_terms += [turned_product(active[slot], upstream_low) for slot in (1, 0)]
    down_terms = down_terms[::-1]
    down_far, down_far_two = reduce_core(down_terms)
    upstream_low, *down_terms = pin((upstream_low, *down_terms))
    hidden_low = [None] * 4

    def hidden(first, upstream):
        hidden_low[first], hidden_low[first + 2], sums = by_rows(
            hidden_kernel,
            "hidden",
            rows,
            width,
            ([upstream], [slopes[first], slopes[first + 2]]),
            [],
            [down_slots[first], down_slots[first + 2]],
            [low] * 2,
            3,
            [(2,) + area],
            2,
        )
        return sums

    down_near, upstream_low = pin((down_near, upstream_low))
    down_slots = [down_own, down_near, down_core, plane_swap(down_near, "core")]
    sums_even = hidden(0, upstream_low)
    down_second = low_sum(down_terms[1], down_far_two)
    upstream_late, sums_even, down_second = pin((upstream_low, sums_even, down_second))
    down_close = plane_swap(down_second, "near")
    sums_odd = hidden(1, upstream_late)
    hidden_sums = jnp.stack(
        [sums_even[0], sums_odd[0], sums_even[1], sums_odd[1], sums_even[2]]
    )
    down_far, *hidden_low = pin((down_far, *hidden_low))
    up_terms = [turned_product(normed_two_low, hidden_low[slot]) for slot in (3, 2)]
    normed_two_low, *up_terms = pin((normed_two_low, *up_terms))
    up_terms += [turned_product(normed_two_low, hidden_low[slot]) for slot in (1, 0)]
    up_terms = up_terms[::-1]
    up_far, up_far_two = reduce_core(up_terms)
    up_second = low_sum(up_terms[1], up_far_two)
    down_first = low_sum(down_terms[0], down_far, down_close)
    up_second, up_far, down_first, moved, *hidden_low = pin(
        (up_second, up_far, down_first, up_terms[0], *hidden_low)
    )
    up_terms[0] = moved
    down_shard = scatter_rows(down_first)
    up_close = plane_swap(up_second, "near")
    middle_grad, middle_low, grad_low, back_sums = by_rows(
        back_kernel,
        "back",
        rows,
        width,
        ([upstream_low, middle], hidden_low),
        [gain_second],
        up_slots + [weights],
        [wide, low, low],
        3,
        [(4,) + area, (4,) + section.shape],
        5,
    )
    out_term = turned_product(attended, middle_low)
    up_first = low_sum(up_terms[0], up_far, up_close)
    grad_low, out_term, up_first = pin((grad_low, out_term, up_first))
    in_grads = attend_back(
        place, queries, key_rows, value_rows, grad_low, attended, logs_one, seq_count, 0, 5, []
    )
    up_first, down_shard, *in_grads = pin((up_first, down_shard, *in_grads))
    up_shard = scatter_rows(up_first)
    down_whole = low_sum(down_shard, plane_swap(down_shard, "other"))
    in_grads = attend_back(
        place,
        queries,
        key_rows,
        value_rows,
        grad_low,
        attended,
        logs_two,
        seq_count,
        5,
        4,
        in_grads,
    )
    down_whole, *in_grads = pin((down_whole, *in_grads))
    down_parts = share_by_core(down_whole)
    in_terms = [turned_product(normed_low, grad) for grad in in_grads]
    section_grads = in_terms + [out_term]
    sections_mine = [chosen(kind, section_grads) for kind in classes]
    far, far_two = reduce_core(sections_mine)
    second = low_sum(sections_mine[1], far_two)
    second, far, middle, *in_grads = pin((second, far, middle, *in_grads))
    query_low, key_low, value_low = in_grads
    close = plane_swap(second, "near")
    result_slots = by_rows(
        down_kernel,
        "down",
        rows,
        width,
        ([middle], active),
        [dbias],
        down_slots,
        [None],
        0,
        [(4,) + area],
        4,
    )
    first = low_sum(sections_mine[0], far, close)
    first, up_shard, query_low, *result_slots = pin(
        (first, up_shard, query_low, *result_slots)
    )
    shard = scatter_rows(first)
    outputs = exchange(result_slots)
    up_whole = low_sum(up_shard, plane_swap(up_shard, "other"))
    *input_slots, last_sums = by_rows(
        last_kernel,
        "last",
        rows,
        width,
        ([query_low, key_low, value_low, rows_in, middle_grad], []),
        [gain_first],
        [weights],
        [None],
        4,
        [(12,) + section.shape],
        3,
    )
    moved = pin((*input_slots, *outputs, *down_parts))
    input_slots, outputs, down_parts = exchange(moved[:4]), moved[4:8], moved[8:]

    back_sums = jnp.concatenate([hidden_sums, back_sums], axis=0)
    back_sums = jnp.sum(back_sums, axis=1)
    last_sums = jnp.sum(last_sums, axis=1)
    hidden_sums = [back_sums[slot].reshape(4, quarter) for slot in range(4)]
    hidden_sums = jnp.stack(
        [chosen(slot_of[kind], hidden_sums) for kind in range(4)], axis=1
    ).reshape(4, 4 * quarter)
    totals = swap_sum(
        scatter_vector(
            jnp.concatenate(
                [back_sums[at].reshape(4, quarter) for at in range(4, 8)]
                + [last_sums[at].reshape(4, quarter) for at in range(4)]
                + [hidden_sums],
                axis=1,
            ),
            z,
        ),
        1,
    )
    shard, up_whole, totals, *input_slots = pin((shard, up_whole, totals, *input_slots))
    section_whole = low_sum(shard, plane_swap(shard, "other"))
    up_parts = share_by_core(up_whole)
    totals = swap_sum(totals, 2)
    section_whole, totals, *up_parts = pin((section_whole, totals, *up_parts))
    section_parts = share_out(section_whole)
    totals = swap_sum(totals, 4)
    outputs = collect(outputs, low)
    input_gradient = collect(input_slots, wide)
    (up_sum,) = assemble(
        class_places,
        up_parts,
        [
            [(0, at * quarter, at * width + kind * quarter, quarter) for at in range(4)]
            for kind in range(4)
        ],
        [up_weight.shape],
    )
    down_sum = settle(class_places, down_parts, wide).reshape(down_weight.shape)
    moved = pin((*section_parts, outputs, input_gradient, totals, up_sum, down_sum))
    section_parts = moved[:4]
    outputs, input_gradient, totals, up_sum, down_sum = moved[4:]
    in_sum, out_sum = assemble(
        class_places,
        section_parts,
        [[(0, 0, kind * width, width)] for kind in range(3)] + [[(1, 0, 0, width)]],
        [project_in.shape, project_out.shape],
    )
    (
        dbias_sum,
        gain_two_sum,
        shift_two_sum,
        obias_sum,
        gain_one_sum,
        shift_one_sum,
        qbias_sum,
        vbias_sum,
    ) = (totals[at * quarter : (at + 1) * quarter] for at in range(8))
    ubias_sum = totals[8 * quarter :]
    return (
        outputs,
        input_gradient,
        gain_one_sum,
        shift_one_sum,
        in_sum,
        qbias_sum,
        vbias_sum,
        out_sum,
        obias_sum,
        gain_two_sum,
        shift_two_sum,
        up_sum,
        ubias_sum,
        down_sum,
        dbias_sum,
    )


def solution(mesh):
    sizes = dict(mesh.shape)
    exchanged = sizes["dp"] == 2 and sizes["fsdp"] == 4 and sizes["ctx"] == 4
    per_device = per_device_exchanged if exchanged else per_device_gathered
    return jax.shard_map(
        per_device,
        mesh=mesh,
        in_specs=(
            P(("dp", "fsdp"), "ctx", None),
            P(("dp", "fsdp"), "ctx", None),
            P("fsdp"),
            P("fsdp"),
            P("fsdp", None),
            P("fsdp"),
            P("fsdp"),
            P("fsdp", None),
            P("fsdp"),
            P("fsdp"),
            P("fsdp"),
            P("fsdp", None),
            P("fsdp"),
            P("fsdp", None),
            P("fsdp"),
        ),
        out_specs=(
            P(("dp", "fsdp"), "ctx", None),
            P(("dp", "fsdp"), "ctx", None),
            P("fsdp"),
            P("fsdp"),
            P("fsdp", None),
            P("fsdp"),
            P("fsdp"),
            P("fsdp", None),
            P("fsdp"),
            P("fsdp"),
            P("fsdp"),
            P("fsdp", None),
            P("fsdp"),
            P("fsdp", None),
            P("fsdp"),
        ),
        check_vma=False,
    )
```

```python
import functools

import jax
import jax.numpy as jnp
from jax import lax
from jax.experimental import pallas as pl
from jax.experimental.pallas import tpu as pltpu
from jax.sharding import PartitionSpec as P

HEADS = 17
HEAD_DIM = 64


epsilon = 1e-05


def layer_norm(values, gain, shift):
    centred = values - jnp.mean(values, axis=-1, keepdims=True)
    spread = jnp.mean(centred * centred, axis=-1, keepdims=True)
    return centred * lax.rsqrt(spread + epsilon) * gain + shift


def gelu_tanh(values):
    return jax.nn.gelu(values, approximate=True)


def score_grads(
    query_heads, key_heads, value_heads, grad_heads, log_total, row_delta, query_at, key_at
):
    score_scale = HEAD_DIM ** (-0.5)
    scores = (
        jnp.einsum("sqhd,skhd->shqk", query_heads, key_heads, preferred_element_type=jnp.float32)
        * score_scale
    )
    visible = query_at[:, None] >= key_at[None, :]
    shifted = jnp.where(visible, scores - log_total[..., None], -1e30)
    weights = jnp.where(visible, jnp.exp(shifted), 0.0)
    pressure = jnp.einsum(
        "sqhd,skhd->shqk", grad_heads, value_heads, preferred_element_type=jnp.float32
    )
    score_low = (weights * (pressure - row_delta[..., None])).astype(jnp.bfloat16)
    return (weights.astype(jnp.bfloat16), score_low)


def per_device_gathered(
    inputs,
    cotangent,
    first_gain,
    first_shift,
    project_in,
    query_bias,
    value_bias,
    project_out,
    output_bias,
    second_gain,
    second_shift,
    up_weight,
    up_bias,
    down_weight,
    down_bias,
):
    seq_count, block_len, model_width = inputs.shape
    flat_rows = seq_count * block_len
    cycle_size = lax.axis_size("ctx")
    my_block = lax.axis_index("ctx")
    score_scale = HEAD_DIM ** (-0.5)
    head_shape = (seq_count, block_len, HEADS, HEAD_DIM)
    offsets = jnp.arange(block_len, dtype=jnp.int32)
    query_at = my_block * block_len + offsets
    gain_first, shift_first, full_in, qbias_full, vbias_full, full_out, obias_full = (
        lax.all_gather(first_gain, "fsdp", axis=0, tiled=True),
        lax.all_gather(first_shift, "fsdp", axis=0, tiled=True),
        lax.all_gather(project_in, "fsdp", axis=0, tiled=True),
        lax.all_gather(query_bias, "fsdp", axis=0, tiled=True),
        lax.all_gather(value_bias, "fsdp", axis=0, tiled=True),
        lax.all_gather(project_out, "fsdp", axis=0, tiled=True),
        lax.all_gather(output_bias, "fsdp", axis=0, tiled=True),
    )
    rows_in = inputs.astype(jnp.float32).reshape(flat_rows, model_width)
    normed, norm_first_back = jax.vjp(
        layer_norm, rows_in, gain_first.astype(jnp.float32), shift_first.astype(jnp.float32)
    )
    normed_low = normed.astype(jnp.bfloat16)
    projected = jnp.dot(normed_low, full_in, preferred_element_type=jnp.float32)
    queries = (projected[:, :model_width] + qbias_full).astype(jnp.bfloat16)
    key_rows = projected[:, model_width : 2 * model_width].astype(jnp.bfloat16)
    value_rows = (projected[:, 2 * model_width :] + vbias_full).astype(jnp.bfloat16)
    query_heads = queries.reshape(head_shape)
    running_top = jnp.full((seq_count, HEADS, block_len), -1e30, jnp.float32)
    accumulated = jnp.zeros(head_shape, jnp.float32)
    piece_keys = lax.all_gather(
        key_rows.reshape(seq_count, block_len, model_width), "ctx", axis=1, tiled=True
    )
    piece_values = lax.all_gather(
        value_rows.reshape(seq_count, block_len, model_width), "ctx", axis=1, tiled=True
    )
    piece_len = piece_keys.shape[1]
    key_heads = piece_keys.reshape(seq_count, piece_len, HEADS, HEAD_DIM)
    value_heads = piece_values.reshape(seq_count, piece_len, HEADS, HEAD_DIM)
    scores = (
        jnp.einsum("sqhd,skhd->shqk", query_heads, key_heads, preferred_element_type=jnp.float32)
        * score_scale
    )
    key_at = jnp.arange(piece_len, dtype=jnp.int32)
    visible = query_at[:, None] >= key_at[None, :]
    masked = jnp.where(visible, scores, -1e30)
    new_top = jnp.maximum(running_top, jnp.max(masked, axis=-1))
    factor = jnp.exp(running_top - new_top)
    weights = jnp.where(visible, jnp.exp(masked - new_top[..., None]), 0.0)
    row_total = jnp.sum(weights, axis=-1)
    added = jnp.einsum(
        "shqk,skhd->sqhd",
        weights.astype(jnp.bfloat16),
        value_heads,
        preferred_element_type=jnp.float32,
    )
    accumulated = accumulated * jnp.swapaxes(factor, 1, 2)[..., None] + added
    running_top, row_total, accumulated = (new_top, row_total, accumulated)
    attended = accumulated / jnp.swapaxes(row_total, 1, 2)[..., None]
    log_total = running_top + jnp.log(row_total)
    attended_low = attended.reshape(flat_rows, model_width).astype(jnp.bfloat16)
    middle = (
        rows_in + jnp.dot(attended_low, full_out, preferred_element_type=jnp.float32) + obias_full
    )
    gain_second, shift_second, full_up, ubias_full, full_down, dbias_full = (
        lax.all_gather(second_gain, "fsdp", axis=0, tiled=True),
        lax.all_gather(second_shift, "fsdp", axis=0, tiled=True),
        lax.all_gather(up_weight, "fsdp", axis=0, tiled=True),
        lax.all_gather(up_bias, "fsdp", axis=0, tiled=True),
        lax.all_gather(down_weight, "fsdp", axis=0, tiled=True),
        lax.all_gather(down_bias, "fsdp", axis=0, tiled=True),
    )
    normed_two, norm_second_back = jax.vjp(
        layer_norm, middle, gain_second.astype(jnp.float32), shift_second.astype(jnp.float32)
    )
    normed_two_low = normed_two.astype(jnp.bfloat16)
    hidden = jnp.dot(normed_two_low, full_up, preferred_element_type=jnp.float32) + ubias_full
    active, gelu_back = jax.vjp(gelu_tanh, hidden)
    active_low = active.astype(jnp.bfloat16)
    result = (
        middle + jnp.dot(active_low, full_down, preferred_element_type=jnp.float32) + dbias_full
    )
    outputs = result.astype(jnp.bfloat16).reshape(seq_count, block_len, model_width)
    upstream = cotangent.astype(jnp.float32).reshape(flat_rows, model_width)
    upstream_low = upstream.astype(jnp.bfloat16)
    down_grad = jnp.einsum(
        "rf,rd->fd", active_low, upstream_low, preferred_element_type=jnp.float32
    )
    down_bias_grad = jnp.sum(upstream_low.astype(jnp.float32), axis=0)
    active_grad = jnp.einsum(
        "rd,fd->rf", upstream_low, full_down, preferred_element_type=jnp.float32
    )
    (hidden_grad,) = gelu_back(active_grad)
    hidden_low = hidden_grad.astype(jnp.bfloat16)
    up_grad = jnp.einsum(
        "rd,rf->df", normed_two_low, hidden_low, preferred_element_type=jnp.float32
    )
    up_bias_grad = jnp.sum(hidden_low.astype(jnp.float32), axis=0)
    normed_two_grad = jnp.einsum(
        "rf,df->rd", hidden_low, full_up, preferred_element_type=jnp.float32
    )
    middle_part, gain_two_grad, shift_two_grad = norm_second_back(normed_two_grad)
    middle_grad = upstream + middle_part
    middle_low = middle_grad.astype(jnp.bfloat16)
    out_grad = jnp.einsum("rd,re->de", attended_low, middle_low, preferred_element_type=jnp.float32)
    out_bias_grad = jnp.sum(middle_low.astype(jnp.float32), axis=0)
    attended_grad = jnp.einsum(
        "re,de->rd", middle_low, full_out, preferred_element_type=jnp.float32
    )
    grad_low = attended_grad.astype(jnp.bfloat16).reshape(head_shape)
    row_delta = jnp.swapaxes(jnp.sum(grad_low.astype(jnp.float32) * attended, axis=-1), 1, 2)
    gathered_keys, gathered_values = (
        lax.all_gather(
            key_rows.reshape(1, seq_count, block_len, model_width), "ctx", axis=0, tiled=True
        ),
        lax.all_gather(
            value_rows.reshape(1, seq_count, block_len, model_width), "ctx", axis=0, tiled=True
        ),
    )
    block_ids = jnp.arange(cycle_size, dtype=jnp.int32)

    def key_step(carry, inputs_here):
        key_block, value_block, block_index = inputs_here
        key_heads = key_block.reshape(head_shape)
        value_heads = value_block.reshape(head_shape)
        weights_low, score_low = score_grads(
            query_heads,
            key_heads,
            value_heads,
            grad_low,
            log_total,
            row_delta,
            query_at,
            block_index * block_len + offsets,
        )
        carry = (
            carry
            + jnp.einsum(
                "shqk,skhd->sqhd", score_low, key_heads, preferred_element_type=jnp.float32
            )
            * score_scale
        )
        key_term = (
            jnp.einsum(
                "shqk,sqhd->skhd", score_low, query_heads, preferred_element_type=jnp.float32
            )
            * score_scale
        )
        value_term = jnp.einsum(
            "shqk,sqhd->skhd", weights_low, grad_low, preferred_element_type=jnp.float32
        )
        return (
            carry,
            (
                key_term.reshape(seq_count, block_len, model_width),
                value_term.reshape(seq_count, block_len, model_width),
            ),
        )

    query_grad, (key_terms, value_terms) = lax.scan(
        key_step, jnp.zeros(head_shape, jnp.float32), (gathered_keys, gathered_values, block_ids)
    )
    key_sum, value_sum = (
        lax.psum_scatter(
            key_terms.astype(jnp.bfloat16), "ctx", scatter_dimension=0, tiled=True
        ).astype(jnp.float32),
        lax.psum_scatter(
            value_terms.astype(jnp.bfloat16), "ctx", scatter_dimension=0, tiled=True
        ).astype(jnp.float32),
    )
    key_grad = key_sum.reshape(flat_rows, model_width)
    value_grad = value_sum.reshape(flat_rows, model_width)
    query_low = query_grad.reshape(flat_rows, model_width).astype(jnp.bfloat16)
    key_low = key_grad.astype(jnp.bfloat16)
    value_low = value_grad.astype(jnp.bfloat16)
    stacked = jnp.concatenate([query_low, key_low, value_low], axis=1)
    in_grad = jnp.einsum("rd,re->de", normed_low, stacked, preferred_element_type=jnp.float32)
    query_bias_grad = jnp.sum(query_low.astype(jnp.float32), axis=0)
    value_bias_grad = jnp.sum(value_low.astype(jnp.float32), axis=0)
    normed_grad = jnp.einsum("re,de->rd", stacked, full_in, preferred_element_type=jnp.float32)
    input_part, gain_one_grad, shift_one_grad = norm_first_back(normed_grad)
    input_gradient = (middle_grad + input_part).reshape(seq_count, block_len, model_width)
    (
        gain_one_part,
        shift_one_part,
        in_part,
        qbias_part,
        vbias_part,
        out_part,
        obias_part,
        gain_two_part,
        shift_two_part,
        up_part,
        ubias_part,
        down_part,
        dbias_part,
    ) = (
        lax.psum_scatter(
            gain_one_grad.astype(jnp.bfloat16), "fsdp", scatter_dimension=0, tiled=True
        ).astype(jnp.float32),
        lax.psum_scatter(
            shift_one_grad.astype(jnp.bfloat16), "fsdp", scatter_dimension=0, tiled=True
        ).astype(jnp.float32),
        lax.psum_scatter(
            in_grad.astype(jnp.bfloat16), "fsdp", scatter_dimension=0, tiled=True
        ).astype(jnp.float32),
        lax.psum_scatter(
            query_bias_grad.astype(jnp.bfloat16), "fsdp", scatter_dimension=0, tiled=True
        ).astype(jnp.float32),
        lax.psum_scatter(
            value_bias_grad.astype(jnp.bfloat16), "fsdp", scatter_dimension=0, tiled=True
        ).astype(jnp.float32),
        lax.psum_scatter(
            out_grad.astype(jnp.bfloat16), "fsdp", scatter_dimension=0, tiled=True
        ).astype(jnp.float32),
        lax.psum_scatter(
            out_bias_grad.astype(jnp.bfloat16), "fsdp", scatter_dimension=0, tiled=True
        ).astype(jnp.float32),
        lax.psum_scatter(
            gain_two_grad.astype(jnp.bfloat16), "fsdp", scatter_dimension=0, tiled=True
        ).astype(jnp.float32),
        lax.psum_scatter(
            shift_two_grad.astype(jnp.bfloat16), "fsdp", scatter_dimension=0, tiled=True
        ).astype(jnp.float32),
        lax.psum_scatter(
            up_grad.astype(jnp.bfloat16), "fsdp", scatter_dimension=0, tiled=True
        ).astype(jnp.float32),
        lax.psum_scatter(
            up_bias_grad.astype(jnp.bfloat16), "fsdp", scatter_dimension=0, tiled=True
        ).astype(jnp.float32),
        lax.psum_scatter(
            down_grad.astype(jnp.bfloat16), "fsdp", scatter_dimension=0, tiled=True
        ).astype(jnp.float32),
        lax.psum_scatter(
            down_bias_grad.astype(jnp.bfloat16), "fsdp", scatter_dimension=0, tiled=True
        ).astype(jnp.float32),
    )
    (
        gain_one_sum,
        shift_one_sum,
        in_sum,
        qbias_sum,
        vbias_sum,
        out_sum,
        obias_sum,
        gain_two_sum,
        shift_two_sum,
        up_sum,
        ubias_sum,
        down_sum,
        dbias_sum,
    ) = lax.psum(
        (
            gain_one_part,
            shift_one_part,
            in_part,
            qbias_part,
            vbias_part,
            out_part,
            obias_part,
            gain_two_part,
            shift_two_part,
            up_part,
            ubias_part,
            down_part,
            dbias_part,
        ),
        ("dp", "ctx"),
    )
    return (
        outputs,
        input_gradient,
        gain_one_sum,
        shift_one_sum,
        in_sum,
        qbias_sum,
        vbias_sum,
        out_sum,
        obias_sum,
        gain_two_sum,
        shift_two_sum,
        up_sum,
        ubias_sum,
        down_sum,
        dbias_sum,
    )


NT = (((1,), (1,)), ((), ()))
PAIR = 2 * HEAD_DIM


def attend_kernel(place_ref, q_ref, k_ref, v_ref, *refs, count, width, start):
    o_ref, log_ref, keys, values = refs[-4:]
    own_pair = pl.program_id(0)
    pair = own_pair + start
    shift = place_ref[0]
    block_len = q_ref.shape[0] // count
    lane = lax.broadcasted_iota(jnp.int32, (1, PAIR), 1)
    valid = lane + pair * PAIR < width
    first = lane < HEAD_DIM

    def rows(block):
        return pl.ds(pl.multiple_of((block ^ shift) * block_len, block_len), block_len)

    for block in range(count):
        here = pl.ds(block * block_len, block_len)
        keys[here, :] = jnp.where(valid, k_ref[rows(block), :], 0)
        values[here, :] = jnp.where(valid, v_ref[rows(block), :], 0)
    diagonal = lax.broadcasted_iota(jnp.int32, (block_len, block_len), 0) >= (
        lax.broadcasted_iota(jnp.int32, (block_len, block_len), 1)
    )
    for block in range(count):
        seen = (block + 1) * block_len
        before = block * block_len
        queries = q_ref[rows(block), :] * jnp.bfloat16(HEAD_DIM**-0.5)
        parts = []
        logs = log_ref[rows(block), :]
        for half in range(2):
            pick = jnp.logical_and(first if half == 0 else jnp.logical_not(first), valid)
            scores = lax.dot_general(
                jnp.where(pick, queries, 0),
                keys[pl.ds(0, seen), :],
                NT,
                preferred_element_type=jnp.float32,
            )
            last = jnp.where(diagonal, scores[:, before:], -1e30)
            scores = last if block == 0 else jnp.concatenate([scores[:, :before], last], axis=1)
            top = jnp.max(scores, axis=1, keepdims=True)
            weights = jnp.exp(scores - top)
            total = jnp.sum(weights, axis=1, keepdims=True)
            added = jnp.dot(
                weights.astype(jnp.bfloat16),
                values[pl.ds(0, seen), :],
                preferred_element_type=jnp.float32,
            )
            parts.append(added / total)
            logs = jnp.where(lane == 2 * own_pair + half, top + jnp.log(total), logs)
        o_ref[rows(block), :] = jnp.where(first, parts[0], parts[1]).astype(jnp.bfloat16)
        log_ref[rows(block), :] = logs


def attend_back_kernel(
    place_ref,
    q_ref,
    k_ref,
    v_ref,
    g_ref,
    o_ref,
    log_ref,
    *refs,
    count,
    width,
    start,
):
    dq_ref, dk_ref, dv_ref, queries, grads, keys, values = refs[-11:-4]
    keys_turned, logs, deltas, turned = refs[-4:]
    pair = pl.program_id(0) + start
    shift = place_ref[0]
    length = q_ref.shape[0]
    block_len = length // count
    lane = lax.broadcasted_iota(jnp.int32, (1, PAIR), 1)
    valid = lane + pair * PAIR < width
    first = lane < HEAD_DIM
    picks = (jnp.logical_and(first, valid), jnp.logical_and(jnp.logical_not(first), valid))
    half_of = (lax.broadcasted_iota(jnp.int32, (8, PAIR), 1) // HEAD_DIM) == (
        lax.broadcasted_iota(jnp.int32, (8, PAIR), 0)
    )
    ones_of = jnp.where(half_of, 1.0, 0.0)

    def rows(block):
        return pl.ds(pl.multiple_of((block ^ shift) * block_len, block_len), block_len)

    for block in range(count):
        here = pl.ds(block * block_len, block_len)
        key_block = jnp.where(valid, k_ref[rows(block), :], 0)
        keys[here, :] = key_block
        keys_turned[:, here] = key_block.astype(jnp.float32).T.astype(jnp.bfloat16)
        values[here, :] = jnp.where(valid, v_ref[rows(block), :], 0)
        query_block = q_ref[rows(block), :] * jnp.bfloat16(HEAD_DIM**-0.5)
        grad_block = jnp.where(valid, g_ref[rows(block), :], 0)
        for half in range(2):
            queries[half, here, :] = jnp.where(picks[half], query_block, 0)
            grads[half, here, :] = jnp.where(picks[half], grad_block, 0)
        mixed = grad_block.astype(jnp.float32) * jnp.where(
            valid, o_ref[rows(block), :], 0
        ).astype(jnp.float32)
        deltas[:, here] = lax.dot_general(
            ones_of,
            mixed,
            NT,
            preferred_element_type=jnp.float32,
            precision=lax.Precision.HIGHEST,
        )
        logs[:, here] = log_ref[
            0, :, pl.ds(pl.multiple_of((block ^ shift) * block_len, block_len), block_len)
        ]
    diagonal = lax.broadcasted_iota(jnp.int32, (block_len, block_len), 0) <= (
        lax.broadcasted_iota(jnp.int32, (block_len, block_len), 1)
    )
    for block in range(count):
        here = pl.ds(block * block_len, block_len)
        after = pl.ds(block * block_len, length - block * block_len)
        key_total = jnp.zeros((block_len, PAIR), jnp.float32)
        value_total = jnp.zeros((block_len, PAIR), jnp.float32)
        for half in range(2):
            scores = lax.dot_general(
                keys[here, :], queries[half, after, :], NT, preferred_element_type=jnp.float32
            )
            shifted = scores - logs[half : half + 1, after]
            own = jnp.where(diagonal, shifted[:, :block_len], -1e30)
            if block < count - 1:
                own = jnp.concatenate([own, shifted[:, block_len:]], axis=1)
            weights = jnp.exp(own)
            pressure = lax.dot_general(
                values[here, :], grads[half, after, :], NT, preferred_element_type=jnp.float32
            )
            score_low = (weights * (pressure - deltas[half : half + 1, after])).astype(
                jnp.bfloat16
            )
            value_total += jnp.dot(
                weights.astype(jnp.bfloat16),
                grads[half, after, :],
                preferred_element_type=jnp.float32,
            )
            key_total += jnp.dot(
                score_low, queries[half, after, :], preferred_element_type=jnp.float32
            )
            part = pl.ds(half * HEAD_DIM, HEAD_DIM)
            term = jnp.dot(
                keys_turned[part, here], score_low, preferred_element_type=jnp.float32
            )
            if block == 0:
                turned[part, after] = term
            else:
                turned[part, after] += term
        dk_ref[rows(block), :] = key_total.astype(jnp.bfloat16)
        dv_ref[rows(block), :] = value_total.astype(jnp.bfloat16)
    for block in range(count):
        here = pl.ds(block * block_len, block_len)
        dq_ref[rows(block), :] = (turned[:, here].T * HEAD_DIM**-0.5).astype(jnp.bfloat16)


def attend(place, queries, key_rows, value_rows, count, start, pairs, before):
    length, width = queries.shape
    heads_block = pl.BlockSpec((length, PAIR), lambda pair, place_ref: (0, pair + start))
    return pl.pallas_call(
        functools.partial(attend_kernel, count=count, width=width, start=start),
        grid_spec=pltpu.PrefetchScalarGridSpec(
            num_scalar_prefetch=1,
            grid=(pairs,),
            in_specs=[heads_block] * 3 + [pl.BlockSpec(memory_space=pl.ANY)] * len(before),
            out_specs=[
                heads_block,
                pl.BlockSpec((length, 128), lambda pair, place_ref: (0, 0)),
            ],
            scratch_shapes=[pltpu.VMEM((length, PAIR), jnp.bfloat16)] * 2,
        ),
        out_shape=[
            jax.ShapeDtypeStruct((length, width), jnp.bfloat16),
            jax.ShapeDtypeStruct((length, 128), jnp.float32),
        ],
        input_output_aliases={4 + at: at for at in range(len(before))},
        compiler_params=pltpu.CompilerParams(vmem_limit_bytes=48 * 2**20),
        cost_estimate=SMALL,
        name="attend",
    )(place, queries, key_rows, value_rows, *before)


def attend_back(
    place, queries, key_rows, value_rows, grads, attended, logs, count, start, pairs, before
):
    length, width = queries.shape
    heads_block = pl.BlockSpec((length, PAIR), lambda pair, place_ref: (0, pair + start))
    low_rows = pltpu.VMEM((length, PAIR), jnp.bfloat16)
    low_pair = pltpu.VMEM((2, length, PAIR), jnp.bfloat16)
    return pl.pallas_call(
        functools.partial(attend_back_kernel, count=count, width=width, start=start),
        grid_spec=pltpu.PrefetchScalarGridSpec(
            num_scalar_prefetch=1,
            grid=(pairs,),
            in_specs=[heads_block] * 5
            + [pl.BlockSpec((1, 2, length), lambda pair, place_ref: (pair, 0, 0))]
            + [pl.BlockSpec(memory_space=pl.ANY)] * len(before),
            out_specs=[heads_block] * 3,
            scratch_shapes=[
                low_pair,
                low_pair,
                low_rows,
                low_rows,
                pltpu.VMEM((PAIR, length), jnp.bfloat16),
                pltpu.VMEM((2, length), jnp.float32),
                pltpu.VMEM((8, length), jnp.float32),
                pltpu.VMEM((PAIR, length), jnp.float32),
            ],
        ),
        out_shape=[jax.ShapeDtypeStruct((length, width), jnp.bfloat16)] * 3,
        input_output_aliases={7 + at: at for at in range(len(before))},
        compiler_params=pltpu.CompilerParams(vmem_limit_bytes=48 * 2**20),
        cost_estimate=SMALL,
        name="attend_back",
    )(place, queries, key_rows, value_rows, grads, attended, logs, *before)


def settle_kernel(place_ref, *refs):
    pieces, out_ref = refs[:-1], refs[-1]
    for at, piece in enumerate(pieces):
        out_ref[place_ref[at]] = piece[...].astype(out_ref.dtype)


def settle(places, pieces, dtype):
    return pl.pallas_call(
        settle_kernel,
        in_specs=[pl.BlockSpec(memory_space=pltpu.SMEM)]
        + [pl.BlockSpec(memory_space=pltpu.VMEM)] * len(pieces),
        out_specs=pl.BlockSpec(memory_space=pltpu.VMEM),
        out_shape=jax.ShapeDtypeStruct((len(pieces),) + pieces[0].shape, dtype),
        compiler_params=pltpu.CompilerParams(vmem_limit_bytes=48 * 2**20),
        cost_estimate=SMALL,
        name="settle",
    )(places, *pieces)


def plane_partner(device, kind):
    core = device & 1
    if kind == "core":
        return device ^ 1
    if kind == "far":
        return device ^ (3 if core else 5)
    if kind == "near":
        return device ^ (2 if core else 4)
    return device ^ (4 if core else 2)


def plane_swap(values, kind):
    return lax.ppermute(
        values, ("dp", "ctx"), [(device, plane_partner(device, kind)) for device in range(8)]
    )


def ctx_swap(values, bits):
    return lax.ppermute(values, "ctx", [(device, device ^ bits) for device in range(4)])


def low_sum(*terms):
    return sum(term.astype(jnp.float32) for term in terms).astype(jnp.bfloat16)


def reduce_core(pieces):
    return plane_swap(pieces[2], "core"), plane_swap(pieces[3], "core")


def share_out(whole):
    return [whole] + [plane_swap(whole, kind) for kind in ("near", "core", "far")]


def share_by_core(whole, near):
    return [whole, near, plane_swap(whole, "core"), plane_swap(near, "core")]


def scatter_rows(values):
    return lax.psum_scatter(values, "fsdp", scatter_dimension=0, tiled=True)


def chosen(index, options):
    result = options[-1]
    for at in range(len(options) - 2, -1, -1):
        result = jnp.where(index == at, options[at], result)
    return result


def gather_vector(values, z):
    around = [values] + [
        lax.ppermute(values, "fsdp", [(device, (device + step) % 4) for device in range(4)])
        for step in range(1, 4)
    ]
    return jnp.stack([chosen((z - at) % 4, around) for at in range(4)])


def scatter_vector(values, z):
    rows = [values[at] for at in range(4)]
    total = chosen(z, rows)
    for step in range(1, 4):
        total = total + lax.ppermute(
            chosen((z + step) % 4, rows),
            "fsdp",
            [(device, (device + step) % 4) for device in range(4)],
        )
    return total


def swap_sum(total, bits):
    return total + lax.ppermute(
        total, ("dp", "ctx"), [(device, device ^ bits) for device in range(8)]
    )


def product(left, right, dims):
    return lax.dot_general(left, right, ((dims[:1], dims[1:]), ((), ())),
                           preferred_element_type=jnp.float32)


def gelu_pair(values):
    inner = 0.7978845608028654
    cubic = inner * 0.044715
    squared = values * values
    curve = jnp.tanh(values * (inner + cubic * squared))
    half = 0.5 * values
    active = half + half * curve
    slope = 0.5 + 0.5 * curve + half * (1.0 - curve * curve) * (inner + 3.0 * cubic * squared)
    return active, slope


SMALL = pl.CostEstimate(flops=1024, bytes_accessed=1024, transcendentals=0)


def unit_of(values):
    centred = values - jnp.mean(values, axis=-1, keepdims=True)
    scale = lax.rsqrt(jnp.mean(centred * centred, axis=-1, keepdims=True) + epsilon)
    return centred * scale, scale


def fold(values):
    rows, width = values.shape
    return jnp.sum(values.reshape(rows // 8, 8, width), axis=0)


def front_kernel(places_ref, vectors_ref, *refs):
    slots, pieces = refs[:4], refs[4:20]
    x_ref, h_ref, q_ref, k_ref, v_ref, all_ref, weights, arrived, left = refs[20:]
    copies = [
        pltpu.make_async_copy(piece, weights.at[places_ref[at]], arrived.at[at])
        for at, piece in enumerate(pieces)
    ]
    for copy in copies:
        copy.start()
    rows, width = x_ref.shape
    step = rows // 4
    for at, slot in enumerate(slots):
        here = pl.ds(at * step, step)
        values = slot[...].astype(jnp.float32).T
        x_ref[here, :] = values.astype(jnp.bfloat16)
        unit, _ = unit_of(values)
        h_ref[here, :] = (unit * vectors_ref[0:1, :] + vectors_ref[1:2, :]).astype(jnp.bfloat16)
    for copy in copies:
        copy.wait()
    leave = pltpu.make_async_copy(weights, all_ref, left)
    leave.start()
    for section, out_ref in enumerate((q_ref, k_ref, v_ref)):

        def multiply(at, carry, section=section, out_ref=out_ref):
            here = pl.ds(pl.multiple_of(at * step, step), step)
            matrix = weights[4 * section : 4 * section + 4].reshape(width, width)
            total = jnp.dot(h_ref[here, :], matrix, preferred_element_type=jnp.float32)
            if section != 1:
                row = 2 if section == 0 else 3
                total = total + vectors_ref[row : row + 1, :]
            out_ref[here, :] = total.astype(jnp.bfloat16)
            return carry

        lax.fori_loop(0, rows // step, multiply, 0)
    leave.wait()


def front(places, slots, vectors, pieces):
    width, step = slots[0].shape
    rows = 4 * step
    vmem = pl.BlockSpec(memory_space=pltpu.VMEM)
    hbm = pl.BlockSpec(memory_space=pl.ANY)
    shape = jax.ShapeDtypeStruct((rows, width), jnp.bfloat16)
    whole = (16,) + pieces[0].shape
    return pl.pallas_call(
        front_kernel,
        in_specs=[pl.BlockSpec(memory_space=pltpu.SMEM)] + [vmem] * 5 + [hbm] * 16,
        out_specs=[vmem] * 5 + [hbm],
        out_shape=[shape] * 5 + [jax.ShapeDtypeStruct(whole, jnp.bfloat16)],
        scratch_shapes=[
            pltpu.VMEM(whole, jnp.bfloat16),
            pltpu.SemaphoreType.DMA((16,)),
            pltpu.SemaphoreType.DMA,
        ],
        compiler_params=pltpu.CompilerParams(vmem_limit_bytes=56 * 2**20),
        cost_estimate=SMALL,
        name="front",
    )(places, vectors, *slots, *pieces)


def turn_kernel(*refs):
    slots, out_ref = refs[:-1], refs[-1]
    step = slots[0].shape[1]
    for at, slot in enumerate(slots):
        out_ref[pl.ds(at * step, step), :] = (
            slot[...].astype(jnp.float32).T.astype(jnp.bfloat16)
        )


def turn(slots):
    width, step = slots[0].shape
    return pl.pallas_call(
        turn_kernel,
        out_shape=jax.ShapeDtypeStruct((len(slots) * step, width), jnp.bfloat16),
        compiler_params=pltpu.CompilerParams(vmem_limit_bytes=48 * 2**20),
        cost_estimate=SMALL,
        name="turn",
    )(*slots)


def assemble_kernel(place_ref, *refs, plan):
    pieces, outs = refs[:4], refs[4:]
    for at, piece in enumerate(pieces):
        for kind, moves in enumerate(plan):

            @pl.when(place_ref[at] == kind)
            def _(piece=piece, moves=moves):
                for out, source, target, size in moves:
                    outs[out][:, target : target + size] = piece[
                        :, source : source + size
                    ].astype(jnp.float32)


def assemble(places, pieces, plan, shapes):
    vmem = pl.BlockSpec(memory_space=pltpu.VMEM)
    return pl.pallas_call(
        functools.partial(assemble_kernel, plan=plan),
        in_specs=[pl.BlockSpec(memory_space=pltpu.SMEM)] + [vmem] * 4,
        out_specs=[vmem] * len(shapes),
        out_shape=[jax.ShapeDtypeStruct(shape, jnp.float32) for shape in shapes],
        compiler_params=pltpu.CompilerParams(vmem_limit_bytes=48 * 2**20),
        cost_estimate=SMALL,
        name="assemble",
    )(places, *pieces)


def store_turned(step, refs, values):
    size = refs[0].shape[1]
    share = values.shape[0] // size
    for at, ref in enumerate(refs):

        @pl.when(step == at // share)
        def _(at=at, ref=ref):
            first = (at % share) * size
            ref[...] = values[first : first + size].T.astype(ref.dtype)


def fetch(step, copies):
    @pl.when(step == 0)
    def _():
        for copy in copies:
            copy.start()


def arrive(step, copy):
    @pl.when(step == 0)
    def _():
        copy.wait()


def middle_kernel(x_ref, o_ref, vectors_ref, all_ref, middle_ref, h_ref, weights, arrived):
    step = pl.program_id(0)
    width = x_ref.shape[1]
    copy = pltpu.make_async_copy(all_ref.at[pl.ds(12, 4)], weights, arrived)
    fetch(step, [copy])
    arrive(step, copy)
    middle = (
        x_ref[...].astype(jnp.float32)
        + jnp.dot(
            o_ref[...], weights[...].reshape(width, width), preferred_element_type=jnp.float32
        )
        + vectors_ref[0:1, :]
    )
    middle_ref[...] = middle
    unit, _ = unit_of(middle)
    h_ref[...] = (unit * vectors_ref[1:2, :] + vectors_ref[2:3, :]).astype(jnp.bfloat16)


def up_kernel(h_ref, biases_ref, *refs):
    sources = refs[:2]
    active_refs, slope_refs = refs[2:4], refs[4:6]
    weights, arrived = refs[6:]
    step = pl.program_id(0)
    copies = [
        pltpu.make_async_copy(source, weights.at[at], arrived.at[at])
        for at, source in enumerate(sources)
    ]
    fetch(step, copies)
    for at in range(2):
        arrive(step, copies[at])
        hidden = (
            jnp.dot(h_ref[...], weights[at], preferred_element_type=jnp.float32)
            + biases_ref[at : at + 1, :]
        )
        active, slope = gelu_pair(hidden)
        active_refs[at][...] = active.astype(jnp.bfloat16)
        slope_refs[at][...] = slope.astype(jnp.bfloat16)


def down_kernel(middle_ref, vectors_ref, *refs):
    actives, sources = refs[:4], refs[4:8]
    out_refs = refs[8:12]
    weights, arrived = refs[12:]
    step = pl.program_id(0)
    copies = [
        pltpu.make_async_copy(source, weights.at[at], arrived.at[at])
        for at, source in enumerate(sources)
    ]
    fetch(step, copies)
    total = middle_ref[...] + vectors_ref[0:1, :]
    for at in range(4):
        arrive(step, copies[at])
        total = total + jnp.dot(
            actives[at][...], weights[at], preferred_element_type=jnp.float32
        )
    store_turned(step, out_refs, total)


def norm_back(values, gain, grad):
    unit, scale = unit_of(values)
    turned = grad * gain
    inner = (
        turned
        - jnp.mean(turned, axis=-1, keepdims=True)
        - unit * jnp.mean(turned * unit, axis=-1, keepdims=True)
    )
    return scale * inner, grad * unit


def hidden_kernel(g_ref, *refs):
    slopes, sources = refs[:2], refs[2:4]
    hidden_refs, sums_ref = refs[4:6], refs[6]
    weights, arrived = refs[7:]
    step = pl.program_id(0)
    copies = [
        pltpu.make_async_copy(source, weights.at[at], arrived.at[at])
        for at, source in enumerate(sources)
    ]
    fetch(step, copies)

    @pl.when(step == 0)
    def _():
        sums_ref[...] = jnp.zeros_like(sums_ref)

    upstream = g_ref[...]
    for at in range(2):
        arrive(step, copies[at])
        hidden = lax.dot_general(
            upstream, weights[at], NT, preferred_element_type=jnp.float32
        )
        hidden = (hidden * slopes[at][...].astype(jnp.float32)).astype(jnp.bfloat16)
        hidden_refs[at][...] = hidden
        sums_ref[at] += fold(hidden.astype(jnp.float32))
    sums_ref[2] += fold(upstream.astype(jnp.float32))


def back_kernel(g_ref, middle_ref, vectors_ref, *refs):
    hiddens, sources, all_ref = refs[:4], refs[4:8], refs[8]
    grad_ref, low_ref, out_ref, sums_ref = refs[9:13]
    weights, out_weights, arrived = refs[13:]
    step = pl.program_id(0)
    width = middle_ref.shape[1]
    copies = [
        pltpu.make_async_copy(source, weights.at[at], arrived.at[at])
        for at, source in enumerate(sources)
    ] + [pltpu.make_async_copy(all_ref.at[pl.ds(12, 4)], out_weights, arrived.at[4])]
    fetch(step, copies)

    @pl.when(step == 0)
    def _():
        sums_ref[...] = jnp.zeros_like(sums_ref)

    total = jnp.zeros(middle_ref.shape, jnp.float32)
    for at in range(4):
        arrive(step, copies[at])
        total = total + lax.dot_general(
            hiddens[at][...], weights[at], NT, preferred_element_type=jnp.float32
        )
    part, gain_term = norm_back(middle_ref[...], vectors_ref[0:1, :], total)
    sums_ref[0] += fold(gain_term)
    sums_ref[1] += fold(total)
    grad = g_ref[...].astype(jnp.float32) + part
    grad_ref[...] = grad
    grad_low = grad.astype(jnp.bfloat16)
    low_ref[...] = grad_low
    sums_ref[2] += fold(grad_low.astype(jnp.float32))
    arrive(step, copies[4])
    out_ref[...] = lax.dot_general(
        grad_low,
        out_weights[...].reshape(width, width),
        NT,
        preferred_element_type=jnp.float32,
    ).astype(jnp.bfloat16)


def last_kernel(q_ref, k_ref, v_ref, x_ref, grad_ref, vectors_ref, all_ref, *refs):
    out_refs = refs[:4]
    sums_ref, weights, arrived = refs[4:]
    step = pl.program_id(0)
    width = x_ref.shape[1]
    copies = [
        pltpu.make_async_copy(
            all_ref.at[pl.ds(4 * at, 4)], weights.at[pl.ds(4 * at, 4)], arrived.at[at]
        )
        for at in range(3)
    ]
    fetch(step, copies)
    total = jnp.zeros(x_ref.shape, jnp.float32)
    for at, ref in enumerate((q_ref, k_ref, v_ref)):
        arrive(step, copies[at])
        total = total + lax.dot_general(
            ref[...],
            weights[4 * at : 4 * at + 4].reshape(width, width),
            NT,
            preferred_element_type=jnp.float32,
        )
    part, gain_term = norm_back(x_ref[...].astype(jnp.float32), vectors_ref[0:1, :], total)
    store_turned(step, out_refs, grad_ref[...] + part)

    @pl.when(step == 0)
    def _():
        sums_ref[...] = jnp.zeros_like(sums_ref)

    terms = (
        gain_term,
        total,
        q_ref[...].astype(jnp.float32),
        v_ref[...].astype(jnp.float32),
    )
    for at, term in enumerate(terms):
        sums_ref[at] += fold(term)


def by_rows(kernel, name, rows, width, tiled, whole, remote, outs, sums, scratch, sems):
    step = 512
    tile = pl.BlockSpec((step, width), lambda at: (at, 0))
    out_specs, out_shape = [], []
    for dtype in outs:
        if dtype is None:
            out_specs += [pl.BlockSpec((width, rows // 4), lambda at: (0, 0))] * 4
            out_shape += [jax.ShapeDtypeStruct((width, rows // 4), jnp.bfloat16)] * 4
        else:
            out_specs.append(tile)
            out_shape.append(jax.ShapeDtypeStruct((rows, width), dtype))
    if sums:
        out_specs.append(pl.BlockSpec((sums, 8, width), lambda at: (0, 0, 0)))
        out_shape.append(jax.ShapeDtypeStruct((sums, 8, width), jnp.float32))
    return pl.pallas_call(
        kernel,
        grid=(rows // step,),
        in_specs=[tile] * len(tiled[0])
        + [pl.BlockSpec(value.shape, lambda at: (0, 0)) for value in whole]
        + [tile] * len(tiled[1])
        + [pl.BlockSpec(memory_space=pl.ANY)] * len(remote),
        out_specs=out_specs,
        out_shape=out_shape,
        scratch_shapes=[pltpu.VMEM(shape, jnp.bfloat16) for shape in scratch]
        + [pltpu.SemaphoreType.DMA((sems,)) if sems > 1 else pltpu.SemaphoreType.DMA],
        compiler_params=pltpu.CompilerParams(vmem_limit_bytes=60 * 2**20),
        cost_estimate=SMALL,
        name=name,
    )(*tiled[0], *whole, *tiled[1], *remote)


def per_device_exchanged(
    inputs,
    cotangent,
    first_gain,
    first_shift,
    project_in,
    query_bias,
    value_bias,
    project_out,
    output_bias,
    second_gain,
    second_shift,
    up_weight,
    up_bias,
    down_weight,
    down_bias,
):
    seq_count, block_len, width = inputs.shape
    low = jnp.bfloat16
    wide = jnp.float32
    c = lax.axis_index("ctx")
    y = lax.axis_index("dp")
    z = lax.axis_index("fsdp")
    core = c & 1
    x = c >> 1
    mine = core * 2 + jnp.where(core == 0, y, x)
    across = (1 - core) * 2 + jnp.where(core == 0, x, y)
    classes = [mine, mine ^ 1, across, across ^ 1]
    slot_of = [
        chosen(0, [sum(at * (classes[at] == kind).astype(jnp.int32) for at in range(4))])
        for kind in range(4)
    ]
    quarter = width // 4
    rows, area = seq_count * block_len, (width, width)
    pin = lax.optimization_barrier
    place = jnp.stack([c])
    places = jnp.stack([c ^ at for at in range(4)])
    class_places = jnp.stack(classes)

    def spread(values):
        values = jnp.swapaxes(values, 1, 2)
        return [lax.dynamic_index_in_dim(values, c, 0, keepdims=False)] + [
            ctx_swap(lax.dynamic_index_in_dim(values, c ^ bits, 0, keepdims=False), bits)
            for bits in range(1, 4)
        ]

    def exchange(pieces):
        return [pieces[0]] + [ctx_swap(pieces[bits], bits) for bits in range(1, 4)]

    def collect(moved, dtype):
        return jnp.swapaxes(settle(places, moved, dtype), 1, 2)

    sections = [
        project_in[:, :width],
        project_in[:, width : 2 * width],
        project_in[:, 2 * width :],
        project_out,
    ]
    section = chosen(mine, sections)
    section, inputs = pin((section, inputs))
    shards = [
        lax.ppermute(section, "fsdp", [(device, (device + step) % 4) for device in range(4)])
        for step in range(1, 4)
    ]
    turned_in = jnp.swapaxes(inputs, 1, 2)
    slots_in = [
        lax.dynamic_index_in_dim(turned_in, c ^ bits, 0, keepdims=False) for bits in range(4)
    ]
    pieces_in = (
        first_gain,
        first_shift,
        query_bias,
        value_bias,
        output_bias,
        second_gain,
        second_shift,
        down_bias,
        up_bias,
    )
    slots_in = [slots_in[0]] + [ctx_swap(slots_in[bits], bits) for bits in range(1, 4)]
    up_weight, down_weight, *moved = pin(
        (up_weight, down_weight, *shards, *slots_in, *pieces_in)
    )
    shards, slots_in, pieces_in = moved[:3], moved[3:7], moved[7:]
    vectors = gather_vector(jnp.concatenate(pieces_in), z).astype(wide)
    up_piece = jnp.concatenate(
        [
            lax.dynamic_slice_in_dim(up_weight, at * width + mine * quarter, quarter, 1)
            for at in range(4)
        ],
        axis=1,
    )
    near_shards = [plane_swap(shard, "near") for shard in shards]
    cotangent, *near_shards = pin((cotangent, *near_shards))
    slots_back = spread(cotangent)
    around = (
        sections
        + shards
        + near_shards
        + [plane_swap(shard, "core") for shard in shards]
        + [plane_swap(shard, "core") for shard in near_shards]
    )
    around_places = jnp.stack(
        [kind * 4 + z for kind in range(4)]
        + [kind * 4 + (z - step) % 4 for kind in classes for step in range(1, 4)]
    )
    up_own = lax.all_gather(up_piece, "fsdp", axis=0, tiled=True)
    down_piece = lax.dynamic_slice_in_dim(down_weight, mine * quarter, quarter, 0)
    gain_first, shift_first, qbias, vbias, obias, gain_second, shift_second, dbias = (
        vectors[:, at * quarter : (at + 1) * quarter].reshape(1, width) for at in range(8)
    )
    ubias = vectors[:, 8 * quarter :].reshape(4, 4, quarter)
    ubias = jnp.concatenate(
        [
            chosen(kind, [ubias[:, at] for at in range(4)]).reshape(1, width)
            for kind in classes
        ],
        axis=0,
    )

    rows_in, normed_low, queries, key_rows, value_rows, weights = front(
        around_places,
        slots_in,
        jnp.concatenate([gain_first, shift_first, qbias, vbias], axis=0),
        around,
    )
    up_own, down_piece, queries = pin((up_own, down_piece, queries))
    down_own = lax.all_gather(down_piece, "fsdp", axis=0, tiled=True)
    up_near, up_core = plane_swap(up_own, "near"), plane_swap(up_own, "core")
    attended, logs = attend(place, queries, key_rows, value_rows, seq_count, 0, 9, [])
    up_core, up_near, attended = pin((up_core, up_near, attended))
    logs = logs.T.reshape(64, 2, rows)
    logs_one, logs_two = logs[:5], logs[5:9]
    middle, normed_two_low = by_rows(
        middle_kernel,
        "middle",
        rows,
        width,
        ([rows_in, attended], []),
        [jnp.concatenate([obias, gain_second, shift_second], axis=0)],
        [weights],
        [wide, low],
        0,
        [(4,) + section.shape],
        1,
    )
    up_slots = [up_own, up_near, up_core, plane_swap(up_near, "core")]
    active, slopes = [None] * 4, [None] * 4

    def up(first):
        outs = by_rows(
            up_kernel,
            "up",
            rows,
            width,
            ([normed_two_low], []),
            [jnp.concatenate([ubias[first : first + 1], ubias[first + 2 : first + 3]], axis=0)],
            [up_slots[first], up_slots[first + 2]],
            [low] * 4,
            0,
            [(2,) + area],
            2,
        )
        active[first], active[first + 2], slopes[first], slopes[first + 2] = outs

    up(0)
    up_slots[3], slots_back[3], down_own, active[0], active[2] = pin(
        (up_slots[3], slots_back[3], down_own, active[0], active[2])
    )
    down_near, down_core = plane_swap(down_own, "near"), plane_swap(down_own, "core")
    upstream_low = turn(slots_back)
    up(1)

    def turned_product(left, right):
        return product(left, right, (0, 0)).astype(low)

    down_terms = [turned_product(active[slot], upstream_low) for slot in (3, 2)]
    upstream_low, down_near, *down_terms = pin((upstream_low, down_near, *down_terms))
    down_terms += [turned_product(active[slot], upstream_low) for slot in (1, 0)]
    down_terms = down_terms[::-1]
    down_far, down_far_two = reduce_core(down_terms)
    upstream_low, *down_terms = pin((upstream_low, *down_terms))
    hidden_low = [None] * 4

    def hidden(first, upstream):
        hidden_low[first], hidden_low[first + 2], sums = by_rows(
            hidden_kernel,
            "hidden",
            rows,
            width,
            ([upstream], [slopes[first], slopes[first + 2]]),
            [],
            [down_slots[first], down_slots[first + 2]],
            [low] * 2,
            3,
            [(2,) + area],
            2,
        )
        return sums

    down_slots = [down_own, down_near, down_core, plane_swap(down_near, "core")]
    sums_even = hidden(0, upstream_low)
    down_second = low_sum(down_terms[1], down_far_two)
    upstream_late, sums_even, down_second = pin((upstream_low, sums_even, down_second))
    down_close = plane_swap(down_second, "near")
    sums_odd = hidden(1, upstream_late)
    hidden_sums = jnp.stack(
        [sums_even[0], sums_odd[0], sums_even[1], sums_odd[1], sums_even[2]]
    )
    down_far, *hidden_low = pin((down_far, *hidden_low))
    up_terms = [turned_product(normed_two_low, hidden_low[slot]) for slot in (3, 2)]
    normed_two_low, *up_terms = pin((normed_two_low, *up_terms))
    up_terms += [turned_product(normed_two_low, hidden_low[slot]) for slot in (1, 0)]
    up_terms = up_terms[::-1]
    up_far, up_far_two = reduce_core(up_terms)
    up_second = low_sum(up_terms[1], up_far_two)
    down_first = low_sum(down_terms[0], down_far, down_close)
    up_second, up_far, down_first, moved, *hidden_low = pin(
        (up_second, up_far, down_first, up_terms[0], *hidden_low)
    )
    up_terms[0] = moved
    down_shard = scatter_rows(down_first)
    up_close = plane_swap(up_second, "near")
    middle_grad, middle_low, grad_low, back_sums = by_rows(
        back_kernel,
        "back",
        rows,
        width,
        ([upstream_low, middle], hidden_low),
        [gain_second],
        up_slots + [weights],
        [wide, low, low],
        3,
        [(4,) + area, (4,) + section.shape],
        5,
    )
    out_term = turned_product(attended, middle_low)
    up_first = low_sum(up_terms[0], up_far, up_close)
    grad_low, out_term, up_first = pin((grad_low, out_term, up_first))
    in_grads = attend_back(
        place, queries, key_rows, value_rows, grad_low, attended, logs_one, seq_count, 0, 5, []
    )
    up_first, down_shard, *in_grads = pin((up_first, down_shard, *in_grads))
    up_shard = scatter_rows(up_first)
    down_whole = low_sum(down_shard, plane_swap(down_shard, "other"))
    in_grads = attend_back(
        place,
        queries,
        key_rows,
        value_rows,
        grad_low,
        attended,
        logs_two,
        seq_count,
        5,
        4,
        in_grads,
    )
    down_whole, *in_grads = pin((down_whole, *in_grads))
    down_beside = plane_swap(down_whole, "near")
    in_terms = [turned_product(normed_low, grad) for grad in in_grads]
    section_grads = in_terms + [out_term]
    sections_mine = [chosen(kind, section_grads) for kind in classes]
    far, far_two = reduce_core(sections_mine)
    second = low_sum(sections_mine[1], far_two)
    second, far, middle, *in_grads = pin((second, far, middle, *in_grads))
    query_low, key_low, value_low = in_grads
    close = plane_swap(second, "near")
    result_slots = by_rows(
        down_kernel,
        "down",
        rows,
        width,
        ([middle], active),
        [dbias],
        down_slots,
        [None],
        0,
        [(4,) + area],
        4,
    )
    first = low_sum(sections_mine[0], far, close)
    first, up_shard, query_low, down_beside, *result_slots = pin(
        (first, up_shard, query_low, down_beside, *result_slots)
    )
    down_parts = share_by_core(down_whole, down_beside)
    shard = scatter_rows(first)
    outputs = exchange(result_slots)
    up_whole = low_sum(up_shard, plane_swap(up_shard, "other"))
    *input_slots, last_sums = by_rows(
        last_kernel,
        "last",
        rows,
        width,
        ([query_low, key_low, value_low, rows_in, middle_grad], []),
        [gain_first],
        [weights],
        [None],
        4,
        [(12,) + section.shape],
        3,
    )
    moved = pin((*input_slots, *outputs, *down_parts))
    input_slots, outputs, down_parts = exchange(moved[:4]), moved[4:8], moved[8:]

    back_sums = jnp.concatenate([hidden_sums, back_sums], axis=0)
    back_sums = jnp.sum(back_sums, axis=1)
    last_sums = jnp.sum(last_sums, axis=1)
    hidden_sums = [back_sums[slot].reshape(4, quarter) for slot in range(4)]
    hidden_sums = jnp.stack(
        [chosen(slot_of[kind], hidden_sums) for kind in range(4)], axis=1
    ).reshape(4, 4 * quarter)
    totals = swap_sum(
        scatter_vector(
            jnp.concatenate(
                [back_sums[at].reshape(4, quarter) for at in range(4, 8)]
                + [last_sums[at].reshape(4, quarter) for at in range(4)]
                + [hidden_sums],
                axis=1,
            ),
            z,
        ),
        1,
    )
    up_beside = plane_swap(up_whole, "near")
    shard, up_whole, up_beside, totals = pin((shard, up_whole, up_beside, totals))
    section_whole = low_sum(shard, plane_swap(shard, "other"))
    up_parts = share_by_core(up_whole, up_beside)
    totals = swap_sum(totals, 2)
    section_whole, totals, *up_parts = pin((section_whole, totals, *up_parts))
    section_parts = share_out(section_whole)
    totals = swap_sum(totals, 4)
    outputs = collect(outputs, low)
    input_gradient = collect(input_slots, wide)
    (up_sum,) = assemble(
        class_places,
        up_parts,
        [
            [(0, at * quarter, at * width + kind * quarter, quarter) for at in range(4)]
            for kind in range(4)
        ],
        [up_weight.shape],
    )
    down_sum = settle(class_places, down_parts, wide).reshape(down_weight.shape)
    moved = pin((*section_parts, outputs, input_gradient, totals, up_sum, down_sum))
    section_parts = moved[:4]
    outputs, input_gradient, totals, up_sum, down_sum = moved[4:]
    in_sum, out_sum = assemble(
        class_places,
        section_parts,
        [[(0, 0, kind * width, width)] for kind in range(3)] + [[(1, 0, 0, width)]],
        [project_in.shape, project_out.shape],
    )
    (
        dbias_sum,
        gain_two_sum,
        shift_two_sum,
        obias_sum,
        gain_one_sum,
        shift_one_sum,
        qbias_sum,
        vbias_sum,
    ) = (totals[at * quarter : (at + 1) * quarter] for at in range(8))
    ubias_sum = totals[8 * quarter :]
    return (
        outputs,
        input_gradient,
        gain_one_sum,
        shift_one_sum,
        in_sum,
        qbias_sum,
        vbias_sum,
        out_sum,
        obias_sum,
        gain_two_sum,
        shift_two_sum,
        up_sum,
        ubias_sum,
        down_sum,
        dbias_sum,
    )


def solution(mesh):
    sizes = dict(mesh.shape)
    exchanged = sizes["dp"] == 2 and sizes["fsdp"] == 4 and sizes["ctx"] == 4
    per_device = per_device_exchanged if exchanged else per_device_gathered
    return jax.shard_map(
        per_device,
        mesh=mesh,
        in_specs=(
            P(("dp", "fsdp"), "ctx", None),
            P(("dp", "fsdp"), "ctx", None),
            P("fsdp"),
            P("fsdp"),
            P("fsdp", None),
            P("fsdp"),
            P("fsdp"),
            P("fsdp", None),
            P("fsdp"),
            P("fsdp"),
            P("fsdp"),
            P("fsdp", None),
            P("fsdp"),
            P("fsdp", None),
            P("fsdp"),
        ),
        out_specs=(
            P(("dp", "fsdp"), "ctx", None),
            P(("dp", "fsdp"), "ctx", None),
            P("fsdp"),
            P("fsdp"),
            P("fsdp", None),
            P("fsdp"),
            P("fsdp"),
            P("fsdp", None),
            P("fsdp"),
            P("fsdp"),
            P("fsdp"),
            P("fsdp", None),
            P("fsdp"),
            P("fsdp", None),
            P("fsdp"),
        ),
        check_vma=False,
    )
```

```python
import functools

import jax
import jax.numpy as jnp
from jax import lax
from jax.experimental import pallas as pl
from jax.experimental.pallas import tpu as pltpu
from jax.sharding import PartitionSpec as P

HEADS = 17
HEAD_DIM = 64


epsilon = 1e-05


def layer_norm(values, gain, shift):
    centred = values - jnp.mean(values, axis=-1, keepdims=True)
    spread = jnp.mean(centred * centred, axis=-1, keepdims=True)
    return centred * lax.rsqrt(spread + epsilon) * gain + shift


def gelu_tanh(values):
    return jax.nn.gelu(values, approximate=True)


def score_grads(
    query_heads, key_heads, value_heads, grad_heads, log_total, row_delta, query_at, key_at
):
    score_scale = HEAD_DIM ** (-0.5)
    scores = (
        jnp.einsum("sqhd,skhd->shqk", query_heads, key_heads, preferred_element_type=jnp.float32)
        * score_scale
    )
    visible = query_at[:, None] >= key_at[None, :]
    shifted = jnp.where(visible, scores - log_total[..., None], -1e30)
    weights = jnp.where(visible, jnp.exp(shifted), 0.0)
    pressure = jnp.einsum(
        "sqhd,skhd->shqk", grad_heads, value_heads, preferred_element_type=jnp.float32
    )
    score_low = (weights * (pressure - row_delta[..., None])).astype(jnp.bfloat16)
    return (weights.astype(jnp.bfloat16), score_low)


def per_device_gathered(
    inputs,
    cotangent,
    first_gain,
    first_shift,
    project_in,
    query_bias,
    value_bias,
    project_out,
    output_bias,
    second_gain,
    second_shift,
    up_weight,
    up_bias,
    down_weight,
    down_bias,
):
    seq_count, block_len, model_width = inputs.shape
    flat_rows = seq_count * block_len
    cycle_size = lax.axis_size("ctx")
    my_block = lax.axis_index("ctx")
    score_scale = HEAD_DIM ** (-0.5)
    head_shape = (seq_count, block_len, HEADS, HEAD_DIM)
    offsets = jnp.arange(block_len, dtype=jnp.int32)
    query_at = my_block * block_len + offsets
    gain_first, shift_first, full_in, qbias_full, vbias_full, full_out, obias_full = (
        lax.all_gather(first_gain, "fsdp", axis=0, tiled=True),
        lax.all_gather(first_shift, "fsdp", axis=0, tiled=True),
        lax.all_gather(project_in, "fsdp", axis=0, tiled=True),
        lax.all_gather(query_bias, "fsdp", axis=0, tiled=True),
        lax.all_gather(value_bias, "fsdp", axis=0, tiled=True),
        lax.all_gather(project_out, "fsdp", axis=0, tiled=True),
        lax.all_gather(output_bias, "fsdp", axis=0, tiled=True),
    )
    rows_in = inputs.astype(jnp.float32).reshape(flat_rows, model_width)
    normed, norm_first_back = jax.vjp(
        layer_norm, rows_in, gain_first.astype(jnp.float32), shift_first.astype(jnp.float32)
    )
    normed_low = normed.astype(jnp.bfloat16)
    projected = jnp.dot(normed_low, full_in, preferred_element_type=jnp.float32)
    queries = (projected[:, :model_width] + qbias_full).astype(jnp.bfloat16)
    key_rows = projected[:, model_width : 2 * model_width].astype(jnp.bfloat16)
    value_rows = (projected[:, 2 * model_width :] + vbias_full).astype(jnp.bfloat16)
    query_heads = queries.reshape(head_shape)
    running_top = jnp.full((seq_count, HEADS, block_len), -1e30, jnp.float32)
    accumulated = jnp.zeros(head_shape, jnp.float32)
    piece_keys = lax.all_gather(
        key_rows.reshape(seq_count, block_len, model_width), "ctx", axis=1, tiled=True
    )
    piece_values = lax.all_gather(
        value_rows.reshape(seq_count, block_len, model_width), "ctx", axis=1, tiled=True
    )
    piece_len = piece_keys.shape[1]
    key_heads = piece_keys.reshape(seq_count, piece_len, HEADS, HEAD_DIM)
    value_heads = piece_values.reshape(seq_count, piece_len, HEADS, HEAD_DIM)
    scores = (
        jnp.einsum("sqhd,skhd->shqk", query_heads, key_heads, preferred_element_type=jnp.float32)
        * score_scale
    )
    key_at = jnp.arange(piece_len, dtype=jnp.int32)
    visible = query_at[:, None] >= key_at[None, :]
    masked = jnp.where(visible, scores, -1e30)
    new_top = jnp.maximum(running_top, jnp.max(masked, axis=-1))
    factor = jnp.exp(running_top - new_top)
    weights = jnp.where(visible, jnp.exp(masked - new_top[..., None]), 0.0)
    row_total = jnp.sum(weights, axis=-1)
    added = jnp.einsum(
        "shqk,skhd->sqhd",
        weights.astype(jnp.bfloat16),
        value_heads,
        preferred_element_type=jnp.float32,
    )
    accumulated = accumulated * jnp.swapaxes(factor, 1, 2)[..., None] + added
    running_top, row_total, accumulated = (new_top, row_total, accumulated)
    attended = accumulated / jnp.swapaxes(row_total, 1, 2)[..., None]
    log_total = running_top + jnp.log(row_total)
    attended_low = attended.reshape(flat_rows, model_width).astype(jnp.bfloat16)
    middle = (
        rows_in + jnp.dot(attended_low, full_out, preferred_element_type=jnp.float32) + obias_full
    )
    gain_second, shift_second, full_up, ubias_full, full_down, dbias_full = (
        lax.all_gather(second_gain, "fsdp", axis=0, tiled=True),
        lax.all_gather(second_shift, "fsdp", axis=0, tiled=True),
        lax.all_gather(up_weight, "fsdp", axis=0, tiled=True),
        lax.all_gather(up_bias, "fsdp", axis=0, tiled=True),
        lax.all_gather(down_weight, "fsdp", axis=0, tiled=True),
        lax.all_gather(down_bias, "fsdp", axis=0, tiled=True),
    )
    normed_two, norm_second_back = jax.vjp(
        layer_norm, middle, gain_second.astype(jnp.float32), shift_second.astype(jnp.float32)
    )
    normed_two_low = normed_two.astype(jnp.bfloat16)
    hidden = jnp.dot(normed_two_low, full_up, preferred_element_type=jnp.float32) + ubias_full
    active, gelu_back = jax.vjp(gelu_tanh, hidden)
    active_low = active.astype(jnp.bfloat16)
    result = (
        middle + jnp.dot(active_low, full_down, preferred_element_type=jnp.float32) + dbias_full
    )
    outputs = result.astype(jnp.bfloat16).reshape(seq_count, block_len, model_width)
    upstream = cotangent.astype(jnp.float32).reshape(flat_rows, model_width)
    upstream_low = upstream.astype(jnp.bfloat16)
    down_grad = jnp.einsum(
        "rf,rd->fd", active_low, upstream_low, preferred_element_type=jnp.float32
    )
    down_bias_grad = jnp.sum(upstream_low.astype(jnp.float32), axis=0)
    active_grad = jnp.einsum(
        "rd,fd->rf", upstream_low, full_down, preferred_element_type=jnp.float32
    )
    (hidden_grad,) = gelu_back(active_grad)
    hidden_low = hidden_grad.astype(jnp.bfloat16)
    up_grad = jnp.einsum(
        "rd,rf->df", normed_two_low, hidden_low, preferred_element_type=jnp.float32
    )
    up_bias_grad = jnp.sum(hidden_low.astype(jnp.float32), axis=0)
    normed_two_grad = jnp.einsum(
        "rf,df->rd", hidden_low, full_up, preferred_element_type=jnp.float32
    )
    middle_part, gain_two_grad, shift_two_grad = norm_second_back(normed_two_grad)
    middle_grad = upstream + middle_part
    middle_low = middle_grad.astype(jnp.bfloat16)
    out_grad = jnp.einsum("rd,re->de", attended_low, middle_low, preferred_element_type=jnp.float32)
    out_bias_grad = jnp.sum(middle_low.astype(jnp.float32), axis=0)
    attended_grad = jnp.einsum(
        "re,de->rd", middle_low, full_out, preferred_element_type=jnp.float32
    )
    grad_low = attended_grad.astype(jnp.bfloat16).reshape(head_shape)
    row_delta = jnp.swapaxes(jnp.sum(grad_low.astype(jnp.float32) * attended, axis=-1), 1, 2)
    gathered_keys, gathered_values = (
        lax.all_gather(
            key_rows.reshape(1, seq_count, block_len, model_width), "ctx", axis=0, tiled=True
        ),
        lax.all_gather(
            value_rows.reshape(1, seq_count, block_len, model_width), "ctx", axis=0, tiled=True
        ),
    )
    block_ids = jnp.arange(cycle_size, dtype=jnp.int32)

    def key_step(carry, inputs_here):
        key_block, value_block, block_index = inputs_here
        key_heads = key_block.reshape(head_shape)
        value_heads = value_block.reshape(head_shape)
        weights_low, score_low = score_grads(
            query_heads,
            key_heads,
            value_heads,
            grad_low,
            log_total,
            row_delta,
            query_at,
            block_index * block_len + offsets,
        )
        carry = (
            carry
            + jnp.einsum(
                "shqk,skhd->sqhd", score_low, key_heads, preferred_element_type=jnp.float32
            )
            * score_scale
        )
        key_term = (
            jnp.einsum(
                "shqk,sqhd->skhd", score_low, query_heads, preferred_element_type=jnp.float32
            )
            * score_scale
        )
        value_term = jnp.einsum(
            "shqk,sqhd->skhd", weights_low, grad_low, preferred_element_type=jnp.float32
        )
        return (
            carry,
            (
                key_term.reshape(seq_count, block_len, model_width),
                value_term.reshape(seq_count, block_len, model_width),
            ),
        )

    query_grad, (key_terms, value_terms) = lax.scan(
        key_step, jnp.zeros(head_shape, jnp.float32), (gathered_keys, gathered_values, block_ids)
    )
    key_sum, value_sum = (
        lax.psum_scatter(
            key_terms.astype(jnp.bfloat16), "ctx", scatter_dimension=0, tiled=True
        ).astype(jnp.float32),
        lax.psum_scatter(
            value_terms.astype(jnp.bfloat16), "ctx", scatter_dimension=0, tiled=True
        ).astype(jnp.float32),
    )
    key_grad = key_sum.reshape(flat_rows, model_width)
    value_grad = value_sum.reshape(flat_rows, model_width)
    query_low = query_grad.reshape(flat_rows, model_width).astype(jnp.bfloat16)
    key_low = key_grad.astype(jnp.bfloat16)
    value_low = value_grad.astype(jnp.bfloat16)
    stacked = jnp.concatenate([query_low, key_low, value_low], axis=1)
    in_grad = jnp.einsum("rd,re->de", normed_low, stacked, preferred_element_type=jnp.float32)
    query_bias_grad = jnp.sum(query_low.astype(jnp.float32), axis=0)
    value_bias_grad = jnp.sum(value_low.astype(jnp.float32), axis=0)
    normed_grad = jnp.einsum("re,de->rd", stacked, full_in, preferred_element_type=jnp.float32)
    input_part, gain_one_grad, shift_one_grad = norm_first_back(normed_grad)
    input_gradient = (middle_grad + input_part).reshape(seq_count, block_len, model_width)
    (
        gain_one_part,
        shift_one_part,
        in_part,
        qbias_part,
        vbias_part,
        out_part,
        obias_part,
        gain_two_part,
        shift_two_part,
        up_part,
        ubias_part,
        down_part,
        dbias_part,
    ) = (
        lax.psum_scatter(
            gain_one_grad.astype(jnp.bfloat16), "fsdp", scatter_dimension=0, tiled=True
        ).astype(jnp.float32),
        lax.psum_scatter(
            shift_one_grad.astype(jnp.bfloat16), "fsdp", scatter_dimension=0, tiled=True
        ).astype(jnp.float32),
        lax.psum_scatter(
            in_grad.astype(jnp.bfloat16), "fsdp", scatter_dimension=0, tiled=True
        ).astype(jnp.float32),
        lax.psum_scatter(
            query_bias_grad.astype(jnp.bfloat16), "fsdp", scatter_dimension=0, tiled=True
        ).astype(jnp.float32),
        lax.psum_scatter(
            value_bias_grad.astype(jnp.bfloat16), "fsdp", scatter_dimension=0, tiled=True
        ).astype(jnp.float32),
        lax.psum_scatter(
            out_grad.astype(jnp.bfloat16), "fsdp", scatter_dimension=0, tiled=True
        ).astype(jnp.float32),
        lax.psum_scatter(
            out_bias_grad.astype(jnp.bfloat16), "fsdp", scatter_dimension=0, tiled=True
        ).astype(jnp.float32),
        lax.psum_scatter(
            gain_two_grad.astype(jnp.bfloat16), "fsdp", scatter_dimension=0, tiled=True
        ).astype(jnp.float32),
        lax.psum_scatter(
            shift_two_grad.astype(jnp.bfloat16), "fsdp", scatter_dimension=0, tiled=True
        ).astype(jnp.float32),
        lax.psum_scatter(
            up_grad.astype(jnp.bfloat16), "fsdp", scatter_dimension=0, tiled=True
        ).astype(jnp.float32),
        lax.psum_scatter(
            up_bias_grad.astype(jnp.bfloat16), "fsdp", scatter_dimension=0, tiled=True
        ).astype(jnp.float32),
        lax.psum_scatter(
            down_grad.astype(jnp.bfloat16), "fsdp", scatter_dimension=0, tiled=True
        ).astype(jnp.float32),
        lax.psum_scatter(
            down_bias_grad.astype(jnp.bfloat16), "fsdp", scatter_dimension=0, tiled=True
        ).astype(jnp.float32),
    )
    (
        gain_one_sum,
        shift_one_sum,
        in_sum,
        qbias_sum,
        vbias_sum,
        out_sum,
        obias_sum,
        gain_two_sum,
        shift_two_sum,
        up_sum,
        ubias_sum,
        down_sum,
        dbias_sum,
    ) = lax.psum(
        (
            gain_one_part,
            shift_one_part,
            in_part,
            qbias_part,
            vbias_part,
            out_part,
            obias_part,
            gain_two_part,
            shift_two_part,
            up_part,
            ubias_part,
            down_part,
            dbias_part,
        ),
        ("dp", "ctx"),
    )
    return (
        outputs,
        input_gradient,
        gain_one_sum,
        shift_one_sum,
        in_sum,
        qbias_sum,
        vbias_sum,
        out_sum,
        obias_sum,
        gain_two_sum,
        shift_two_sum,
        up_sum,
        ubias_sum,
        down_sum,
        dbias_sum,
    )


NT = (((1,), (1,)), ((), ()))
PAIR = 2 * HEAD_DIM


def attend_kernel(place_ref, q_ref, k_ref, v_ref, *refs, count, width, start):
    o_ref, log_ref, keys, values = refs[-4:]
    own_pair = pl.program_id(0)
    pair = own_pair + start
    shift = place_ref[0]
    block_len = q_ref.shape[0] // count
    lane = lax.broadcasted_iota(jnp.int32, (1, PAIR), 1)
    valid = lane + pair * PAIR < width
    first = lane < HEAD_DIM

    def rows(block):
        return pl.ds(pl.multiple_of((block ^ shift) * block_len, block_len), block_len)

    for block in range(count):
        here = pl.ds(block * block_len, block_len)
        keys[here, :] = jnp.where(valid, k_ref[rows(block), :], 0)
        values[here, :] = jnp.where(valid, v_ref[rows(block), :], 0)
    diagonal = lax.broadcasted_iota(jnp.int32, (block_len, block_len), 0) >= (
        lax.broadcasted_iota(jnp.int32, (block_len, block_len), 1)
    )
    for block in range(count):
        seen = (block + 1) * block_len
        before = block * block_len
        queries = q_ref[rows(block), :] * jnp.bfloat16(HEAD_DIM**-0.5)
        parts = []
        logs = log_ref[rows(block), :]
        for half in range(2):
            pick = jnp.logical_and(first if half == 0 else jnp.logical_not(first), valid)
            scores = lax.dot_general(
                jnp.where(pick, queries, 0),
                keys[pl.ds(0, seen), :],
                NT,
                preferred_element_type=jnp.float32,
            )
            last = jnp.where(diagonal, scores[:, before:], -1e30)
            scores = last if block == 0 else jnp.concatenate([scores[:, :before], last], axis=1)
            top = jnp.max(scores, axis=1, keepdims=True)
            weights = jnp.exp(scores - top)
            total = jnp.sum(weights, axis=1, keepdims=True)
            added = jnp.dot(
                weights.astype(jnp.bfloat16),
                values[pl.ds(0, seen), :],
                preferred_element_type=jnp.float32,
            )
            parts.append(added / total)
            logs = jnp.where(lane == 2 * own_pair + half, top + jnp.log(total), logs)
        o_ref[rows(block), :] = jnp.where(first, parts[0], parts[1]).astype(jnp.bfloat16)
        log_ref[rows(block), :] = logs


def attend_back_kernel(
    place_ref,
    q_ref,
    k_ref,
    v_ref,
    g_ref,
    o_ref,
    log_ref,
    *refs,
    count,
    width,
    start,
):
    dq_ref, dk_ref, dv_ref, queries, grads, keys, values = refs[-11:-4]
    keys_turned, logs, deltas, turned = refs[-4:]
    pair = pl.program_id(0) + start
    shift = place_ref[0]
    length = q_ref.shape[0]
    block_len = length // count
    lane = lax.broadcasted_iota(jnp.int32, (1, PAIR), 1)
    valid = lane + pair * PAIR < width
    first = lane < HEAD_DIM
    picks = (jnp.logical_and(first, valid), jnp.logical_and(jnp.logical_not(first), valid))
    half_of = (lax.broadcasted_iota(jnp.int32, (8, PAIR), 1) // HEAD_DIM) == (
        lax.broadcasted_iota(jnp.int32, (8, PAIR), 0)
    )
    ones_of = jnp.where(half_of, 1.0, 0.0)

    def rows(block):
        return pl.ds(pl.multiple_of((block ^ shift) * block_len, block_len), block_len)

    for block in range(count):
        here = pl.ds(block * block_len, block_len)
        key_block = jnp.where(valid, k_ref[rows(block), :], 0)
        keys[here, :] = key_block
        keys_turned[:, here] = key_block.astype(jnp.float32).T.astype(jnp.bfloat16)
        values[here, :] = jnp.where(valid, v_ref[rows(block), :], 0)
        query_block = q_ref[rows(block), :] * jnp.bfloat16(HEAD_DIM**-0.5)
        grad_block = jnp.where(valid, g_ref[rows(block), :], 0)
        for half in range(2):
            queries[half, here, :] = jnp.where(picks[half], query_block, 0)
            grads[half, here, :] = jnp.where(picks[half], grad_block, 0)
        mixed = grad_block.astype(jnp.float32) * jnp.where(
            valid, o_ref[rows(block), :], 0
        ).astype(jnp.float32)
        deltas[:, here] = lax.dot_general(
            ones_of,
            mixed,
            NT,
            preferred_element_type=jnp.float32,
            precision=lax.Precision.HIGHEST,
        )
        logs[:, here] = log_ref[
            0, :, pl.ds(pl.multiple_of((block ^ shift) * block_len, block_len), block_len)
        ]
    diagonal = lax.broadcasted_iota(jnp.int32, (block_len, block_len), 0) <= (
        lax.broadcasted_iota(jnp.int32, (block_len, block_len), 1)
    )
    for block in range(count):
        here = pl.ds(block * block_len, block_len)
        after = pl.ds(block * block_len, length - block * block_len)
        key_total = jnp.zeros((block_len, PAIR), jnp.float32)
        value_total = jnp.zeros((block_len, PAIR), jnp.float32)
        for half in range(2):
            scores = lax.dot_general(
                keys[here, :], queries[half, after, :], NT, preferred_element_type=jnp.float32
            )
            shifted = scores - logs[half : half + 1, after]
            own = jnp.where(diagonal, shifted[:, :block_len], -1e30)
            if block < count - 1:
                own = jnp.concatenate([own, shifted[:, block_len:]], axis=1)
            weights = jnp.exp(own)
            pressure = lax.dot_general(
                values[here, :], grads[half, after, :], NT, preferred_element_type=jnp.float32
            )
            score_low = (weights * (pressure - deltas[half : half + 1, after])).astype(
                jnp.bfloat16
            )
            value_total += jnp.dot(
                weights.astype(jnp.bfloat16),
                grads[half, after, :],
                preferred_element_type=jnp.float32,
            )
            key_total += jnp.dot(
                score_low, queries[half, after, :], preferred_element_type=jnp.float32
            )
            part = pl.ds(half * HEAD_DIM, HEAD_DIM)
            term = jnp.dot(
                keys_turned[part, here], score_low, preferred_element_type=jnp.float32
            )
            if block == 0:
                turned[part, after] = term
            else:
                turned[part, after] += term
        dk_ref[rows(block), :] = key_total.astype(jnp.bfloat16)
        dv_ref[rows(block), :] = value_total.astype(jnp.bfloat16)
    for block in range(count):
        here = pl.ds(block * block_len, block_len)
        dq_ref[rows(block), :] = (turned[:, here].T * HEAD_DIM**-0.5).astype(jnp.bfloat16)


def attend(place, queries, key_rows, value_rows, count, start, pairs, before):
    length, width = queries.shape
    heads_block = pl.BlockSpec((length, PAIR), lambda pair, place_ref: (0, pair + start))
    return pl.pallas_call(
        functools.partial(attend_kernel, count=count, width=width, start=start),
        grid_spec=pltpu.PrefetchScalarGridSpec(
            num_scalar_prefetch=1,
            grid=(pairs,),
            in_specs=[heads_block] * 3 + [pl.BlockSpec(memory_space=pl.ANY)] * len(before),
            out_specs=[
                heads_block,
                pl.BlockSpec((length, 128), lambda pair, place_ref: (0, 0)),
            ],
            scratch_shapes=[pltpu.VMEM((length, PAIR), jnp.bfloat16)] * 2,
        ),
        out_shape=[
            jax.ShapeDtypeStruct((length, width), jnp.bfloat16),
            jax.ShapeDtypeStruct((length, 128), jnp.float32),
        ],
        input_output_aliases={4 + at: at for at in range(len(before))},
        compiler_params=pltpu.CompilerParams(vmem_limit_bytes=48 * 2**20),
        cost_estimate=SMALL,
        name="attend",
    )(place, queries, key_rows, value_rows, *before)


def attend_back(
    place, queries, key_rows, value_rows, grads, attended, logs, count, start, pairs, before
):
    length, width = queries.shape
    heads_block = pl.BlockSpec((length, PAIR), lambda pair, place_ref: (0, pair + start))
    low_rows = pltpu.VMEM((length, PAIR), jnp.bfloat16)
    low_pair = pltpu.VMEM((2, length, PAIR), jnp.bfloat16)
    return pl.pallas_call(
        functools.partial(attend_back_kernel, count=count, width=width, start=start),
        grid_spec=pltpu.PrefetchScalarGridSpec(
            num_scalar_prefetch=1,
            grid=(pairs,),
            in_specs=[heads_block] * 5
            + [pl.BlockSpec((1, 2, length), lambda pair, place_ref: (pair, 0, 0))]
            + [pl.BlockSpec(memory_space=pl.ANY)] * len(before),
            out_specs=[heads_block] * 3,
            scratch_shapes=[
                low_pair,
                low_pair,
                low_rows,
                low_rows,
                pltpu.VMEM((PAIR, length), jnp.bfloat16),
                pltpu.VMEM((2, length), jnp.float32),
                pltpu.VMEM((8, length), jnp.float32),
                pltpu.VMEM((PAIR, length), jnp.float32),
            ],
        ),
        out_shape=[jax.ShapeDtypeStruct((length, width), jnp.bfloat16)] * 3,
        input_output_aliases={7 + at: at for at in range(len(before))},
        compiler_params=pltpu.CompilerParams(vmem_limit_bytes=48 * 2**20),
        cost_estimate=SMALL,
        name="attend_back",
    )(place, queries, key_rows, value_rows, grads, attended, logs, *before)


def settle_kernel(place_ref, *refs):
    pieces, out_ref = refs[:-1], refs[-1]
    for at, piece in enumerate(pieces):
        out_ref[place_ref[at]] = piece[...].astype(out_ref.dtype)


def settle(places, pieces, dtype):
    return pl.pallas_call(
        settle_kernel,
        in_specs=[pl.BlockSpec(memory_space=pltpu.SMEM)]
        + [pl.BlockSpec(memory_space=pltpu.VMEM)] * len(pieces),
        out_specs=pl.BlockSpec(memory_space=pltpu.VMEM),
        out_shape=jax.ShapeDtypeStruct((len(pieces),) + pieces[0].shape, dtype),
        compiler_params=pltpu.CompilerParams(vmem_limit_bytes=48 * 2**20),
        cost_estimate=SMALL,
        name="settle",
    )(places, *pieces)


def plane_partner(device, kind):
    core = device & 1
    if kind == "core":
        return device ^ 1
    if kind == "far":
        return device ^ (3 if core else 5)
    if kind == "near":
        return device ^ (2 if core else 4)
    return device ^ (4 if core else 2)


def plane_swap(values, kind):
    return lax.ppermute(
        values, ("dp", "ctx"), [(device, plane_partner(device, kind)) for device in range(8)]
    )


def ctx_swap(values, bits):
    return lax.ppermute(values, "ctx", [(device, device ^ bits) for device in range(4)])


def low_sum(*terms):
    return sum(term.astype(jnp.float32) for term in terms).astype(jnp.bfloat16)


def reduce_core(pieces):
    return plane_swap(pieces[2], "core"), plane_swap(pieces[3], "core")


def share_out(whole):
    return [whole] + [plane_swap(whole, kind) for kind in ("near", "core", "far")]


def share_by_core(whole, near):
    return [whole, near, plane_swap(whole, "core"), plane_swap(near, "core")]


def scatter_rows(values):
    return lax.psum_scatter(values, "fsdp", scatter_dimension=0, tiled=True)


def scatter_pieces(values, z):
    rows = values.reshape(4, values.shape[0] // 4, values.shape[1])

    def share(step):
        return lax.dynamic_index_in_dim(rows, (z + step) % 4, 0, keepdims=False)

    return [share(0)] + [
        lax.ppermute(
            share(step), "fsdp", [(device, (device + step) % 4) for device in range(4)]
        )
        for step in range(1, 4)
    ]


def chosen(index, options):
    result = options[-1]
    for at in range(len(options) - 2, -1, -1):
        result = jnp.where(index == at, options[at], result)
    return result


def gather_vector(values, z):
    around = [values] + [
        lax.ppermute(values, "fsdp", [(device, (device + step) % 4) for device in range(4)])
        for step in range(1, 4)
    ]
    return jnp.stack([chosen((z - at) % 4, around) for at in range(4)])


def scatter_vector(values, z):
    rows = [values[at] for at in range(4)]
    total = chosen(z, rows)
    for step in range(1, 4):
        total = total + lax.ppermute(
            chosen((z + step) % 4, rows),
            "fsdp",
            [(device, (device + step) % 4) for device in range(4)],
        )
    return total


def swap_sum(total, bits):
    return total + lax.ppermute(
        total, ("dp", "ctx"), [(device, device ^ bits) for device in range(8)]
    )


def product(left, right, dims):
    return lax.dot_general(left, right, ((dims[:1], dims[1:]), ((), ())),
                           preferred_element_type=jnp.float32)


def gelu_pair(values):
    inner = 0.7978845608028654
    cubic = inner * 0.044715
    squared = values * values
    curve = jnp.tanh(values * (inner + cubic * squared))
    half = 0.5 * values
    active = half + half * curve
    slope = 0.5 + 0.5 * curve + half * (1.0 - curve * curve) * (inner + 3.0 * cubic * squared)
    return active, slope


SMALL = pl.CostEstimate(flops=1024, bytes_accessed=1024, transcendentals=0)


def unit_of(values):
    centred = values - jnp.mean(values, axis=-1, keepdims=True)
    scale = lax.rsqrt(jnp.mean(centred * centred, axis=-1, keepdims=True) + epsilon)
    return centred * scale, scale


def fold(values):
    rows, width = values.shape
    return jnp.sum(values.reshape(rows // 8, 8, width), axis=0)


def front_kernel(places_ref, vectors_ref, *refs):
    slots, pieces = refs[:4], refs[4:20]
    x_ref, h_ref, q_ref, k_ref, v_ref, all_ref, weights, arrived, left = refs[20:]
    copies = [
        pltpu.make_async_copy(piece, weights.at[places_ref[at]], arrived.at[at])
        for at, piece in enumerate(pieces)
    ]
    for copy in copies:
        copy.start()
    rows, width = x_ref.shape
    step = rows // 4
    for at, slot in enumerate(slots):
        here = pl.ds(at * step, step)
        values = slot[...].astype(jnp.float32).T
        x_ref[here, :] = values.astype(jnp.bfloat16)
        unit, _ = unit_of(values)
        h_ref[here, :] = (unit * vectors_ref[0:1, :] + vectors_ref[1:2, :]).astype(jnp.bfloat16)
    for copy in copies:
        copy.wait()
    leave = pltpu.make_async_copy(weights, all_ref, left)
    leave.start()
    for section, out_ref in enumerate((q_ref, k_ref, v_ref)):

        def multiply(at, carry, section=section, out_ref=out_ref):
            here = pl.ds(pl.multiple_of(at * step, step), step)
            matrix = weights[4 * section : 4 * section + 4].reshape(width, width)
            total = jnp.dot(h_ref[here, :], matrix, preferred_element_type=jnp.float32)
            if section != 1:
                row = 2 if section == 0 else 3
                total = total + vectors_ref[row : row + 1, :]
            out_ref[here, :] = total.astype(jnp.bfloat16)
            return carry

        lax.fori_loop(0, rows // step, multiply, 0)
    leave.wait()


def front(places, slots, vectors, pieces):
    width, step = slots[0].shape
    rows = 4 * step
    vmem = pl.BlockSpec(memory_space=pltpu.VMEM)
    hbm = pl.BlockSpec(memory_space=pl.ANY)
    shape = jax.ShapeDtypeStruct((rows, width), jnp.bfloat16)
    whole = (16,) + pieces[0].shape
    return pl.pallas_call(
        front_kernel,
        in_specs=[pl.BlockSpec(memory_space=pltpu.SMEM)] + [vmem] * 5 + [hbm] * 16,
        out_specs=[vmem] * 5 + [hbm],
        out_shape=[shape] * 5 + [jax.ShapeDtypeStruct(whole, jnp.bfloat16)],
        scratch_shapes=[
            pltpu.VMEM(whole, jnp.bfloat16),
            pltpu.SemaphoreType.DMA((16,)),
            pltpu.SemaphoreType.DMA,
        ],
        compiler_params=pltpu.CompilerParams(vmem_limit_bytes=56 * 2**20),
        cost_estimate=SMALL,
        name="front",
    )(places, vectors, *slots, *pieces)


def turn_kernel(*refs):
    slots, out_ref = refs[:-1], refs[-1]
    step = slots[0].shape[1]
    for at, slot in enumerate(slots):
        out_ref[pl.ds(at * step, step), :] = (
            slot[...].astype(jnp.float32).T.astype(jnp.bfloat16)
        )


def turn(slots):
    width, step = slots[0].shape
    return pl.pallas_call(
        turn_kernel,
        out_shape=jax.ShapeDtypeStruct((len(slots) * step, width), jnp.bfloat16),
        compiler_params=pltpu.CompilerParams(vmem_limit_bytes=48 * 2**20),
        cost_estimate=SMALL,
        name="turn",
    )(*slots)


def assemble_kernel(place_ref, *refs, plan):
    pieces, outs = refs[:4], refs[4:]
    for at, piece in enumerate(pieces):
        for kind, moves in enumerate(plan):

            @pl.when(place_ref[at] == kind)
            def _(piece=piece, moves=moves):
                for out, source, target, size in moves:
                    outs[out][:, target : target + size] = piece[
                        :, source : source + size
                    ].astype(jnp.float32)


def assemble(places, pieces, plan, shapes):
    vmem = pl.BlockSpec(memory_space=pltpu.VMEM)
    return pl.pallas_call(
        functools.partial(assemble_kernel, plan=plan),
        in_specs=[pl.BlockSpec(memory_space=pltpu.SMEM)] + [vmem] * 4,
        out_specs=[vmem] * len(shapes),
        out_shape=[jax.ShapeDtypeStruct(shape, jnp.float32) for shape in shapes],
        compiler_params=pltpu.CompilerParams(vmem_limit_bytes=48 * 2**20),
        cost_estimate=SMALL,
        name="assemble",
    )(places, *pieces)


def store_turned(step, refs, values):
    size = refs[0].shape[1]
    share = values.shape[0] // size
    for at, ref in enumerate(refs):

        @pl.when(step == at // share)
        def _(at=at, ref=ref):
            first = (at % share) * size
            ref[...] = values[first : first + size].T.astype(ref.dtype)


def fetch(step, copies):
    @pl.when(step == 0)
    def _():
        for copy in copies:
            copy.start()


def arrive(step, copy):
    @pl.when(step == 0)
    def _():
        copy.wait()


def middle_kernel(x_ref, o_ref, vectors_ref, all_ref, middle_ref, h_ref, weights, arrived):
    step = pl.program_id(0)
    width = x_ref.shape[1]
    copy = pltpu.make_async_copy(all_ref.at[pl.ds(12, 4)], weights, arrived)
    fetch(step, [copy])
    arrive(step, copy)
    middle = (
        x_ref[...].astype(jnp.float32)
        + jnp.dot(
            o_ref[...], weights[...].reshape(width, width), preferred_element_type=jnp.float32
        )
        + vectors_ref[0:1, :]
    )
    middle_ref[...] = middle
    unit, _ = unit_of(middle)
    h_ref[...] = (unit * vectors_ref[1:2, :] + vectors_ref[2:3, :]).astype(jnp.bfloat16)


def up_kernel(h_ref, biases_ref, *refs):
    sources = refs[:2]
    active_refs, slope_refs = refs[2:4], refs[4:6]
    weights, arrived = refs[6:]
    step = pl.program_id(0)
    copies = [
        pltpu.make_async_copy(source, weights.at[at], arrived.at[at])
        for at, source in enumerate(sources)
    ]
    fetch(step, copies)
    for at in range(2):
        arrive(step, copies[at])
        hidden = (
            jnp.dot(h_ref[...], weights[at], preferred_element_type=jnp.float32)
            + biases_ref[at : at + 1, :]
        )
        active, slope = gelu_pair(hidden)
        active_refs[at][...] = active.astype(jnp.bfloat16)
        slope_refs[at][...] = slope.astype(jnp.bfloat16)


def down_kernel(middle_ref, vectors_ref, *refs):
    actives, sources = refs[:4], refs[4:8]
    out_refs = refs[8:12]
    weights, arrived = refs[12:]
    step = pl.program_id(0)
    copies = [
        pltpu.make_async_copy(source, weights.at[at], arrived.at[at])
        for at, source in enumerate(sources)
    ]
    fetch(step, copies)
    total = middle_ref[...] + vectors_ref[0:1, :]
    for at in range(4):
        arrive(step, copies[at])
        total = total + jnp.dot(
            actives[at][...], weights[at], preferred_element_type=jnp.float32
        )
    store_turned(step, out_refs, total)


def norm_back(values, gain, grad):
    unit, scale = unit_of(values)
    turned = grad * gain
    inner = (
        turned
        - jnp.mean(turned, axis=-1, keepdims=True)
        - unit * jnp.mean(turned * unit, axis=-1, keepdims=True)
    )
    return scale * inner, grad * unit


def hidden_kernel(g_ref, *refs):
    slopes, sources = refs[:2], refs[2:4]
    hidden_refs, sums_ref = refs[4:6], refs[6]
    weights, arrived = refs[7:]
    step = pl.program_id(0)
    copies = [
        pltpu.make_async_copy(source, weights.at[at], arrived.at[at])
        for at, source in enumerate(sources)
    ]
    fetch(step, copies)

    @pl.when(step == 0)
    def _():
        sums_ref[...] = jnp.zeros_like(sums_ref)

    upstream = g_ref[...]
    for at in range(2):
        arrive(step, copies[at])
        hidden = lax.dot_general(
            upstream, weights[at], NT, preferred_element_type=jnp.float32
        )
        hidden = (hidden * slopes[at][...].astype(jnp.float32)).astype(jnp.bfloat16)
        hidden_refs[at][...] = hidden
        sums_ref[at] += fold(hidden.astype(jnp.float32))
    sums_ref[2] += fold(upstream.astype(jnp.float32))


def back_kernel(g_ref, middle_ref, vectors_ref, *refs):
    hiddens, sources, all_ref = refs[:4], refs[4:8], refs[8]
    grad_ref, low_ref, out_ref, sums_ref = refs[9:13]
    weights, out_weights, arrived = refs[13:]
    step = pl.program_id(0)
    width = middle_ref.shape[1]
    copies = [
        pltpu.make_async_copy(source, weights.at[at], arrived.at[at])
        for at, source in enumerate(sources)
    ] + [pltpu.make_async_copy(all_ref.at[pl.ds(12, 4)], out_weights, arrived.at[4])]
    fetch(step, copies)

    @pl.when(step == 0)
    def _():
        sums_ref[...] = jnp.zeros_like(sums_ref)

    total = jnp.zeros(middle_ref.shape, jnp.float32)
    for at in range(4):
        arrive(step, copies[at])
        total = total + lax.dot_general(
            hiddens[at][...], weights[at], NT, preferred_element_type=jnp.float32
        )
    part, gain_term = norm_back(middle_ref[...], vectors_ref[0:1, :], total)
    sums_ref[0] += fold(gain_term)
    sums_ref[1] += fold(total)
    grad = g_ref[...].astype(jnp.float32) + part
    grad_ref[...] = grad
    grad_low = grad.astype(jnp.bfloat16)
    low_ref[...] = grad_low
    sums_ref[2] += fold(grad_low.astype(jnp.float32))
    arrive(step, copies[4])
    out_ref[...] = lax.dot_general(
        grad_low,
        out_weights[...].reshape(width, width),
        NT,
        preferred_element_type=jnp.float32,
    ).astype(jnp.bfloat16)


def last_kernel(q_ref, k_ref, v_ref, x_ref, grad_ref, vectors_ref, all_ref, *refs):
    out_refs = refs[:4]
    sums_ref, weights, arrived = refs[4:]
    step = pl.program_id(0)
    width = x_ref.shape[1]
    copies = [
        pltpu.make_async_copy(
            all_ref.at[pl.ds(4 * at, 4)], weights.at[pl.ds(4 * at, 4)], arrived.at[at]
        )
        for at in range(3)
    ]
    fetch(step, copies)
    total = jnp.zeros(x_ref.shape, jnp.float32)
    for at, ref in enumerate((q_ref, k_ref, v_ref)):
        arrive(step, copies[at])
        total = total + lax.dot_general(
            ref[...],
            weights[4 * at : 4 * at + 4].reshape(width, width),
            NT,
            preferred_element_type=jnp.float32,
        )
    part, gain_term = norm_back(x_ref[...].astype(jnp.float32), vectors_ref[0:1, :], total)
    store_turned(step, out_refs, grad_ref[...] + part)

    @pl.when(step == 0)
    def _():
        sums_ref[...] = jnp.zeros_like(sums_ref)

    terms = (
        gain_term,
        total,
        q_ref[...].astype(jnp.float32),
        v_ref[...].astype(jnp.float32),
    )
    for at, term in enumerate(terms):
        sums_ref[at] += fold(term)


def by_rows(kernel, name, rows, width, tiled, whole, remote, outs, sums, scratch, sems):
    step = 512
    tile = pl.BlockSpec((step, width), lambda at: (at, 0))
    out_specs, out_shape = [], []
    for dtype in outs:
        if dtype is None:
            out_specs += [pl.BlockSpec((width, rows // 4), lambda at: (0, 0))] * 4
            out_shape += [jax.ShapeDtypeStruct((width, rows // 4), jnp.bfloat16)] * 4
        else:
            out_specs.append(tile)
            out_shape.append(jax.ShapeDtypeStruct((rows, width), dtype))
    if sums:
        out_specs.append(pl.BlockSpec((sums, 8, width), lambda at: (0, 0, 0)))
        out_shape.append(jax.ShapeDtypeStruct((sums, 8, width), jnp.float32))
    return pl.pallas_call(
        kernel,
        grid=(rows // step,),
        in_specs=[tile] * len(tiled[0])
        + [pl.BlockSpec(value.shape, lambda at: (0, 0)) for value in whole]
        + [tile] * len(tiled[1])
        + [pl.BlockSpec(memory_space=pl.ANY)] * len(remote),
        out_specs=out_specs,
        out_shape=out_shape,
        scratch_shapes=[pltpu.VMEM(shape, jnp.bfloat16) for shape in scratch]
        + [pltpu.SemaphoreType.DMA((sems,)) if sems > 1 else pltpu.SemaphoreType.DMA],
        compiler_params=pltpu.CompilerParams(vmem_limit_bytes=60 * 2**20),
        cost_estimate=SMALL,
        name=name,
    )(*tiled[0], *whole, *tiled[1], *remote)


def per_device_exchanged(
    inputs,
    cotangent,
    first_gain,
    first_shift,
    project_in,
    query_bias,
    value_bias,
    project_out,
    output_bias,
    second_gain,
    second_shift,
    up_weight,
    up_bias,
    down_weight,
    down_bias,
):
    seq_count, block_len, width = inputs.shape
    low = jnp.bfloat16
    wide = jnp.float32
    c = lax.axis_index("ctx")
    y = lax.axis_index("dp")
    z = lax.axis_index("fsdp")
    core = c & 1
    x = c >> 1
    mine = core * 2 + jnp.where(core == 0, y, x)
    across = (1 - core) * 2 + jnp.where(core == 0, x, y)
    classes = [mine, mine ^ 1, across, across ^ 1]
    slot_of = [
        chosen(0, [sum(at * (classes[at] == kind).astype(jnp.int32) for at in range(4))])
        for kind in range(4)
    ]
    quarter = width // 4
    rows, area = seq_count * block_len, (width, width)
    pin = lax.optimization_barrier
    place = jnp.stack([c])
    places = jnp.stack([c ^ at for at in range(4)])
    class_places = jnp.stack(classes)

    def spread(values):
        values = jnp.swapaxes(values, 1, 2)
        return [lax.dynamic_index_in_dim(values, c, 0, keepdims=False)] + [
            ctx_swap(lax.dynamic_index_in_dim(values, c ^ bits, 0, keepdims=False), bits)
            for bits in range(1, 4)
        ]

    def exchange(pieces):
        return [pieces[0]] + [ctx_swap(pieces[bits], bits) for bits in range(1, 4)]

    def collect(moved, dtype):
        return jnp.swapaxes(settle(places, moved, dtype), 1, 2)

    sections = [
        project_in[:, :width],
        project_in[:, width : 2 * width],
        project_in[:, 2 * width :],
        project_out,
    ]
    section = chosen(mine, sections)
    section, inputs = pin((section, inputs))
    shards = [
        lax.ppermute(section, "fsdp", [(device, (device + step) % 4) for device in range(4)])
        for step in range(1, 4)
    ]
    turned_in = jnp.swapaxes(inputs, 1, 2)
    slots_in = [
        lax.dynamic_index_in_dim(turned_in, c ^ bits, 0, keepdims=False) for bits in range(4)
    ]
    pieces_in = (
        first_gain,
        first_shift,
        query_bias,
        value_bias,
        output_bias,
        second_gain,
        second_shift,
        down_bias,
        up_bias,
    )
    slots_in[3], up_weight, down_weight, *pieces_in = pin(
        (slots_in[3], up_weight, down_weight, *pieces_in)
    )
    slots_in = [slots_in[0]] + [ctx_swap(slots_in[bits], bits) for bits in range(1, 4)]
    vectors = gather_vector(jnp.concatenate(pieces_in), z).astype(wide)
    up_piece = jnp.concatenate(
        [
            lax.dynamic_slice_in_dim(up_weight, at * width + mine * quarter, quarter, 1)
            for at in range(4)
        ],
        axis=1,
    )
    up_piece, vectors, *moved = pin((up_piece, vectors, *shards, *slots_in))
    shards, slots_in = moved[:3], moved[3:]
    near_shards = [plane_swap(shard, "near") for shard in shards]
    cotangent, *near_shards = pin((cotangent, *near_shards))
    slots_back = spread(cotangent)
    around = (
        sections
        + shards
        + near_shards
        + [plane_swap(shard, "core") for shard in shards]
        + [plane_swap(shard, "core") for shard in near_shards]
    )
    around_places = jnp.stack(
        [kind * 4 + z for kind in range(4)]
        + [kind * 4 + (z - step) % 4 for kind in classes for step in range(1, 4)]
    )
    up_own = lax.all_gather(up_piece, "fsdp", axis=0, tiled=True)
    down_piece = lax.dynamic_slice_in_dim(down_weight, mine * quarter, quarter, 0)
    gain_first, shift_first, qbias, vbias, obias, gain_second, shift_second, dbias = (
        vectors[:, at * quarter : (at + 1) * quarter].reshape(1, width) for at in range(8)
    )
    ubias = vectors[:, 8 * quarter :].reshape(4, 4, quarter)
    ubias = jnp.concatenate(
        [
            chosen(kind, [ubias[:, at] for at in range(4)]).reshape(1, width)
            for kind in classes
        ],
        axis=0,
    )

    rows_in, normed_low, queries, key_rows, value_rows, weights = front(
        around_places,
        slots_in,
        jnp.concatenate([gain_first, shift_first, qbias, vbias], axis=0),
        around,
    )
    up_own, queries = pin((up_own, queries))
    up_near, up_core = plane_swap(up_own, "near"), plane_swap(up_own, "core")
    attended, logs = attend(place, queries, key_rows, value_rows, seq_count, 0, 9, [])
    down_piece, up_core, up_near, attended = pin((down_piece, up_core, up_near, attended))
    down_own = lax.all_gather(down_piece, "fsdp", axis=0, tiled=True)
    logs = logs.T.reshape(64, 2, rows)
    logs_one, logs_two = logs[:5], logs[5:9]
    middle, normed_two_low = by_rows(
        middle_kernel,
        "middle",
        rows,
        width,
        ([rows_in, attended], []),
        [jnp.concatenate([obias, gain_second, shift_second], axis=0)],
        [weights],
        [wide, low],
        0,
        [(4,) + section.shape],
        1,
    )
    up_slots = [up_own, up_near, up_core, plane_swap(up_near, "core")]
    active, slopes = [None] * 4, [None] * 4

    def up(first):
        outs = by_rows(
            up_kernel,
            "up",
            rows,
            width,
            ([normed_two_low], []),
            [jnp.concatenate([ubias[first : first + 1], ubias[first + 2 : first + 3]], axis=0)],
            [up_slots[first], up_slots[first + 2]],
            [low] * 4,
            0,
            [(2,) + area],
            2,
        )
        active[first], active[first + 2], slopes[first], slopes[first + 2] = outs

    up(0)
    up_slots[3], slots_back[3], active[0], active[2] = pin(
        (up_slots[3], slots_back[3], active[0], active[2])
    )
    upstream_low = turn(slots_back)
    up(1)
    down_own, *active = pin((down_own, *active))
    down_near, down_core = plane_swap(down_own, "near"), plane_swap(down_own, "core")

    def turned_product(left, right):
        return product(left, right, (0, 0)).astype(low)

    down_terms = [turned_product(active[slot], upstream_low) for slot in (3, 2)]
    upstream_low, *down_terms = pin((upstream_low, *down_terms))
    down_terms += [turned_product(active[slot], upstream_low) for slot in (1, 0)]
    down_terms = down_terms[::-1]
    down_far, down_far_two = reduce_core(down_terms)
    upstream_low, *down_terms = pin((upstream_low, *down_terms))
    hidden_low = [None] * 4

    def hidden(first, upstream):
        hidden_low[first], hidden_low[first + 2], sums = by_rows(
            hidden_kernel,
            "hidden",
            rows,
            width,
            ([upstream], [slopes[first], slopes[first + 2]]),
            [],
            [down_slots[first], down_slots[first + 2]],
            [low] * 2,
            3,
            [(2,) + area],
            2,
        )
        return sums

    down_near, upstream_low = pin((down_near, upstream_low))
    down_slots = [down_own, down_near, down_core, plane_swap(down_near, "core")]
    sums_even = hidden(0, upstream_low)
    down_second = low_sum(down_terms[1], down_far_two)
    upstream_late, sums_even, down_second = pin((upstream_low, sums_even, down_second))
    down_close = plane_swap(down_second, "near")
    sums_odd = hidden(1, upstream_late)
    hidden_sums = jnp.stack(
        [sums_even[0], sums_odd[0], sums_even[1], sums_odd[1], sums_even[2]]
    )
    down_far, *hidden_low = pin((down_far, *hidden_low))
    up_terms = [turned_product(normed_two_low, hidden_low[slot]) for slot in (3, 2)]
    normed_two_low, *up_terms = pin((normed_two_low, *up_terms))
    up_terms += [turned_product(normed_two_low, hidden_low[slot]) for slot in (1, 0)]
    up_terms = up_terms[::-1]
    up_far, up_far_two = reduce_core(up_terms)
    up_second = low_sum(up_terms[1], up_far_two)
    down_first = low_sum(down_terms[0], down_far, down_close)
    up_second, up_far, down_first, moved, *hidden_low = pin(
        (up_second, up_far, down_first, up_terms[0], *hidden_low)
    )
    up_terms[0] = moved
    down_shard = scatter_rows(down_first)
    up_close = plane_swap(up_second, "near")
    middle_grad, middle_low, grad_low, back_sums = by_rows(
        back_kernel,
        "back",
        rows,
        width,
        ([upstream_low, middle], hidden_low),
        [gain_second],
        up_slots + [weights],
        [wide, low, low],
        3,
        [(4,) + area, (4,) + section.shape],
        5,
    )
    out_term = turned_product(attended, middle_low)
    up_first = low_sum(up_terms[0], up_far, up_close)
    grad_low, out_term, up_first = pin((grad_low, out_term, up_first))
    up_pieces = scatter_pieces(up_first, z)
    in_grads = attend_back(
        place, queries, key_rows, value_rows, grad_low, attended, logs_one, seq_count, 0, 5, []
    )
    down_shard, *in_grads = pin((down_shard, *in_grads))
    down_whole = low_sum(down_shard, plane_swap(down_shard, "other"))
    in_grads = attend_back(
        place,
        queries,
        key_rows,
        value_rows,
        grad_low,
        attended,
        logs_two,
        seq_count,
        5,
        4,
        in_grads,
    )
    down_whole, *moved = pin((down_whole, *up_pieces, *in_grads))
    up_pieces, in_grads = moved[:4], moved[4:]
    down_beside = plane_swap(down_whole, "near")
    up_shard = low_sum(*up_pieces)
    up_whole = low_sum(up_shard, plane_swap(up_shard, "other"))
    in_terms = [turned_product(normed_low, grad) for grad in in_grads]
    section_grads = in_terms + [out_term]
    sections_mine = [chosen(kind, section_grads) for kind in classes]
    far, far_two = reduce_core(sections_mine)
    second = low_sum(sections_mine[1], far_two)
    second, far, middle, up_whole, down_beside, *in_grads = pin(
        (second, far, middle, up_whole, down_beside, *in_grads)
    )
    up_beside = plane_swap(up_whole, "near")
    query_low, key_low, value_low = in_grads
    close = plane_swap(second, "near")
    result_slots = by_rows(
        down_kernel,
        "down",
        rows,
        width,
        ([middle], active),
        [dbias],
        down_slots,
        [None],
        0,
        [(4,) + area],
        4,
    )
    first = low_sum(sections_mine[0], far, close)
    first, up_beside, query_low, *result_slots = pin(
        (first, up_beside, query_low, *result_slots)
    )
    down_parts = share_by_core(down_whole, down_beside)
    up_parts = share_by_core(up_whole, up_beside)
    shard = scatter_rows(first)
    outputs = exchange(result_slots)
    *input_slots, last_sums = by_rows(
        last_kernel,
        "last",
        rows,
        width,
        ([query_low, key_low, value_low, rows_in, middle_grad], []),
        [gain_first],
        [weights],
        [None],
        4,
        [(12,) + section.shape],
        3,
    )
    moved = pin((*input_slots, *outputs, *down_parts, *up_parts))
    input_slots, outputs = exchange(moved[:4]), moved[4:8]
    down_parts, up_parts = moved[8:12], moved[12:]

    back_sums = jnp.concatenate([hidden_sums, back_sums], axis=0)
    back_sums = jnp.sum(back_sums, axis=1)
    last_sums = jnp.sum(last_sums, axis=1)
    hidden_sums = [back_sums[slot].reshape(4, quarter) for slot in range(4)]
    hidden_sums = jnp.stack(
        [chosen(slot_of[kind], hidden_sums) for kind in range(4)], axis=1
    ).reshape(4, 4 * quarter)
    totals = swap_sum(
        scatter_vector(
            jnp.concatenate(
                [back_sums[at].reshape(4, quarter) for at in range(4, 8)]
                + [last_sums[at].reshape(4, quarter) for at in range(4)]
                + [hidden_sums],
                axis=1,
            ),
            z,
        ),
        1,
    )
    shard, totals, *input_slots = pin((shard, totals, *input_slots))
    section_whole = low_sum(shard, plane_swap(shard, "other"))
    totals = swap_sum(totals, 2)
    section_whole, totals = pin((section_whole, totals))
    section_parts = share_out(section_whole)
    totals = swap_sum(totals, 4)
    outputs = collect(outputs, low)
    input_gradient = collect(input_slots, wide)
    (up_sum,) = assemble(
        class_places,
        up_parts,
        [
            [(0, at * quarter, at * width + kind * quarter, quarter) for at in range(4)]
            for kind in range(4)
        ],
        [up_weight.shape],
    )
    down_sum = settle(class_places, down_parts, wide).reshape(down_weight.shape)
    moved = pin((*section_parts, outputs, input_gradient, totals, up_sum, down_sum))
    section_parts = moved[:4]
    outputs, input_gradient, totals, up_sum, down_sum = moved[4:]
    in_sum, out_sum = assemble(
        class_places,
        section_parts,
        [[(0, 0, kind * width, width)] for kind in range(3)] + [[(1, 0, 0, width)]],
        [project_in.shape, project_out.shape],
    )
    (
        dbias_sum,
        gain_two_sum,
        shift_two_sum,
        obias_sum,
        gain_one_sum,
        shift_one_sum,
        qbias_sum,
        vbias_sum,
    ) = (totals[at * quarter : (at + 1) * quarter] for at in range(8))
    ubias_sum = totals[8 * quarter :]
    return (
        outputs,
        input_gradient,
        gain_one_sum,
        shift_one_sum,
        in_sum,
        qbias_sum,
        vbias_sum,
        out_sum,
        obias_sum,
        gain_two_sum,
        shift_two_sum,
        up_sum,
        ubias_sum,
        down_sum,
        dbias_sum,
    )


def solution(mesh):
    sizes = dict(mesh.shape)
    exchanged = sizes["dp"] == 2 and sizes["fsdp"] == 4 and sizes["ctx"] == 4
    per_device = per_device_exchanged if exchanged else per_device_gathered
    return jax.shard_map(
        per_device,
        mesh=mesh,
        in_specs=(
            P(("dp", "fsdp"), "ctx", None),
            P(("dp", "fsdp"), "ctx", None),
            P("fsdp"),
            P("fsdp"),
            P("fsdp", None),
            P("fsdp"),
            P("fsdp"),
            P("fsdp", None),
            P("fsdp"),
            P("fsdp"),
            P("fsdp"),
            P("fsdp", None),
            P("fsdp"),
            P("fsdp", None),
            P("fsdp"),
        ),
        out_specs=(
            P(("dp", "fsdp"), "ctx", None),
            P(("dp", "fsdp"), "ctx", None),
            P("fsdp"),
            P("fsdp"),
            P("fsdp", None),
            P("fsdp"),
            P("fsdp"),
            P("fsdp", None),
            P("fsdp"),
            P("fsdp"),
            P("fsdp"),
            P("fsdp", None),
            P("fsdp"),
            P("fsdp", None),
            P("fsdp"),
        ),
        check_vma=False,
    )
```

```python
import functools

import jax
import jax.numpy as jnp
from jax import lax
from jax.experimental import pallas as pl
from jax.experimental.pallas import tpu as pltpu
from jax.sharding import PartitionSpec as P

HEADS = 17
HEAD_DIM = 64


epsilon = 1e-05


def layer_norm(values, gain, shift):
    centred = values - jnp.mean(values, axis=-1, keepdims=True)
    spread = jnp.mean(centred * centred, axis=-1, keepdims=True)
    return centred * lax.rsqrt(spread + epsilon) * gain + shift


def gelu_tanh(values):
    return jax.nn.gelu(values, approximate=True)


def score_grads(
    query_heads, key_heads, value_heads, grad_heads, log_total, row_delta, query_at, key_at
):
    score_scale = HEAD_DIM ** (-0.5)
    scores = (
        jnp.einsum("sqhd,skhd->shqk", query_heads, key_heads, preferred_element_type=jnp.float32)
        * score_scale
    )
    visible = query_at[:, None] >= key_at[None, :]
    shifted = jnp.where(visible, scores - log_total[..., None], -1e30)
    weights = jnp.where(visible, jnp.exp(shifted), 0.0)
    pressure = jnp.einsum(
        "sqhd,skhd->shqk", grad_heads, value_heads, preferred_element_type=jnp.float32
    )
    score_low = (weights * (pressure - row_delta[..., None])).astype(jnp.bfloat16)
    return (weights.astype(jnp.bfloat16), score_low)


def per_device_gathered(
    inputs,
    cotangent,
    first_gain,
    first_shift,
    project_in,
    query_bias,
    value_bias,
    project_out,
    output_bias,
    second_gain,
    second_shift,
    up_weight,
    up_bias,
    down_weight,
    down_bias,
):
    seq_count, block_len, model_width = inputs.shape
    flat_rows = seq_count * block_len
    cycle_size = lax.axis_size("ctx")
    my_block = lax.axis_index("ctx")
    score_scale = HEAD_DIM ** (-0.5)
    head_shape = (seq_count, block_len, HEADS, HEAD_DIM)
    offsets = jnp.arange(block_len, dtype=jnp.int32)
    query_at = my_block * block_len + offsets
    gain_first, shift_first, full_in, qbias_full, vbias_full, full_out, obias_full = (
        lax.all_gather(first_gain, "fsdp", axis=0, tiled=True),
        lax.all_gather(first_shift, "fsdp", axis=0, tiled=True),
        lax.all_gather(project_in, "fsdp", axis=0, tiled=True),
        lax.all_gather(query_bias, "fsdp", axis=0, tiled=True),
        lax.all_gather(value_bias, "fsdp", axis=0, tiled=True),
        lax.all_gather(project_out, "fsdp", axis=0, tiled=True),
        lax.all_gather(output_bias, "fsdp", axis=0, tiled=True),
    )
    rows_in = inputs.astype(jnp.float32).reshape(flat_rows, model_width)
    normed, norm_first_back = jax.vjp(
        layer_norm, rows_in, gain_first.astype(jnp.float32), shift_first.astype(jnp.float32)
    )
    normed_low = normed.astype(jnp.bfloat16)
    projected = jnp.dot(normed_low, full_in, preferred_element_type=jnp.float32)
    queries = (projected[:, :model_width] + qbias_full).astype(jnp.bfloat16)
    key_rows = projected[:, model_width : 2 * model_width].astype(jnp.bfloat16)
    value_rows = (projected[:, 2 * model_width :] + vbias_full).astype(jnp.bfloat16)
    query_heads = queries.reshape(head_shape)
    running_top = jnp.full((seq_count, HEADS, block_len), -1e30, jnp.float32)
    accumulated = jnp.zeros(head_shape, jnp.float32)
    piece_keys = lax.all_gather(
        key_rows.reshape(seq_count, block_len, model_width), "ctx", axis=1, tiled=True
    )
    piece_values = lax.all_gather(
        value_rows.reshape(seq_count, block_len, model_width), "ctx", axis=1, tiled=True
    )
    piece_len = piece_keys.shape[1]
    key_heads = piece_keys.reshape(seq_count, piece_len, HEADS, HEAD_DIM)
    value_heads = piece_values.reshape(seq_count, piece_len, HEADS, HEAD_DIM)
    scores = (
        jnp.einsum("sqhd,skhd->shqk", query_heads, key_heads, preferred_element_type=jnp.float32)
        * score_scale
    )
    key_at = jnp.arange(piece_len, dtype=jnp.int32)
    visible = query_at[:, None] >= key_at[None, :]
    masked = jnp.where(visible, scores, -1e30)
    new_top = jnp.maximum(running_top, jnp.max(masked, axis=-1))
    factor = jnp.exp(running_top - new_top)
    weights = jnp.where(visible, jnp.exp(masked - new_top[..., None]), 0.0)
    row_total = jnp.sum(weights, axis=-1)
    added = jnp.einsum(
        "shqk,skhd->sqhd",
        weights.astype(jnp.bfloat16),
        value_heads,
        preferred_element_type=jnp.float32,
    )
    accumulated = accumulated * jnp.swapaxes(factor, 1, 2)[..., None] + added
    running_top, row_total, accumulated = (new_top, row_total, accumulated)
    attended = accumulated / jnp.swapaxes(row_total, 1, 2)[..., None]
    log_total = running_top + jnp.log(row_total)
    attended_low = attended.reshape(flat_rows, model_width).astype(jnp.bfloat16)
    middle = (
        rows_in + jnp.dot(attended_low, full_out, preferred_element_type=jnp.float32) + obias_full
    )
    gain_second, shift_second, full_up, ubias_full, full_down, dbias_full = (
        lax.all_gather(second_gain, "fsdp", axis=0, tiled=True),
        lax.all_gather(second_shift, "fsdp", axis=0, tiled=True),
        lax.all_gather(up_weight, "fsdp", axis=0, tiled=True),
        lax.all_gather(up_bias, "fsdp", axis=0, tiled=True),
        lax.all_gather(down_weight, "fsdp", axis=0, tiled=True),
        lax.all_gather(down_bias, "fsdp", axis=0, tiled=True),
    )
    normed_two, norm_second_back = jax.vjp(
        layer_norm, middle, gain_second.astype(jnp.float32), shift_second.astype(jnp.float32)
    )
    normed_two_low = normed_two.astype(jnp.bfloat16)
    hidden = jnp.dot(normed_two_low, full_up, preferred_element_type=jnp.float32) + ubias_full
    active, gelu_back = jax.vjp(gelu_tanh, hidden)
    active_low = active.astype(jnp.bfloat16)
    result = (
        middle + jnp.dot(active_low, full_down, preferred_element_type=jnp.float32) + dbias_full
    )
    outputs = result.astype(jnp.bfloat16).reshape(seq_count, block_len, model_width)
    upstream = cotangent.astype(jnp.float32).reshape(flat_rows, model_width)
    upstream_low = upstream.astype(jnp.bfloat16)
    down_grad = jnp.einsum(
        "rf,rd->fd", active_low, upstream_low, preferred_element_type=jnp.float32
    )
    down_bias_grad = jnp.sum(upstream_low.astype(jnp.float32), axis=0)
    active_grad = jnp.einsum(
        "rd,fd->rf", upstream_low, full_down, preferred_element_type=jnp.float32
    )
    (hidden_grad,) = gelu_back(active_grad)
    hidden_low = hidden_grad.astype(jnp.bfloat16)
    up_grad = jnp.einsum(
        "rd,rf->df", normed_two_low, hidden_low, preferred_element_type=jnp.float32
    )
    up_bias_grad = jnp.sum(hidden_low.astype(jnp.float32), axis=0)
    normed_two_grad = jnp.einsum(
        "rf,df->rd", hidden_low, full_up, preferred_element_type=jnp.float32
    )
    middle_part, gain_two_grad, shift_two_grad = norm_second_back(normed_two_grad)
    middle_grad = upstream + middle_part
    middle_low = middle_grad.astype(jnp.bfloat16)
    out_grad = jnp.einsum("rd,re->de", attended_low, middle_low, preferred_element_type=jnp.float32)
    out_bias_grad = jnp.sum(middle_low.astype(jnp.float32), axis=0)
    attended_grad = jnp.einsum(
        "re,de->rd", middle_low, full_out, preferred_element_type=jnp.float32
    )
    grad_low = attended_grad.astype(jnp.bfloat16).reshape(head_shape)
    row_delta = jnp.swapaxes(jnp.sum(grad_low.astype(jnp.float32) * attended, axis=-1), 1, 2)
    gathered_keys, gathered_values = (
        lax.all_gather(
            key_rows.reshape(1, seq_count, block_len, model_width), "ctx", axis=0, tiled=True
        ),
        lax.all_gather(
            value_rows.reshape(1, seq_count, block_len, model_width), "ctx", axis=0, tiled=True
        ),
    )
    block_ids = jnp.arange(cycle_size, dtype=jnp.int32)

    def key_step(carry, inputs_here):
        key_block, value_block, block_index = inputs_here
        key_heads = key_block.reshape(head_shape)
        value_heads = value_block.reshape(head_shape)
        weights_low, score_low = score_grads(
            query_heads,
            key_heads,
            value_heads,
            grad_low,
            log_total,
            row_delta,
            query_at,
            block_index * block_len + offsets,
        )
        carry = (
            carry
            + jnp.einsum(
                "shqk,skhd->sqhd", score_low, key_heads, preferred_element_type=jnp.float32
            )
            * score_scale
        )
        key_term = (
            jnp.einsum(
                "shqk,sqhd->skhd", score_low, query_heads, preferred_element_type=jnp.float32
            )
            * score_scale
        )
        value_term = jnp.einsum(
            "shqk,sqhd->skhd", weights_low, grad_low, preferred_element_type=jnp.float32
        )
        return (
            carry,
            (
                key_term.reshape(seq_count, block_len, model_width),
                value_term.reshape(seq_count, block_len, model_width),
            ),
        )

    query_grad, (key_terms, value_terms) = lax.scan(
        key_step, jnp.zeros(head_shape, jnp.float32), (gathered_keys, gathered_values, block_ids)
    )
    key_sum, value_sum = (
        lax.psum_scatter(
            key_terms.astype(jnp.bfloat16), "ctx", scatter_dimension=0, tiled=True
        ).astype(jnp.float32),
        lax.psum_scatter(
            value_terms.astype(jnp.bfloat16), "ctx", scatter_dimension=0, tiled=True
        ).astype(jnp.float32),
    )
    key_grad = key_sum.reshape(flat_rows, model_width)
    value_grad = value_sum.reshape(flat_rows, model_width)
    query_low = query_grad.reshape(flat_rows, model_width).astype(jnp.bfloat16)
    key_low = key_grad.astype(jnp.bfloat16)
    value_low = value_grad.astype(jnp.bfloat16)
    stacked = jnp.concatenate([query_low, key_low, value_low], axis=1)
    in_grad = jnp.einsum("rd,re->de", normed_low, stacked, preferred_element_type=jnp.float32)
    query_bias_grad = jnp.sum(query_low.astype(jnp.float32), axis=0)
    value_bias_grad = jnp.sum(value_low.astype(jnp.float32), axis=0)
    normed_grad = jnp.einsum("re,de->rd", stacked, full_in, preferred_element_type=jnp.float32)
    input_part, gain_one_grad, shift_one_grad = norm_first_back(normed_grad)
    input_gradient = (middle_grad + input_part).reshape(seq_count, block_len, model_width)
    (
        gain_one_part,
        shift_one_part,
        in_part,
        qbias_part,
        vbias_part,
        out_part,
        obias_part,
        gain_two_part,
        shift_two_part,
        up_part,
        ubias_part,
        down_part,
        dbias_part,
    ) = (
        lax.psum_scatter(
            gain_one_grad.astype(jnp.bfloat16), "fsdp", scatter_dimension=0, tiled=True
        ).astype(jnp.float32),
        lax.psum_scatter(
            shift_one_grad.astype(jnp.bfloat16), "fsdp", scatter_dimension=0, tiled=True
        ).astype(jnp.float32),
        lax.psum_scatter(
            in_grad.astype(jnp.bfloat16), "fsdp", scatter_dimension=0, tiled=True
        ).astype(jnp.float32),
        lax.psum_scatter(
            query_bias_grad.astype(jnp.bfloat16), "fsdp", scatter_dimension=0, tiled=True
        ).astype(jnp.float32),
        lax.psum_scatter(
            value_bias_grad.astype(jnp.bfloat16), "fsdp", scatter_dimension=0, tiled=True
        ).astype(jnp.float32),
        lax.psum_scatter(
            out_grad.astype(jnp.bfloat16), "fsdp", scatter_dimension=0, tiled=True
        ).astype(jnp.float32),
        lax.psum_scatter(
            out_bias_grad.astype(jnp.bfloat16), "fsdp", scatter_dimension=0, tiled=True
        ).astype(jnp.float32),
        lax.psum_scatter(
            gain_two_grad.astype(jnp.bfloat16), "fsdp", scatter_dimension=0, tiled=True
        ).astype(jnp.float32),
        lax.psum_scatter(
            shift_two_grad.astype(jnp.bfloat16), "fsdp", scatter_dimension=0, tiled=True
        ).astype(jnp.float32),
        lax.psum_scatter(
            up_grad.astype(jnp.bfloat16), "fsdp", scatter_dimension=0, tiled=True
        ).astype(jnp.float32),
        lax.psum_scatter(
            up_bias_grad.astype(jnp.bfloat16), "fsdp", scatter_dimension=0, tiled=True
        ).astype(jnp.float32),
        lax.psum_scatter(
            down_grad.astype(jnp.bfloat16), "fsdp", scatter_dimension=0, tiled=True
        ).astype(jnp.float32),
        lax.psum_scatter(
            down_bias_grad.astype(jnp.bfloat16), "fsdp", scatter_dimension=0, tiled=True
        ).astype(jnp.float32),
    )
    (
        gain_one_sum,
        shift_one_sum,
        in_sum,
        qbias_sum,
        vbias_sum,
        out_sum,
        obias_sum,
        gain_two_sum,
        shift_two_sum,
        up_sum,
        ubias_sum,
        down_sum,
        dbias_sum,
    ) = lax.psum(
        (
            gain_one_part,
            shift_one_part,
            in_part,
            qbias_part,
            vbias_part,
            out_part,
            obias_part,
            gain_two_part,
            shift_two_part,
            up_part,
            ubias_part,
            down_part,
            dbias_part,
        ),
        ("dp", "ctx"),
    )
    return (
        outputs,
        input_gradient,
        gain_one_sum,
        shift_one_sum,
        in_sum,
        qbias_sum,
        vbias_sum,
        out_sum,
        obias_sum,
        gain_two_sum,
        shift_two_sum,
        up_sum,
        ubias_sum,
        down_sum,
        dbias_sum,
    )


NT = (((1,), (1,)), ((), ()))
PAIR = 2 * HEAD_DIM


def attend_kernel(place_ref, q_ref, k_ref, v_ref, *refs, count, width, start):
    o_ref, log_ref, keys, values = refs[-4:]
    own_pair = pl.program_id(0)
    pair = own_pair + start
    shift = place_ref[0]
    block_len = q_ref.shape[0] // count
    lane = lax.broadcasted_iota(jnp.int32, (1, PAIR), 1)
    valid = lane + pair * PAIR < width
    first = lane < HEAD_DIM

    def rows(block):
        return pl.ds(pl.multiple_of((block ^ shift) * block_len, block_len), block_len)

    for block in range(count):
        here = pl.ds(block * block_len, block_len)
        keys[here, :] = jnp.where(valid, k_ref[rows(block), :], 0)
        values[here, :] = jnp.where(valid, v_ref[rows(block), :], 0)
    diagonal = lax.broadcasted_iota(jnp.int32, (block_len, block_len), 0) >= (
        lax.broadcasted_iota(jnp.int32, (block_len, block_len), 1)
    )
    for block in range(count):
        seen = (block + 1) * block_len
        before = block * block_len
        queries = q_ref[rows(block), :] * jnp.bfloat16(HEAD_DIM**-0.5)
        parts = []
        logs = log_ref[rows(block), :]
        for half in range(2):
            pick = jnp.logical_and(first if half == 0 else jnp.logical_not(first), valid)
            scores = lax.dot_general(
                jnp.where(pick, queries, 0),
                keys[pl.ds(0, seen), :],
                NT,
                preferred_element_type=jnp.float32,
            )
            last = jnp.where(diagonal, scores[:, before:], -1e30)
            scores = last if block == 0 else jnp.concatenate([scores[:, :before], last], axis=1)
            top = jnp.max(scores, axis=1, keepdims=True)
            weights = jnp.exp(scores - top)
            total = jnp.sum(weights, axis=1, keepdims=True)
            added = jnp.dot(
                weights.astype(jnp.bfloat16),
                values[pl.ds(0, seen), :],
                preferred_element_type=jnp.float32,
            )
            parts.append(added / total)
            logs = jnp.where(lane == 2 * own_pair + half, top + jnp.log(total), logs)
        o_ref[rows(block), :] = jnp.where(first, parts[0], parts[1]).astype(jnp.bfloat16)
        log_ref[rows(block), :] = logs


def attend_back_kernel(
    place_ref,
    q_ref,
    k_ref,
    v_ref,
    g_ref,
    o_ref,
    log_ref,
    *refs,
    count,
    width,
    start,
):
    dq_ref, dk_ref, dv_ref, queries, grads, keys, values = refs[-11:-4]
    keys_turned, logs, deltas, turned = refs[-4:]
    pair = pl.program_id(0) + start
    shift = place_ref[0]
    length = q_ref.shape[0]
    block_len = length // count
    lane = lax.broadcasted_iota(jnp.int32, (1, PAIR), 1)
    valid = lane + pair * PAIR < width
    first = lane < HEAD_DIM
    picks = (jnp.logical_and(first, valid), jnp.logical_and(jnp.logical_not(first), valid))
    half_of = (lax.broadcasted_iota(jnp.int32, (8, PAIR), 1) // HEAD_DIM) == (
        lax.broadcasted_iota(jnp.int32, (8, PAIR), 0)
    )
    ones_of = jnp.where(half_of, 1.0, 0.0)

    def rows(block):
        return pl.ds(pl.multiple_of((block ^ shift) * block_len, block_len), block_len)

    for block in range(count):
        here = pl.ds(block * block_len, block_len)
        key_block = jnp.where(valid, k_ref[rows(block), :], 0)
        keys[here, :] = key_block
        keys_turned[:, here] = key_block.astype(jnp.float32).T.astype(jnp.bfloat16)
        values[here, :] = jnp.where(valid, v_ref[rows(block), :], 0)
        query_block = q_ref[rows(block), :] * jnp.bfloat16(HEAD_DIM**-0.5)
        grad_block = jnp.where(valid, g_ref[rows(block), :], 0)
        for half in range(2):
            queries[half, here, :] = jnp.where(picks[half], query_block, 0)
            grads[half, here, :] = jnp.where(picks[half], grad_block, 0)
        mixed = grad_block.astype(jnp.float32) * jnp.where(
            valid, o_ref[rows(block), :], 0
        ).astype(jnp.float32)
        deltas[:, here] = lax.dot_general(
            ones_of,
            mixed,
            NT,
            preferred_element_type=jnp.float32,
            precision=lax.Precision.HIGHEST,
        )
        logs[:, here] = log_ref[
            0, :, pl.ds(pl.multiple_of((block ^ shift) * block_len, block_len), block_len)
        ]
    diagonal = lax.broadcasted_iota(jnp.int32, (block_len, block_len), 0) <= (
        lax.broadcasted_iota(jnp.int32, (block_len, block_len), 1)
    )
    for block in range(count):
        here = pl.ds(block * block_len, block_len)
        after = pl.ds(block * block_len, length - block * block_len)
        key_total = jnp.zeros((block_len, PAIR), jnp.float32)
        value_total = jnp.zeros((block_len, PAIR), jnp.float32)
        for half in range(2):
            scores = lax.dot_general(
                keys[here, :], queries[half, after, :], NT, preferred_element_type=jnp.float32
            )
            shifted = scores - logs[half : half + 1, after]
            own = jnp.where(diagonal, shifted[:, :block_len], -1e30)
            if block < count - 1:
                own = jnp.concatenate([own, shifted[:, block_len:]], axis=1)
            weights = jnp.exp(own)
            pressure = lax.dot_general(
                values[here, :], grads[half, after, :], NT, preferred_element_type=jnp.float32
            )
            score_low = (weights * (pressure - deltas[half : half + 1, after])).astype(
                jnp.bfloat16
            )
            value_total += jnp.dot(
                weights.astype(jnp.bfloat16),
                grads[half, after, :],
                preferred_element_type=jnp.float32,
            )
            key_total += jnp.dot(
                score_low, queries[half, after, :], preferred_element_type=jnp.float32
            )
            part = pl.ds(half * HEAD_DIM, HEAD_DIM)
            term = jnp.dot(
                keys_turned[part, here], score_low, preferred_element_type=jnp.float32
            )
            if block == 0:
                turned[part, after] = term
            else:
                turned[part, after] += term
        dk_ref[rows(block), :] = key_total.astype(jnp.bfloat16)
        dv_ref[rows(block), :] = value_total.astype(jnp.bfloat16)
    for block in range(count):
        here = pl.ds(block * block_len, block_len)
        dq_ref[rows(block), :] = (turned[:, here].T * HEAD_DIM**-0.5).astype(jnp.bfloat16)


def attend(place, queries, key_rows, value_rows, count, start, pairs, before):
    length, width = queries.shape
    heads_block = pl.BlockSpec((length, PAIR), lambda pair, place_ref: (0, pair + start))
    return pl.pallas_call(
        functools.partial(attend_kernel, count=count, width=width, start=start),
        grid_spec=pltpu.PrefetchScalarGridSpec(
            num_scalar_prefetch=1,
            grid=(pairs,),
            in_specs=[heads_block] * 3 + [pl.BlockSpec(memory_space=pl.ANY)] * len(before),
            out_specs=[
                heads_block,
                pl.BlockSpec((length, 128), lambda pair, place_ref: (0, 0)),
            ],
            scratch_shapes=[pltpu.VMEM((length, PAIR), jnp.bfloat16)] * 2,
        ),
        out_shape=[
            jax.ShapeDtypeStruct((length, width), jnp.bfloat16),
            jax.ShapeDtypeStruct((length, 128), jnp.float32),
        ],
        input_output_aliases={4 + at: at for at in range(len(before))},
        compiler_params=pltpu.CompilerParams(vmem_limit_bytes=48 * 2**20),
        cost_estimate=SMALL,
        name="attend",
    )(place, queries, key_rows, value_rows, *before)


def attend_back(
    place, queries, key_rows, value_rows, grads, attended, logs, count, start, pairs, before
):
    length, width = queries.shape
    heads_block = pl.BlockSpec((length, PAIR), lambda pair, place_ref: (0, pair + start))
    low_rows = pltpu.VMEM((length, PAIR), jnp.bfloat16)
    low_pair = pltpu.VMEM((2, length, PAIR), jnp.bfloat16)
    return pl.pallas_call(
        functools.partial(attend_back_kernel, count=count, width=width, start=start),
        grid_spec=pltpu.PrefetchScalarGridSpec(
            num_scalar_prefetch=1,
            grid=(pairs,),
            in_specs=[heads_block] * 5
            + [pl.BlockSpec((1, 2, length), lambda pair, place_ref: (pair, 0, 0))]
            + [pl.BlockSpec(memory_space=pl.ANY)] * len(before),
            out_specs=[heads_block] * 3,
            scratch_shapes=[
                low_pair,
                low_pair,
                low_rows,
                low_rows,
                pltpu.VMEM((PAIR, length), jnp.bfloat16),
                pltpu.VMEM((2, length), jnp.float32),
                pltpu.VMEM((8, length), jnp.float32),
                pltpu.VMEM((PAIR, length), jnp.float32),
            ],
        ),
        out_shape=[jax.ShapeDtypeStruct((length, width), jnp.bfloat16)] * 3,
        input_output_aliases={7 + at: at for at in range(len(before))},
        compiler_params=pltpu.CompilerParams(vmem_limit_bytes=48 * 2**20),
        cost_estimate=SMALL,
        name="attend_back",
    )(place, queries, key_rows, value_rows, grads, attended, logs, *before)


def settle_kernel(place_ref, *refs):
    pieces, out_ref = refs[:-1], refs[-1]
    for at, piece in enumerate(pieces):
        out_ref[place_ref[at]] = piece[...].astype(out_ref.dtype)


def settle(places, pieces, dtype):
    return pl.pallas_call(
        settle_kernel,
        in_specs=[pl.BlockSpec(memory_space=pltpu.SMEM)]
        + [pl.BlockSpec(memory_space=pltpu.VMEM)] * len(pieces),
        out_specs=pl.BlockSpec(memory_space=pltpu.VMEM),
        out_shape=jax.ShapeDtypeStruct((len(pieces),) + pieces[0].shape, dtype),
        compiler_params=pltpu.CompilerParams(vmem_limit_bytes=48 * 2**20),
        cost_estimate=SMALL,
        name="settle",
    )(places, *pieces)


def plane_partner(device, kind):
    core = device & 1
    if kind == "core":
        return device ^ 1
    if kind == "far":
        return device ^ (3 if core else 5)
    if kind == "near":
        return device ^ (2 if core else 4)
    return device ^ (4 if core else 2)


def plane_swap(values, kind):
    return lax.ppermute(
        values, ("dp", "ctx"), [(device, plane_partner(device, kind)) for device in range(8)]
    )


def ctx_swap(values, bits):
    return lax.ppermute(values, "ctx", [(device, device ^ bits) for device in range(4)])


def low_sum(*terms):
    return sum(term.astype(jnp.float32) for term in terms).astype(jnp.bfloat16)


def reduce_core(pieces):
    return plane_swap(pieces[2], "core"), plane_swap(pieces[3], "core")


def share_out(whole):
    return [whole] + [plane_swap(whole, kind) for kind in ("near", "core", "far")]


def share_by_core(whole, near):
    return [whole, near, plane_swap(whole, "core"), plane_swap(near, "core")]


def scatter_rows(values):
    return lax.psum_scatter(values, "fsdp", scatter_dimension=0, tiled=True)


def cut_pieces(values, z):
    rows = values.reshape(4, values.shape[0] // 4, values.shape[1])
    return [
        lax.dynamic_index_in_dim(rows, (z + step) % 4, 0, keepdims=False) for step in range(4)
    ]


def send_pieces(pieces):
    return [pieces[0]] + [
        lax.ppermute(
            pieces[step], "fsdp", [(device, (device + step) % 4) for device in range(4)]
        )
        for step in range(1, 4)
    ]


def chosen(index, options):
    result = options[-1]
    for at in range(len(options) - 2, -1, -1):
        result = jnp.where(index == at, options[at], result)
    return result


def gather_vector(values, z):
    around = [values] + [
        lax.ppermute(values, "fsdp", [(device, (device + step) % 4) for device in range(4)])
        for step in range(1, 4)
    ]
    return jnp.stack([chosen((z - at) % 4, around) for at in range(4)])


def scatter_vector(values, z):
    rows = [values[at] for at in range(4)]
    total = chosen(z, rows)
    for step in range(1, 4):
        total = total + lax.ppermute(
            chosen((z + step) % 4, rows),
            "fsdp",
            [(device, (device + step) % 4) for device in range(4)],
        )
    return total


def swap_sum(total, bits):
    return total + lax.ppermute(
        total, ("dp", "ctx"), [(device, device ^ bits) for device in range(8)]
    )


def product(left, right, dims):
    return lax.dot_general(left, right, ((dims[:1], dims[1:]), ((), ())),
                           preferred_element_type=jnp.float32)


def gelu_pair(values):
    inner = 0.7978845608028654
    cubic = inner * 0.044715
    squared = values * values
    curve = jnp.tanh(values * (inner + cubic * squared))
    half = 0.5 * values
    active = half + half * curve
    slope = 0.5 + 0.5 * curve + half * (1.0 - curve * curve) * (inner + 3.0 * cubic * squared)
    return active, slope


SMALL = pl.CostEstimate(flops=1024, bytes_accessed=1024, transcendentals=0)


def unit_of(values):
    centred = values - jnp.mean(values, axis=-1, keepdims=True)
    scale = lax.rsqrt(jnp.mean(centred * centred, axis=-1, keepdims=True) + epsilon)
    return centred * scale, scale


def fold(values):
    rows, width = values.shape
    return jnp.sum(values.reshape(rows // 8, 8, width), axis=0)


def front_kernel(places_ref, vectors_ref, *refs):
    slots, pieces = refs[:4], refs[4:20]
    x_ref, h_ref, q_ref, k_ref, v_ref, all_ref, weights, arrived, left = refs[20:]
    copies = [
        pltpu.make_async_copy(piece, weights.at[places_ref[at]], arrived.at[at])
        for at, piece in enumerate(pieces)
    ]
    for copy in copies:
        copy.start()
    rows, width = x_ref.shape
    step = rows // 4
    for at, slot in enumerate(slots):
        here = pl.ds(at * step, step)
        values = slot[...].astype(jnp.float32).T
        x_ref[here, :] = values.astype(jnp.bfloat16)
        unit, _ = unit_of(values)
        h_ref[here, :] = (unit * vectors_ref[0:1, :] + vectors_ref[1:2, :]).astype(jnp.bfloat16)
    for copy in copies:
        copy.wait()
    leave = pltpu.make_async_copy(weights, all_ref, left)
    leave.start()
    for section, out_ref in enumerate((q_ref, k_ref, v_ref)):

        def multiply(at, carry, section=section, out_ref=out_ref):
            here = pl.ds(pl.multiple_of(at * step, step), step)
            matrix = weights[4 * section : 4 * section + 4].reshape(width, width)
            total = jnp.dot(h_ref[here, :], matrix, preferred_element_type=jnp.float32)
            if section != 1:
                row = 2 if section == 0 else 3
                total = total + vectors_ref[row : row + 1, :]
            out_ref[here, :] = total.astype(jnp.bfloat16)
            return carry

        lax.fori_loop(0, rows // step, multiply, 0)
    leave.wait()


def front(places, slots, vectors, pieces):
    width, step = slots[0].shape
    rows = 4 * step
    vmem = pl.BlockSpec(memory_space=pltpu.VMEM)
    hbm = pl.BlockSpec(memory_space=pl.ANY)
    shape = jax.ShapeDtypeStruct((rows, width), jnp.bfloat16)
    whole = (16,) + pieces[0].shape
    return pl.pallas_call(
        front_kernel,
        in_specs=[pl.BlockSpec(memory_space=pltpu.SMEM)] + [vmem] * 5 + [hbm] * 16,
        out_specs=[vmem] * 5 + [hbm],
        out_shape=[shape] * 5 + [jax.ShapeDtypeStruct(whole, jnp.bfloat16)],
        scratch_shapes=[
            pltpu.VMEM(whole, jnp.bfloat16),
            pltpu.SemaphoreType.DMA((16,)),
            pltpu.SemaphoreType.DMA,
        ],
        compiler_params=pltpu.CompilerParams(vmem_limit_bytes=56 * 2**20),
        cost_estimate=SMALL,
        name="front",
    )(places, vectors, *slots, *pieces)


def turn_kernel(*refs):
    slots, out_ref = refs[:-1], refs[-1]
    step = slots[0].shape[1]
    for at, slot in enumerate(slots):
        out_ref[pl.ds(at * step, step), :] = (
            slot[...].astype(jnp.float32).T.astype(jnp.bfloat16)
        )


def turn(slots):
    width, step = slots[0].shape
    return pl.pallas_call(
        turn_kernel,
        out_shape=jax.ShapeDtypeStruct((len(slots) * step, width), jnp.bfloat16),
        compiler_params=pltpu.CompilerParams(vmem_limit_bytes=48 * 2**20),
        cost_estimate=SMALL,
        name="turn",
    )(*slots)


def assemble_kernel(place_ref, *refs, plan):
    pieces, outs = refs[:4], refs[4:]
    for at, piece in enumerate(pieces):
        for kind, moves in enumerate(plan):

            @pl.when(place_ref[at] == kind)
            def _(piece=piece, moves=moves):
                for out, source, target, size in moves:
                    outs[out][:, target : target + size] = piece[
                        :, source : source + size
                    ].astype(jnp.float32)


def assemble(places, pieces, plan, shapes):
    vmem = pl.BlockSpec(memory_space=pltpu.VMEM)
    return pl.pallas_call(
        functools.partial(assemble_kernel, plan=plan),
        in_specs=[pl.BlockSpec(memory_space=pltpu.SMEM)] + [vmem] * 4,
        out_specs=[vmem] * len(shapes),
        out_shape=[jax.ShapeDtypeStruct(shape, jnp.float32) for shape in shapes],
        compiler_params=pltpu.CompilerParams(vmem_limit_bytes=48 * 2**20),
        cost_estimate=SMALL,
        name="assemble",
    )(places, *pieces)


def store_turned(step, refs, values):
    size = refs[0].shape[1]
    share = values.shape[0] // size
    for at, ref in enumerate(refs):

        @pl.when(step == at // share)
        def _(at=at, ref=ref):
            first = (at % share) * size
            ref[...] = values[first : first + size].T.astype(ref.dtype)


def fetch(step, copies):
    @pl.when(step == 0)
    def _():
        for copy in copies:
            copy.start()


def arrive(step, copy):
    @pl.when(step == 0)
    def _():
        copy.wait()


def middle_kernel(x_ref, o_ref, vectors_ref, all_ref, middle_ref, h_ref, weights, arrived):
    step = pl.program_id(0)
    width = x_ref.shape[1]
    copy = pltpu.make_async_copy(all_ref.at[pl.ds(12, 4)], weights, arrived)
    fetch(step, [copy])
    arrive(step, copy)
    middle = (
        x_ref[...].astype(jnp.float32)
        + jnp.dot(
            o_ref[...], weights[...].reshape(width, width), preferred_element_type=jnp.float32
        )
        + vectors_ref[0:1, :]
    )
    middle_ref[...] = middle
    unit, _ = unit_of(middle)
    h_ref[...] = (unit * vectors_ref[1:2, :] + vectors_ref[2:3, :]).astype(jnp.bfloat16)


def up_kernel(h_ref, biases_ref, *refs):
    sources = refs[:2]
    active_refs, slope_refs = refs[2:4], refs[4:6]
    weights, arrived = refs[6:]
    step = pl.program_id(0)
    copies = [
        pltpu.make_async_copy(source, weights.at[at], arrived.at[at])
        for at, source in enumerate(sources)
    ]
    fetch(step, copies)
    for at in range(2):
        arrive(step, copies[at])
        hidden = (
            jnp.dot(h_ref[...], weights[at], preferred_element_type=jnp.float32)
            + biases_ref[at : at + 1, :]
        )
        active, slope = gelu_pair(hidden)
        active_refs[at][...] = active.astype(jnp.bfloat16)
        slope_refs[at][...] = slope.astype(jnp.bfloat16)


def down_kernel(middle_ref, vectors_ref, *refs):
    actives, sources = refs[:4], refs[4:8]
    out_refs = refs[8:12]
    weights, arrived = refs[12:]
    step = pl.program_id(0)
    copies = [
        pltpu.make_async_copy(source, weights.at[at], arrived.at[at])
        for at, source in enumerate(sources)
    ]
    fetch(step, copies)
    total = middle_ref[...] + vectors_ref[0:1, :]
    for at in range(4):
        arrive(step, copies[at])
        total = total + jnp.dot(
            actives[at][...], weights[at], preferred_element_type=jnp.float32
        )
    store_turned(step, out_refs, total)


def norm_back(values, gain, grad):
    unit, scale = unit_of(values)
    turned = grad * gain
    inner = (
        turned
        - jnp.mean(turned, axis=-1, keepdims=True)
        - unit * jnp.mean(turned * unit, axis=-1, keepdims=True)
    )
    return scale * inner, grad * unit


def hidden_kernel(g_ref, *refs):
    slopes, sources = refs[:2], refs[2:4]
    hidden_refs, sums_ref = refs[4:6], refs[6]
    weights, arrived = refs[7:]
    step = pl.program_id(0)
    copies = [
        pltpu.make_async_copy(source, weights.at[at], arrived.at[at])
        for at, source in enumerate(sources)
    ]
    fetch(step, copies)

    @pl.when(step == 0)
    def _():
        sums_ref[...] = jnp.zeros_like(sums_ref)

    upstream = g_ref[...]
    for at in range(2):
        arrive(step, copies[at])
        hidden = lax.dot_general(
            upstream, weights[at], NT, preferred_element_type=jnp.float32
        )
        hidden = (hidden * slopes[at][...].astype(jnp.float32)).astype(jnp.bfloat16)
        hidden_refs[at][...] = hidden
        sums_ref[at] += fold(hidden.astype(jnp.float32))
    sums_ref[2] += fold(upstream.astype(jnp.float32))


def back_kernel(g_ref, middle_ref, vectors_ref, *refs):
    hiddens, sources, all_ref = refs[:4], refs[4:8], refs[8]
    grad_ref, low_ref, out_ref, sums_ref = refs[9:13]
    weights, out_weights, arrived = refs[13:]
    step = pl.program_id(0)
    width = middle_ref.shape[1]
    copies = [
        pltpu.make_async_copy(source, weights.at[at], arrived.at[at])
        for at, source in enumerate(sources)
    ] + [pltpu.make_async_copy(all_ref.at[pl.ds(12, 4)], out_weights, arrived.at[4])]
    fetch(step, copies)

    @pl.when(step == 0)
    def _():
        sums_ref[...] = jnp.zeros_like(sums_ref)

    total = jnp.zeros(middle_ref.shape, jnp.float32)
    for at in range(4):
        arrive(step, copies[at])
        total = total + lax.dot_general(
            hiddens[at][...], weights[at], NT, preferred_element_type=jnp.float32
        )
    part, gain_term = norm_back(middle_ref[...], vectors_ref[0:1, :], total)
    sums_ref[0] += fold(gain_term)
    sums_ref[1] += fold(total)
    grad = g_ref[...].astype(jnp.float32) + part
    grad_ref[...] = grad
    grad_low = grad.astype(jnp.bfloat16)
    low_ref[...] = grad_low
    sums_ref[2] += fold(grad_low.astype(jnp.float32))
    arrive(step, copies[4])
    out_ref[...] = lax.dot_general(
        grad_low,
        out_weights[...].reshape(width, width),
        NT,
        preferred_element_type=jnp.float32,
    ).astype(jnp.bfloat16)


def last_kernel(q_ref, k_ref, v_ref, x_ref, grad_ref, vectors_ref, all_ref, *refs):
    out_refs = refs[:4]
    sums_ref, weights, arrived = refs[4:]
    step = pl.program_id(0)
    width = x_ref.shape[1]
    copies = [
        pltpu.make_async_copy(
            all_ref.at[pl.ds(4 * at, 4)], weights.at[pl.ds(4 * at, 4)], arrived.at[at]
        )
        for at in range(3)
    ]
    fetch(step, copies)
    total = jnp.zeros(x_ref.shape, jnp.float32)
    for at, ref in enumerate((q_ref, k_ref, v_ref)):
        arrive(step, copies[at])
        total = total + lax.dot_general(
            ref[...],
            weights[4 * at : 4 * at + 4].reshape(width, width),
            NT,
            preferred_element_type=jnp.float32,
        )
    part, gain_term = norm_back(x_ref[...].astype(jnp.float32), vectors_ref[0:1, :], total)
    store_turned(step, out_refs, grad_ref[...] + part)

    @pl.when(step == 0)
    def _():
        sums_ref[...] = jnp.zeros_like(sums_ref)

    terms = (
        gain_term,
        total,
        q_ref[...].astype(jnp.float32),
        v_ref[...].astype(jnp.float32),
    )
    for at, term in enumerate(terms):
        sums_ref[at] += fold(term)


def by_rows(kernel, name, rows, width, tiled, whole, remote, outs, sums, scratch, sems):
    step = 512
    tile = pl.BlockSpec((step, width), lambda at: (at, 0))
    out_specs, out_shape = [], []
    for dtype in outs:
        if dtype is None:
            out_specs += [pl.BlockSpec((width, rows // 4), lambda at: (0, 0))] * 4
            out_shape += [jax.ShapeDtypeStruct((width, rows // 4), jnp.bfloat16)] * 4
        else:
            out_specs.append(tile)
            out_shape.append(jax.ShapeDtypeStruct((rows, width), dtype))
    if sums:
        out_specs.append(pl.BlockSpec((sums, 8, width), lambda at: (0, 0, 0)))
        out_shape.append(jax.ShapeDtypeStruct((sums, 8, width), jnp.float32))
    return pl.pallas_call(
        kernel,
        grid=(rows // step,),
        in_specs=[tile] * len(tiled[0])
        + [pl.BlockSpec(value.shape, lambda at: (0, 0)) for value in whole]
        + [tile] * len(tiled[1])
        + [pl.BlockSpec(memory_space=pl.ANY)] * len(remote),
        out_specs=out_specs,
        out_shape=out_shape,
        scratch_shapes=[pltpu.VMEM(shape, jnp.bfloat16) for shape in scratch]
        + [pltpu.SemaphoreType.DMA((sems,)) if sems > 1 else pltpu.SemaphoreType.DMA],
        compiler_params=pltpu.CompilerParams(vmem_limit_bytes=60 * 2**20),
        cost_estimate=SMALL,
        name=name,
    )(*tiled[0], *whole, *tiled[1], *remote)


def per_device_exchanged(
    inputs,
    cotangent,
    first_gain,
    first_shift,
    project_in,
    query_bias,
    value_bias,
    project_out,
    output_bias,
    second_gain,
    second_shift,
    up_weight,
    up_bias,
    down_weight,
    down_bias,
):
    seq_count, block_len, width = inputs.shape
    low = jnp.bfloat16
    wide = jnp.float32
    c = lax.axis_index("ctx")
    y = lax.axis_index("dp")
    z = lax.axis_index("fsdp")
    core = c & 1
    x = c >> 1
    mine = core * 2 + jnp.where(core == 0, y, x)
    across = (1 - core) * 2 + jnp.where(core == 0, x, y)
    classes = [mine, mine ^ 1, across, across ^ 1]
    slot_of = [
        chosen(0, [sum(at * (classes[at] == kind).astype(jnp.int32) for at in range(4))])
        for kind in range(4)
    ]
    quarter = width // 4
    rows, area = seq_count * block_len, (width, width)
    pin = lax.optimization_barrier
    place = jnp.stack([c])
    places = jnp.stack([c ^ at for at in range(4)])
    class_places = jnp.stack(classes)

    def spread(values):
        values = jnp.swapaxes(values, 1, 2)
        return [lax.dynamic_index_in_dim(values, c, 0, keepdims=False)] + [
            ctx_swap(lax.dynamic_index_in_dim(values, c ^ bits, 0, keepdims=False), bits)
            for bits in range(1, 4)
        ]

    def exchange(pieces):
        return [pieces[0]] + [ctx_swap(pieces[bits], bits) for bits in range(1, 4)]

    def collect(moved, dtype):
        return jnp.swapaxes(settle(places, moved, dtype), 1, 2)

    sections = [
        project_in[:, :width],
        project_in[:, width : 2 * width],
        project_in[:, 2 * width :],
        project_out,
    ]
    section = chosen(mine, sections)
    section, inputs = pin((section, inputs))
    shards = [
        lax.ppermute(section, "fsdp", [(device, (device + step) % 4) for device in range(4)])
        for step in range(1, 4)
    ]
    turned_in = jnp.swapaxes(inputs, 1, 2)
    slots_in = [
        lax.dynamic_index_in_dim(turned_in, c ^ bits, 0, keepdims=False) for bits in range(4)
    ]
    pieces_in = (
        first_gain,
        first_shift,
        query_bias,
        value_bias,
        output_bias,
        second_gain,
        second_shift,
        down_bias,
        up_bias,
    )
    slots_in[3], up_weight, down_weight, *pieces_in = pin(
        (slots_in[3], up_weight, down_weight, *pieces_in)
    )
    slots_in = [slots_in[0]] + [ctx_swap(slots_in[bits], bits) for bits in range(1, 4)]
    vectors = gather_vector(jnp.concatenate(pieces_in), z).astype(wide)
    up_piece = jnp.concatenate(
        [
            lax.dynamic_slice_in_dim(up_weight, at * width + mine * quarter, quarter, 1)
            for at in range(4)
        ],
        axis=1,
    )
    up_piece, vectors, *moved = pin((up_piece, vectors, *shards, *slots_in))
    shards, slots_in = moved[:3], moved[3:]
    near_shards = [plane_swap(shard, "near") for shard in shards]
    cotangent, *near_shards = pin((cotangent, *near_shards))
    slots_back = spread(cotangent)
    around = (
        sections
        + shards
        + near_shards
        + [plane_swap(shard, "core") for shard in shards]
        + [plane_swap(shard, "core") for shard in near_shards]
    )
    around_places = jnp.stack(
        [kind * 4 + z for kind in range(4)]
        + [kind * 4 + (z - step) % 4 for kind in classes for step in range(1, 4)]
    )
    up_own = lax.all_gather(up_piece, "fsdp", axis=0, tiled=True)
    down_piece = lax.dynamic_slice_in_dim(down_weight, mine * quarter, quarter, 0)
    gain_first, shift_first, qbias, vbias, obias, gain_second, shift_second, dbias = (
        vectors[:, at * quarter : (at + 1) * quarter].reshape(1, width) for at in range(8)
    )
    ubias = vectors[:, 8 * quarter :].reshape(4, 4, quarter)
    ubias = jnp.concatenate(
        [
            chosen(kind, [ubias[:, at] for at in range(4)]).reshape(1, width)
            for kind in classes
        ],
        axis=0,
    )

    rows_in, normed_low, queries, key_rows, value_rows, weights = front(
        around_places,
        slots_in,
        jnp.concatenate([gain_first, shift_first, qbias, vbias], axis=0),
        around,
    )
    up_own, queries = pin((up_own, queries))
    up_near, up_core = plane_swap(up_own, "near"), plane_swap(up_own, "core")
    attended, logs = attend(place, queries, key_rows, value_rows, seq_count, 0, 9, [])
    down_piece, up_core, up_near, attended = pin((down_piece, up_core, up_near, attended))
    down_own = lax.all_gather(down_piece, "fsdp", axis=0, tiled=True)
    logs = logs.T.reshape(64, 2, rows)
    logs_one, logs_two = logs[:5], logs[5:9]
    middle, normed_two_low = by_rows(
        middle_kernel,
        "middle",
        rows,
        width,
        ([rows_in, attended], []),
        [jnp.concatenate([obias, gain_second, shift_second], axis=0)],
        [weights],
        [wide, low],
        0,
        [(4,) + section.shape],
        1,
    )
    up_slots = [up_own, up_near, up_core, plane_swap(up_near, "core")]
    active, slopes = [None] * 4, [None] * 4

    def up(first):
        outs = by_rows(
            up_kernel,
            "up",
            rows,
            width,
            ([normed_two_low], []),
            [jnp.concatenate([ubias[first : first + 1], ubias[first + 2 : first + 3]], axis=0)],
            [up_slots[first], up_slots[first + 2]],
            [low] * 4,
            0,
            [(2,) + area],
            2,
        )
        active[first], active[first + 2], slopes[first], slopes[first + 2] = outs

    up(0)
    up_slots[3], slots_back[3], active[0], active[2] = pin(
        (up_slots[3], slots_back[3], active[0], active[2])
    )
    upstream_low = turn(slots_back)
    up(1)
    down_own, *active = pin((down_own, *active))
    down_near, down_core = plane_swap(down_own, "near"), plane_swap(down_own, "core")

    def turned_product(left, right):
        return product(left, right, (0, 0)).astype(low)

    down_terms = [turned_product(active[slot], upstream_low) for slot in (3, 2)]
    upstream_low, *down_terms = pin((upstream_low, *down_terms))
    down_terms += [turned_product(active[slot], upstream_low) for slot in (1, 0)]
    down_terms = down_terms[::-1]
    down_far, down_far_two = reduce_core(down_terms)
    upstream_low, *down_terms = pin((upstream_low, *down_terms))
    hidden_low = [None] * 4

    def hidden(first, upstream):
        hidden_low[first], hidden_low[first + 2], sums = by_rows(
            hidden_kernel,
            "hidden",
            rows,
            width,
            ([upstream], [slopes[first], slopes[first + 2]]),
            [],
            [down_slots[first], down_slots[first + 2]],
            [low] * 2,
            3,
            [(2,) + area],
            2,
        )
        return sums

    down_near, upstream_low = pin((down_near, upstream_low))
    down_slots = [down_own, down_near, down_core, plane_swap(down_near, "core")]
    sums_even = hidden(0, upstream_low)
    down_second = low_sum(down_terms[1], down_far_two)
    upstream_late, sums_even, down_second = pin((upstream_low, sums_even, down_second))
    down_close = plane_swap(down_second, "near")
    sums_odd = hidden(1, upstream_late)
    hidden_sums = jnp.stack(
        [sums_even[0], sums_odd[0], sums_even[1], sums_odd[1], sums_even[2]]
    )
    down_far, *hidden_low = pin((down_far, *hidden_low))
    up_terms = [turned_product(normed_two_low, hidden_low[slot]) for slot in (3, 2)]
    normed_two_low, *up_terms = pin((normed_two_low, *up_terms))
    up_terms += [turned_product(normed_two_low, hidden_low[slot]) for slot in (1, 0)]
    up_terms = up_terms[::-1]
    up_far, up_far_two = reduce_core(up_terms)
    up_second = low_sum(up_terms[1], up_far_two)
    down_first = low_sum(down_terms[0], down_far, down_close)
    up_second, up_far, down_first, moved, *hidden_low = pin(
        (up_second, up_far, down_first, up_terms[0], *hidden_low)
    )
    up_terms[0] = moved
    down_shard = scatter_rows(down_first)
    up_close = plane_swap(up_second, "near")
    middle_grad, middle_low, grad_low, back_sums = by_rows(
        back_kernel,
        "back",
        rows,
        width,
        ([upstream_low, middle], hidden_low),
        [gain_second],
        up_slots + [weights],
        [wide, low, low],
        3,
        [(4,) + area, (4,) + section.shape],
        5,
    )
    out_term = turned_product(attended, middle_low)
    up_first = low_sum(up_terms[0], up_far, up_close)
    up_pieces = cut_pieces(up_first, z)
    grad_low, out_term, *up_pieces = pin((grad_low, out_term, *up_pieces))
    up_pieces = send_pieces(up_pieces)
    in_grads = attend_back(
        place, queries, key_rows, value_rows, grad_low, attended, logs_one, seq_count, 0, 5, []
    )
    down_shard, up_pieces[1], *in_grads = pin((down_shard, up_pieces[1], *in_grads))
    down_whole = low_sum(down_shard, plane_swap(down_shard, "other"))
    in_grads = attend_back(
        place,
        queries,
        key_rows,
        value_rows,
        grad_low,
        attended,
        logs_two,
        seq_count,
        5,
        4,
        in_grads,
    )
    down_whole, *moved = pin((down_whole, *up_pieces, *in_grads))
    up_pieces, in_grads = moved[:4], moved[4:]
    down_beside = plane_swap(down_whole, "near")
    up_shard = low_sum(*up_pieces)
    up_whole = low_sum(up_shard, plane_swap(up_shard, "other"))
    in_terms = [turned_product(normed_low, grad) for grad in in_grads]
    section_grads = in_terms + [out_term]
    sections_mine = [chosen(kind, section_grads) for kind in classes]
    far, far_two = reduce_core(sections_mine)
    second = low_sum(sections_mine[1], far_two)
    second, far, middle, *in_grads = pin((second, far, middle, *in_grads))
    query_low, key_low, value_low = in_grads
    close = plane_swap(second, "near")
    result_slots = by_rows(
        down_kernel,
        "down",
        rows,
        width,
        ([middle], active),
        [dbias],
        down_slots,
        [None],
        0,
        [(4,) + area],
        4,
    )
    first = low_sum(sections_mine[0], far, close)
    first, up_whole, down_beside, query_low, *result_slots = pin(
        (first, up_whole, down_beside, query_low, *result_slots)
    )
    up_beside = plane_swap(up_whole, "near")
    down_parts = share_by_core(down_whole, down_beside)
    up_parts = share_by_core(up_whole, up_beside)
    shard = scatter_rows(first)
    outputs = exchange(result_slots)
    *input_slots, last_sums = by_rows(
        last_kernel,
        "last",
        rows,
        width,
        ([query_low, key_low, value_low, rows_in, middle_grad], []),
        [gain_first],
        [weights],
        [None],
        4,
        [(12,) + section.shape],
        3,
    )
    moved = pin((*input_slots, *outputs, *down_parts, *up_parts))
    input_slots, outputs = exchange(moved[:4]), moved[4:8]
    down_parts, up_parts = moved[8:12], moved[12:]

    back_sums = jnp.concatenate([hidden_sums, back_sums], axis=0)
    back_sums = jnp.sum(back_sums, axis=1)
    last_sums = jnp.sum(last_sums, axis=1)
    hidden_sums = [back_sums[slot].reshape(4, quarter) for slot in range(4)]
    hidden_sums = jnp.stack(
        [chosen(slot_of[kind], hidden_sums) for kind in range(4)], axis=1
    ).reshape(4, 4 * quarter)
    totals = swap_sum(
        scatter_vector(
            jnp.concatenate(
                [back_sums[at].reshape(4, quarter) for at in range(4, 8)]
                + [last_sums[at].reshape(4, quarter) for at in range(4)]
                + [hidden_sums],
                axis=1,
            ),
            z,
        ),
        1,
    )
    shard, totals, *input_slots = pin((shard, totals, *input_slots))
    section_whole = low_sum(shard, plane_swap(shard, "other"))
    totals = swap_sum(totals, 2)
    section_whole, totals = pin((section_whole, totals))
    section_parts = share_out(section_whole)
    totals = swap_sum(totals, 4)
    outputs = collect(outputs, low)
    input_gradient = collect(input_slots, wide)
    (up_sum,) = assemble(
        class_places,
        up_parts,
        [
            [(0, at * quarter, at * width + kind * quarter, quarter) for at in range(4)]
            for kind in range(4)
        ],
        [up_weight.shape],
    )
    down_sum = settle(class_places, down_parts, wide).reshape(down_weight.shape)
    moved = pin((*section_parts, outputs, input_gradient, totals, up_sum, down_sum))
    section_parts = moved[:4]
    outputs, input_gradient, totals, up_sum, down_sum = moved[4:]
    in_sum, out_sum = assemble(
        class_places,
        section_parts,
        [[(0, 0, kind * width, width)] for kind in range(3)] + [[(1, 0, 0, width)]],
        [project_in.shape, project_out.shape],
    )
    (
        dbias_sum,
        gain_two_sum,
        shift_two_sum,
        obias_sum,
        gain_one_sum,
        shift_one_sum,
        qbias_sum,
        vbias_sum,
    ) = (totals[at * quarter : (at + 1) * quarter] for at in range(8))
    ubias_sum = totals[8 * quarter :]
    return (
        outputs,
        input_gradient,
        gain_one_sum,
        shift_one_sum,
        in_sum,
        qbias_sum,
        vbias_sum,
        out_sum,
        obias_sum,
        gain_two_sum,
        shift_two_sum,
        up_sum,
        ubias_sum,
        down_sum,
        dbias_sum,
    )


def solution(mesh):
    sizes = dict(mesh.shape)
    exchanged = sizes["dp"] == 2 and sizes["fsdp"] == 4 and sizes["ctx"] == 4
    per_device = per_device_exchanged if exchanged else per_device_gathered
    return jax.shard_map(
        per_device,
        mesh=mesh,
        in_specs=(
            P(("dp", "fsdp"), "ctx", None),
            P(("dp", "fsdp"), "ctx", None),
            P("fsdp"),
            P("fsdp"),
            P("fsdp", None),
            P("fsdp"),
            P("fsdp"),
            P("fsdp", None),
            P("fsdp"),
            P("fsdp"),
            P("fsdp"),
            P("fsdp", None),
            P("fsdp"),
            P("fsdp", None),
            P("fsdp"),
        ),
        out_specs=(
            P(("dp", "fsdp"), "ctx", None),
            P(("dp", "fsdp"), "ctx", None),
            P("fsdp"),
            P("fsdp"),
            P("fsdp", None),
            P("fsdp"),
            P("fsdp"),
            P("fsdp", None),
            P("fsdp"),
            P("fsdp"),
            P("fsdp"),
            P("fsdp", None),
            P("fsdp"),
            P("fsdp", None),
            P("fsdp"),
        ),
        check_vma=False,
    )
```

```python
import functools

import jax
import jax.numpy as jnp
from jax import lax
from jax.experimental import pallas as pl
from jax.experimental.pallas import tpu as pltpu
from jax.sharding import PartitionSpec as P

HEADS = 17
HEAD_DIM = 64


epsilon = 1e-05


def layer_norm(values, gain, shift):
    centred = values - jnp.mean(values, axis=-1, keepdims=True)
    spread = jnp.mean(centred * centred, axis=-1, keepdims=True)
    return centred * lax.rsqrt(spread + epsilon) * gain + shift


def gelu_tanh(values):
    return jax.nn.gelu(values, approximate=True)


def score_grads(
    query_heads, key_heads, value_heads, grad_heads, log_total, row_delta, query_at, key_at
):
    score_scale = HEAD_DIM ** (-0.5)
    scores = (
        jnp.einsum("sqhd,skhd->shqk", query_heads, key_heads, preferred_element_type=jnp.float32)
        * score_scale
    )
    visible = query_at[:, None] >= key_at[None, :]
    shifted = jnp.where(visible, scores - log_total[..., None], -1e30)
    weights = jnp.where(visible, jnp.exp(shifted), 0.0)
    pressure = jnp.einsum(
        "sqhd,skhd->shqk", grad_heads, value_heads, preferred_element_type=jnp.float32
    )
    score_low = (weights * (pressure - row_delta[..., None])).astype(jnp.bfloat16)
    return (weights.astype(jnp.bfloat16), score_low)


def per_device_gathered(
    inputs,
    cotangent,
    first_gain,
    first_shift,
    project_in,
    query_bias,
    value_bias,
    project_out,
    output_bias,
    second_gain,
    second_shift,
    up_weight,
    up_bias,
    down_weight,
    down_bias,
):
    seq_count, block_len, model_width = inputs.shape
    flat_rows = seq_count * block_len
    cycle_size = lax.axis_size("ctx")
    my_block = lax.axis_index("ctx")
    score_scale = HEAD_DIM ** (-0.5)
    head_shape = (seq_count, block_len, HEADS, HEAD_DIM)
    offsets = jnp.arange(block_len, dtype=jnp.int32)
    query_at = my_block * block_len + offsets
    gain_first, shift_first, full_in, qbias_full, vbias_full, full_out, obias_full = (
        lax.all_gather(first_gain, "fsdp", axis=0, tiled=True),
        lax.all_gather(first_shift, "fsdp", axis=0, tiled=True),
        lax.all_gather(project_in, "fsdp", axis=0, tiled=True),
        lax.all_gather(query_bias, "fsdp", axis=0, tiled=True),
        lax.all_gather(value_bias, "fsdp", axis=0, tiled=True),
        lax.all_gather(project_out, "fsdp", axis=0, tiled=True),
        lax.all_gather(output_bias, "fsdp", axis=0, tiled=True),
    )
    rows_in = inputs.astype(jnp.float32).reshape(flat_rows, model_width)
    normed, norm_first_back = jax.vjp(
        layer_norm, rows_in, gain_first.astype(jnp.float32), shift_first.astype(jnp.float32)
    )
    normed_low = normed.astype(jnp.bfloat16)
    projected = jnp.dot(normed_low, full_in, preferred_element_type=jnp.float32)
    queries = (projected[:, :model_width] + qbias_full).astype(jnp.bfloat16)
    key_rows = projected[:, model_width : 2 * model_width].astype(jnp.bfloat16)
    value_rows = (projected[:, 2 * model_width :] + vbias_full).astype(jnp.bfloat16)
    query_heads = queries.reshape(head_shape)
    running_top = jnp.full((seq_count, HEADS, block_len), -1e30, jnp.float32)
    accumulated = jnp.zeros(head_shape, jnp.float32)
    piece_keys = lax.all_gather(
        key_rows.reshape(seq_count, block_len, model_width), "ctx", axis=1, tiled=True
    )
    piece_values = lax.all_gather(
        value_rows.reshape(seq_count, block_len, model_width), "ctx", axis=1, tiled=True
    )
    piece_len = piece_keys.shape[1]
    key_heads = piece_keys.reshape(seq_count, piece_len, HEADS, HEAD_DIM)
    value_heads = piece_values.reshape(seq_count, piece_len, HEADS, HEAD_DIM)
    scores = (
        jnp.einsum("sqhd,skhd->shqk", query_heads, key_heads, preferred_element_type=jnp.float32)
        * score_scale
    )
    key_at = jnp.arange(piece_len, dtype=jnp.int32)
    visible = query_at[:, None] >= key_at[None, :]
    masked = jnp.where(visible, scores, -1e30)
    new_top = jnp.maximum(running_top, jnp.max(masked, axis=-1))
    factor = jnp.exp(running_top - new_top)
    weights = jnp.where(visible, jnp.exp(masked - new_top[..., None]), 0.0)
    row_total = jnp.sum(weights, axis=-1)
    added = jnp.einsum(
        "shqk,skhd->sqhd",
        weights.astype(jnp.bfloat16),
        value_heads,
        preferred_element_type=jnp.float32,
    )
    accumulated = accumulated * jnp.swapaxes(factor, 1, 2)[..., None] + added
    running_top, row_total, accumulated = (new_top, row_total, accumulated)
    attended = accumulated / jnp.swapaxes(row_total, 1, 2)[..., None]
    log_total = running_top + jnp.log(row_total)
    attended_low = attended.reshape(flat_rows, model_width).astype(jnp.bfloat16)
    middle = (
        rows_in + jnp.dot(attended_low, full_out, preferred_element_type=jnp.float32) + obias_full
    )
    gain_second, shift_second, full_up, ubias_full, full_down, dbias_full = (
        lax.all_gather(second_gain, "fsdp", axis=0, tiled=True),
        lax.all_gather(second_shift, "fsdp", axis=0, tiled=True),
        lax.all_gather(up_weight, "fsdp", axis=0, tiled=True),
        lax.all_gather(up_bias, "fsdp", axis=0, tiled=True),
        lax.all_gather(down_weight, "fsdp", axis=0, tiled=True),
        lax.all_gather(down_bias, "fsdp", axis=0, tiled=True),
    )
    normed_two, norm_second_back = jax.vjp(
        layer_norm, middle, gain_second.astype(jnp.float32), shift_second.astype(jnp.float32)
    )
    normed_two_low = normed_two.astype(jnp.bfloat16)
    hidden = jnp.dot(normed_two_low, full_up, preferred_element_type=jnp.float32) + ubias_full
    active, gelu_back = jax.vjp(gelu_tanh, hidden)
    active_low = active.astype(jnp.bfloat16)
    result = (
        middle + jnp.dot(active_low, full_down, preferred_element_type=jnp.float32) + dbias_full
    )
    outputs = result.astype(jnp.bfloat16).reshape(seq_count, block_len, model_width)
    upstream = cotangent.astype(jnp.float32).reshape(flat_rows, model_width)
    upstream_low = upstream.astype(jnp.bfloat16)
    down_grad = jnp.einsum(
        "rf,rd->fd", active_low, upstream_low, preferred_element_type=jnp.float32
    )
    down_bias_grad = jnp.sum(upstream_low.astype(jnp.float32), axis=0)
    active_grad = jnp.einsum(
        "rd,fd->rf", upstream_low, full_down, preferred_element_type=jnp.float32
    )
    (hidden_grad,) = gelu_back(active_grad)
    hidden_low = hidden_grad.astype(jnp.bfloat16)
    up_grad = jnp.einsum(
        "rd,rf->df", normed_two_low, hidden_low, preferred_element_type=jnp.float32
    )
    up_bias_grad = jnp.sum(hidden_low.astype(jnp.float32), axis=0)
    normed_two_grad = jnp.einsum(
        "rf,df->rd", hidden_low, full_up, preferred_element_type=jnp.float32
    )
    middle_part, gain_two_grad, shift_two_grad = norm_second_back(normed_two_grad)
    middle_grad = upstream + middle_part
    middle_low = middle_grad.astype(jnp.bfloat16)
    out_grad = jnp.einsum("rd,re->de", attended_low, middle_low, preferred_element_type=jnp.float32)
    out_bias_grad = jnp.sum(middle_low.astype(jnp.float32), axis=0)
    attended_grad = jnp.einsum(
        "re,de->rd", middle_low, full_out, preferred_element_type=jnp.float32
    )
    grad_low = attended_grad.astype(jnp.bfloat16).reshape(head_shape)
    row_delta = jnp.swapaxes(jnp.sum(grad_low.astype(jnp.float32) * attended, axis=-1), 1, 2)
    gathered_keys, gathered_values = (
        lax.all_gather(
            key_rows.reshape(1, seq_count, block_len, model_width), "ctx", axis=0, tiled=True
        ),
        lax.all_gather(
            value_rows.reshape(1, seq_count, block_len, model_width), "ctx", axis=0, tiled=True
        ),
    )
    block_ids = jnp.arange(cycle_size, dtype=jnp.int32)

    def key_step(carry, inputs_here):
        key_block, value_block, block_index = inputs_here
        key_heads = key_block.reshape(head_shape)
        value_heads = value_block.reshape(head_shape)
        weights_low, score_low = score_grads(
            query_heads,
            key_heads,
            value_heads,
            grad_low,
            log_total,
            row_delta,
            query_at,
            block_index * block_len + offsets,
        )
        carry = (
            carry
            + jnp.einsum(
                "shqk,skhd->sqhd", score_low, key_heads, preferred_element_type=jnp.float32
            )
            * score_scale
        )
        key_term = (
            jnp.einsum(
                "shqk,sqhd->skhd", score_low, query_heads, preferred_element_type=jnp.float32
            )
            * score_scale
        )
        value_term = jnp.einsum(
            "shqk,sqhd->skhd", weights_low, grad_low, preferred_element_type=jnp.float32
        )
        return (
            carry,
            (
                key_term.reshape(seq_count, block_len, model_width),
                value_term.reshape(seq_count, block_len, model_width),
            ),
        )

    query_grad, (key_terms, value_terms) = lax.scan(
        key_step, jnp.zeros(head_shape, jnp.float32), (gathered_keys, gathered_values, block_ids)
    )
    key_sum, value_sum = (
        lax.psum_scatter(
            key_terms.astype(jnp.bfloat16), "ctx", scatter_dimension=0, tiled=True
        ).astype(jnp.float32),
        lax.psum_scatter(
            value_terms.astype(jnp.bfloat16), "ctx", scatter_dimension=0, tiled=True
        ).astype(jnp.float32),
    )
    key_grad = key_sum.reshape(flat_rows, model_width)
    value_grad = value_sum.reshape(flat_rows, model_width)
    query_low = query_grad.reshape(flat_rows, model_width).astype(jnp.bfloat16)
    key_low = key_grad.astype(jnp.bfloat16)
    value_low = value_grad.astype(jnp.bfloat16)
    stacked = jnp.concatenate([query_low, key_low, value_low], axis=1)
    in_grad = jnp.einsum("rd,re->de", normed_low, stacked, preferred_element_type=jnp.float32)
    query_bias_grad = jnp.sum(query_low.astype(jnp.float32), axis=0)
    value_bias_grad = jnp.sum(value_low.astype(jnp.float32), axis=0)
    normed_grad = jnp.einsum("re,de->rd", stacked, full_in, preferred_element_type=jnp.float32)
    input_part, gain_one_grad, shift_one_grad = norm_first_back(normed_grad)
    input_gradient = (middle_grad + input_part).reshape(seq_count, block_len, model_width)
    (
        gain_one_part,
        shift_one_part,
        in_part,
        qbias_part,
        vbias_part,
        out_part,
        obias_part,
        gain_two_part,
        shift_two_part,
        up_part,
        ubias_part,
        down_part,
        dbias_part,
    ) = (
        lax.psum_scatter(
            gain_one_grad.astype(jnp.bfloat16), "fsdp", scatter_dimension=0, tiled=True
        ).astype(jnp.float32),
        lax.psum_scatter(
            shift_one_grad.astype(jnp.bfloat16), "fsdp", scatter_dimension=0, tiled=True
        ).astype(jnp.float32),
        lax.psum_scatter(
            in_grad.astype(jnp.bfloat16), "fsdp", scatter_dimension=0, tiled=True
        ).astype(jnp.float32),
        lax.psum_scatter(
            query_bias_grad.astype(jnp.bfloat16), "fsdp", scatter_dimension=0, tiled=True
        ).astype(jnp.float32),
        lax.psum_scatter(
            value_bias_grad.astype(jnp.bfloat16), "fsdp", scatter_dimension=0, tiled=True
        ).astype(jnp.float32),
        lax.psum_scatter(
            out_grad.astype(jnp.bfloat16), "fsdp", scatter_dimension=0, tiled=True
        ).astype(jnp.float32),
        lax.psum_scatter(
            out_bias_grad.astype(jnp.bfloat16), "fsdp", scatter_dimension=0, tiled=True
        ).astype(jnp.float32),
        lax.psum_scatter(
            gain_two_grad.astype(jnp.bfloat16), "fsdp", scatter_dimension=0, tiled=True
        ).astype(jnp.float32),
        lax.psum_scatter(
            shift_two_grad.astype(jnp.bfloat16), "fsdp", scatter_dimension=0, tiled=True
        ).astype(jnp.float32),
        lax.psum_scatter(
            up_grad.astype(jnp.bfloat16), "fsdp", scatter_dimension=0, tiled=True
        ).astype(jnp.float32),
        lax.psum_scatter(
            up_bias_grad.astype(jnp.bfloat16), "fsdp", scatter_dimension=0, tiled=True
        ).astype(jnp.float32),
        lax.psum_scatter(
            down_grad.astype(jnp.bfloat16), "fsdp", scatter_dimension=0, tiled=True
        ).astype(jnp.float32),
        lax.psum_scatter(
            down_bias_grad.astype(jnp.bfloat16), "fsdp", scatter_dimension=0, tiled=True
        ).astype(jnp.float32),
    )
    (
        gain_one_sum,
        shift_one_sum,
        in_sum,
        qbias_sum,
        vbias_sum,
        out_sum,
        obias_sum,
        gain_two_sum,
        shift_two_sum,
        up_sum,
        ubias_sum,
        down_sum,
        dbias_sum,
    ) = lax.psum(
        (
            gain_one_part,
            shift_one_part,
            in_part,
            qbias_part,
            vbias_part,
            out_part,
            obias_part,
            gain_two_part,
            shift_two_part,
            up_part,
            ubias_part,
            down_part,
            dbias_part,
        ),
        ("dp", "ctx"),
    )
    return (
        outputs,
        input_gradient,
        gain_one_sum,
        shift_one_sum,
        in_sum,
        qbias_sum,
        vbias_sum,
        out_sum,
        obias_sum,
        gain_two_sum,
        shift_two_sum,
        up_sum,
        ubias_sum,
        down_sum,
        dbias_sum,
    )


NT = (((1,), (1,)), ((), ()))
PAIR = 2 * HEAD_DIM


def attend_kernel(place_ref, q_ref, k_ref, v_ref, *refs, count, width, start):
    o_ref, log_ref, keys, values = refs[-4:]
    own_pair = pl.program_id(0)
    pair = own_pair + start
    shift = place_ref[0]
    block_len = q_ref.shape[0] // count
    lane = lax.broadcasted_iota(jnp.int32, (1, PAIR), 1)
    valid = lane + pair * PAIR < width
    first = lane < HEAD_DIM

    def rows(block):
        return pl.ds(pl.multiple_of((block ^ shift) * block_len, block_len), block_len)

    for block in range(count):
        here = pl.ds(block * block_len, block_len)
        keys[here, :] = jnp.where(valid, k_ref[rows(block), :], 0)
        values[here, :] = jnp.where(valid, v_ref[rows(block), :], 0)
    diagonal = lax.broadcasted_iota(jnp.int32, (block_len, block_len), 0) >= (
        lax.broadcasted_iota(jnp.int32, (block_len, block_len), 1)
    )
    for block in range(count):
        seen = (block + 1) * block_len
        before = block * block_len
        queries = q_ref[rows(block), :] * jnp.bfloat16(HEAD_DIM**-0.5)
        parts = []
        logs = log_ref[rows(block), :]
        for half in range(2):
            pick = jnp.logical_and(first if half == 0 else jnp.logical_not(first), valid)
            scores = lax.dot_general(
                jnp.where(pick, queries, 0),
                keys[pl.ds(0, seen), :],
                NT,
                preferred_element_type=jnp.float32,
            )
            last = jnp.where(diagonal, scores[:, before:], -1e30)
            scores = last if block == 0 else jnp.concatenate([scores[:, :before], last], axis=1)
            top = jnp.max(scores, axis=1, keepdims=True)
            weights = jnp.exp(scores - top)
            total = jnp.sum(weights, axis=1, keepdims=True)
            added = jnp.dot(
                weights.astype(jnp.bfloat16),
                values[pl.ds(0, seen), :],
                preferred_element_type=jnp.float32,
            )
            parts.append(added / total)
            logs = jnp.where(lane == 2 * own_pair + half, top + jnp.log(total), logs)
        o_ref[rows(block), :] = jnp.where(first, parts[0], parts[1]).astype(jnp.bfloat16)
        log_ref[rows(block), :] = logs


def attend_back_kernel(
    place_ref,
    q_ref,
    k_ref,
    v_ref,
    g_ref,
    o_ref,
    log_ref,
    *refs,
    count,
    width,
    start,
):
    dq_ref, dk_ref, dv_ref, queries, grads, keys, values = refs[-11:-4]
    keys_turned, logs, deltas, turned = refs[-4:]
    pair = pl.program_id(0) + start
    shift = place_ref[0]
    length = q_ref.shape[0]
    block_len = length // count
    lane = lax.broadcasted_iota(jnp.int32, (1, PAIR), 1)
    valid = lane + pair * PAIR < width
    first = lane < HEAD_DIM
    picks = (jnp.logical_and(first, valid), jnp.logical_and(jnp.logical_not(first), valid))
    half_of = (lax.broadcasted_iota(jnp.int32, (8, PAIR), 1) // HEAD_DIM) == (
        lax.broadcasted_iota(jnp.int32, (8, PAIR), 0)
    )
    ones_of = jnp.where(half_of, 1.0, 0.0)

    def rows(block):
        return pl.ds(pl.multiple_of((block ^ shift) * block_len, block_len), block_len)

    for block in range(count):
        here = pl.ds(block * block_len, block_len)
        key_block = jnp.where(valid, k_ref[rows(block), :], 0)
        keys[here, :] = key_block
        keys_turned[:, here] = key_block.astype(jnp.float32).T.astype(jnp.bfloat16)
        values[here, :] = jnp.where(valid, v_ref[rows(block), :], 0)
        query_block = q_ref[rows(block), :] * jnp.bfloat16(HEAD_DIM**-0.5)
        grad_block = jnp.where(valid, g_ref[rows(block), :], 0)
        for half in range(2):
            queries[half, here, :] = jnp.where(picks[half], query_block, 0)
            grads[half, here, :] = jnp.where(picks[half], grad_block, 0)
        mixed = grad_block.astype(jnp.float32) * jnp.where(
            valid, o_ref[rows(block), :], 0
        ).astype(jnp.float32)
        deltas[:, here] = lax.dot_general(
            ones_of,
            mixed,
            NT,
            preferred_element_type=jnp.float32,
            precision=lax.Precision.HIGHEST,
        )
        logs[:, here] = log_ref[
            0, :, pl.ds(pl.multiple_of((block ^ shift) * block_len, block_len), block_len)
        ]
    diagonal = lax.broadcasted_iota(jnp.int32, (block_len, block_len), 0) <= (
        lax.broadcasted_iota(jnp.int32, (block_len, block_len), 1)
    )
    for block in range(count):
        here = pl.ds(block * block_len, block_len)
        after = pl.ds(block * block_len, length - block * block_len)
        key_total = jnp.zeros((block_len, PAIR), jnp.float32)
        value_total = jnp.zeros((block_len, PAIR), jnp.float32)
        for half in range(2):
            scores = lax.dot_general(
                keys[here, :], queries[half, after, :], NT, preferred_element_type=jnp.float32
            )
            shifted = scores - logs[half : half + 1, after]
            own = jnp.where(diagonal, shifted[:, :block_len], -1e30)
            if block < count - 1:
                own = jnp.concatenate([own, shifted[:, block_len:]], axis=1)
            weights = jnp.exp(own)
            pressure = lax.dot_general(
                values[here, :], grads[half, after, :], NT, preferred_element_type=jnp.float32
            )
            score_low = (weights * (pressure - deltas[half : half + 1, after])).astype(
                jnp.bfloat16
            )
            value_total += jnp.dot(
                weights.astype(jnp.bfloat16),
                grads[half, after, :],
                preferred_element_type=jnp.float32,
            )
            key_total += jnp.dot(
                score_low, queries[half, after, :], preferred_element_type=jnp.float32
            )
            part = pl.ds(half * HEAD_DIM, HEAD_DIM)
            term = jnp.dot(
                keys_turned[part, here], score_low, preferred_element_type=jnp.float32
            )
            if block == 0:
                turned[part, after] = term
            else:
                turned[part, after] += term
        dk_ref[rows(block), :] = key_total.astype(jnp.bfloat16)
        dv_ref[rows(block), :] = value_total.astype(jnp.bfloat16)
    for block in range(count):
        here = pl.ds(block * block_len, block_len)
        dq_ref[rows(block), :] = (turned[:, here].T * HEAD_DIM**-0.5).astype(jnp.bfloat16)


def attend(place, queries, key_rows, value_rows, count, start, pairs, before):
    length, width = queries.shape
    heads_block = pl.BlockSpec((length, PAIR), lambda pair, place_ref: (0, pair + start))
    return pl.pallas_call(
        functools.partial(attend_kernel, count=count, width=width, start=start),
        grid_spec=pltpu.PrefetchScalarGridSpec(
            num_scalar_prefetch=1,
            grid=(pairs,),
            in_specs=[heads_block] * 3 + [pl.BlockSpec(memory_space=pl.ANY)] * len(before),
            out_specs=[
                heads_block,
                pl.BlockSpec((length, 128), lambda pair, place_ref: (0, 0)),
            ],
            scratch_shapes=[pltpu.VMEM((length, PAIR), jnp.bfloat16)] * 2,
        ),
        out_shape=[
            jax.ShapeDtypeStruct((length, width), jnp.bfloat16),
            jax.ShapeDtypeStruct((length, 128), jnp.float32),
        ],
        input_output_aliases={4 + at: at for at in range(len(before))},
        compiler_params=pltpu.CompilerParams(vmem_limit_bytes=48 * 2**20),
        cost_estimate=SMALL,
        name="attend",
    )(place, queries, key_rows, value_rows, *before)


def attend_back(
    place, queries, key_rows, value_rows, grads, attended, logs, count, start, pairs, before
):
    length, width = queries.shape
    heads_block = pl.BlockSpec((length, PAIR), lambda pair, place_ref: (0, pair + start))
    low_rows = pltpu.VMEM((length, PAIR), jnp.bfloat16)
    low_pair = pltpu.VMEM((2, length, PAIR), jnp.bfloat16)
    return pl.pallas_call(
        functools.partial(attend_back_kernel, count=count, width=width, start=start),
        grid_spec=pltpu.PrefetchScalarGridSpec(
            num_scalar_prefetch=1,
            grid=(pairs,),
            in_specs=[heads_block] * 5
            + [pl.BlockSpec((1, 2, length), lambda pair, place_ref: (pair, 0, 0))]
            + [pl.BlockSpec(memory_space=pl.ANY)] * len(before),
            out_specs=[heads_block] * 3,
            scratch_shapes=[
                low_pair,
                low_pair,
                low_rows,
                low_rows,
                pltpu.VMEM((PAIR, length), jnp.bfloat16),
                pltpu.VMEM((2, length), jnp.float32),
                pltpu.VMEM((8, length), jnp.float32),
                pltpu.VMEM((PAIR, length), jnp.float32),
            ],
        ),
        out_shape=[jax.ShapeDtypeStruct((length, width), jnp.bfloat16)] * 3,
        input_output_aliases={7 + at: at for at in range(len(before))},
        compiler_params=pltpu.CompilerParams(vmem_limit_bytes=48 * 2**20),
        cost_estimate=SMALL,
        name="attend_back",
    )(place, queries, key_rows, value_rows, grads, attended, logs, *before)


def settle_kernel(place_ref, *refs):
    pieces, out_ref = refs[:-1], refs[-1]
    for at, piece in enumerate(pieces):
        out_ref[place_ref[at]] = piece[...].astype(out_ref.dtype)


def settle(places, pieces, dtype):
    return pl.pallas_call(
        settle_kernel,
        in_specs=[pl.BlockSpec(memory_space=pltpu.SMEM)]
        + [pl.BlockSpec(memory_space=pltpu.VMEM)] * len(pieces),
        out_specs=pl.BlockSpec(memory_space=pltpu.VMEM),
        out_shape=jax.ShapeDtypeStruct((len(pieces),) + pieces[0].shape, dtype),
        compiler_params=pltpu.CompilerParams(vmem_limit_bytes=48 * 2**20),
        cost_estimate=SMALL,
        name="settle",
    )(places, *pieces)


def plane_partner(device, kind):
    core = device & 1
    if kind == "core":
        return device ^ 1
    if kind == "far":
        return device ^ (3 if core else 5)
    if kind == "near":
        return device ^ (2 if core else 4)
    return device ^ (4 if core else 2)


def plane_swap(values, kind):
    return lax.ppermute(
        values, ("dp", "ctx"), [(device, plane_partner(device, kind)) for device in range(8)]
    )


def ctx_swap(values, bits):
    return lax.ppermute(values, "ctx", [(device, device ^ bits) for device in range(4)])


def low_sum(*terms):
    return sum(term.astype(jnp.float32) for term in terms).astype(jnp.bfloat16)


def reduce_core(pieces):
    return plane_swap(pieces[2], "core"), plane_swap(pieces[3], "core")


def share_out(whole):
    return [whole] + [plane_swap(whole, kind) for kind in ("near", "core", "far")]


def share_by_core(whole, near):
    return [whole, near, plane_swap(whole, "core"), plane_swap(near, "core")]


def scatter_rows(values):
    return lax.psum_scatter(values, "fsdp", scatter_dimension=0, tiled=True)


def cut_pieces(values, z):
    rows = values.reshape(4, values.shape[0] // 4, values.shape[1])
    return [
        lax.dynamic_index_in_dim(rows, (z + step) % 4, 0, keepdims=False) for step in range(4)
    ]


def send_pieces(pieces):
    return [pieces[0]] + [
        lax.ppermute(
            pieces[step], "fsdp", [(device, (device + step) % 4) for device in range(4)]
        )
        for step in range(1, 4)
    ]


def chosen(index, options):
    result = options[-1]
    for at in range(len(options) - 2, -1, -1):
        result = jnp.where(index == at, options[at], result)
    return result


def gather_vector(values, z):
    around = [values] + [
        lax.ppermute(values, "fsdp", [(device, (device + step) % 4) for device in range(4)])
        for step in range(1, 4)
    ]
    return jnp.stack([chosen((z - at) % 4, around) for at in range(4)])


def scatter_vector(values, z):
    rows = [values[at] for at in range(4)]
    total = chosen(z, rows)
    for step in range(1, 4):
        total = total + lax.ppermute(
            chosen((z + step) % 4, rows),
            "fsdp",
            [(device, (device + step) % 4) for device in range(4)],
        )
    return total


def swap_sum(total, bits):
    return total + lax.ppermute(
        total, ("dp", "ctx"), [(device, device ^ bits) for device in range(8)]
    )


def product(left, right, dims):
    return lax.dot_general(left, right, ((dims[:1], dims[1:]), ((), ())),
                           preferred_element_type=jnp.float32)


def gelu_pair(values):
    inner = 0.7978845608028654
    cubic = inner * 0.044715
    squared = values * values
    curve = jnp.tanh(values * (inner + cubic * squared))
    half = 0.5 * values
    active = half + half * curve
    slope = 0.5 + 0.5 * curve + half * (1.0 - curve * curve) * (inner + 3.0 * cubic * squared)
    return active, slope


SMALL = pl.CostEstimate(flops=1024, bytes_accessed=1024, transcendentals=0)


def unit_of(values):
    centred = values - jnp.mean(values, axis=-1, keepdims=True)
    scale = lax.rsqrt(jnp.mean(centred * centred, axis=-1, keepdims=True) + epsilon)
    return centred * scale, scale


def fold(values):
    rows, width = values.shape
    return jnp.sum(values.reshape(rows // 8, 8, width), axis=0)


def front_kernel(places_ref, vectors_ref, *refs):
    slots, pieces = refs[:4], refs[4:20]
    x_ref, h_ref, q_ref, k_ref, v_ref, all_ref, weights, arrived, left = refs[20:]
    copies = [
        pltpu.make_async_copy(piece, weights.at[places_ref[at]], arrived.at[at])
        for at, piece in enumerate(pieces)
    ]
    for copy in copies:
        copy.start()
    rows, width = x_ref.shape
    step = rows // 4
    for at, slot in enumerate(slots):
        here = pl.ds(at * step, step)
        values = slot[...].astype(jnp.float32).T
        x_ref[here, :] = values.astype(jnp.bfloat16)
        unit, _ = unit_of(values)
        h_ref[here, :] = (unit * vectors_ref[0:1, :] + vectors_ref[1:2, :]).astype(jnp.bfloat16)
    for copy in copies:
        copy.wait()
    leave = pltpu.make_async_copy(weights, all_ref, left)
    leave.start()
    for section, out_ref in enumerate((q_ref, k_ref, v_ref)):

        def multiply(at, carry, section=section, out_ref=out_ref):
            here = pl.ds(pl.multiple_of(at * step, step), step)
            matrix = weights[4 * section : 4 * section + 4].reshape(width, width)
            total = jnp.dot(h_ref[here, :], matrix, preferred_element_type=jnp.float32)
            if section != 1:
                row = 2 if section == 0 else 3
                total = total + vectors_ref[row : row + 1, :]
            out_ref[here, :] = total.astype(jnp.bfloat16)
            return carry

        lax.fori_loop(0, rows // step, multiply, 0)
    leave.wait()


def front(places, slots, vectors, pieces):
    width, step = slots[0].shape
    rows = 4 * step
    vmem = pl.BlockSpec(memory_space=pltpu.VMEM)
    hbm = pl.BlockSpec(memory_space=pl.ANY)
    shape = jax.ShapeDtypeStruct((rows, width), jnp.bfloat16)
    whole = (16,) + pieces[0].shape
    return pl.pallas_call(
        front_kernel,
        in_specs=[pl.BlockSpec(memory_space=pltpu.SMEM)] + [vmem] * 5 + [hbm] * 16,
        out_specs=[vmem] * 5 + [hbm],
        out_shape=[shape] * 5 + [jax.ShapeDtypeStruct(whole, jnp.bfloat16)],
        scratch_shapes=[
            pltpu.VMEM(whole, jnp.bfloat16),
            pltpu.SemaphoreType.DMA((16,)),
            pltpu.SemaphoreType.DMA,
        ],
        compiler_params=pltpu.CompilerParams(vmem_limit_bytes=56 * 2**20),
        cost_estimate=SMALL,
        name="front",
    )(places, vectors, *slots, *pieces)


def turn_kernel(*refs):
    slots, out_ref = refs[:-1], refs[-1]
    step = slots[0].shape[1]
    for at, slot in enumerate(slots):
        out_ref[pl.ds(at * step, step), :] = (
            slot[...].astype(jnp.float32).T.astype(jnp.bfloat16)
        )


def turn(slots):
    width, step = slots[0].shape
    return pl.pallas_call(
        turn_kernel,
        out_shape=jax.ShapeDtypeStruct((len(slots) * step, width), jnp.bfloat16),
        compiler_params=pltpu.CompilerParams(vmem_limit_bytes=48 * 2**20),
        cost_estimate=SMALL,
        name="turn",
    )(*slots)


def assemble_kernel(place_ref, *refs, plan):
    pieces, outs = refs[:4], refs[4:]
    for at, piece in enumerate(pieces):
        for kind, moves in enumerate(plan):

            @pl.when(place_ref[at] == kind)
            def _(piece=piece, moves=moves):
                for out, source, target, size in moves:
                    outs[out][:, target : target + size] = piece[
                        :, source : source + size
                    ].astype(jnp.float32)


def assemble(places, pieces, plan, shapes):
    vmem = pl.BlockSpec(memory_space=pltpu.VMEM)
    return pl.pallas_call(
        functools.partial(assemble_kernel, plan=plan),
        in_specs=[pl.BlockSpec(memory_space=pltpu.SMEM)] + [vmem] * 4,
        out_specs=[vmem] * len(shapes),
        out_shape=[jax.ShapeDtypeStruct(shape, jnp.float32) for shape in shapes],
        compiler_params=pltpu.CompilerParams(vmem_limit_bytes=48 * 2**20),
        cost_estimate=SMALL,
        name="assemble",
    )(places, *pieces)


def store_turned(step, refs, values):
    size = refs[0].shape[1]
    share = values.shape[0] // size
    for at, ref in enumerate(refs):

        @pl.when(step == at // share)
        def _(at=at, ref=ref):
            first = (at % share) * size
            ref[...] = values[first : first + size].T.astype(ref.dtype)


def fetch(step, copies):
    @pl.when(step == 0)
    def _():
        for copy in copies:
            copy.start()


def arrive(step, copy):
    @pl.when(step == 0)
    def _():
        copy.wait()


def middle_kernel(x_ref, o_ref, vectors_ref, all_ref, middle_ref, h_ref, weights, arrived):
    step = pl.program_id(0)
    width = x_ref.shape[1]
    copy = pltpu.make_async_copy(all_ref.at[pl.ds(12, 4)], weights, arrived)
    fetch(step, [copy])
    arrive(step, copy)
    middle = (
        x_ref[...].astype(jnp.float32)
        + jnp.dot(
            o_ref[...], weights[...].reshape(width, width), preferred_element_type=jnp.float32
        )
        + vectors_ref[0:1, :]
    )
    middle_ref[...] = middle
    unit, _ = unit_of(middle)
    h_ref[...] = (unit * vectors_ref[1:2, :] + vectors_ref[2:3, :]).astype(jnp.bfloat16)


def up_kernel(h_ref, biases_ref, *refs):
    sources = refs[:2]
    active_refs, slope_refs = refs[2:4], refs[4:6]
    weights, arrived = refs[6:]
    step = pl.program_id(0)
    copies = [
        pltpu.make_async_copy(source, weights.at[at], arrived.at[at])
        for at, source in enumerate(sources)
    ]
    fetch(step, copies)
    for at in range(2):
        arrive(step, copies[at])
        hidden = (
            jnp.dot(h_ref[...], weights[at], preferred_element_type=jnp.float32)
            + biases_ref[at : at + 1, :]
        )
        active, slope = gelu_pair(hidden)
        active_refs[at][...] = active.astype(jnp.bfloat16)
        slope_refs[at][...] = slope.astype(jnp.bfloat16)


def down_kernel(middle_ref, vectors_ref, *refs):
    actives, sources = refs[:4], refs[4:8]
    out_refs = refs[8:12]
    weights, arrived = refs[12:]
    step = pl.program_id(0)
    copies = [
        pltpu.make_async_copy(source, weights.at[at], arrived.at[at])
        for at, source in enumerate(sources)
    ]
    fetch(step, copies)
    total = middle_ref[...] + vectors_ref[0:1, :]
    for at in range(4):
        arrive(step, copies[at])
        total = total + jnp.dot(
            actives[at][...], weights[at], preferred_element_type=jnp.float32
        )
    store_turned(step, out_refs, total)


def norm_back(values, gain, grad):
    unit, scale = unit_of(values)
    turned = grad * gain
    inner = (
        turned
        - jnp.mean(turned, axis=-1, keepdims=True)
        - unit * jnp.mean(turned * unit, axis=-1, keepdims=True)
    )
    return scale * inner, grad * unit


def hidden_kernel(g_ref, *refs):
    slopes, sources = refs[:2], refs[2:4]
    hidden_refs, sums_ref = refs[4:6], refs[6]
    weights, arrived = refs[7:]
    step = pl.program_id(0)
    copies = [
        pltpu.make_async_copy(source, weights.at[at], arrived.at[at])
        for at, source in enumerate(sources)
    ]
    fetch(step, copies)

    @pl.when(step == 0)
    def _():
        sums_ref[...] = jnp.zeros_like(sums_ref)

    upstream = g_ref[...]
    for at in range(2):
        arrive(step, copies[at])
        hidden = lax.dot_general(
            upstream, weights[at], NT, preferred_element_type=jnp.float32
        )
        hidden = (hidden * slopes[at][...].astype(jnp.float32)).astype(jnp.bfloat16)
        hidden_refs[at][...] = hidden
        sums_ref[at] += fold(hidden.astype(jnp.float32))
    sums_ref[2] += fold(upstream.astype(jnp.float32))


def back_kernel(g_ref, middle_ref, vectors_ref, *refs):
    hiddens, sources, all_ref = refs[:4], refs[4:8], refs[8]
    grad_ref, low_ref, out_ref, sums_ref = refs[9:13]
    weights, out_weights, arrived = refs[13:]
    step = pl.program_id(0)
    width = middle_ref.shape[1]
    copies = [
        pltpu.make_async_copy(source, weights.at[at], arrived.at[at])
        for at, source in enumerate(sources)
    ] + [pltpu.make_async_copy(all_ref.at[pl.ds(12, 4)], out_weights, arrived.at[4])]
    fetch(step, copies)

    @pl.when(step == 0)
    def _():
        sums_ref[...] = jnp.zeros_like(sums_ref)

    total = jnp.zeros(middle_ref.shape, jnp.float32)
    for at in range(4):
        arrive(step, copies[at])
        total = total + lax.dot_general(
            hiddens[at][...], weights[at], NT, preferred_element_type=jnp.float32
        )
    part, gain_term = norm_back(middle_ref[...], vectors_ref[0:1, :], total)
    sums_ref[0] += fold(gain_term)
    sums_ref[1] += fold(total)
    grad = g_ref[...].astype(jnp.float32) + part
    grad_ref[...] = grad
    grad_low = grad.astype(jnp.bfloat16)
    low_ref[...] = grad_low
    sums_ref[2] += fold(grad_low.astype(jnp.float32))
    arrive(step, copies[4])
    out_ref[...] = lax.dot_general(
        grad_low,
        out_weights[...].reshape(width, width),
        NT,
        preferred_element_type=jnp.float32,
    ).astype(jnp.bfloat16)


def last_kernel(q_ref, k_ref, v_ref, x_ref, grad_ref, vectors_ref, all_ref, *refs):
    out_refs = refs[:4]
    sums_ref, weights, arrived = refs[4:]
    step = pl.program_id(0)
    width = x_ref.shape[1]
    copies = [
        pltpu.make_async_copy(
            all_ref.at[pl.ds(4 * at, 4)], weights.at[pl.ds(4 * at, 4)], arrived.at[at]
        )
        for at in range(3)
    ]
    fetch(step, copies)
    total = jnp.zeros(x_ref.shape, jnp.float32)
    for at, ref in enumerate((q_ref, k_ref, v_ref)):
        arrive(step, copies[at])
        total = total + lax.dot_general(
            ref[...],
            weights[4 * at : 4 * at + 4].reshape(width, width),
            NT,
            preferred_element_type=jnp.float32,
        )
    part, gain_term = norm_back(x_ref[...].astype(jnp.float32), vectors_ref[0:1, :], total)
    store_turned(step, out_refs, grad_ref[...] + part)

    @pl.when(step == 0)
    def _():
        sums_ref[...] = jnp.zeros_like(sums_ref)

    terms = (
        gain_term,
        total,
        q_ref[...].astype(jnp.float32),
        v_ref[...].astype(jnp.float32),
    )
    for at, term in enumerate(terms):
        sums_ref[at] += fold(term)


def by_rows(kernel, name, rows, width, tiled, whole, remote, outs, sums, scratch, sems):
    step = 512
    tile = pl.BlockSpec((step, width), lambda at: (at, 0))
    out_specs, out_shape = [], []
    for dtype in outs:
        if dtype is None:
            out_specs += [pl.BlockSpec((width, rows // 4), lambda at: (0, 0))] * 4
            out_shape += [jax.ShapeDtypeStruct((width, rows // 4), jnp.bfloat16)] * 4
        else:
            out_specs.append(tile)
            out_shape.append(jax.ShapeDtypeStruct((rows, width), dtype))
    if sums:
        out_specs.append(pl.BlockSpec((sums, 8, width), lambda at: (0, 0, 0)))
        out_shape.append(jax.ShapeDtypeStruct((sums, 8, width), jnp.float32))
    return pl.pallas_call(
        kernel,
        grid=(rows // step,),
        in_specs=[tile] * len(tiled[0])
        + [pl.BlockSpec(value.shape, lambda at: (0, 0)) for value in whole]
        + [tile] * len(tiled[1])
        + [pl.BlockSpec(memory_space=pl.ANY)] * len(remote),
        out_specs=out_specs,
        out_shape=out_shape,
        scratch_shapes=[pltpu.VMEM(shape, jnp.bfloat16) for shape in scratch]
        + [pltpu.SemaphoreType.DMA((sems,)) if sems > 1 else pltpu.SemaphoreType.DMA],
        compiler_params=pltpu.CompilerParams(vmem_limit_bytes=60 * 2**20),
        cost_estimate=SMALL,
        name=name,
    )(*tiled[0], *whole, *tiled[1], *remote)


def per_device_exchanged(
    inputs,
    cotangent,
    first_gain,
    first_shift,
    project_in,
    query_bias,
    value_bias,
    project_out,
    output_bias,
    second_gain,
    second_shift,
    up_weight,
    up_bias,
    down_weight,
    down_bias,
):
    seq_count, block_len, width = inputs.shape
    low = jnp.bfloat16
    wide = jnp.float32
    c = lax.axis_index("ctx")
    y = lax.axis_index("dp")
    z = lax.axis_index("fsdp")
    core = c & 1
    x = c >> 1
    mine = core * 2 + jnp.where(core == 0, y, x)
    across = (1 - core) * 2 + jnp.where(core == 0, x, y)
    classes = [mine, mine ^ 1, across, across ^ 1]
    slot_of = [
        chosen(0, [sum(at * (classes[at] == kind).astype(jnp.int32) for at in range(4))])
        for kind in range(4)
    ]
    quarter = width // 4
    rows, area = seq_count * block_len, (width, width)
    pin = lax.optimization_barrier
    place = jnp.stack([c])
    places = jnp.stack([c ^ at for at in range(4)])
    class_places = jnp.stack(classes)

    def spread(values):
        values = jnp.swapaxes(values, 1, 2)
        return [lax.dynamic_index_in_dim(values, c, 0, keepdims=False)] + [
            ctx_swap(lax.dynamic_index_in_dim(values, c ^ bits, 0, keepdims=False), bits)
            for bits in range(1, 4)
        ]

    def exchange(pieces):
        return [pieces[0]] + [ctx_swap(pieces[bits], bits) for bits in range(1, 4)]

    def collect(moved, dtype):
        return jnp.swapaxes(settle(places, moved, dtype), 1, 2)

    sections = [
        project_in[:, :width],
        project_in[:, width : 2 * width],
        project_in[:, 2 * width :],
        project_out,
    ]
    section = chosen(mine, sections)
    section, inputs = pin((section, inputs))
    shards = [
        lax.ppermute(section, "fsdp", [(device, (device + step) % 4) for device in range(4)])
        for step in range(1, 4)
    ]
    turned_in = jnp.swapaxes(inputs, 1, 2)
    slots_in = [
        lax.dynamic_index_in_dim(turned_in, c ^ bits, 0, keepdims=False) for bits in range(4)
    ]
    pieces_in = (
        first_gain,
        first_shift,
        query_bias,
        value_bias,
        output_bias,
        second_gain,
        second_shift,
        down_bias,
        up_bias,
    )
    slots_in[3], up_weight, down_weight, *pieces_in = pin(
        (slots_in[3], up_weight, down_weight, *pieces_in)
    )
    slots_in = [slots_in[0]] + [ctx_swap(slots_in[bits], bits) for bits in range(1, 4)]
    vectors = gather_vector(jnp.concatenate(pieces_in), z).astype(wide)
    up_piece = jnp.concatenate(
        [
            lax.dynamic_slice_in_dim(up_weight, at * width + mine * quarter, quarter, 1)
            for at in range(4)
        ],
        axis=1,
    )
    up_piece, vectors, *moved = pin((up_piece, vectors, *shards, *slots_in))
    shards, slots_in = moved[:3], moved[3:]
    near_shards = [plane_swap(shard, "near") for shard in shards]
    cotangent, *near_shards = pin((cotangent, *near_shards))
    slots_back = spread(cotangent)
    around = (
        sections
        + shards
        + near_shards
        + [plane_swap(shard, "core") for shard in shards]
        + [plane_swap(shard, "core") for shard in near_shards]
    )
    around_places = jnp.stack(
        [kind * 4 + z for kind in range(4)]
        + [kind * 4 + (z - step) % 4 for kind in classes for step in range(1, 4)]
    )
    up_own = lax.all_gather(up_piece, "fsdp", axis=0, tiled=True)
    down_piece = lax.dynamic_slice_in_dim(down_weight, mine * quarter, quarter, 0)
    gain_first, shift_first, qbias, vbias, obias, gain_second, shift_second, dbias = (
        vectors[:, at * quarter : (at + 1) * quarter].reshape(1, width) for at in range(8)
    )
    ubias = vectors[:, 8 * quarter :].reshape(4, 4, quarter)
    ubias = jnp.concatenate(
        [
            chosen(kind, [ubias[:, at] for at in range(4)]).reshape(1, width)
            for kind in classes
        ],
        axis=0,
    )

    rows_in, normed_low, queries, key_rows, value_rows, weights = front(
        around_places,
        slots_in,
        jnp.concatenate([gain_first, shift_first, qbias, vbias], axis=0),
        around,
    )
    up_own, queries = pin((up_own, queries))
    up_near, up_core = plane_swap(up_own, "near"), plane_swap(up_own, "core")
    attended, logs = attend(place, queries, key_rows, value_rows, seq_count, 0, 9, [])
    down_piece, up_core, up_near, attended = pin((down_piece, up_core, up_near, attended))
    down_own = lax.all_gather(down_piece, "fsdp", axis=0, tiled=True)
    logs = logs.T.reshape(64, 2, rows)
    logs_one, logs_two = logs[:5], logs[5:9]
    middle, normed_two_low = by_rows(
        middle_kernel,
        "middle",
        rows,
        width,
        ([rows_in, attended], []),
        [jnp.concatenate([obias, gain_second, shift_second], axis=0)],
        [weights],
        [wide, low],
        0,
        [(4,) + section.shape],
        1,
    )
    up_slots = [up_own, up_near, up_core, plane_swap(up_near, "core")]
    active, slopes = [None] * 4, [None] * 4

    def up(first):
        outs = by_rows(
            up_kernel,
            "up",
            rows,
            width,
            ([normed_two_low], []),
            [jnp.concatenate([ubias[first : first + 1], ubias[first + 2 : first + 3]], axis=0)],
            [up_slots[first], up_slots[first + 2]],
            [low] * 4,
            0,
            [(2,) + area],
            2,
        )
        active[first], active[first + 2], slopes[first], slopes[first + 2] = outs

    up(0)
    up_slots[3], slots_back[3], active[0], active[2] = pin(
        (up_slots[3], slots_back[3], active[0], active[2])
    )
    upstream_low = turn(slots_back)
    up(1)
    down_own, *active = pin((down_own, *active))
    down_near, down_core = plane_swap(down_own, "near"), plane_swap(down_own, "core")

    def turned_product(left, right):
        return product(left, right, (0, 0)).astype(low)

    down_terms = [turned_product(active[slot], upstream_low) for slot in (3, 2)]
    upstream_low, *down_terms = pin((upstream_low, *down_terms))
    down_terms += [turned_product(active[slot], upstream_low) for slot in (1, 0)]
    down_terms = down_terms[::-1]
    down_far, down_far_two = reduce_core(down_terms)
    upstream_low, *down_terms = pin((upstream_low, *down_terms))
    hidden_low = [None] * 4

    def hidden(first, upstream):
        hidden_low[first], hidden_low[first + 2], sums = by_rows(
            hidden_kernel,
            "hidden",
            rows,
            width,
            ([upstream], [slopes[first], slopes[first + 2]]),
            [],
            [down_slots[first], down_slots[first + 2]],
            [low] * 2,
            3,
            [(2,) + area],
            2,
        )
        return sums

    down_near, upstream_low = pin((down_near, upstream_low))
    down_slots = [down_own, down_near, down_core, plane_swap(down_near, "core")]
    sums_even = hidden(0, upstream_low)
    down_second = low_sum(down_terms[1], down_far_two)
    upstream_late, sums_even, down_second = pin((upstream_low, sums_even, down_second))
    down_close = plane_swap(down_second, "near")
    sums_odd = hidden(1, upstream_late)
    hidden_sums = jnp.stack(
        [sums_even[0], sums_odd[0], sums_even[1], sums_odd[1], sums_even[2]]
    )
    down_far, *hidden_low = pin((down_far, *hidden_low))
    up_terms = [turned_product(normed_two_low, hidden_low[slot]) for slot in (3, 2)]
    normed_two_low, *up_terms = pin((normed_two_low, *up_terms))
    up_terms += [turned_product(normed_two_low, hidden_low[slot]) for slot in (1, 0)]
    up_terms = up_terms[::-1]
    up_far, up_far_two = reduce_core(up_terms)
    up_second = low_sum(up_terms[1], up_far_two)
    down_first = low_sum(down_terms[0], down_far, down_close)
    up_second, up_far, down_first, moved, *hidden_low = pin(
        (up_second, up_far, down_first, up_terms[0], *hidden_low)
    )
    up_terms[0] = moved
    down_shard = scatter_rows(down_first)
    up_close = plane_swap(up_second, "near")
    middle_grad, middle_low, grad_low, back_sums = by_rows(
        back_kernel,
        "back",
        rows,
        width,
        ([upstream_low, middle], hidden_low),
        [gain_second],
        up_slots + [weights],
        [wide, low, low],
        3,
        [(4,) + area, (4,) + section.shape],
        5,
    )
    out_term = turned_product(attended, middle_low)
    up_first = low_sum(up_terms[0], up_far, up_close)
    up_pieces = cut_pieces(up_first, z)
    grad_low, out_term, *up_pieces = pin((grad_low, out_term, *up_pieces))
    up_pieces = send_pieces(up_pieces)
    in_grads = attend_back(
        place, queries, key_rows, value_rows, grad_low, attended, logs_one, seq_count, 0, 5, []
    )
    down_shard, up_pieces[1], *in_grads = pin((down_shard, up_pieces[1], *in_grads))
    down_whole = low_sum(down_shard, plane_swap(down_shard, "other"))
    in_grads = attend_back(
        place,
        queries,
        key_rows,
        value_rows,
        grad_low,
        attended,
        logs_two,
        seq_count,
        5,
        4,
        in_grads,
    )
    down_whole, *moved = pin((down_whole, *up_pieces, *in_grads))
    up_pieces, in_grads = moved[:4], moved[4:]
    down_beside = plane_swap(down_whole, "near")
    up_shard = low_sum(*up_pieces)
    up_other = plane_swap(up_shard, "other")
    in_terms = [turned_product(normed_low, grad) for grad in in_grads]
    section_grads = in_terms + [out_term]
    sections_mine = [chosen(kind, section_grads) for kind in classes]
    far, far_two = reduce_core(sections_mine)
    second = low_sum(sections_mine[1], far_two)
    second, far, middle, *in_grads = pin((second, far, middle, *in_grads))
    query_low, key_low, value_low = in_grads
    close = plane_swap(second, "near")
    result_slots = by_rows(
        down_kernel,
        "down",
        rows,
        width,
        ([middle], active),
        [dbias],
        down_slots,
        [None],
        0,
        [(4,) + area],
        4,
    )
    first = low_sum(sections_mine[0], far, close)
    first, up_other, down_beside, query_low, *result_slots = pin(
        (first, up_other, down_beside, query_low, *result_slots)
    )
    up_whole = low_sum(up_shard, up_other)
    up_beside = plane_swap(up_whole, "near")
    down_parts = share_by_core(down_whole, down_beside)
    shard = scatter_rows(first)
    outputs = exchange(result_slots)
    *input_slots, last_sums = by_rows(
        last_kernel,
        "last",
        rows,
        width,
        ([query_low, key_low, value_low, rows_in, middle_grad], []),
        [gain_first],
        [weights],
        [None],
        4,
        [(12,) + section.shape],
        3,
    )
    moved = pin((*input_slots, *outputs, *down_parts, up_beside))
    input_slots, outputs = exchange(moved[:4]), moved[4:8]
    down_parts, up_beside = moved[8:12], moved[12]
    up_parts = share_by_core(up_whole, up_beside)

    back_sums = jnp.concatenate([hidden_sums, back_sums], axis=0)
    back_sums = jnp.sum(back_sums, axis=1)
    last_sums = jnp.sum(last_sums, axis=1)
    hidden_sums = [back_sums[slot].reshape(4, quarter) for slot in range(4)]
    hidden_sums = jnp.stack(
        [chosen(slot_of[kind], hidden_sums) for kind in range(4)], axis=1
    ).reshape(4, 4 * quarter)
    totals = swap_sum(
        scatter_vector(
            jnp.concatenate(
                [back_sums[at].reshape(4, quarter) for at in range(4, 8)]
                + [last_sums[at].reshape(4, quarter) for at in range(4)]
                + [hidden_sums],
                axis=1,
            ),
            z,
        ),
        1,
    )
    shard, totals, *input_slots = pin((shard, totals, *input_slots))
    section_whole = low_sum(shard, plane_swap(shard, "other"))
    totals = swap_sum(totals, 2)
    section_whole, totals = pin((section_whole, totals))
    section_parts = share_out(section_whole)
    totals = swap_sum(totals, 4)
    outputs = collect(outputs, low)
    input_gradient = collect(input_slots, wide)
    (up_sum,) = assemble(
        class_places,
        up_parts,
        [
            [(0, at * quarter, at * width + kind * quarter, quarter) for at in range(4)]
            for kind in range(4)
        ],
        [up_weight.shape],
    )
    down_sum = settle(class_places, down_parts, wide).reshape(down_weight.shape)
    moved = pin((*section_parts, outputs, input_gradient, totals, up_sum, down_sum))
    section_parts = moved[:4]
    outputs, input_gradient, totals, up_sum, down_sum = moved[4:]
    in_sum, out_sum = assemble(
        class_places,
        section_parts,
        [[(0, 0, kind * width, width)] for kind in range(3)] + [[(1, 0, 0, width)]],
        [project_in.shape, project_out.shape],
    )
    (
        dbias_sum,
        gain_two_sum,
        shift_two_sum,
        obias_sum,
        gain_one_sum,
        shift_one_sum,
        qbias_sum,
        vbias_sum,
    ) = (totals[at * quarter : (at + 1) * quarter] for at in range(8))
    ubias_sum = totals[8 * quarter :]
    return (
        outputs,
        input_gradient,
        gain_one_sum,
        shift_one_sum,
        in_sum,
        qbias_sum,
        vbias_sum,
        out_sum,
        obias_sum,
        gain_two_sum,
        shift_two_sum,
        up_sum,
        ubias_sum,
        down_sum,
        dbias_sum,
    )


def solution(mesh):
    sizes = dict(mesh.shape)
    exchanged = sizes["dp"] == 2 and sizes["fsdp"] == 4 and sizes["ctx"] == 4
    per_device = per_device_exchanged if exchanged else per_device_gathered
    return jax.shard_map(
        per_device,
        mesh=mesh,
        in_specs=(
            P(("dp", "fsdp"), "ctx", None),
            P(("dp", "fsdp"), "ctx", None),
            P("fsdp"),
            P("fsdp"),
            P("fsdp", None),
            P("fsdp"),
            P("fsdp"),
            P("fsdp", None),
            P("fsdp"),
            P("fsdp"),
            P("fsdp"),
            P("fsdp", None),
            P("fsdp"),
            P("fsdp", None),
            P("fsdp"),
        ),
        out_specs=(
            P(("dp", "fsdp"), "ctx", None),
            P(("dp", "fsdp"), "ctx", None),
            P("fsdp"),
            P("fsdp"),
            P("fsdp", None),
            P("fsdp"),
            P("fsdp"),
            P("fsdp", None),
            P("fsdp"),
            P("fsdp"),
            P("fsdp"),
            P("fsdp", None),
            P("fsdp"),
            P("fsdp", None),
            P("fsdp"),
        ),
        check_vma=False,
    )
```
